32 devices in a mesh: dom: 8 (over z, x), grp: 4 (over y, core).
Axes of the slice: x: 2, y: 2, z: 4, core: 2. Of those that a mesh axis runs over, the one named last changes fastest.
Arguments:
- node_feats: bfloat16 [8192, 1024], P(('dom', 'grp')), may hold values from -6 to 6
- weight: bfloat16 [1024, 512], replicated, may hold values from -0.1875 to 0.1875
- bias: float32 [512], replicated, may hold values from -4 to 4
- cotangent: bfloat16 [8192, 512], P(('dom', 'grp')), may hold values from -6 to 6
- tile_bank: bfloat16 [16, 128, 128], replicated, may hold values from -0.125 to 0.125
- local_cols: int32 [8, 8, 16], P('dom'), may hold values from 0 to 7
- local_banks: int32 [8, 8, 16], P('dom'), may hold values from 0 to 15
- published: int32 [8, 4], P('dom'), may hold values from 0 to 7, as said below
- send_table: int32 [8, 8, 2], replicated, may hold values from -1 to 3, as said below
- halo_rows: int32 [8, 8, 2], P('dom'), may hold values from 0 to 7
- halo_banks: int32 [8, 8, 2], P('dom'), may hold values from 0 to 15
Outputs:
- activations: bfloat16 [8192, 512], P(('dom', 'grp'))
- grad_nodes: bfloat16 [8192, 1024], P(('dom', 'grp'))
- grad_weight: float32 [1024, 512], replicated
- grad_bias: float32 [512], replicated
The draws below stay inside these ranges and needn't reach their ends.
Inputs may be any that keep to these rules, and one draw needn't show every extreme that they name: `published`: the 4 entries of a partition are distinct block numbers of that partition; 0 and 7 each appear in some partition's list. `send_table`: entry s of the pair (src, p) is -1 or an index into the offered list of src; the live entries of a pair come first and are distinct; a pair (p, p) has none; some pair has all 2 entries live.
All inputs are finite; a program needn't handle non-finite values.
Results may differ from the reference program's by a relative error of at most 0.019.
The reference program's roundings to bfloat16 on the way (of `aggregated`, `grad_pre` and `grad_agg`) count: a program that leaves them out, or rounds other values in their place, can miss the bound.
Values may be sent and summed in bfloat16 or wider, within the bound.
No kernel may reach another device: no remote copies, remote signals or barrier semaphores. Data moves between devices by JAX's collectives and lax.ppermute only.
A program may use at most 64 MiB of HBM per device.

```python
import jax
import jax.numpy as jnp
from jax import lax

EMBED = 1024
HIDDEN_SIZE = 512
TILE = 128
LOCAL_TILES = 16
BANK_TILES = 16
PUB_BLOCKS = 4
SLOTS = 2
DOMAINS = 8
BLOCKS = 8
NODES = 8192


def draw_published(key, part):
    key_perm, key_pick = jax.random.split(key, 2)
    part_keys = jax.random.split(key_perm, DOMAINS)

    def offered(single):
        return jax.random.permutation(single, BLOCKS)[:PUB_BLOCKS]
    lists = jax.vmap(offered)(part_keys).astype(jnp.int32)
    chosen = jax.random.randint(key_pick, (), 0, DOMAINS)
    after = (chosen + 1) % DOMAINS
    domain_ids = jnp.arange(DOMAINS)[:, None]
    shift_top = (BLOCKS - 1 - lists[:, :1]) % BLOCKS
    shift_low = (BLOCKS - lists[:, :1]) % BLOCKS
    shifts = jnp.where(domain_ids == chosen, shift_top, jnp.where(domain_ids == after, shift_low, 0))
    return ((lists + shifts) % BLOCKS).astype(jnp.int32)


def draw_send_table(key, part):
    key_heavy, key_light, key_offset, key_pick = jax.random.split(key, 4)
    source = jnp.arange(DOMAINS)[:, None]
    target = jnp.arange(DOMAINS)[None, :]
    chosen = jax.random.randint(key_pick, (), 0, DOMAINS)
    heavy_rows = jax.random.randint(key_heavy, (DOMAINS, 1), 0, 2)
    heavy_rows = jnp.maximum(heavy_rows, (source == chosen).astype(jnp.int32))
    light_counts = jax.random.randint(key_light, (DOMAINS, DOMAINS), 0, SLOTS)
    counts = jnp.where(heavy_rows > 0, SLOTS, light_counts)
    counts = jnp.where(source == target, 0, counts)
    offsets = jax.random.randint(key_offset, (DOMAINS, DOMAINS), 0, PUB_BLOCKS)
    forced = (source == chosen) & (target == (chosen + 1) % DOMAINS)
    offsets = jnp.where(forced, PUB_BLOCKS - 1, offsets)
    slot_index = jnp.arange(SLOTS)[None, None, :]
    pair_table = (offsets[:, :, None] + slot_index) % PUB_BLOCKS
    return jnp.where(slot_index < counts[:, :, None], pair_table, -1).astype(jnp.int32)


def plant(array, stream_key, low, high):
    longest = array.shape.index(max(array.shape))
    spots = []
    for shift in (0, 1):
        where = [jax.random.randint(jax.random.fold_in(stream_key, axis), (), 0, length) for axis, length in enumerate(array.shape)]
        where[longest] = (where[longest] + shift) % array.shape[longest]
        spots.append(tuple(where))
    return array.at[spots[0]].set(low).at[spots[1]].set(high)


def levels(rng, extent, cuts, low, largest):
    level, own = 1.0, jax.random.fold_in(rng, 6)
    for dim, shards_of in cuts:
        steps = jnp.exp(jax.random.uniform(jax.random.fold_in(own, dim), (shards_of,), jnp.float32, low / len(cuts), largest / len(cuts)))
        level = level * jnp.repeat(steps, extent[dim] // shards_of).reshape([-1 if axis == dim else 1 for axis in range(len(extent))])
    return level


def scatter_about(rng, extent, spread, most, cuts=(), kind=jnp.bfloat16):
    entries = spread * jax.random.normal(rng, extent, jnp.float32)
    if cuts:
        entries = entries * levels(rng, extent, cuts, -0.22, 0.18)
    return jnp.clip(entries, -most, most).astype(kind)


def setup_inputs(seed: int = 0) -> dict:
    key_of = jax.random.split(jax.random.key(seed), 12)
    return {
        "node_feats": scatter_about(key_of[0], (NODES, EMBED), 1.0, 6.0, ((0, 32),)),
        "weight": scatter_about(key_of[1], (EMBED, HIDDEN_SIZE), EMBED ** -0.5, 0.1875),
        "bias": scatter_about(key_of[2], (HIDDEN_SIZE,), 1.0, 4.0, (), jnp.float32),
        "cotangent": scatter_about(key_of[3], (NODES, HIDDEN_SIZE), 1.0, 6.0, ((0, 32),)),
        "tile_bank": scatter_about(key_of[4], (BANK_TILES, TILE, TILE), (TILE * (LOCAL_TILES + 2)) ** -0.5, 0.125),
        "local_cols": plant(jax.random.randint(key_of[5], (DOMAINS, BLOCKS, LOCAL_TILES), 0, BLOCKS), jax.random.fold_in(key_of[5], 1), 0, BLOCKS - 1).astype(jnp.int32),
        "local_banks": plant(jax.random.randint(key_of[6], (DOMAINS, BLOCKS, LOCAL_TILES), 0, BANK_TILES), jax.random.fold_in(key_of[6], 1), 0, BANK_TILES - 1).astype(jnp.int32),
        "published": draw_published(jax.random.fold_in(key_of[11], 71), 0),
        "send_table": draw_send_table(jax.random.fold_in(key_of[11], 71), 0),
        "halo_rows": plant(jax.random.randint(key_of[9], (DOMAINS, DOMAINS, SLOTS), 0, BLOCKS), jax.random.fold_in(key_of[9], 1), 0, BLOCKS - 1).astype(jnp.int32),
        "halo_banks": plant(jax.random.randint(key_of[10], (DOMAINS, DOMAINS, SLOTS), 0, BANK_TILES), jax.random.fold_in(key_of[10], 1), 0, BANK_TILES - 1).astype(jnp.int32),
    }


def block_view(whole):
    return whole.reshape(DOMAINS, BLOCKS, TILE, whole.shape[1])


def reference(node_feats, weight, bias, cotangent, tile_bank, local_cols, local_banks, published, send_table, halo_rows, halo_banks):
    feat_blocks = block_view(node_feats)
    bank_wide = tile_bank.astype(jnp.float32)
    embed_width = node_feats.shape[1]
    sources = jnp.broadcast_to(jnp.arange(DOMAINS, dtype=jnp.int32)[:, None], (DOMAINS, SLOTS))
    domain_ids = jnp.arange(DOMAINS, dtype=jnp.int32)

    def forward_part(domain):
        own_blocks = feat_blocks[domain].astype(jnp.float32)
        cols_here = local_cols[domain]
        banks_here = local_banks[domain]

        def add_tiles(position, running):
            column = lax.dynamic_index_in_dim(cols_here, position, 1, keepdims=False)
            bank_ids = lax.dynamic_index_in_dim(banks_here, position, 1, keepdims=False)
            return running + jnp.einsum("rij,rjf->rif", bank_wide[bank_ids], own_blocks[column])

        running = lax.fori_loop(0, LOCAL_TILES, add_tiles, jnp.zeros((BLOCKS, TILE, embed_width), jnp.float32))
        incoming = send_table[:, domain, :]
        live_in = (incoming >= 0).astype(jnp.float32)[:, :, None, None]
        block_ids = published[sources, jnp.maximum(incoming, 0)]
        remote = feat_blocks[sources, block_ids].astype(jnp.float32)
        halo_terms = jnp.einsum("dsij,dsjf->dsif", bank_wide[halo_banks[domain]], remote) * live_in
        running = running + jax.ops.segment_sum(halo_terms.reshape(DOMAINS * SLOTS, TILE, embed_width), halo_rows[domain].reshape(-1), num_segments=BLOCKS)
        return running.astype(jnp.bfloat16)

    aggregated = lax.map(forward_part, domain_ids).reshape(NODES, embed_width)
    pre_act = jnp.dot(aggregated, weight, preferred_element_type=jnp.float32) + bias.astype(jnp.float32)
    activations = jnp.maximum(pre_act, 0.0).astype(jnp.bfloat16)
    grad_pre = jnp.where(pre_act > 0, cotangent.astype(jnp.float32), 0.0).astype(jnp.bfloat16)
    norm_scale = NODES ** -0.5
    grad_weight = jnp.dot(aggregated.T, grad_pre, preferred_element_type=jnp.float32) * norm_scale
    grad_bias = jnp.sum(grad_pre.astype(jnp.float32), axis=0) * norm_scale
    grad_agg = jnp.dot(grad_pre, weight.T, preferred_element_type=jnp.float32).astype(jnp.bfloat16)
    grad_blocks = block_view(grad_agg)

    def backward_part(domain):
        own_grads = grad_blocks[domain].astype(jnp.float32)
        cols_here = local_cols[domain]
        banks_here = local_banks[domain]

        def add_tiles(position, running):
            column = lax.dynamic_index_in_dim(cols_here, position, 1, keepdims=False)
            bank_ids = lax.dynamic_index_in_dim(banks_here, position, 1, keepdims=False)
            contrib = jnp.einsum("rji,rjf->rif", bank_wide[bank_ids], own_grads)
            return running + jax.ops.segment_sum(contrib, column, num_segments=BLOCKS)

        running = lax.fori_loop(0, LOCAL_TILES, add_tiles, jnp.zeros((BLOCKS, TILE, embed_width), jnp.float32))
        outgoing = send_table[domain]
        live_out = (outgoing >= 0).astype(jnp.float32)[:, :, None, None]
        targets = jnp.where(outgoing >= 0, published[domain][jnp.maximum(outgoing, 0)], BLOCKS).astype(jnp.int32)
        reader_rows = halo_rows[:, domain, :]
        reader_banks = halo_banks[:, domain, :]
        read_grads = grad_blocks[sources, reader_rows].astype(jnp.float32)
        back_terms = jnp.einsum("dsji,dsjf->dsif", bank_wide[reader_banks], read_grads) * live_out
        back_total = jax.ops.segment_sum(back_terms.reshape(DOMAINS * SLOTS, TILE, embed_width), targets.reshape(-1), num_segments=BLOCKS + 1)
        running = running + back_total[:BLOCKS]
        return running.astype(jnp.bfloat16)

    grad_nodes = lax.map(backward_part, domain_ids).reshape(NODES, embed_width)
    return activations, grad_nodes, grad_weight, grad_bias
```

```python
import functools

import jax
import jax.numpy as jnp
from jax import lax
from jax.experimental import pallas as pl
from jax.experimental.pallas import tpu as pltpu
from jax.sharding import PartitionSpec as P

VMEM = pl.BlockSpec(memory_space=pltpu.VMEM)
SMEM = pl.BlockSpec(memory_space=pltpu.SMEM)
EXTRA = 16
F32 = jnp.float32
BF16 = jnp.bfloat16


def call(body, out_shape, specs, scratch=(), flops=0, nbytes=0, name=None):
    return pl.pallas_call(
        body,
        out_shape=out_shape,
        in_specs=specs,
        out_specs=jax.tree.map(lambda _: VMEM, out_shape),
        scratch_shapes=list(scratch),
        compiler_params=pltpu.CompilerParams(vmem_limit_bytes=48 * 1024 * 1024),
        cost_estimate=pl.CostEstimate(flops=flops, bytes_accessed=nbytes, transcendentals=0),
        name=name,
    )


def dot(a, b):
    return jnp.dot(a, b, preferred_element_type=F32)


def split_two(value):
    high = value.astype(BF16)
    return high, (value - high.astype(F32)).astype(BF16)


def pick_blocks(pub_at, out_at, tab, x, out):
    for i in range(out.shape[0]):
        block = tab[pub_at + jnp.maximum(tab[out_at + i], 0)]
        out[i] = x[block]


def local_sum(per_row, cols_at, banks_at, tab, bank, x, out):
    tile = bank.shape[1]
    pair = 2 if per_row % 2 == 0 else 1

    @pl.loop(0, out.shape[0])
    def _(r):
        acc = jnp.zeros(out.shape[1:], F32)
        for k in range(0, per_row, pair):
            at = [r * per_row + k + j for j in range(pair)]
            left = jnp.concatenate([bank[tab[banks_at + a]] for a in at], axis=1)
            right = jnp.concatenate([x[tab[cols_at + a]] for a in at], axis=0)
            acc += dot(left, right)
        out[r] = acc


def add_halo(in_at, rows_at, banks_at, tab, bank, recv, local, out, acc):
    acc[...] = local[...]

    @pl.loop(0, recv.shape[0])
    def _(i):
        @pl.when(tab[in_at + i] >= 0)
        def _():
            row = tab[rows_at + i]
            acc[row] += dot(bank[tab[banks_at + i]], recv[i])

    out[...] = acc[...].astype(BF16)


def dense(agg, weight, bias, cot, act, grad):
    groups, _, narrow = agg.shape
    hidden = cot.shape[1]
    wide = hidden // groups
    pre = jnp.broadcast_to(bias[...], cot.shape)
    total = dot(agg[0], weight[:narrow])
    for s in range(1, groups):
        total += dot(agg[s], weight[s * narrow : (s + 1) * narrow])
    pre = total + pre
    act[...] = jnp.maximum(pre, 0.0).astype(BF16)
    masked = jnp.where(pre > 0, cot[...].astype(F32), 0.0).astype(BF16)
    for s in range(groups):
        grad[s] = masked[:, s * wide : (s + 1) * wide]


def back_halo(me_at, masks, in_at, rows_at, banks_at, slots, tab, bank_t, *refs):
    parts, (terms, own) = refs[: len(masks)], refs[len(masks) :]
    group = tab[me_at]
    tile = bank_t.shape[1]
    per = parts[0].shape[1] // tile
    total = jnp.zeros((1, own.shape[2]), F32)
    for mask, part in zip(masks, parts):
        owner = jnp.bitwise_xor(group, mask)
        piece = part[group]
        total += jnp.sum(piece.astype(F32), axis=0, keepdims=True)
        for j in range(per):
            own[owner * per + j] = piece[j * tile : (j + 1) * tile]
    high, low = split_two(total)
    tail = jnp.concatenate(
        [high.astype(F32), low.astype(F32), jnp.zeros((EXTRA - 2, own.shape[2]), F32)], axis=0
    ).astype(BF16)
    for d in range(terms.shape[0]):
        for s in range(slots):
            i = d * slots + s
            live = (tab[in_at + i] >= 0).astype(F32)
            value = dot(bank_t[tab[banks_at + i]], own[tab[rows_at + i]]) * live
            terms[d, s * tile : (s + 1) * tile] = value.astype(BF16)
        terms[d, slots * tile :] = tail


def back_local(per_row, cols_at, banks_at, tab, bank_t, own, out):
    out[...] = jnp.zeros_like(out)

    @pl.loop(0, own.shape[0])
    def _(r):
        right = own[r]
        for k in range(per_row):
            at = r * per_row + k
            out[tab[cols_at + at]] += dot(bank_t[tab[banks_at + at]], right)


def weight_slice(me_at, masks, tab, agg, *refs):
    parts, out = refs[: len(masks)], refs[len(masks)]
    group = tab[me_at]
    rows = parts[0].shape[1]
    total = None
    for mask, part in zip(masks, parts):
        owner = jnp.bitwise_xor(group, mask)
        left = agg[pl.ds(pl.multiple_of(owner * rows, rows), rows)]
        right = jnp.concatenate([part[s] for s in range(part.shape[0])], axis=1)
        term = lax.dot_general(left, right, (((0,), (0,)), ((), ())), preferred_element_type=F32)
        total = term if total is None else total + term
    out[...] = total.astype(BF16)


def finish_nodes(scale, slots, pub_at, out_at, tab, recv, local, out, acc):
    tile = local.shape[1]
    groups = out.shape[0]
    per = local.shape[0] // groups
    acc[...] = local[...]
    total = jnp.zeros((EXTRA, local.shape[2]), F32)
    for d in range(recv.shape[0]):
        total += recv[d, slots * tile :].astype(F32)
        for s in range(slots):
            i = d * slots + s
            entry = tab[out_at + i]

            @pl.when(entry >= 0)
            def _(d=d, s=s, entry=entry):
                block = tab[pub_at + jnp.maximum(entry, 0)]
                acc[block] += recv[d, s * tile : (s + 1) * tile].astype(F32)

    high, low = split_two((total[0:1] + total[1:2]) * scale)
    tail = jnp.concatenate(
        [high.astype(F32), low.astype(F32), jnp.zeros((EXTRA - 2, local.shape[2]), F32)], axis=0
    ).astype(BF16)
    for g in range(groups):
        for j in range(per):
            out[g, j * tile : (j + 1) * tile] = acc[g * per + j].astype(BF16)
        out[g, per * tile :] = tail


def node_grads(hid, weight, out, bias_out):
    groups = hid.shape[0]
    rows = out.shape[0]
    left = jnp.concatenate([hid[s, :rows] for s in range(groups)], axis=1)
    out[...] = lax.dot_general(
        left, weight[...], (((1,), (1,)), ((), ())), preferred_element_type=F32
    ).astype(BF16)
    tail = jnp.concatenate([hid[s, rows:] for s in range(groups)], axis=1).astype(F32)
    bias_out[...] = tail[0:1] + tail[1:2]


def place_weight(me_at, masks, tab, *refs):
    parts, out = refs[: len(masks)], refs[len(masks)]
    group = tab[me_at]
    rows = parts[0].shape[0]
    for mask, part in zip(masks, parts):
        owner = jnp.bitwise_xor(group, mask)
        out[pl.ds(pl.multiple_of(owner * rows, rows), rows)] = part[...].astype(F32)


def spread(value, axis):
    size = lax.axis_size(axis)
    parts, masks = [value], [0]
    bit = size // 2
    while bit:
        pairs = [(i, i ^ bit) for i in range(size)]
        parts = parts + [lax.ppermute(part, axis, pairs) for part in parts]
        masks = masks + [mask ^ bit for mask in masks]
        bit //= 2
    return parts, masks


def per_device(
    node_feats,
    weight,
    bias,
    cotangent,
    tile_bank,
    local_cols,
    local_banks,
    published,
    send_table,
    halo_rows,
    halo_banks,
):
    domains = lax.axis_size("dom")
    groups = lax.axis_size("grp")
    domain_index = lax.axis_index("dom")
    rows_here, embed = node_feats.shape
    hidden = weight.shape[1]
    tile = tile_bank.shape[1]
    slots = send_table.shape[2]
    per_row = local_cols.shape[2]
    part_rows = rows_here * groups
    blocks = part_rows // tile
    narrow = embed // groups
    wide = hidden // groups
    pairs = domains * slots
    per_device_blocks = rows_here // tile

    outgoing = lax.dynamic_index_in_dim(send_table, domain_index, 0, keepdims=False)
    incoming = lax.dynamic_index_in_dim(send_table, domain_index, 1, keepdims=False)
    pieces = [
        local_cols[0],
        local_banks[0],
        published[0],
        outgoing,
        incoming,
        halo_rows[0],
        halo_banks[0],
        lax.axis_index("grp").astype(jnp.int32),
    ]
    pieces = [piece.reshape(-1) for piece in pieces]
    places = [0]
    for piece in pieces:
        places.append(places[-1] + piece.shape[0])
    cols_at, banks_at, pub_at, out_at, in_at, rows_at, hbanks_at, me_at = places[:8]
    tab = jnp.concatenate(pieces)
    bank_t = jnp.swapaxes(tile_bank, 1, 2)

    feats = lax.all_to_all(
        node_feats.reshape(rows_here, groups, narrow), "grp", split_axis=1, concat_axis=0, tiled=False
    )
    feats = feats.reshape(blocks, tile, narrow)
    offered = call(
        functools.partial(pick_blocks, pub_at, out_at),
        jax.ShapeDtypeStruct((pairs, tile, narrow), BF16),
        [SMEM, VMEM],
        nbytes=2 * pairs * tile * narrow * 2,
        name="pick_blocks",
    )(tab, feats)
    arrived = lax.all_to_all(
        offered.reshape(domains, slots * tile, narrow), "dom", split_axis=0, concat_axis=0, tiled=True
    ).reshape(pairs, tile, narrow)
    local = call(
        functools.partial(local_sum, per_row, cols_at, banks_at),
        jax.ShapeDtypeStruct((blocks, tile, narrow), F32),
        [SMEM, VMEM, VMEM],
        flops=2 * blocks * per_row * tile * tile * narrow,
        nbytes=blocks * tile * narrow * 6,
        name="local_sum",
    )(tab, tile_bank, feats)
    agg = call(
        functools.partial(add_halo, in_at, rows_at, hbanks_at),
        jax.ShapeDtypeStruct((blocks, tile, narrow), BF16),
        [SMEM, VMEM, VMEM, VMEM],
        [pltpu.VMEM((blocks, tile, narrow), F32)],
        flops=2 * pairs * tile * tile * narrow,
        nbytes=blocks * tile * narrow * 8,
        name="add_halo",
    )(tab, tile_bank, arrived, local)
    agg = agg.reshape(part_rows, narrow)
    mine = lax.all_to_all(
        agg.reshape(groups, rows_here, narrow), "grp", split_axis=0, concat_axis=0, tiled=True
    )
    activations, grad = call(
        dense,
        (
            jax.ShapeDtypeStruct((rows_here, hidden), BF16),
            jax.ShapeDtypeStruct((groups, rows_here, wide), BF16),
        ),
        [VMEM] * 4,
        flops=2 * rows_here * embed * hidden,
        nbytes=embed * hidden * 2 + rows_here * (embed + 3 * hidden) * 2,
        name="dense",
    )(mine, weight, bias.reshape(1, hidden), cotangent)

    grads, masks = spread(grad, "grp")
    terms, own = call(
        functools.partial(back_halo, me_at, masks, in_at, rows_at, hbanks_at, slots),
        (
            jax.ShapeDtypeStruct((domains, slots * tile + EXTRA, wide), BF16),
            jax.ShapeDtypeStruct((blocks, tile, wide), BF16),
        ),
        [SMEM, VMEM] + [VMEM] * len(masks),
        flops=2 * pairs * tile * tile * wide,
        nbytes=(pairs + blocks) * tile * wide * 2,
        name="back_halo",
    )(tab, bank_t, *grads)
    returned = lax.all_to_all(terms, "dom", split_axis=0, concat_axis=0, tiled=True)
    part = call(
        functools.partial(weight_slice, me_at, masks),
        jax.ShapeDtypeStruct((narrow, hidden), BF16),
        [SMEM, VMEM] + [VMEM] * len(masks),
        flops=2 * part_rows * narrow * hidden,
        nbytes=part_rows * (narrow + hidden) * 2,
        name="weight_slice",
    )(tab, agg, *grads)
    shares = lax.all_to_all(
        part.reshape(domains, narrow // domains, hidden), "dom", split_axis=0, concat_axis=0, tiled=True
    )
    back = call(
        functools.partial(back_local, per_row, cols_at, banks_at),
        jax.ShapeDtypeStruct((blocks, tile, wide), F32),
        [SMEM, VMEM, VMEM],
        flops=2 * blocks * per_row * tile * tile * wide,
        nbytes=blocks * tile * wide * 6,
        name="back_local",
    )(tab, bank_t, own)
    norm_scale = float(rows_here * groups * domains) ** (-0.5)
    summed = (jnp.sum(shares.astype(F32), axis=0) * norm_scale).astype(BF16)
    whole = lax.all_to_all(
        jnp.broadcast_to(summed, (domains,) + summed.shape), "dom", split_axis=0, concat_axis=0, tiled=True
    ).reshape(narrow, hidden)

    hid = call(
        functools.partial(finish_nodes, norm_scale, slots, pub_at, out_at),
        jax.ShapeDtypeStruct((groups, rows_here + EXTRA, wide), BF16),
        [SMEM, VMEM, VMEM],
        [pltpu.VMEM((blocks, tile, wide), F32)],
        nbytes=pairs * tile * wide * 2 + blocks * tile * wide * 6,
        name="finish_nodes",
    )(tab, returned, back)
    hid = lax.all_to_all(hid, "grp", split_axis=0, concat_axis=0, tiled=True)
    weights, masks = spread(whole, "grp")
    grad_nodes, grad_bias = call(
        node_grads,
        (
            jax.ShapeDtypeStruct((rows_here, embed), BF16),
            jax.ShapeDtypeStruct((1, hidden), F32),
        ),
        [VMEM, VMEM],
        flops=2 * rows_here * embed * hidden,
        nbytes=embed * hidden * 2 + rows_here * (embed + hidden) * 2,
        name="node_grads",
    )(hid, weight)
    grad_weight = call(
        functools.partial(place_weight, me_at, masks),
        jax.ShapeDtypeStruct((embed, hidden), F32),
        [SMEM] + [VMEM] * len(masks),
        nbytes=embed * hidden * 6,
        name="place_weight",
    )(tab, *weights)
    return (activations, grad_nodes, grad_weight, grad_bias.reshape(hidden))


def solution(mesh):
    in_specs = (
        P(("dom", "grp"), None),
        P(),
        P(),
        P(("dom", "grp"), None),
        P(),
        P("dom", None, None),
        P("dom", None, None),
        P("dom", None),
        P(),
        P("dom", None, None),
        P("dom", None, None),
    )
    out_specs = (P(("dom", "grp"), None), P(("dom", "grp"), None), P(), P())
    return jax.shard_map(
        per_device, mesh=mesh, in_specs=in_specs, out_specs=out_specs, check_vma=False
    )
```

```python
import functools

import jax
import jax.numpy as jnp
from jax import lax
from jax.experimental import pallas as pl
from jax.experimental.pallas import tpu as pltpu
from jax.sharding import PartitionSpec as P

VMEM = pl.BlockSpec(memory_space=pltpu.VMEM)
SMEM = pl.BlockSpec(memory_space=pltpu.SMEM)
EXTRA = 16
F32 = jnp.float32
BF16 = jnp.bfloat16


def call(body, out_shape, specs, scratch=(), flops=0, nbytes=0, name=None, out_specs=None):
    return pl.pallas_call(
        body,
        out_shape=out_shape,
        in_specs=specs,
        out_specs=jax.tree.map(lambda _: VMEM, out_shape) if out_specs is None else out_specs,
        scratch_shapes=list(scratch),
        compiler_params=pltpu.CompilerParams(vmem_limit_bytes=48 * 1024 * 1024),
        cost_estimate=pl.CostEstimate(flops=flops, bytes_accessed=nbytes, transcendentals=0),
        name=name,
    )


def shape(dims, kind):
    return jax.ShapeDtypeStruct(tuple(dims), kind)


def dot(a, b):
    return jnp.dot(a, b, preferred_element_type=F32)


def bias_rows(total):
    high = total.astype(BF16).astype(F32)
    rest = jnp.zeros((EXTRA - 2, total.shape[1]), F32)
    return jnp.concatenate([high, total - high, rest], axis=0).astype(BF16)


def aligned(start, step):
    return pl.ds(pl.multiple_of(start * step, step), step)


def exchange(parts, axis):
    size = lax.axis_size(axis)
    return [
        parts[m] if m == 0 else lax.ppermute(parts[m], axis, [(i, i ^ m) for i in range(size)])
        for m in range(size)
    ]


def spread(value, axis):
    size = lax.axis_size(axis)
    parts, masks = [value], [0]
    bit = size // 2
    while bit:
        pairs = [(i, i ^ bit) for i in range(size)]
        parts = parts + [lax.ppermute(part, axis, pairs) for part in parts]
        masks = masks + [mask ^ bit for mask in masks]
        bit //= 2
    return parts, masks


def split_features(ids, feats, *outs):
    group = ids[1]
    narrow = outs[0].shape[1]
    for m, out in enumerate(outs):
        out[...] = feats[:, aligned(jnp.bitwise_xor(group, m), narrow)]


def pick_blocks(groups, slots, at, tab, *refs):
    parts, (x, *outs) = refs[:groups], refs[groups:]
    domain, group = tab[at["me"]], tab[at["me"] + 1]
    tile = x.shape[1]
    per = x.shape[0] // groups
    for m, part in enumerate(parts):
        owner = jnp.bitwise_xor(group, m)
        for j in range(per):
            x[owner * per + j] = part[j * tile : (j + 1) * tile]
    for m, out in enumerate(outs, 1):
        reader = jnp.bitwise_xor(domain, m)
        for s in range(slots):
            entry = jnp.maximum(tab[at["out"] + reader * slots + s], 0)
            out[s * tile : (s + 1) * tile] = x[tab[at["pub"] + entry]]


def local_sum(per_row, at, tab, bank, x, out):
    pair = 2 if per_row % 2 == 0 else 1

    @pl.loop(0, out.shape[0])
    def _(r):
        acc = jnp.zeros(out.shape[1:], F32)
        for k in range(0, per_row, pair):
            spots = [r * per_row + k + j for j in range(pair)]
            left = jnp.concatenate([bank[tab[at["banks"] + a]] for a in spots], axis=1)
            right = jnp.concatenate([x[tab[at["cols"] + a]] for a in spots], axis=0)
            acc += dot(left, right)
        out[r] = acc


def add_halo(domains, groups, slots, at, tab, bank, local, *refs):
    recv, outs, acc = refs[: domains - 1], refs[domains - 1 : -1], refs[-1]
    domain, group = tab[at["me"]], tab[at["me"] + 1]
    tile = local.shape[1]
    per = local.shape[0] // groups
    acc[...] = local[...]
    for m, block in enumerate(recv, 1):
        source = jnp.bitwise_xor(domain, m)
        for s in range(slots):
            i = source * slots + s

            @pl.when(tab[at["in"] + i] >= 0)
            def _(i=i, s=s, block=block):
                tile_here = bank[tab[at["hbanks"] + i]]
                acc[tab[at["hrows"] + i]] += dot(tile_here, block[s * tile : (s + 1) * tile])

    for m, out in enumerate(outs):
        owner = jnp.bitwise_xor(group, m)
        for j in range(per):
            out[j * tile : (j + 1) * tile] = acc[owner * per + j].astype(BF16)


def dense(groups, ids, weight, bias, cot, *refs):
    parts, (act, grad) = refs[:groups], refs[groups:]
    group = ids[1]
    narrow = parts[0].shape[1]
    wide = cot.shape[1] // groups
    total = None
    for m, part in enumerate(parts):
        term = dot(part[...], weight[aligned(jnp.bitwise_xor(group, m), narrow)])
        total = term if total is None else total + term
    pre = total + bias[...]
    act[...] = jnp.maximum(pre, 0.0).astype(BF16)
    masked = jnp.where(pre > 0, cot[...].astype(F32), 0.0).astype(BF16)
    for s in range(groups):
        grad[s] = masked[:, s * wide : (s + 1) * wide]


def back_halo(masks, slots, at, tab, bank_t, *refs):
    parts, (own, mine, *terms) = refs[: len(masks)], refs[len(masks) :]
    domain, group = tab[at["me"]], tab[at["me"] + 1]
    tile = bank_t.shape[1]
    per = parts[0].shape[1] // tile
    total = jnp.zeros((1, own.shape[2]), F32)
    for mask, part in zip(masks, parts):
        owner = jnp.bitwise_xor(group, mask)
        piece = part[group]
        total += jnp.sum(piece.astype(F32), axis=0, keepdims=True)
        for j in range(per):
            own[owner * per + j] = piece[j * tile : (j + 1) * tile]
    mine[...] = total
    tail = bias_rows(total)
    for m, term in enumerate(terms, 1):
        source = jnp.bitwise_xor(domain, m)
        for s in range(slots):
            i = source * slots + s
            live = (tab[at["in"] + i] >= 0).astype(F32)
            value = dot(bank_t[tab[at["hbanks"] + i]], own[tab[at["hrows"] + i]]) * live
            term[s * tile : (s + 1) * tile] = value.astype(BF16)
        term[slots * tile :] = tail


def back_local(per_row, at, tab, bank_t, own, out):
    out[...] = jnp.zeros_like(out)

    @pl.loop(0, own.shape[0])
    def _(r):
        right = own[r]
        for k in range(per_row):
            spot = r * per_row + k
            out[tab[at["cols"] + spot]] += dot(bank_t[tab[at["banks"] + spot]], right)


def weight_slice(groups, masks, ids, *refs):
    aggs, parts = refs[:groups], refs[groups : groups + len(masks)]
    kept, *outs = refs[groups + len(masks) : -1]
    total = refs[-1]
    domain = ids[0]
    sum_here = None
    for mask, part in zip(masks, parts):
        right = jnp.concatenate([part[s] for s in range(part.shape[0])], axis=1)
        term = lax.dot_general(
            aggs[mask][...], right, (((0,), (0,)), ((), ())), preferred_element_type=F32
        )
        sum_here = term if sum_here is None else sum_here + term
    rows = kept.shape[0]
    for d in range(total.shape[0]):
        total[d] = sum_here[d * rows : (d + 1) * rows]
    kept[...] = total[domain]
    for m, out in enumerate(outs, 1):
        out[...] = total[jnp.bitwise_xor(domain, m)].astype(BF16)


def sum_shares(scale, kept, *refs):
    out = refs[-1]
    total = kept[...]
    for share in refs[:-1]:
        total += share[...].astype(F32)
    out[...] = (total * scale).astype(BF16)


def join_shares(ids, *refs):
    out = refs[-1]
    for m, share in enumerate(refs[:-1]):
        out[jnp.bitwise_xor(ids[0], m)] = share[...]


def finish_nodes(domains, groups, slots, scale, at, tab, local, mine, *refs):
    recv, outs, acc = refs[: domains - 1], refs[domains - 1 : -1], refs[-1]
    domain, group = tab[at["me"]], tab[at["me"] + 1]
    tile = local.shape[1]
    per = local.shape[0] // groups
    acc[...] = local[...]
    total = jnp.zeros((EXTRA, local.shape[2]), F32)
    for m, block in enumerate(recv, 1):
        total += block[slots * tile :].astype(F32)
        reader = jnp.bitwise_xor(domain, m)
        for s in range(slots):
            entry = tab[at["out"] + reader * slots + s]

            @pl.when(entry >= 0)
            def _(s=s, entry=entry, block=block):
                spot = tab[at["pub"] + jnp.maximum(entry, 0)]
                acc[spot] += block[s * tile : (s + 1) * tile].astype(F32)

    tail = bias_rows((mine[...] + total[0:1] + total[1:2]) * scale)
    for m, out in enumerate(outs):
        owner = jnp.bitwise_xor(group, m)
        for j in range(per):
            out[j * tile : (j + 1) * tile] = acc[owner * per + j].astype(BF16)
        out[per * tile :] = tail


def node_grads(groups, ids, weight, *refs):
    parts, (out, bias_out, hid) = refs[:groups], refs[groups:]
    group = ids[1]
    rows = out.shape[0]
    for m, part in enumerate(parts):
        hid[jnp.bitwise_xor(group, m)] = part[...]
    left = jnp.concatenate([hid[s, :rows] for s in range(groups)], axis=1)
    out[...] = lax.dot_general(
        left, weight[...], (((1,), (1,)), ((), ())), preferred_element_type=F32
    ).astype(BF16)
    tail = jnp.concatenate([hid[s, rows:] for s in range(groups)], axis=1).astype(F32)
    bias_out[...] = tail[0:1] + tail[1:2]


def place_weight(masks, ids, *refs):
    parts, (out, wide, sems) = refs[: len(masks)], refs[len(masks) :]
    group = ids[1]
    rows = parts[0].shape[0]
    copies = []
    for i, (mask, part) in enumerate(zip(masks, parts)):
        wide[i] = part[...].astype(F32)
        spot = out.at[aligned(jnp.bitwise_xor(group, mask), rows)]
        copies.append(pltpu.make_async_copy(wide.at[i], spot, sems.at[i]))
        copies[-1].start()
    for copy in copies:
        copy.wait()


def per_device(
    node_feats,
    weight,
    bias,
    cotangent,
    tile_bank,
    local_cols,
    local_banks,
    published,
    send_table,
    halo_rows,
    halo_banks,
):
    domains = lax.axis_size("dom")
    groups = lax.axis_size("grp")
    domain_index = lax.axis_index("dom")
    rows_here, embed = node_feats.shape
    hidden = weight.shape[1]
    tile = tile_bank.shape[1]
    slots = send_table.shape[2]
    per_row = local_cols.shape[2]
    part_rows = rows_here * groups
    blocks = part_rows // tile
    narrow = embed // groups
    wide = hidden // groups
    share = narrow // domains
    peers = domains - 1

    ids = jnp.stack([domain_index, lax.axis_index("grp")]).astype(jnp.int32)
    tables = {
        "cols": local_cols[0],
        "banks": local_banks[0],
        "pub": published[0],
        "out": lax.dynamic_index_in_dim(send_table, domain_index, 0, keepdims=False),
        "in": lax.dynamic_index_in_dim(send_table, domain_index, 1, keepdims=False),
        "hrows": halo_rows[0],
        "hbanks": halo_banks[0],
        "me": ids,
    }
    at, place = {}, 0
    for name, table in tables.items():
        at[name] = place
        place += table.size
    tab = jnp.concatenate([table.reshape(-1) for table in tables.values()])
    bank_t = jnp.swapaxes(tile_bank, 1, 2)

    feats = call(
        split_features,
        [shape((rows_here, narrow), BF16)] * groups,
        [SMEM, VMEM],
        nbytes=4 * rows_here * embed,
        name="split_features",
    )(ids, node_feats)
    feats = exchange(feats, "grp")
    x, *offered = call(
        functools.partial(pick_blocks, groups, slots, at),
        [shape((blocks, tile, narrow), BF16)] + [shape((slots * tile, narrow), BF16)] * peers,
        [SMEM] + [VMEM] * groups,
        nbytes=4 * (peers * slots + blocks) * tile * narrow,
        name="pick_blocks",
    )(tab, *feats)
    arrived = exchange([None] + offered, "dom")[1:]
    local = call(
        functools.partial(local_sum, per_row, at),
        shape((blocks, tile, narrow), F32),
        [SMEM, VMEM, VMEM],
        flops=2 * blocks * per_row * tile * tile * narrow,
        nbytes=blocks * tile * narrow * 6,
        name="local_sum",
    )(tab, tile_bank, x)
    aggs = call(
        functools.partial(add_halo, domains, groups, slots, at),
        [shape((rows_here, narrow), BF16)] * groups,
        [SMEM, VMEM, VMEM] + [VMEM] * peers,
        [pltpu.VMEM((blocks, tile, narrow), F32)],
        flops=2 * peers * slots * tile * tile * narrow,
        nbytes=blocks * tile * narrow * 8,
        name="add_halo",
    )(tab, tile_bank, local, *arrived)
    activations, grad = call(
        functools.partial(dense, groups),
        [shape((rows_here, hidden), BF16), shape((groups, rows_here, wide), BF16)],
        [SMEM] + [VMEM] * (3 + groups),
        flops=2 * rows_here * embed * hidden,
        nbytes=embed * hidden * 2 + rows_here * (embed + 3 * hidden) * 2,
        name="dense",
    )(ids, weight, bias.reshape(1, hidden), cotangent, *exchange(aggs, "grp"))

    grads, masks = spread(grad, "grp")
    own, mine, *terms = call(
        functools.partial(back_halo, masks, slots, at),
        [shape((blocks, tile, wide), BF16), shape((1, wide), F32)]
        + [shape((slots * tile + EXTRA, wide), BF16)] * peers,
        [SMEM, VMEM] + [VMEM] * len(masks),
        flops=2 * peers * slots * tile * tile * wide,
        nbytes=(peers * slots + blocks) * tile * wide * 2,
        name="back_halo",
    )(tab, bank_t, *grads)
    returned = exchange([None] + terms, "dom")[1:]
    kept, *parts = call(
        functools.partial(weight_slice, groups, masks),
        [shape((share, hidden), F32)] + [shape((share, hidden), BF16)] * peers,
        [SMEM] + [VMEM] * (groups + len(masks)),
        [pltpu.VMEM((domains, share, hidden), F32)],
        flops=2 * part_rows * narrow * hidden,
        nbytes=part_rows * (narrow + hidden) * 2,
        name="weight_slice",
    )(ids, *aggs, *grads)
    parts = exchange([None] + parts, "dom")[1:]
    back = call(
        functools.partial(back_local, per_row, at),
        shape((blocks, tile, wide), F32),
        [SMEM, VMEM, VMEM],
        flops=2 * blocks * per_row * tile * tile * wide,
        nbytes=blocks * tile * wide * 6,
        name="back_local",
    )(tab, bank_t, own)
    norm_scale = float(rows_here * groups * domains) ** (-0.5)
    summed = call(
        functools.partial(sum_shares, norm_scale),
        shape((share, hidden), BF16),
        [VMEM] * domains,
        nbytes=domains * share * hidden * 2,
        name="sum_shares",
    )(kept, *parts)
    joined = call(
        join_shares,
        shape((domains, share, hidden), BF16),
        [SMEM] + [VMEM] * domains,
        nbytes=4 * narrow * hidden,
        name="join_shares",
    )(ids, *exchange([summed] * domains, "dom")).reshape(narrow, hidden)

    hid = call(
        functools.partial(finish_nodes, domains, groups, slots, norm_scale, at),
        [shape((rows_here + EXTRA, wide), BF16)] * groups,
        [SMEM, VMEM, VMEM] + [VMEM] * peers,
        [pltpu.VMEM((blocks, tile, wide), F32)],
        nbytes=peers * slots * tile * wide * 2 + blocks * tile * wide * 6,
        name="finish_nodes",
    )(tab, back, mine, *returned)
    grad_nodes, grad_bias = call(
        functools.partial(node_grads, groups),
        [shape((rows_here, embed), BF16), shape((1, hidden), F32)],
        [SMEM, VMEM] + [VMEM] * groups,
        [pltpu.VMEM((groups, rows_here + EXTRA, wide), BF16)],
        flops=2 * rows_here * embed * hidden,
        nbytes=embed * hidden * 2 + rows_here * (embed + hidden) * 2,
        name="node_grads",
    )(ids, weight, *exchange(hid, "grp"))
    weights, masks = spread(joined, "grp")
    grad_weight = call(
        functools.partial(place_weight, masks),
        shape((embed, hidden), F32),
        [SMEM] + [VMEM] * len(masks),
        [pltpu.VMEM((groups, narrow, hidden), F32), pltpu.SemaphoreType.DMA((groups,))],
        nbytes=embed * hidden * 6,
        name="place_weight",
        out_specs=pl.BlockSpec(memory_space=pl.ANY),
    )(ids, *weights)
    return (activations, grad_nodes, grad_weight, grad_bias.reshape(hidden))


def solution(mesh):
    in_specs = (
        P(("dom", "grp"), None),
        P(),
        P(),
        P(("dom", "grp"), None),
        P(),
        P("dom", None, None),
        P("dom", None, None),
        P("dom", None),
        P(),
        P("dom", None, None),
        P("dom", None, None),
    )
    out_specs = (P(("dom", "grp"), None), P(("dom", "grp"), None), P(), P())
    return jax.shard_map(
        per_device, mesh=mesh, in_specs=in_specs, out_specs=out_specs, check_vma=False
    )
```

```python
import functools

import jax
import jax.numpy as jnp
from jax import lax
from jax.experimental import pallas as pl
from jax.experimental.pallas import tpu as pltpu
from jax.sharding import PartitionSpec as P

VMEM = pl.BlockSpec(memory_space=pltpu.VMEM)
SMEM = pl.BlockSpec(memory_space=pltpu.SMEM)
EXTRA = 16
F32 = jnp.float32
BF16 = jnp.bfloat16


def call(body, out_shape, specs, scratch=(), flops=0, nbytes=0, name=None, out_specs=None):
    return pl.pallas_call(
        body,
        out_shape=out_shape,
        in_specs=specs,
        out_specs=jax.tree.map(lambda _: VMEM, out_shape) if out_specs is None else out_specs,
        scratch_shapes=list(scratch),
        compiler_params=pltpu.CompilerParams(vmem_limit_bytes=48 * 1024 * 1024),
        cost_estimate=pl.CostEstimate(flops=flops, bytes_accessed=nbytes, transcendentals=0),
        name=name,
    )


def shape(dims, kind):
    return jax.ShapeDtypeStruct(tuple(dims), kind)


def dot(a, b):
    return jnp.dot(a, b, preferred_element_type=F32)


def bias_rows(total):
    high = total.astype(BF16).astype(F32)
    rest = jnp.zeros((EXTRA - 2, total.shape[1]), F32)
    return jnp.concatenate([high, total - high, rest], axis=0).astype(BF16)


def aligned(start, step):
    return pl.ds(pl.multiple_of(start * step, step), step)


def exchange(parts, axis):
    size = lax.axis_size(axis)
    return [
        parts[m] if m == 0 else lax.ppermute(parts[m], axis, [(i, i ^ m) for i in range(size)])
        for m in range(size)
    ]


def spread(value, axis):
    size = lax.axis_size(axis)
    parts, masks = [value], [0]
    bit = size // 2
    while bit:
        pairs = [(i, i ^ bit) for i in range(size)]
        parts = parts + [lax.ppermute(part, axis, pairs) for part in parts]
        masks = masks + [mask ^ bit for mask in masks]
        bit //= 2
    return parts, masks


def split_features(ids, feats, *outs):
    group = ids[1]
    narrow = outs[0].shape[1]
    for m, out in enumerate(outs):
        out[...] = feats[:, aligned(jnp.bitwise_xor(group, m), narrow)]


def pick_blocks(groups, slots, at, tab, *refs):
    parts, (x, *outs) = refs[:groups], refs[groups:]
    domain, group = tab[at["me"]], tab[at["me"] + 1]
    tile = x.shape[1]
    per = x.shape[0] // groups
    for m, part in enumerate(parts):
        owner = jnp.bitwise_xor(group, m)
        for j in range(per):
            x[owner * per + j] = part[j * tile : (j + 1) * tile]
    for m, out in enumerate(outs, 1):
        reader = jnp.bitwise_xor(domain, m)
        for s in range(slots):
            entry = jnp.maximum(tab[at["out"] + reader * slots + s], 0)
            out[s * tile : (s + 1) * tile] = x[tab[at["pub"] + entry]]


def local_sum(per_row, at, tab, bank, x, out):
    pair = 2 if per_row % 2 == 0 else 1

    @pl.loop(0, out.shape[0])
    def _(r):
        acc = jnp.zeros(out.shape[1:], F32)
        for k in range(0, per_row, pair):
            spots = [r * per_row + k + j for j in range(pair)]
            left = jnp.concatenate([bank[tab[at["banks"] + a]] for a in spots], axis=1)
            right = jnp.concatenate([x[tab[at["cols"] + a]] for a in spots], axis=0)
            acc += dot(left, right)
        out[r] = acc


def add_halo(domains, groups, slots, at, tab, bank, local, *refs):
    recv, outs, acc = refs[: domains - 1], refs[domains - 1 : -1], refs[-1]
    domain, group = tab[at["me"]], tab[at["me"] + 1]
    tile = local.shape[1]
    per = local.shape[0] // groups
    acc[...] = local[...]
    for m, block in enumerate(recv, 1):
        source = jnp.bitwise_xor(domain, m)
        for s in range(slots):
            i = source * slots + s

            @pl.when(tab[at["in"] + i] >= 0)
            def _(i=i, s=s, block=block):
                tile_here = bank[tab[at["hbanks"] + i]]
                acc[tab[at["hrows"] + i]] += dot(tile_here, block[s * tile : (s + 1) * tile])

    for m, out in enumerate(outs):
        owner = jnp.bitwise_xor(group, m)
        for j in range(per):
            out[j * tile : (j + 1) * tile] = acc[owner * per + j].astype(BF16)


def dense(groups, ids, weight, bias, cot, *refs):
    parts, (act, grad) = refs[:groups], refs[groups:]
    group = ids[1]
    narrow = parts[0].shape[1]
    wide = cot.shape[1] // groups
    total = None
    for m, part in enumerate(parts):
        term = dot(part[...], weight[aligned(jnp.bitwise_xor(group, m), narrow)])
        total = term if total is None else total + term
    pre = total + bias[...]
    act[...] = jnp.maximum(pre, 0.0).astype(BF16)
    masked = jnp.where(pre > 0, cot[...].astype(F32), 0.0).astype(BF16)
    for s in range(groups):
        grad[s] = masked[:, s * wide : (s + 1) * wide]


def back_halo(masks, slots, at, tab, bank_t, *refs):
    parts, (own, terms) = refs[: len(masks)], refs[len(masks) :]
    group = tab[at["me"] + 1]
    tile = bank_t.shape[1]
    per = parts[0].shape[1] // tile
    total = jnp.zeros((1, own.shape[2]), F32)
    for mask, part in zip(masks, parts):
        owner = jnp.bitwise_xor(group, mask)
        piece = part[group]
        total += jnp.sum(piece.astype(F32), axis=0, keepdims=True)
        for j in range(per):
            own[owner * per + j] = piece[j * tile : (j + 1) * tile]
    tail = bias_rows(total)
    for d in range(terms.shape[0]):
        for s in range(slots):
            i = d * slots + s
            live = (tab[at["in"] + i] >= 0).astype(F32)
            value = dot(bank_t[tab[at["hbanks"] + i]], own[tab[at["hrows"] + i]]) * live
            terms[d, s * tile : (s + 1) * tile] = value.astype(BF16)
        terms[d, slots * tile :] = tail


def back_local(per_row, at, tab, bank_t, own, out):
    out[...] = jnp.zeros_like(out)

    @pl.loop(0, own.shape[0])
    def _(r):
        right = own[r]
        for k in range(per_row):
            spot = r * per_row + k
            out[tab[at["cols"] + spot]] += dot(bank_t[tab[at["banks"] + spot]], right)


def weight_slice(groups, masks, *refs):
    aggs, parts = refs[:groups], refs[groups : groups + len(masks)]
    out = refs[-1]
    sum_here = None
    for mask, part in zip(masks, parts):
        right = jnp.concatenate([part[s] for s in range(part.shape[0])], axis=1)
        term = lax.dot_general(
            aggs[mask][...], right, (((0,), (0,)), ((), ())), preferred_element_type=F32
        )
        sum_here = term if sum_here is None else sum_here + term
    rows = out.shape[1]
    for d in range(out.shape[0]):
        out[d] = sum_here[d * rows : (d + 1) * rows].astype(BF16)


def sum_shares(scale, shares, out):
    total = shares[0].astype(F32)
    for d in range(1, shares.shape[0]):
        total += shares[d].astype(F32)
    summed = (total * scale).astype(BF16)
    for d in range(out.shape[0]):
        out[d] = summed


def finish_nodes(slots, scale, at, tab, local, recv, *refs):
    outs, acc = refs[:-1], refs[-1]
    groups = len(outs)
    group = tab[at["me"] + 1]
    tile = local.shape[1]
    per = local.shape[0] // groups
    acc[...] = local[...]
    total = jnp.zeros((EXTRA, local.shape[2]), F32)
    for d in range(recv.shape[0]):
        total += recv[d, slots * tile :].astype(F32)
        for s in range(slots):
            entry = tab[at["out"] + d * slots + s]

            @pl.when(entry >= 0)
            def _(d=d, s=s, entry=entry):
                spot = tab[at["pub"] + jnp.maximum(entry, 0)]
                acc[spot] += recv[d, s * tile : (s + 1) * tile].astype(F32)

    tail = bias_rows((total[0:1] + total[1:2]) * scale)
    for m, out in enumerate(outs):
        owner = jnp.bitwise_xor(group, m)
        for j in range(per):
            out[j * tile : (j + 1) * tile] = acc[owner * per + j].astype(BF16)
        out[per * tile :] = tail


def node_grads(groups, ids, weight, *refs):
    parts, (out, bias_out, hid) = refs[:groups], refs[groups:]
    group = ids[1]
    rows = out.shape[0]
    for m, part in enumerate(parts):
        hid[jnp.bitwise_xor(group, m)] = part[...]
    left = jnp.concatenate([hid[s, :rows] for s in range(groups)], axis=1)
    out[...] = lax.dot_general(
        left, weight[...], (((1,), (1,)), ((), ())), preferred_element_type=F32
    ).astype(BF16)
    tail = jnp.concatenate([hid[s, rows:] for s in range(groups)], axis=1).astype(F32)
    bias_out[...] = tail[0:1] + tail[1:2]


def place_weight(masks, ids, *refs):
    parts, (out, wide, sems) = refs[: len(masks)], refs[len(masks) :]
    group = ids[1]
    rows = parts[0].shape[0]
    copies = []
    for i, (mask, part) in enumerate(zip(masks, parts)):
        wide[i] = part[...].astype(F32)
        spot = out.at[aligned(jnp.bitwise_xor(group, mask), rows)]
        copies.append(pltpu.make_async_copy(wide.at[i], spot, sems.at[i]))
        copies[-1].start()
    for copy in copies:
        copy.wait()


def per_device(
    node_feats,
    weight,
    bias,
    cotangent,
    tile_bank,
    local_cols,
    local_banks,
    published,
    send_table,
    halo_rows,
    halo_banks,
):
    domains = lax.axis_size("dom")
    groups = lax.axis_size("grp")
    domain_index = lax.axis_index("dom")
    rows_here, embed = node_feats.shape
    hidden = weight.shape[1]
    tile = tile_bank.shape[1]
    slots = send_table.shape[2]
    per_row = local_cols.shape[2]
    part_rows = rows_here * groups
    blocks = part_rows // tile
    narrow = embed // groups
    wide = hidden // groups
    share = narrow // domains
    peers = domains - 1

    ids = jnp.stack([domain_index, lax.axis_index("grp")]).astype(jnp.int32)
    tables = {
        "cols": local_cols[0],
        "banks": local_banks[0],
        "pub": published[0],
        "out": lax.dynamic_index_in_dim(send_table, domain_index, 0, keepdims=False),
        "in": lax.dynamic_index_in_dim(send_table, domain_index, 1, keepdims=False),
        "hrows": halo_rows[0],
        "hbanks": halo_banks[0],
        "me": ids,
    }
    at, place = {}, 0
    for name, table in tables.items():
        at[name] = place
        place += table.size
    tab = jnp.concatenate([table.reshape(-1) for table in tables.values()])
    bank_t = jnp.swapaxes(tile_bank, 1, 2)

    feats = call(
        split_features,
        [shape((rows_here, narrow), BF16)] * groups,
        [SMEM, VMEM],
        nbytes=4 * rows_here * embed,
        name="split_features",
    )(ids, node_feats)
    feats = exchange(feats, "grp")
    x, *offered = call(
        functools.partial(pick_blocks, groups, slots, at),
        [shape((blocks, tile, narrow), BF16)] + [shape((slots * tile, narrow), BF16)] * peers,
        [SMEM] + [VMEM] * groups,
        nbytes=4 * (peers * slots + blocks) * tile * narrow,
        name="pick_blocks",
    )(tab, *feats)
    arrived = exchange([None] + offered, "dom")[1:]
    local = call(
        functools.partial(local_sum, per_row, at),
        shape((blocks, tile, narrow), F32),
        [SMEM, VMEM, VMEM],
        flops=2 * blocks * per_row * tile * tile * narrow,
        nbytes=blocks * tile * narrow * 6,
        name="local_sum",
    )(tab, tile_bank, x)
    aggs = call(
        functools.partial(add_halo, domains, groups, slots, at),
        [shape((rows_here, narrow), BF16)] * groups,
        [SMEM, VMEM, VMEM] + [VMEM] * peers,
        [pltpu.VMEM((blocks, tile, narrow), F32)],
        flops=2 * peers * slots * tile * tile * narrow,
        nbytes=blocks * tile * narrow * 8,
        name="add_halo",
    )(tab, tile_bank, local, *arrived)
    activations, grad = call(
        functools.partial(dense, groups),
        [shape((rows_here, hidden), BF16), shape((groups, rows_here, wide), BF16)],
        [SMEM] + [VMEM] * (3 + groups),
        flops=2 * rows_here * embed * hidden,
        nbytes=embed * hidden * 2 + rows_here * (embed + 3 * hidden) * 2,
        name="dense",
    )(ids, weight, bias.reshape(1, hidden), cotangent, *exchange(aggs, "grp"))

    grads, masks = spread(grad, "grp")
    own, terms = call(
        functools.partial(back_halo, masks, slots, at),
        [
            shape((blocks, tile, wide), BF16),
            shape((domains, slots * tile + EXTRA, wide), BF16),
        ],
        [SMEM, VMEM] + [VMEM] * len(masks),
        flops=2 * domains * slots * tile * tile * wide,
        nbytes=(domains * slots + blocks) * tile * wide * 2,
        name="back_halo",
    )(tab, bank_t, *grads)
    returned = lax.all_to_all(terms, "dom", split_axis=0, concat_axis=0, tiled=True)
    part = call(
        functools.partial(weight_slice, groups, masks),
        shape((domains, share, hidden), BF16),
        [VMEM] * (groups + len(masks)),
        flops=2 * part_rows * narrow * hidden,
        nbytes=part_rows * (narrow + hidden) * 2,
        name="weight_slice",
    )(*aggs, *grads)
    shares = lax.all_to_all(part, "dom", split_axis=0, concat_axis=0, tiled=True)
    back = call(
        functools.partial(back_local, per_row, at),
        shape((blocks, tile, wide), F32),
        [SMEM, VMEM, VMEM],
        flops=2 * blocks * per_row * tile * tile * wide,
        nbytes=blocks * tile * wide * 6,
        name="back_local",
    )(tab, bank_t, own)
    norm_scale = float(rows_here * groups * domains) ** (-0.5)
    summed = call(
        functools.partial(sum_shares, norm_scale),
        shape((domains, share, hidden), BF16),
        [VMEM],
        nbytes=domains * share * hidden * 4,
        name="sum_shares",
    )(shares)
    joined = lax.all_to_all(summed, "dom", split_axis=0, concat_axis=0, tiled=True)
    joined = joined.reshape(narrow, hidden)

    hid = call(
        functools.partial(finish_nodes, slots, norm_scale, at),
        [shape((rows_here + EXTRA, wide), BF16)] * groups,
        [SMEM, VMEM, VMEM],
        [pltpu.VMEM((blocks, tile, wide), F32)],
        nbytes=domains * slots * tile * wide * 2 + blocks * tile * wide * 6,
        name="finish_nodes",
    )(tab, back, returned)
    grad_nodes, grad_bias = call(
        functools.partial(node_grads, groups),
        [shape((rows_here, embed), BF16), shape((1, hidden), F32)],
        [SMEM, VMEM] + [VMEM] * groups,
        [pltpu.VMEM((groups, rows_here + EXTRA, wide), BF16)],
        flops=2 * rows_here * embed * hidden,
        nbytes=embed * hidden * 2 + rows_here * (embed + hidden) * 2,
        name="node_grads",
    )(ids, weight, *exchange(hid, "grp"))
    weights, masks = spread(joined, "grp")
    grad_weight = call(
        functools.partial(place_weight, masks),
        shape((embed, hidden), F32),
        [SMEM] + [VMEM] * len(masks),
        [pltpu.VMEM((groups, narrow, hidden), F32), pltpu.SemaphoreType.DMA((groups,))],
        nbytes=embed * hidden * 6,
        name="place_weight",
        out_specs=pl.BlockSpec(memory_space=pl.ANY),
    )(ids, *weights)
    return (activations, grad_nodes, grad_weight, grad_bias.reshape(hidden))


def solution(mesh):
    in_specs = (
        P(("dom", "grp"), None),
        P(),
        P(),
        P(("dom", "grp"), None),
        P(),
        P("dom", None, None),
        P("dom", None, None),
        P("dom", None),
        P(),
        P("dom", None, None),
        P("dom", None, None),
    )
    out_specs = (P(("dom", "grp"), None), P(("dom", "grp"), None), P(), P())
    return jax.shard_map(
        per_device, mesh=mesh, in_specs=in_specs, out_specs=out_specs, check_vma=False
    )
```

```python
import functools

import jax
import jax.numpy as jnp
from jax import lax
from jax.experimental import pallas as pl
from jax.experimental.pallas import tpu as pltpu
from jax.sharding import PartitionSpec as P

VMEM = pl.BlockSpec(memory_space=pltpu.VMEM)
SMEM = pl.BlockSpec(memory_space=pltpu.SMEM)
EXTRA = 16
F32 = jnp.float32
BF16 = jnp.bfloat16


def call(body, out_shape, specs, scratch=(), flops=0, nbytes=0, name=None, out_specs=None, aliases=()):
    return pl.pallas_call(
        body,
        out_shape=out_shape,
        in_specs=specs,
        out_specs=jax.tree.map(lambda _: VMEM, out_shape) if out_specs is None else out_specs,
        scratch_shapes=list(scratch),
        input_output_aliases=dict(aliases),
        compiler_params=pltpu.CompilerParams(vmem_limit_bytes=48 * 1024 * 1024),
        cost_estimate=pl.CostEstimate(flops=flops, bytes_accessed=nbytes, transcendentals=0),
        name=name,
    )


def shape(dims, kind):
    return jax.ShapeDtypeStruct(tuple(dims), kind)


def dot(a, b):
    return jnp.dot(a, b, preferred_element_type=F32)


def bias_rows(total):
    high = total.astype(BF16).astype(F32)
    rest = jnp.zeros((EXTRA - 2, total.shape[1]), F32)
    return jnp.concatenate([high, total - high, rest], axis=0).astype(BF16)


def aligned(start, step):
    return pl.ds(pl.multiple_of(start * step, step), step)


def exchange(parts, axis):
    size = lax.axis_size(axis)
    got = {0: parts[0]}
    for m in reversed(range(1, size)):
        got[m] = lax.ppermute(parts[m], axis, [(i, i ^ m) for i in range(size)])
    return [got[m] for m in range(size)]


def spread(value, axis):
    size = lax.axis_size(axis)
    parts, masks = [value], [0]
    bit = size // 2
    while bit:
        pairs = [(i, i ^ bit) for i in range(size)]
        parts = parts + [lax.ppermute(part, axis, pairs) for part in parts]
        masks = masks + [mask ^ bit for mask in masks]
        bit //= 2
    return parts, masks


def split_features(ids, feats, *refs):
    outs, sems = refs[:-1], refs[-1]
    group = ids[1]
    narrow = outs[0].shape[1]
    copies = [
        pltpu.make_async_copy(
            feats.at[:, aligned(jnp.bitwise_xor(group, m), narrow)], out, sems.at[m]
        )
        for m, out in enumerate(outs)
    ]
    for copy in copies:
        copy.start()
    for copy in copies:
        copy.wait()


def pick_blocks(groups, slots, at, tab, *refs):
    parts, (x, *outs) = refs[:groups], refs[groups:]
    domain, group = tab[at["me"]], tab[at["me"] + 1]
    tile = x.shape[1]
    per = x.shape[0] // groups
    for m, part in enumerate(parts):
        owner = jnp.bitwise_xor(group, m)
        for j in range(per):
            x[owner * per + j] = part[j * tile : (j + 1) * tile]
    for m, out in enumerate(outs, 1):
        reader = jnp.bitwise_xor(domain, m)
        for s in range(slots):
            entry = jnp.maximum(tab[at["out"] + reader * slots + s], 0)
            out[s * tile : (s + 1) * tile] = x[tab[at["pub"] + entry]]


def local_sum(per_row, at, tab, bank, x, out):
    pair = 2 if per_row % 2 == 0 else 1

    @pl.loop(0, out.shape[0])
    def _(r):
        acc = jnp.zeros(out.shape[1:], F32)
        for k in range(0, per_row, pair):
            spots = [r * per_row + k + j for j in range(pair)]
            left = jnp.concatenate([bank[tab[at["banks"] + a]] for a in spots], axis=1)
            right = jnp.concatenate([x[tab[at["cols"] + a]] for a in spots], axis=0)
            acc += dot(left, right)
        out[r] = acc


def add_halo(domains, groups, slots, at, tab, bank, local, *refs):
    recv, outs, acc = refs[: domains - 1], refs[domains - 1 : -1], refs[-1]
    domain, group = tab[at["me"]], tab[at["me"] + 1]
    tile = local.shape[1]
    per = local.shape[0] // groups
    acc[...] = local[...]
    for m, block in enumerate(recv, 1):
        source = jnp.bitwise_xor(domain, m)
        for s in range(slots):
            i = source * slots + s

            @pl.when(tab[at["in"] + i] >= 0)
            def _(i=i, s=s, block=block):
                tile_here = bank[tab[at["hbanks"] + i]]
                acc[tab[at["hrows"] + i]] += dot(tile_here, block[s * tile : (s + 1) * tile])

    for m, out in enumerate(outs):
        owner = jnp.bitwise_xor(group, m)
        for j in range(per):
            out[j * tile : (j + 1) * tile] = acc[owner * per + j].astype(BF16)


def dense(groups, ids, weight, bias, cot, *refs):
    parts, (act, grad) = refs[:groups], refs[groups:]
    group = ids[1]
    narrow = parts[0].shape[1]
    wide = cot.shape[1] // groups
    total = None
    for m, part in enumerate(parts):
        term = dot(part[...], weight[aligned(jnp.bitwise_xor(group, m), narrow)])
        total = term if total is None else total + term
    pre = total + bias[...]
    act[...] = jnp.maximum(pre, 0.0).astype(BF16)
    masked = jnp.where(pre > 0, cot[...].astype(F32), 0.0).astype(BF16)
    for s in range(groups):
        grad[s] = masked[:, s * wide : (s + 1) * wide]


def back_terms(masks, slots, at, tab, bank_t, *refs):
    groups = len(masks)
    aggs, parts, (own, terms) = refs[:groups], refs[groups : 2 * groups], refs[2 * groups :]
    group = tab[at["me"] + 1]
    tile = bank_t.shape[1]
    domains, rows, wide = terms.shape
    per = parts[0].shape[1] // tile
    total = jnp.zeros((1, wide), F32)
    for mask, part in zip(masks, parts):
        owner = jnp.bitwise_xor(group, mask)
        piece = part[group]
        total += jnp.sum(piece.astype(F32), axis=0, keepdims=True)
        for j in range(per):
            own[owner * per + j] = piece[j * tile : (j + 1) * tile]
    weight_sum = None
    for mask, part in zip(masks, parts):
        right = jnp.concatenate([part[s] for s in range(groups)], axis=1)
        term = lax.dot_general(
            aggs[mask][...], right, (((0,), (0,)), ((), ())), preferred_element_type=F32
        )
        weight_sum = term if weight_sum is None else weight_sum + term
    share = weight_sum.shape[0] // domains
    tail = bias_rows(total)
    base = slots * tile + EXTRA
    step = (rows - base) // groups
    for d in range(domains):
        for s in range(slots):
            i = d * slots + s
            live = (tab[at["in"] + i] >= 0).astype(F32)
            value = dot(bank_t[tab[at["hbanks"] + i]], own[tab[at["hrows"] + i]]) * live
            terms[d, s * tile : (s + 1) * tile] = value.astype(BF16)
        terms[d, slots * tile : base] = tail
        for s in range(groups):
            piece = weight_sum[d * share : (d + 1) * share, s * wide : (s + 1) * wide]
            terms[d, base + s * step : base + s * step + share] = piece.astype(BF16)


def back_local(per_row, at, tab, bank_t, own, out):
    out[...] = jnp.zeros_like(out)

    @pl.loop(0, own.shape[0])
    def _(r):
        right = own[r]
        for k in range(per_row):
            spot = r * per_row + k
            out[tab[at["cols"] + spot]] += dot(bank_t[tab[at["banks"] + spot]], right)


def sum_shares(scale, base, recv, out):
    domains, share, hidden = out.shape
    wide = recv.shape[2]
    groups = hidden // wide
    step = (recv.shape[1] - base) // groups
    total = recv[0, base:].astype(F32)
    for d in range(1, domains):
        total += recv[d, base:].astype(F32)
    total = (total * scale).astype(BF16)
    pieces = [total[s * step : s * step + share] for s in range(groups)]
    summed = jnp.concatenate(pieces, axis=1)
    for d in range(domains):
        out[d] = summed


def finish_nodes(slots, scale, at, tab, local, recv, *refs):
    outs, acc = refs[:-1], refs[-1]
    groups = len(outs)
    group = tab[at["me"] + 1]
    tile = local.shape[1]
    per = local.shape[0] // groups
    acc[...] = local[...]
    total = jnp.zeros((EXTRA, local.shape[2]), F32)
    for d in range(recv.shape[0]):
        total += recv[d, slots * tile : slots * tile + EXTRA].astype(F32)
        for s in range(slots):
            entry = tab[at["out"] + d * slots + s]

            @pl.when(entry >= 0)
            def _(d=d, s=s, entry=entry):
                spot = tab[at["pub"] + jnp.maximum(entry, 0)]
                acc[spot] += recv[d, s * tile : (s + 1) * tile].astype(F32)

    tail = bias_rows((total[0:1] + total[1:2]) * scale)
    for m, out in enumerate(outs):
        owner = jnp.bitwise_xor(group, m)
        for j in range(per):
            out[j * tile : (j + 1) * tile] = acc[owner * per + j].astype(BF16)
        out[per * tile :] = tail


def node_grads(groups, ids, weight, *refs):
    parts, (out, bias_out, hid) = refs[:groups], refs[groups:]
    group = ids[1]
    rows = out.shape[0]
    for m, part in enumerate(parts):
        hid[jnp.bitwise_xor(group, m)] = part[...]
    left = jnp.concatenate([hid[s, :rows] for s in range(groups)], axis=1)
    out[...] = lax.dot_general(
        left, weight[...], (((1,), (1,)), ((), ())), preferred_element_type=F32
    ).astype(BF16)
    tail = jnp.concatenate([hid[s, rows:] for s in range(groups)], axis=1).astype(F32)
    bias_out[...] = tail[0:1] + tail[1:2]


def place_weight(masks, ids, *refs):
    parts, (out, wide, sems) = refs[: len(masks)], refs[-3:]
    group = ids[1]
    rows = parts[0].shape[0]
    copies = []
    for i, (mask, part) in enumerate(zip(masks, parts)):
        wide[i] = part[...].astype(F32)
        spot = out.at[aligned(jnp.bitwise_xor(group, mask), rows)]
        copies.append(pltpu.make_async_copy(wide.at[i], spot, sems.at[i]))
        copies[-1].start()
    for copy in copies:
        copy.wait()


def per_device(
    node_feats,
    weight,
    bias,
    cotangent,
    tile_bank,
    local_cols,
    local_banks,
    published,
    send_table,
    halo_rows,
    halo_banks,
):
    domains = lax.axis_size("dom")
    groups = lax.axis_size("grp")
    domain_index = lax.axis_index("dom")
    rows_here, embed = node_feats.shape
    hidden = weight.shape[1]
    tile = tile_bank.shape[1]
    slots = send_table.shape[2]
    per_row = local_cols.shape[2]
    part_rows = rows_here * groups
    blocks = part_rows // tile
    narrow = embed // groups
    wide = hidden // groups
    share = narrow // domains
    peers = domains - 1

    ids = jnp.stack([domain_index, lax.axis_index("grp")]).astype(jnp.int32)
    tables = {
        "cols": local_cols[0],
        "banks": local_banks[0],
        "pub": published[0],
        "out": lax.dynamic_index_in_dim(send_table, domain_index, 0, keepdims=False),
        "in": lax.dynamic_index_in_dim(send_table, domain_index, 1, keepdims=False),
        "hrows": halo_rows[0],
        "hbanks": halo_banks[0],
        "me": ids,
    }
    at, place = {}, 0
    for name, table in tables.items():
        at[name] = place
        place += table.size
    tab = jnp.concatenate([table.reshape(-1) for table in tables.values()])
    bank_t = jnp.swapaxes(tile_bank, 1, 2)

    feats = call(
        split_features,
        [shape((rows_here, narrow), BF16)] * groups,
        [SMEM, pl.BlockSpec(memory_space=pl.ANY)],
        [pltpu.SemaphoreType.DMA((groups,))],
        nbytes=4 * rows_here * embed,
        name="split_features",
    )(ids, node_feats)
    feats = exchange(feats, "grp")
    x, *offered = call(
        functools.partial(pick_blocks, groups, slots, at),
        [shape((blocks, tile, narrow), BF16)] + [shape((slots * tile, narrow), BF16)] * peers,
        [SMEM] + [VMEM] * groups,
        nbytes=4 * (peers * slots + blocks) * tile * narrow,
        name="pick_blocks",
    )(tab, *feats)
    arrived = exchange([None] + offered, "dom")[1:]
    local = call(
        functools.partial(local_sum, per_row, at),
        shape((blocks, tile, narrow), F32),
        [SMEM, VMEM, VMEM],
        flops=2 * blocks * per_row * tile * tile * narrow,
        nbytes=blocks * tile * narrow * 6,
        name="local_sum",
    )(tab, tile_bank, x)
    aggs = call(
        functools.partial(add_halo, domains, groups, slots, at),
        [shape((rows_here, narrow), BF16)] * groups,
        [SMEM, VMEM, VMEM] + [VMEM] * peers,
        [pltpu.VMEM((blocks, tile, narrow), F32)],
        flops=2 * peers * slots * tile * tile * narrow,
        nbytes=blocks * tile * narrow * 8,
        name="add_halo",
    )(tab, tile_bank, local, *arrived)
    activations, grad = call(
        functools.partial(dense, groups),
        [shape((rows_here, hidden), BF16), shape((groups, rows_here, wide), BF16)],
        [SMEM] + [VMEM] * (3 + groups),
        flops=2 * rows_here * embed * hidden,
        nbytes=embed * hidden * 2 + rows_here * (embed + 3 * hidden) * 2,
        name="dense",
    )(ids, weight, bias.reshape(1, hidden), cotangent, *exchange(aggs, "grp"))

    grads, masks = spread(grad, "grp")
    base = slots * tile + EXTRA
    step = -(-share // 16) * 16
    own, terms = call(
        functools.partial(back_terms, masks, slots, at),
        [
            shape((blocks, tile, wide), BF16),
            shape((domains, base + groups * step, wide), BF16),
        ],
        [SMEM, VMEM] + [VMEM] * (2 * groups),
        flops=2 * domains * slots * tile * tile * wide + 2 * part_rows * narrow * hidden,
        nbytes=(domains * slots + blocks) * tile * wide * 2 + part_rows * (narrow + hidden) * 2,
        name="back_terms",
    )(tab, bank_t, *aggs, *grads)
    returned = lax.all_to_all(terms, "dom", split_axis=0, concat_axis=0, tiled=True)
    back = call(
        functools.partial(back_local, per_row, at),
        shape((blocks, tile, wide), F32),
        [SMEM, VMEM, VMEM],
        flops=2 * blocks * per_row * tile * tile * wide,
        nbytes=blocks * tile * wide * 6,
        name="back_local",
    )(tab, bank_t, own)
    norm_scale = float(rows_here * groups * domains) ** (-0.5)
    summed = call(
        functools.partial(sum_shares, norm_scale, base),
        shape((domains, share, hidden), BF16),
        [VMEM],
        nbytes=domains * share * hidden * 4,
        name="sum_shares",
    )(returned)
    joined = lax.all_to_all(summed, "dom", split_axis=0, concat_axis=0, tiled=True)
    joined = joined.reshape(narrow, hidden)

    hid = call(
        functools.partial(finish_nodes, slots, norm_scale, at),
        [shape((rows_here + EXTRA, wide), BF16)] * groups,
        [SMEM, VMEM, VMEM],
        [pltpu.VMEM((blocks, tile, wide), F32)],
        nbytes=domains * slots * tile * wide * 2 + blocks * tile * wide * 6,
        name="finish_nodes",
    )(tab, back, returned)
    grad_nodes, grad_bias = call(
        functools.partial(node_grads, groups),
        [shape((rows_here, embed), BF16), shape((1, hidden), F32)],
        [SMEM, VMEM] + [VMEM] * groups,
        [pltpu.VMEM((groups, rows_here + EXTRA, wide), BF16)],
        flops=2 * rows_here * embed * hidden,
        nbytes=embed * hidden * 2 + rows_here * (embed + hidden) * 2,
        name="node_grads",
    )(ids, weight, *exchange(hid, "grp"))
    weights, masks = spread(joined, "grp")
    half = groups // 2
    grad_weight = None
    for chosen in ([m for m in range(groups) if m < half], [m for m in range(groups) if m >= half]):
        spots = [masks.index(m) for m in chosen]
        before = [] if grad_weight is None else [grad_weight]
        grad_weight = call(
            functools.partial(place_weight, chosen),
            shape((embed, hidden), F32),
            [SMEM] + [VMEM] * half + [pl.BlockSpec(memory_space=pl.ANY)] * len(before),
            [pltpu.VMEM((half, narrow, hidden), F32), pltpu.SemaphoreType.DMA((half,))],
            nbytes=embed * hidden * 3,
            name="place_weight",
            out_specs=pl.BlockSpec(memory_space=pl.ANY),
            aliases={half + 1: 0} if before else {},
        )(ids, *[weights[i] for i in spots], *before)
    return (activations, grad_nodes, grad_weight, grad_bias.reshape(hidden))


def solution(mesh):
    in_specs = (
        P(("dom", "grp"), None),
        P(),
        P(),
        P(("dom", "grp"), None),
        P(),
        P("dom", None, None),
        P("dom", None, None),
        P("dom", None),
        P(),
        P("dom", None, None),
        P("dom", None, None),
    )
    out_specs = (P(("dom", "grp"), None), P(("dom", "grp"), None), P(), P())
    return jax.shard_map(
        per_device, mesh=mesh, in_specs=in_specs, out_specs=out_specs, check_vma=False
    )
```

```python
import functools

import jax
import jax.numpy as jnp
from jax import lax
from jax.experimental import pallas as pl
from jax.experimental.pallas import tpu as pltpu
from jax.sharding import PartitionSpec as P

VMEM = pl.BlockSpec(memory_space=pltpu.VMEM)
SMEM = pl.BlockSpec(memory_space=pltpu.SMEM)
EXTRA = 16
F32 = jnp.float32
BF16 = jnp.bfloat16


def call(body, out_shape, specs, scratch=(), flops=0, nbytes=0, name=None, out_specs=None, aliases=()):
    return pl.pallas_call(
        body,
        out_shape=out_shape,
        in_specs=specs,
        out_specs=jax.tree.map(lambda _: VMEM, out_shape) if out_specs is None else out_specs,
        scratch_shapes=list(scratch),
        input_output_aliases=dict(aliases),
        compiler_params=pltpu.CompilerParams(vmem_limit_bytes=48 * 1024 * 1024),
        cost_estimate=pl.CostEstimate(flops=flops, bytes_accessed=nbytes, transcendentals=0),
        name=name,
    )


def shape(dims, kind):
    return jax.ShapeDtypeStruct(tuple(dims), kind)


def dot(a, b):
    return jnp.dot(a, b, preferred_element_type=F32)


def bias_rows(total):
    high = total.astype(BF16).astype(F32)
    rest = jnp.zeros((EXTRA - 2, total.shape[1]), F32)
    return jnp.concatenate([high, total - high, rest], axis=0).astype(BF16)


def aligned(start, step):
    return pl.ds(pl.multiple_of(start * step, step), step)


def exchange(parts, axis):
    size = lax.axis_size(axis)
    got = {0: parts[0]}
    for m in reversed(range(1, size)):
        got[m] = lax.ppermute(parts[m], axis, [(i, i ^ m) for i in range(size)])
    return [got[m] for m in range(size)]


def spread(value, axis):
    size = lax.axis_size(axis)
    parts, masks = [value], [0]
    bit = size // 2
    while bit:
        pairs = [(i, i ^ bit) for i in range(size)]
        parts = parts + [lax.ppermute(part, axis, pairs) for part in parts]
        masks = masks + [mask ^ bit for mask in masks]
        bit //= 2
    return parts, masks


def split_features(ids, feats, *refs):
    outs, sems = refs[:-1], refs[-1]
    group = ids[1]
    narrow = outs[0].shape[1]
    copies = [
        pltpu.make_async_copy(
            feats.at[:, aligned(jnp.bitwise_xor(group, m), narrow)], out, sems.at[m]
        )
        for m, out in enumerate(outs)
    ]
    for copy in copies:
        copy.start()
    for copy in copies:
        copy.wait()


def pick_blocks(groups, slots, at, tab, *refs):
    parts, (x, *outs) = refs[:groups], refs[groups:]
    domain, group = tab[at["me"]], tab[at["me"] + 1]
    tile = x.shape[1]
    per = x.shape[0] // groups
    for m, part in zip(reversed(range(groups)), parts):
        owner = jnp.bitwise_xor(group, m)
        for j in range(per):
            x[owner * per + j] = part[j * tile : (j + 1) * tile]
    for m, out in enumerate(outs, 1):
        reader = jnp.bitwise_xor(domain, m)
        for s in range(slots):
            entry = jnp.maximum(tab[at["out"] + reader * slots + s], 0)
            out[s * tile : (s + 1) * tile] = x[tab[at["pub"] + entry]]


def local_sum(per_row, at, tab, bank, x, out):
    pair = 2 if per_row % 2 == 0 else 1

    @pl.loop(0, out.shape[0])
    def _(r):
        acc = jnp.zeros(out.shape[1:], F32)
        for k in range(0, per_row, pair):
            spots = [r * per_row + k + j for j in range(pair)]
            left = jnp.concatenate([bank[tab[at["banks"] + a]] for a in spots], axis=1)
            right = jnp.concatenate([x[tab[at["cols"] + a]] for a in spots], axis=0)
            acc += dot(left, right)
        out[r] = acc


def add_halo(domains, groups, slots, at, tab, bank, local, *refs):
    recv, outs, acc = refs[: domains - 1], refs[domains - 1 : -1], refs[-1]
    domain, group = tab[at["me"]], tab[at["me"] + 1]
    tile = local.shape[1]
    per = local.shape[0] // groups
    acc[...] = local[...]
    for m, block in zip(reversed(range(1, domains)), recv):
        source = jnp.bitwise_xor(domain, m)
        for s in range(slots):
            i = source * slots + s

            @pl.when(tab[at["in"] + i] >= 0)
            def _(i=i, s=s, block=block):
                tile_here = bank[tab[at["hbanks"] + i]]
                acc[tab[at["hrows"] + i]] += dot(tile_here, block[s * tile : (s + 1) * tile])

    for m, out in enumerate(outs):
        owner = jnp.bitwise_xor(group, m)
        for j in range(per):
            out[j * tile : (j + 1) * tile] = acc[owner * per + j].astype(BF16)


def dense(groups, ids, weight, bias, cot, *refs):
    parts, (act, grad) = refs[:groups], refs[groups:]
    group = ids[1]
    narrow = parts[0].shape[1]
    wide = cot.shape[1] // groups
    total = None
    for m, part in zip(reversed(range(groups)), parts):
        term = dot(part[...], weight[aligned(jnp.bitwise_xor(group, m), narrow)])
        total = term if total is None else total + term
    pre = total + bias[...]
    act[...] = jnp.maximum(pre, 0.0).astype(BF16)
    masked = jnp.where(pre > 0, cot[...].astype(F32), 0.0).astype(BF16)
    for s in range(groups):
        grad[s] = masked[:, s * wide : (s + 1) * wide]


def back_halo(masks, slots, at, tab, bank_t, *refs):
    parts, (own, terms) = refs[: len(masks)], refs[len(masks) :]
    group = tab[at["me"] + 1]
    tile = bank_t.shape[1]
    per = parts[0].shape[1] // tile
    total = jnp.zeros((1, own.shape[2]), F32)
    for mask, part in zip(masks, parts):
        owner = jnp.bitwise_xor(group, mask)
        piece = part[group]
        total += jnp.sum(piece.astype(F32), axis=0, keepdims=True)
        for j in range(per):
            own[owner * per + j] = piece[j * tile : (j + 1) * tile]
    tail = bias_rows(total)
    for d in range(terms.shape[0]):
        for s in range(slots):
            i = d * slots + s
            live = (tab[at["in"] + i] >= 0).astype(F32)
            value = dot(bank_t[tab[at["hbanks"] + i]], own[tab[at["hrows"] + i]]) * live
            terms[d, s * tile : (s + 1) * tile] = value.astype(BF16)
        terms[d, slots * tile :] = tail


def weight_slice(scale, masks, *refs):
    groups = len(masks)
    aggs, parts, out = refs[:groups], refs[groups : 2 * groups], refs[2 * groups]
    total = None
    for agg, part in zip(aggs, parts):
        right = jnp.concatenate([part[s] for s in range(groups)], axis=1)
        term = lax.dot_general(
            agg[...], right, (((0,), (0,)), ((), ())), preferred_element_type=F32
        )
        total = term if total is None else total + term
    out[...] = (total * scale).astype(BF16)


def back_local(per_row, at, tab, bank_t, own, out):
    out[...] = jnp.zeros_like(out)

    @pl.loop(0, own.shape[0])
    def _(r):
        right = own[r]
        for k in range(per_row):
            spot = r * per_row + k
            out[tab[at["cols"] + spot]] += dot(bank_t[tab[at["banks"] + spot]], right)


def finish_nodes(slots, scale, at, tab, local, recv, *refs):
    outs, acc = refs[:-1], refs[-1]
    groups = len(outs)
    group = tab[at["me"] + 1]
    tile = local.shape[1]
    per = local.shape[0] // groups
    acc[...] = local[...]
    total = jnp.zeros((EXTRA, local.shape[2]), F32)
    for d in range(recv.shape[0]):
        total += recv[d, slots * tile : slots * tile + EXTRA].astype(F32)
        for s in range(slots):
            entry = tab[at["out"] + d * slots + s]

            @pl.when(entry >= 0)
            def _(d=d, s=s, entry=entry):
                spot = tab[at["pub"] + jnp.maximum(entry, 0)]
                acc[spot] += recv[d, s * tile : (s + 1) * tile].astype(F32)

    tail = bias_rows((total[0:1] + total[1:2]) * scale)
    for m, out in enumerate(outs):
        owner = jnp.bitwise_xor(group, m)
        for j in range(per):
            out[j * tile : (j + 1) * tile] = acc[owner * per + j].astype(BF16)
        out[per * tile :] = tail


def node_grads(groups, ids, weight, *refs):
    parts, (out, bias_out, hid) = refs[:groups], refs[groups:]
    group = ids[1]
    rows = out.shape[0]
    for m, part in zip(reversed(range(groups)), parts):
        hid[jnp.bitwise_xor(group, m)] = part[...]
    left = jnp.concatenate([hid[s, :rows] for s in range(groups)], axis=1)
    out[...] = lax.dot_general(
        left, weight[...], (((1,), (1,)), ((), ())), preferred_element_type=F32
    ).astype(BF16)
    tail = jnp.concatenate([hid[s, rows:] for s in range(groups)], axis=1).astype(F32)
    bias_out[...] = tail[0:1] + tail[1:2]


def place_weight(masks, ids, *refs):
    parts, (out, wide, sems) = refs[: len(masks)], refs[-3:]
    group = ids[1]
    rows = parts[0].shape[0]
    copies = []
    for i, (mask, part) in enumerate(zip(masks, parts)):
        wide[i] = part[...].astype(F32)
        spot = out.at[aligned(jnp.bitwise_xor(group, mask), rows)]
        copies.append(pltpu.make_async_copy(wide.at[i], spot, sems.at[i]))
        copies[-1].start()
    for copy in copies:
        copy.wait()


def per_device(
    node_feats,
    weight,
    bias,
    cotangent,
    tile_bank,
    local_cols,
    local_banks,
    published,
    send_table,
    halo_rows,
    halo_banks,
):
    domains = lax.axis_size("dom")
    groups = lax.axis_size("grp")
    domain_index = lax.axis_index("dom")
    rows_here, embed = node_feats.shape
    hidden = weight.shape[1]
    tile = tile_bank.shape[1]
    slots = send_table.shape[2]
    per_row = local_cols.shape[2]
    part_rows = rows_here * groups
    blocks = part_rows // tile
    narrow = embed // groups
    wide = hidden // groups
    share = narrow // domains
    peers = domains - 1

    ids = jnp.stack([domain_index, lax.axis_index("grp")]).astype(jnp.int32)
    tables = {
        "cols": local_cols[0],
        "banks": local_banks[0],
        "pub": published[0],
        "out": lax.dynamic_index_in_dim(send_table, domain_index, 0, keepdims=False),
        "in": lax.dynamic_index_in_dim(send_table, domain_index, 1, keepdims=False),
        "hrows": halo_rows[0],
        "hbanks": halo_banks[0],
        "me": ids,
    }
    at, place = {}, 0
    for name, table in tables.items():
        at[name] = place
        place += table.size
    tab = jnp.concatenate([table.reshape(-1) for table in tables.values()])
    bank_t = jnp.swapaxes(tile_bank, 1, 2)

    feats = call(
        split_features,
        [shape((rows_here, narrow), BF16)] * groups,
        [SMEM, pl.BlockSpec(memory_space=pl.ANY)],
        [pltpu.SemaphoreType.DMA((groups,))],
        nbytes=4 * rows_here * embed,
        name="split_features",
    )(ids, node_feats)
    feats = exchange(feats, "grp")
    x, *offered = call(
        functools.partial(pick_blocks, groups, slots, at),
        [shape((blocks, tile, narrow), BF16)] + [shape((slots * tile, narrow), BF16)] * peers,
        [SMEM] + [VMEM] * groups,
        nbytes=4 * (peers * slots + blocks) * tile * narrow,
        name="pick_blocks",
    )(tab, *reversed(feats))
    arrived = exchange([None] + offered, "dom")[1:]
    local = call(
        functools.partial(local_sum, per_row, at),
        shape((blocks, tile, narrow), F32),
        [SMEM, VMEM, VMEM],
        flops=2 * blocks * per_row * tile * tile * narrow,
        nbytes=blocks * tile * narrow * 6,
        name="local_sum",
    )(tab, tile_bank, x)
    aggs = call(
        functools.partial(add_halo, domains, groups, slots, at),
        [shape((rows_here, narrow), BF16)] * groups,
        [SMEM, VMEM, VMEM] + [VMEM] * peers,
        [pltpu.VMEM((blocks, tile, narrow), F32)],
        flops=2 * peers * slots * tile * tile * narrow,
        nbytes=blocks * tile * narrow * 8,
        name="add_halo",
    )(tab, tile_bank, local, *reversed(arrived))
    activations, grad = call(
        functools.partial(dense, groups),
        [shape((rows_here, hidden), BF16), shape((groups, rows_here, wide), BF16)],
        [SMEM] + [VMEM] * (3 + groups),
        flops=2 * rows_here * embed * hidden,
        nbytes=embed * hidden * 2 + rows_here * (embed + 3 * hidden) * 2,
        name="dense",
    )(ids, weight, bias.reshape(1, hidden), cotangent, *reversed(exchange(aggs, "grp")))

    grads, masks = spread(grad, "grp")
    norm_scale = float(rows_here * groups * domains) ** (-0.5)
    part = call(
        functools.partial(weight_slice, norm_scale, masks),
        shape((narrow, hidden), BF16),
        [VMEM] * (2 * groups),
        flops=2 * part_rows * narrow * hidden,
        nbytes=part_rows * (narrow + hidden) * 2,
        name="weight_slice",
    )(*[aggs[m] for m in masks], *grads)
    joined = lax.psum(part, "dom")
    own, terms = call(
        functools.partial(back_halo, masks, slots, at),
        [
            shape((blocks, tile, wide), BF16),
            shape((domains, slots * tile + EXTRA, wide), BF16),
        ],
        [SMEM, VMEM] + [VMEM] * len(masks),
        flops=2 * domains * slots * tile * tile * wide,
        nbytes=(domains * slots + blocks) * tile * wide * 2,
        name="back_halo",
    )(tab, bank_t, *grads)
    returned = lax.all_to_all(terms, "dom", split_axis=0, concat_axis=0, tiled=True)
    back = call(
        functools.partial(back_local, per_row, at),
        shape((blocks, tile, wide), F32),
        [SMEM, VMEM, VMEM],
        flops=2 * blocks * per_row * tile * tile * wide,
        nbytes=blocks * tile * wide * 6,
        name="back_local",
    )(tab, bank_t, own)
    joined, returned, back = lax.optimization_barrier((joined, returned, back))
    hid = call(
        functools.partial(finish_nodes, slots, norm_scale, at),
        [shape((rows_here + EXTRA, wide), BF16)] * groups,
        [SMEM, VMEM, VMEM],
        [pltpu.VMEM((blocks, tile, wide), F32)],
        nbytes=domains * slots * tile * wide * 2 + blocks * tile * wide * 6,
        name="finish_nodes",
    )(tab, back, returned)
    grad_nodes, grad_bias = call(
        functools.partial(node_grads, groups),
        [shape((rows_here, embed), BF16), shape((1, hidden), F32)],
        [SMEM, VMEM] + [VMEM] * groups,
        [pltpu.VMEM((groups, rows_here + EXTRA, wide), BF16)],
        flops=2 * rows_here * embed * hidden,
        nbytes=embed * hidden * 2 + rows_here * (embed + hidden) * 2,
        name="node_grads",
    )(ids, weight, *reversed(exchange(hid, "grp")))
    weights, masks = spread(joined, "grp")
    half = groups // 2
    grad_weight = None
    for chosen in ([m for m in range(groups) if m < half], [m for m in range(groups) if m >= half]):
        spots = [masks.index(m) for m in chosen]
        before = [] if grad_weight is None else [grad_weight]
        grad_weight = call(
            functools.partial(place_weight, chosen),
            shape((embed, hidden), F32),
            [SMEM] + [VMEM] * half + [pl.BlockSpec(memory_space=pl.ANY)] * len(before),
            [pltpu.VMEM((half, narrow, hidden), F32), pltpu.SemaphoreType.DMA((half,))],
            nbytes=embed * hidden * 3,
            name="place_weight",
            out_specs=pl.BlockSpec(memory_space=pl.ANY),
            aliases={half + 1: 0} if before else {},
        )(ids, *[weights[i] for i in spots], *before)
    return (activations, grad_nodes, grad_weight, grad_bias.reshape(hidden))


def solution(mesh):
    in_specs = (
        P(("dom", "grp"), None),
        P(),
        P(),
        P(("dom", "grp"), None),
        P(),
        P("dom", None, None),
        P("dom", None, None),
        P("dom", None),
        P(),
        P("dom", None, None),
        P("dom", None, None),
    )
    out_specs = (P(("dom", "grp"), None), P(("dom", "grp"), None), P(), P())
    return jax.shard_map(
        per_device, mesh=mesh, in_specs=in_specs, out_specs=out_specs, check_vma=False
    )
```

```python
import functools

import jax
import jax.numpy as jnp
from jax import lax
from jax.experimental import pallas as pl
from jax.experimental.pallas import tpu as pltpu
from jax.sharding import PartitionSpec as P

VMEM = pl.BlockSpec(memory_space=pltpu.VMEM)
SMEM = pl.BlockSpec(memory_space=pltpu.SMEM)
EXTRA = 16
F32 = jnp.float32
BF16 = jnp.bfloat16


def call(body, out_shape, specs, scratch=(), flops=0, nbytes=0, name=None, out_specs=None, aliases=()):
    return pl.pallas_call(
        body,
        out_shape=out_shape,
        in_specs=specs,
        out_specs=jax.tree.map(lambda _: VMEM, out_shape) if out_specs is None else out_specs,
        scratch_shapes=list(scratch),
        input_output_aliases=dict(aliases),
        compiler_params=pltpu.CompilerParams(vmem_limit_bytes=16 * 1024 * 1024),
        cost_estimate=pl.CostEstimate(flops=flops, bytes_accessed=nbytes, transcendentals=0),
        name=name,
    )


def shape(dims, kind):
    return jax.ShapeDtypeStruct(tuple(dims), kind)


def dot(a, b):
    return jnp.dot(a, b, preferred_element_type=F32)


def bias_rows(total):
    high = total.astype(BF16).astype(F32)
    rest = jnp.zeros((EXTRA - 2, total.shape[1]), F32)
    return jnp.concatenate([high, total - high, rest], axis=0).astype(BF16)


def aligned(start, step):
    return pl.ds(pl.multiple_of(start * step, step), step)


def exchange(parts, axis):
    size = lax.axis_size(axis)
    got = {0: parts[0]}
    for m in reversed(range(1, size)):
        got[m] = lax.ppermute(parts[m], axis, [(i, i ^ m) for i in range(size)])
    return [got[m] for m in range(size)]


def spread(value, axis):
    size = lax.axis_size(axis)
    parts, masks = [value], [0]
    bit = size // 2
    while bit:
        pairs = [(i, i ^ bit) for i in range(size)]
        parts = parts + [lax.ppermute(part, axis, pairs) for part in parts]
        masks = masks + [mask ^ bit for mask in masks]
        bit //= 2
    return parts, masks


def split_features(ids, feats, *refs):
    outs, sems = refs[:-1], refs[-1]
    group = ids[1]
    narrow = outs[0].shape[1]
    copies = [
        pltpu.make_async_copy(
            feats.at[:, aligned(jnp.bitwise_xor(group, m), narrow)], out, sems.at[m]
        )
        for m, out in enumerate(outs)
    ]
    for copy in copies:
        copy.start()
    for copy in copies:
        copy.wait()


def pick_blocks(groups, slots, at, tab, *refs):
    parts, (x, *outs) = refs[:groups], refs[groups:]
    domain, group = tab[at["me"]], tab[at["me"] + 1]
    tile = x.shape[1]
    per = x.shape[0] // groups
    for m, part in zip(reversed(range(groups)), parts):
        owner = jnp.bitwise_xor(group, m)
        for j in range(per):
            x[owner * per + j] = part[j * tile : (j + 1) * tile]
    for m, out in enumerate(outs, 1):
        reader = jnp.bitwise_xor(domain, m)
        for s in range(slots):
            entry = jnp.maximum(tab[at["out"] + reader * slots + s], 0)
            out[s * tile : (s + 1) * tile] = x[tab[at["pub"] + entry]]


def local_sum(per_row, at, tab, bank, x, out):
    pair = 2 if per_row % 2 == 0 else 1

    @pl.loop(0, out.shape[0])
    def _(r):
        acc = jnp.zeros(out.shape[1:], F32)
        for k in range(0, per_row, pair):
            spots = [r * per_row + k + j for j in range(pair)]
            left = jnp.concatenate([bank[tab[at["banks"] + a]] for a in spots], axis=1)
            right = jnp.concatenate([x[tab[at["cols"] + a]] for a in spots], axis=0)
            acc += dot(left, right)
        out[r] = acc


def add_halo(domains, groups, slots, at, tab, bank, local, *refs):
    recv, outs, acc = refs[: domains - 1], refs[domains - 1 : -1], refs[-1]
    domain, group = tab[at["me"]], tab[at["me"] + 1]
    tile = local.shape[1]
    per = local.shape[0] // groups
    acc[...] = local[...]
    for m, block in zip(reversed(range(1, domains)), recv):
        source = jnp.bitwise_xor(domain, m)
        for s in range(slots):
            i = source * slots + s

            @pl.when(tab[at["in"] + i] >= 0)
            def _(i=i, s=s, block=block):
                tile_here = bank[tab[at["hbanks"] + i]]
                acc[tab[at["hrows"] + i]] += dot(tile_here, block[s * tile : (s + 1) * tile])

    for m, out in enumerate(outs):
        owner = jnp.bitwise_xor(group, m)
        for j in range(per):
            out[j * tile : (j + 1) * tile] = acc[owner * per + j].astype(BF16)


def dense(groups, ids, weight, bias, cot, *refs):
    parts, (act, grad) = refs[:groups], refs[groups:]
    group = ids[1]
    narrow = parts[0].shape[1]
    wide = cot.shape[1] // groups
    total = None
    for m, part in zip(reversed(range(groups)), parts):
        term = dot(part[...], weight[aligned(jnp.bitwise_xor(group, m), narrow)])
        total = term if total is None else total + term
    pre = total + bias[...]
    act[...] = jnp.maximum(pre, 0.0).astype(BF16)
    masked = jnp.where(pre > 0, cot[...].astype(F32), 0.0).astype(BF16)
    for s in range(groups):
        grad[s] = masked[:, s * wide : (s + 1) * wide]


def back_halo(masks, slots, at, tab, bank_t, *refs):
    parts, (own, terms) = refs[: len(masks)], refs[len(masks) :]
    group = tab[at["me"] + 1]
    tile = bank_t.shape[1]
    per = parts[0].shape[1] // tile
    total = jnp.zeros((1, own.shape[2]), F32)
    for mask, part in zip(masks, parts):
        owner = jnp.bitwise_xor(group, mask)
        piece = part[group]
        total += jnp.sum(piece.astype(F32), axis=0, keepdims=True)
        for j in range(per):
            own[owner * per + j] = piece[j * tile : (j + 1) * tile]
    tail = bias_rows(total)
    for d in range(terms.shape[0]):
        for s in range(slots):
            i = d * slots + s
            live = (tab[at["in"] + i] >= 0).astype(F32)
            value = dot(bank_t[tab[at["hbanks"] + i]], own[tab[at["hrows"] + i]]) * live
            terms[d, s * tile : (s + 1) * tile] = value.astype(BF16)
        terms[d, slots * tile :] = tail


def weight_slice(masks, *refs):
    groups = len(masks)
    aggs, parts, out = refs[:groups], refs[groups : 2 * groups], refs[2 * groups]
    total = None
    for agg, part in zip(aggs, parts):
        right = jnp.concatenate([part[s] for s in range(groups)], axis=1)
        term = lax.dot_general(
            agg[...], right, (((0,), (0,)), ((), ())), preferred_element_type=F32
        )
        total = term if total is None else total + term
    rows = out.shape[1]
    for d in range(out.shape[0]):
        out[d] = total[d * rows : (d + 1) * rows].astype(BF16)


def sum_shares(scale, shares, out):
    total = shares[0].astype(F32)
    for d in range(1, shares.shape[0]):
        total += shares[d].astype(F32)
    summed = (total * scale).astype(BF16)
    for d in range(out.shape[0]):
        out[d] = summed


def back_local(per_row, at, tab, bank_t, own, out):
    out[...] = jnp.zeros_like(out)

    @pl.loop(0, own.shape[0])
    def _(r):
        right = own[r]
        for k in range(per_row):
            spot = r * per_row + k
            out[tab[at["cols"] + spot]] += dot(bank_t[tab[at["banks"] + spot]], right)


def finish_nodes(slots, scale, at, tab, local, recv, *refs):
    outs, acc = refs[:-1], refs[-1]
    groups = len(outs)
    group = tab[at["me"] + 1]
    tile = local.shape[1]
    per = local.shape[0] // groups
    acc[...] = local[...]
    total = jnp.zeros((EXTRA, local.shape[2]), F32)
    for d in range(recv.shape[0]):
        total += recv[d, slots * tile : slots * tile + EXTRA].astype(F32)
        for s in range(slots):
            entry = tab[at["out"] + d * slots + s]

            @pl.when(entry >= 0)
            def _(d=d, s=s, entry=entry):
                spot = tab[at["pub"] + jnp.maximum(entry, 0)]
                acc[spot] += recv[d, s * tile : (s + 1) * tile].astype(F32)

    tail = bias_rows((total[0:1] + total[1:2]) * scale)
    for m, out in enumerate(outs):
        owner = jnp.bitwise_xor(group, m)
        for j in range(per):
            out[j * tile : (j + 1) * tile] = acc[owner * per + j].astype(BF16)
        out[per * tile :] = tail


def node_grads(groups, ids, weight, *refs):
    parts, (out, bias_out, hid) = refs[:groups], refs[groups:]
    group = ids[1]
    rows = out.shape[0]
    for m, part in zip(reversed(range(groups)), parts):
        hid[jnp.bitwise_xor(group, m)] = part[...]
    left = jnp.concatenate([hid[s, :rows] for s in range(groups)], axis=1)
    out[...] = lax.dot_general(
        left, weight[...], (((1,), (1,)), ((), ())), preferred_element_type=F32
    ).astype(BF16)
    tail = jnp.concatenate([hid[s, rows:] for s in range(groups)], axis=1).astype(F32)
    bias_out[...] = tail[0:1] + tail[1:2]


def place_weight(masks, ids, *refs):
    parts, (out, wide, sems) = refs[: len(masks)], refs[-3:]
    group = ids[1]
    rows = parts[0].shape[0]
    copies = []
    for i, (mask, part) in enumerate(zip(masks, parts)):
        wide[i] = part[...].astype(F32)
        spot = out.at[aligned(jnp.bitwise_xor(group, mask), rows)]
        copies.append(pltpu.make_async_copy(wide.at[i], spot, sems.at[i]))
        copies[-1].start()
    for copy in copies:
        copy.wait()


def per_device(
    node_feats,
    weight,
    bias,
    cotangent,
    tile_bank,
    local_cols,
    local_banks,
    published,
    send_table,
    halo_rows,
    halo_banks,
):
    domains = lax.axis_size("dom")
    groups = lax.axis_size("grp")
    domain_index = lax.axis_index("dom")
    rows_here, embed = node_feats.shape
    hidden = weight.shape[1]
    tile = tile_bank.shape[1]
    slots = send_table.shape[2]
    per_row = local_cols.shape[2]
    part_rows = rows_here * groups
    blocks = part_rows // tile
    narrow = embed // groups
    wide = hidden // groups
    share = narrow // domains
    peers = domains - 1

    ids = jnp.stack([domain_index, lax.axis_index("grp")]).astype(jnp.int32)
    tables = {
        "cols": local_cols[0],
        "banks": local_banks[0],
        "pub": published[0],
        "out": lax.dynamic_index_in_dim(send_table, domain_index, 0, keepdims=False),
        "in": lax.dynamic_index_in_dim(send_table, domain_index, 1, keepdims=False),
        "hrows": halo_rows[0],
        "hbanks": halo_banks[0],
        "me": ids,
    }
    at, place = {}, 0
    for name, table in tables.items():
        at[name] = place
        place += table.size
    tab = jnp.concatenate([table.reshape(-1) for table in tables.values()])
    bank_t = jnp.swapaxes(tile_bank, 1, 2)

    feats = call(
        split_features,
        [shape((rows_here, narrow), BF16)] * groups,
        [SMEM, pl.BlockSpec(memory_space=pl.ANY)],
        [pltpu.SemaphoreType.DMA((groups,))],
        nbytes=4 * rows_here * embed,
        name="split_features",
    )(ids, node_feats)
    feats = exchange(feats, "grp")
    x, *offered = call(
        functools.partial(pick_blocks, groups, slots, at),
        [shape((blocks, tile, narrow), BF16)] + [shape((slots * tile, narrow), BF16)] * peers,
        [SMEM] + [VMEM] * groups,
        nbytes=4 * (peers * slots + blocks) * tile * narrow,
        name="pick_blocks",
    )(tab, *reversed(feats))
    arrived = exchange([None] + offered, "dom")[1:]
    local = call(
        functools.partial(local_sum, per_row, at),
        shape((blocks, tile, narrow), F32),
        [SMEM, VMEM, VMEM],
        flops=2 * blocks * per_row * tile * tile * narrow,
        nbytes=blocks * tile * narrow * 6,
        name="local_sum",
    )(tab, tile_bank, x)
    aggs = call(
        functools.partial(add_halo, domains, groups, slots, at),
        [shape((rows_here, narrow), BF16)] * groups,
        [SMEM, VMEM, VMEM] + [VMEM] * peers,
        [pltpu.VMEM((blocks, tile, narrow), F32)],
        flops=2 * peers * slots * tile * tile * narrow,
        nbytes=blocks * tile * narrow * 8,
        name="add_halo",
    )(tab, tile_bank, local, *reversed(arrived))
    activations, grad = call(
        functools.partial(dense, groups),
        [shape((rows_here, hidden), BF16), shape((groups, rows_here, wide), BF16)],
        [SMEM] + [VMEM] * (3 + groups),
        flops=2 * rows_here * embed * hidden,
        nbytes=embed * hidden * 2 + rows_here * (embed + 3 * hidden) * 2,
        name="dense",
    )(ids, weight, bias.reshape(1, hidden), cotangent, *reversed(exchange(aggs, "grp")))

    grads, masks = spread(grad, "grp")
    norm_scale = float(rows_here * groups * domains) ** (-0.5)
    part = call(
        functools.partial(weight_slice, masks),
        shape((domains, share, hidden), BF16),
        [VMEM] * (2 * groups),
        flops=2 * part_rows * narrow * hidden,
        nbytes=part_rows * (narrow + hidden) * 2,
        name="weight_slice",
    )(*[aggs[m] for m in masks], *grads)
    shares = lax.all_to_all(part, "dom", split_axis=0, concat_axis=0, tiled=True)
    tab_after, _ = lax.optimization_barrier((tab, part))
    own, terms = call(
        functools.partial(back_halo, masks, slots, at),
        [
            shape((blocks, tile, wide), BF16),
            shape((domains, slots * tile + EXTRA, wide), BF16),
        ],
        [SMEM, VMEM] + [VMEM] * len(masks),
        flops=2 * domains * slots * tile * tile * wide,
        nbytes=(domains * slots + blocks) * tile * wide * 2,
        name="back_halo",
    )(tab_after, bank_t, *grads)
    returned = lax.all_to_all(terms, "dom", split_axis=0, concat_axis=0, tiled=True)
    back = call(
        functools.partial(back_local, per_row, at),
        shape((blocks, tile, wide), F32),
        [SMEM, VMEM, VMEM],
        flops=2 * blocks * per_row * tile * tile * wide,
        nbytes=blocks * tile * wide * 6,
        name="back_local",
    )(tab, bank_t, own)
    shares, _ = lax.optimization_barrier((shares, terms))
    summed = call(
        functools.partial(sum_shares, norm_scale),
        shape((domains, share, hidden), BF16),
        [VMEM],
        nbytes=domains * share * hidden * 4,
        name="sum_shares",
    )(shares)
    joined = lax.all_to_all(summed, "dom", split_axis=0, concat_axis=0, tiled=True)
    joined = joined.reshape(narrow, hidden)
    joined, returned, back = lax.optimization_barrier((joined, returned, back))
    hid = call(
        functools.partial(finish_nodes, slots, norm_scale, at),
        [shape((rows_here + EXTRA, wide), BF16)] * groups,
        [SMEM, VMEM, VMEM],
        [pltpu.VMEM((blocks, tile, wide), F32)],
        nbytes=domains * slots * tile * wide * 2 + blocks * tile * wide * 6,
        name="finish_nodes",
    )(tab, back, returned)
    weights, masks = spread(joined, "grp")
    half = groups // 2
    near = [masks.index(m) for m in range(half)]
    far = [masks.index(m) for m in range(half, groups)]
    placing = dict(
        out_shape=shape((embed, hidden), F32),
        scratch=[pltpu.VMEM((half, narrow, hidden), F32), pltpu.SemaphoreType.DMA((half,))],
        nbytes=embed * hidden * 3,
        name="place_weight",
        out_specs=pl.BlockSpec(memory_space=pl.ANY),
    )
    grad_weight = call(
        functools.partial(place_weight, [masks[i] for i in near]),
        specs=[SMEM] + [VMEM] * half,
        **placing,
    )(ids, *[weights[i] for i in near])
    hid = exchange(hid, "grp")
    grad_weight, *hid = lax.optimization_barrier((grad_weight, *hid))
    grad_nodes, grad_bias = call(
        functools.partial(node_grads, groups),
        [shape((rows_here, embed), BF16), shape((1, hidden), F32)],
        [SMEM, VMEM] + [VMEM] * groups,
        [pltpu.VMEM((groups, rows_here + EXTRA, wide), BF16)],
        flops=2 * rows_here * embed * hidden,
        nbytes=embed * hidden * 2 + rows_here * (embed + hidden) * 2,
        name="node_grads",
    )(ids, weight, *reversed(hid))
    grad_weight = call(
        functools.partial(place_weight, [masks[i] for i in far]),
        specs=[SMEM] + [VMEM] * half + [pl.BlockSpec(memory_space=pl.ANY)],
        aliases={half + 1: 0},
        **placing,
    )(ids, *[weights[i] for i in far], grad_weight)
    return (activations, grad_nodes, grad_weight, grad_bias.reshape(hidden))


def solution(mesh):
    in_specs = (
        P(("dom", "grp"), None),
        P(),
        P(),
        P(("dom", "grp"), None),
        P(),
        P("dom", None, None),
        P("dom", None, None),
        P("dom", None),
        P(),
        P("dom", None, None),
        P("dom", None, None),
    )
    out_specs = (P(("dom", "grp"), None), P(("dom", "grp"), None), P(), P())
    return jax.shard_map(
        per_device, mesh=mesh, in_specs=in_specs, out_specs=out_specs, check_vma=False
    )
```

```python
import functools

import jax
import jax.numpy as jnp
from jax import lax
from jax.experimental import pallas as pl
from jax.experimental.pallas import tpu as pltpu
from jax.sharding import PartitionSpec as P

VMEM = pl.BlockSpec(memory_space=pltpu.VMEM)
SMEM = pl.BlockSpec(memory_space=pltpu.SMEM)
EXTRA = 16
F32 = jnp.float32
BF16 = jnp.bfloat16


def call(body, out_shape, specs, scratch=(), flops=0, nbytes=0, name=None, out_specs=None, aliases=()):
    return pl.pallas_call(
        body,
        out_shape=out_shape,
        in_specs=specs,
        out_specs=jax.tree.map(lambda _: VMEM, out_shape) if out_specs is None else out_specs,
        scratch_shapes=list(scratch),
        input_output_aliases=dict(aliases),
        compiler_params=pltpu.CompilerParams(vmem_limit_bytes=16 * 1024 * 1024),
        cost_estimate=pl.CostEstimate(flops=flops, bytes_accessed=nbytes, transcendentals=0),
        name=name,
    )


def shape(dims, kind):
    return jax.ShapeDtypeStruct(tuple(dims), kind)


def dot(a, b):
    return jnp.dot(a, b, preferred_element_type=F32)


def bias_rows(total):
    high = total.astype(BF16).astype(F32)
    rest = jnp.zeros((EXTRA - 2, total.shape[1]), F32)
    return jnp.concatenate([high, total - high, rest], axis=0).astype(BF16)


def aligned(start, step):
    return pl.ds(pl.multiple_of(start * step, step), step)


def swap(value, axis, mask):
    return lax.ppermute(value, axis, [(i, i ^ mask) for i in range(lax.axis_size(axis))])


def exchange(parts, axis):
    return list(parts[:1]) + [swap(part, axis, m) for m, part in enumerate(parts[1:], 1)]


def spread(value, axis):
    size = lax.axis_size(axis)
    parts, masks = [value], [0]
    bit = size // 2
    while bit:
        parts = parts + [swap(part, axis, bit) for part in parts]
        masks = masks + [mask ^ bit for mask in masks]
        bit //= 2
    return parts, masks


def split_features(ids, feats, *refs):
    outs, sems = refs[:-1], refs[-1]
    group = ids[1]
    narrow = outs[0].shape[1]
    copies = [
        pltpu.make_async_copy(
            feats.at[:, aligned(jnp.bitwise_xor(group, m), narrow)], out, sems.at[m]
        )
        for m, out in enumerate(outs)
    ]
    for copy in copies:
        copy.start()
    for copy in copies:
        copy.wait()


def pick_blocks(groups, slots, at, tab, *refs):
    parts, (x, offered, *outs) = refs[:groups], refs[groups:]
    domain, group = tab[at["me"]], tab[at["me"] + 1]
    tile = x.shape[1]
    per = x.shape[0] // groups
    for m, part in enumerate(parts):
        owner = jnp.bitwise_xor(group, m)
        for j in range(per):
            x[owner * per + j] = part[j * tile : (j + 1) * tile]
    for j in range(offered.shape[0]):
        offered[j] = x[tab[at["pub"] + j]]
    for m, out in enumerate(outs, 1):
        reader = jnp.bitwise_xor(domain, m)
        for s in range(slots):
            entry = jnp.maximum(tab[at["out"] + reader * slots + s], 0)
            out[s * tile : (s + 1) * tile] = x[tab[at["pub"] + entry]]


def pick_relayed(slots, at, tab, offered, *outs):
    tile = offered.shape[1]
    for m, out in enumerate(outs, 1):
        reader = jnp.bitwise_xor(tab[at["me"]], m)
        for s in range(slots):
            entry = jnp.maximum(tab[at["out2"] + reader * slots + s], 0)
            out[s * tile : (s + 1) * tile] = offered[entry]


def local_sum(per_row, at, tab, bank, x, out):
    pair = 2 if per_row % 2 == 0 else 1

    @pl.loop(0, out.shape[0])
    def _(r):
        acc = jnp.zeros(out.shape[1:], F32)
        for k in range(0, per_row, pair):
            spots = [r * per_row + k + j for j in range(pair)]
            left = jnp.concatenate([bank[tab[at["banks"] + a]] for a in spots], axis=1)
            right = jnp.concatenate([x[tab[at["cols"] + a]] for a in spots], axis=0)
            acc += dot(left, right)
        out[r] = acc


def add_halo(half, groups, slots, at, tab, bank, local, mirrored, *refs):
    near, far = refs[: half - 1], refs[half - 1 : 2 * half - 2]
    outs, acc = refs[2 * half - 2 : -1], refs[-1]
    domain, group = tab[at["me"]], tab[at["me"] + 1]
    tile = local.shape[1]
    per = local.shape[0] // groups
    acc[...] = local[...]

    def add(source, get):
        for s in range(slots):
            i = source * slots + s
            entry = tab[at["in"] + i]

            @pl.when(entry >= 0)
            def _(i=i, s=s, entry=entry):
                acc[tab[at["hrows"] + i]] += dot(bank[tab[at["hbanks"] + i]], get(s, entry))

    for m, block in enumerate(near, 1):
        add(jnp.bitwise_xor(domain, m), lambda s, _, block=block: block[s * tile : (s + 1) * tile])
    add(jnp.bitwise_xor(domain, half), lambda _, entry: mirrored[jnp.maximum(entry, 0)])
    for m, block in enumerate(far, half + 1):
        add(jnp.bitwise_xor(domain, m), lambda s, _, block=block: block[s * tile : (s + 1) * tile])
    for m, out in enumerate(outs):
        owner = jnp.bitwise_xor(group, m)
        for j in range(per):
            out[j * tile : (j + 1) * tile] = acc[owner * per + j].astype(BF16)


def dense(groups, ids, weight, bias, cot, *refs):
    parts, (act, grad) = refs[:groups], refs[groups:]
    group = ids[1]
    narrow = parts[0].shape[1]
    wide = cot.shape[1] // groups
    total = None
    for m, part in enumerate(parts):
        term = dot(part[...], weight[aligned(jnp.bitwise_xor(group, m), narrow)])
        total = term if total is None else total + term
    pre = total + bias[...]
    act[...] = jnp.maximum(pre, 0.0).astype(BF16)
    masked = jnp.where(pre > 0, cot[...].astype(F32), 0.0).astype(BF16)
    for s in range(groups):
        grad[s] = masked[:, s * wide : (s + 1) * wide]


def back_halo(masks, slots, at, tab, bank_t, *refs):
    parts, (own, mine, kept, *terms) = refs[: len(masks)], refs[len(masks) :]
    domain, group = tab[at["me"]], tab[at["me"] + 1]
    tile = bank_t.shape[1]
    per = parts[0].shape[1] // tile
    half = len(terms) + 1
    total = jnp.zeros((1, own.shape[2]), F32)
    for mask, part in zip(masks, parts):
        owner = jnp.bitwise_xor(group, mask)
        piece = part[group]
        total += jnp.sum(piece.astype(F32), axis=0, keepdims=True)
        for j in range(per):
            own[owner * per + j] = piece[j * tile : (j + 1) * tile]
    mine[...] = total
    tail = bias_rows(total)

    def put(out, place, source):
        for s in range(slots):
            i = source * slots + s
            live = (tab[at["in"] + i] >= 0).astype(F32)
            value = dot(bank_t[tab[at["hbanks"] + i]], own[tab[at["hrows"] + i]]) * live
            spot = (place * slots + s) * tile
            out[spot : spot + tile] = value.astype(BF16)

    for m, term in enumerate(terms, 1):
        peer = jnp.bitwise_xor(domain, m)
        put(term, 0, peer)
        put(term, 1, jnp.bitwise_xor(peer, half))
        term[2 * slots * tile :] = tail
    put(kept, 0, jnp.bitwise_xor(domain, half))


def sum_mirror(slots, at, tab, mine, kept, *refs):
    recv, out, acc = refs[:-2], refs[-2], refs[-1]
    domain = tab[at["me"]]
    offered, tile = acc.shape[:2]
    acc[...] = jnp.zeros_like(acc)
    total = mine[...]
    for m, block in enumerate((kept,) + recv):
        reader = jnp.bitwise_xor(domain, m)
        for s in range(slots):
            entry = tab[at["out2"] + reader * slots + s]
            spot = (s + (slots if m else 0)) * tile

            @pl.when(entry >= 0)
            def _(entry=entry, spot=spot, block=block):
                acc[jnp.maximum(entry, 0)] += block[spot : spot + tile].astype(F32)

        if m:
            tail = block[2 * slots * tile :].astype(F32)
            total += tail[0:1] + tail[1:2]
    for j in range(offered):
        out[j * tile : (j + 1) * tile] = acc[j].astype(BF16)
    out[offered * tile :] = bias_rows(total)


def weight_slice(masks, *refs):
    groups = len(masks)
    aggs, parts, out = refs[:groups], refs[groups : 2 * groups], refs[2 * groups]
    total = None
    for agg, part in zip(aggs, parts):
        right = jnp.concatenate([part[s] for s in range(groups)], axis=1)
        term = lax.dot_general(
            agg[...], right, (((0,), (0,)), ((), ())), preferred_element_type=F32
        )
        total = term if total is None else total + term
    rows = out.shape[1]
    for d in range(out.shape[0]):
        out[d] = total[d * rows : (d + 1) * rows].astype(BF16)


def sum_shares(scale, shares, out):
    total = shares[0].astype(F32)
    for d in range(1, shares.shape[0]):
        total += shares[d].astype(F32)
    summed = (total * scale).astype(BF16)
    for d in range(out.shape[0]):
        out[d] = summed


def back_local(per_row, at, tab, bank_t, own, out):
    out[...] = jnp.zeros_like(out)

    @pl.loop(0, own.shape[0])
    def _(r):
        right = own[r]
        for k in range(per_row):
            spot = r * per_row + k
            out[tab[at["cols"] + spot]] += dot(bank_t[tab[at["banks"] + spot]], right)


def finish_nodes(half, slots, scale, at, tab, local, mine, mirrored, *refs):
    recv, outs, acc = refs[: half - 1], refs[half - 1 : -1], refs[-1]
    groups = len(outs)
    domain, group = tab[at["me"]], tab[at["me"] + 1]
    tile = local.shape[1]
    per = local.shape[0] // groups
    offered = (mirrored.shape[0] - EXTRA) // tile
    acc[...] = local[...]
    tail = mirrored[offered * tile :].astype(F32)
    for j in range(offered):
        acc[tab[at["pub"] + j]] += mirrored[j * tile : (j + 1) * tile].astype(F32)
    for m, block in enumerate(recv, 1):
        tail += block[2 * slots * tile :].astype(F32)
        reader = jnp.bitwise_xor(domain, m)
        for s in range(slots):
            entry = tab[at["out"] + reader * slots + s]

            @pl.when(entry >= 0)
            def _(s=s, entry=entry, block=block):
                spot = tab[at["pub"] + jnp.maximum(entry, 0)]
                acc[spot] += block[s * tile : (s + 1) * tile].astype(F32)

    rows = bias_rows((mine[...] + tail[0:1] + tail[1:2]) * scale)
    for m, out in enumerate(outs):
        owner = jnp.bitwise_xor(group, m)
        for j in range(per):
            out[j * tile : (j + 1) * tile] = acc[owner * per + j].astype(BF16)
        out[per * tile :] = rows


def node_grads(groups, ids, weight, *refs):
    parts, (out, bias_out, hid) = refs[:groups], refs[groups:]
    group = ids[1]
    rows = out.shape[0]
    for m, part in enumerate(parts):
        hid[jnp.bitwise_xor(group, m)] = part[...]
    left = jnp.concatenate([hid[s, :rows] for s in range(groups)], axis=1)
    out[...] = lax.dot_general(
        left, weight[...], (((1,), (1,)), ((), ())), preferred_element_type=F32
    ).astype(BF16)
    tail = jnp.concatenate([hid[s, rows:] for s in range(groups)], axis=1).astype(F32)
    bias_out[...] = tail[0:1] + tail[1:2]


def place_weight(masks, ids, *refs):
    parts, (out, wide, sems) = refs[: len(masks)], refs[-3:]
    group = ids[1]
    rows = parts[0].shape[0]
    copies = []
    for i, (mask, part) in enumerate(zip(masks, parts)):
        wide[i] = part[...].astype(F32)
        spot = out.at[aligned(jnp.bitwise_xor(group, mask), rows)]
        copies.append(pltpu.make_async_copy(wide.at[i], spot, sems.at[i]))
        copies[-1].start()
    for copy in copies:
        copy.wait()


def per_device(
    node_feats,
    weight,
    bias,
    cotangent,
    tile_bank,
    local_cols,
    local_banks,
    published,
    send_table,
    halo_rows,
    halo_banks,
):
    domains = lax.axis_size("dom")
    groups = lax.axis_size("grp")
    domain_index = lax.axis_index("dom")
    rows_here, embed = node_feats.shape
    hidden = weight.shape[1]
    tile = tile_bank.shape[1]
    slots = send_table.shape[2]
    per_row = local_cols.shape[2]
    part_rows = rows_here * groups
    blocks = part_rows // tile
    narrow = embed // groups
    wide = hidden // groups
    share = narrow // domains
    half = domains // 2
    peers = half - 1
    offers = published.shape[1]

    ids = jnp.stack([domain_index, lax.axis_index("grp")]).astype(jnp.int32)
    tables = {
        "cols": local_cols[0],
        "banks": local_banks[0],
        "pub": published[0],
        "out": lax.dynamic_index_in_dim(send_table, domain_index, 0, keepdims=False),
        "out2": lax.dynamic_index_in_dim(send_table, domain_index ^ half, 0, keepdims=False),
        "in": lax.dynamic_index_in_dim(send_table, domain_index, 1, keepdims=False),
        "hrows": halo_rows[0],
        "hbanks": halo_banks[0],
        "me": ids,
    }
    at, place = {}, 0
    for name, table in tables.items():
        at[name] = place
        place += table.size
    tab = jnp.concatenate([table.reshape(-1) for table in tables.values()])
    bank_t = jnp.swapaxes(tile_bank, 1, 2)

    feats = call(
        split_features,
        [shape((rows_here, narrow), BF16)] * groups,
        [SMEM, pl.BlockSpec(memory_space=pl.ANY)],
        [pltpu.SemaphoreType.DMA((groups,))],
        nbytes=4 * rows_here * embed,
        name="split_features",
    )(ids, node_feats)
    feats = exchange(feats, "grp")
    x, offered, *picked = call(
        functools.partial(pick_blocks, groups, slots, at),
        [shape((blocks, tile, narrow), BF16), shape((offers, tile, narrow), BF16)]
        + [shape((slots * tile, narrow), BF16)] * peers,
        [SMEM] + [VMEM] * groups,
        nbytes=4 * (peers * slots + blocks + offers) * tile * narrow,
        name="pick_blocks",
    )(tab, *feats)
    mirrored = swap(offered, "dom", half)
    near = exchange([None] + picked, "dom")[1:]
    local = call(
        functools.partial(local_sum, per_row, at),
        shape((blocks, tile, narrow), F32),
        [SMEM, VMEM, VMEM],
        flops=2 * blocks * per_row * tile * tile * narrow,
        nbytes=blocks * tile * narrow * 6,
        name="local_sum",
    )(tab, tile_bank, x)
    mirrored, local = lax.optimization_barrier((mirrored, local))
    relayed = call(
        functools.partial(pick_relayed, slots, at),
        [shape((slots * tile, narrow), BF16)] * peers,
        [SMEM, VMEM],
        nbytes=4 * peers * slots * tile * narrow,
        name="pick_relayed",
    )(tab, mirrored)
    far = exchange([None, *relayed], "dom")[1:]
    aggs = call(
        functools.partial(add_halo, half, groups, slots, at),
        [shape((rows_here, narrow), BF16)] * groups,
        [SMEM, VMEM, VMEM, VMEM] + [VMEM] * (2 * peers),
        [pltpu.VMEM((blocks, tile, narrow), F32)],
        flops=4 * half * slots * tile * tile * narrow,
        nbytes=blocks * tile * narrow * 8,
        name="add_halo",
    )(tab, tile_bank, local, mirrored, *near, *far)
    activations, grad = call(
        functools.partial(dense, groups),
        [shape((rows_here, hidden), BF16), shape((groups, rows_here, wide), BF16)],
        [SMEM] + [VMEM] * (3 + groups),
        flops=2 * rows_here * embed * hidden,
        nbytes=embed * hidden * 2 + rows_here * (embed + 3 * hidden) * 2,
        name="dense",
    )(ids, weight, bias.reshape(1, hidden), cotangent, *exchange(aggs, "grp"))

    grads, masks = spread(grad, "grp")
    norm_scale = float(rows_here * groups * domains) ** (-0.5)
    part = call(
        functools.partial(weight_slice, masks),
        shape((domains, share, hidden), BF16),
        [VMEM] * (2 * groups),
        flops=2 * part_rows * narrow * hidden,
        nbytes=part_rows * (narrow + hidden) * 2,
        name="weight_slice",
    )(*[aggs[m] for m in masks], *grads)
    shares = lax.all_to_all(part, "dom", split_axis=0, concat_axis=0, tiled=True)
    tab_after, _ = lax.optimization_barrier((tab, part))
    own, bias_here, kept, *terms = call(
        functools.partial(back_halo, masks, slots, at),
        [
            shape((blocks, tile, wide), BF16),
            shape((1, wide), F32),
            shape((slots * tile, wide), BF16),
        ]
        + [shape((2 * slots * tile + EXTRA, wide), BF16)] * peers,
        [SMEM, VMEM] + [VMEM] * len(masks),
        flops=2 * domains * slots * tile * tile * wide,
        nbytes=(domains * slots + blocks) * tile * wide * 2,
        name="back_halo",
    )(tab_after, bank_t, *grads)
    terms = exchange([None] + terms, "dom")[1:]
    crossing = call(
        functools.partial(sum_mirror, slots, at),
        shape((offers * tile + EXTRA, wide), BF16),
        [SMEM] + [VMEM] * (2 + peers),
        [pltpu.VMEM((offers, tile, wide), F32)],
        nbytes=4 * domains * slots * tile * wide,
        name="sum_mirror",
    )(tab, bias_here, kept, *terms)
    returned = swap(crossing, "dom", half)
    back = call(
        functools.partial(back_local, per_row, at),
        shape((blocks, tile, wide), F32),
        [SMEM, VMEM, VMEM],
        flops=2 * blocks * per_row * tile * tile * wide,
        nbytes=blocks * tile * wide * 6,
        name="back_local",
    )(tab, bank_t, own)
    shares, _ = lax.optimization_barrier((shares, terms))
    summed = call(
        functools.partial(sum_shares, norm_scale),
        shape((domains, share, hidden), BF16),
        [VMEM],
        nbytes=domains * share * hidden * 4,
        name="sum_shares",
    )(shares)
    summed, _ = lax.optimization_barrier((summed, crossing))
    joined = lax.all_to_all(summed, "dom", split_axis=0, concat_axis=0, tiled=True)
    joined = joined.reshape(narrow, hidden)
    joined, returned, back = lax.optimization_barrier((joined, returned, back))
    hid = call(
        functools.partial(finish_nodes, half, slots, norm_scale, at),
        [shape((rows_here + EXTRA, wide), BF16)] * groups,
        [SMEM, VMEM, VMEM, VMEM] + [VMEM] * peers,
        [pltpu.VMEM((blocks, tile, wide), F32)],
        nbytes=domains * slots * tile * wide * 2 + blocks * tile * wide * 6,
        name="finish_nodes",
    )(tab, back, bias_here, returned, *terms)
    weights, masks = spread(joined, "grp")
    count = groups // 2
    first = [masks.index(m) for m in range(count)]
    last = [masks.index(m) for m in range(count, groups)]
    placing = dict(
        out_shape=shape((embed, hidden), F32),
        scratch=[pltpu.VMEM((count, narrow, hidden), F32), pltpu.SemaphoreType.DMA((count,))],
        nbytes=embed * hidden * 3,
        name="place_weight",
        out_specs=pl.BlockSpec(memory_space=pl.ANY),
    )
    grad_weight = call(
        functools.partial(place_weight, [masks[i] for i in first]),
        specs=[SMEM] + [VMEM] * count,
        **placing,
    )(ids, *[weights[i] for i in first])
    hid = exchange(hid, "grp")
    grad_weight, *hid = lax.optimization_barrier((grad_weight, *hid))
    grad_nodes, grad_bias = call(
        functools.partial(node_grads, groups),
        [shape((rows_here, embed), BF16), shape((1, hidden), F32)],
        [SMEM, VMEM] + [VMEM] * groups,
        [pltpu.VMEM((groups, rows_here + EXTRA, wide), BF16)],
        flops=2 * rows_here * embed * hidden,
        nbytes=embed * hidden * 2 + rows_here * (embed + hidden) * 2,
        name="node_grads",
    )(ids, weight, *hid)
    grad_weight = call(
        functools.partial(place_weight, [masks[i] for i in last]),
        specs=[SMEM] + [VMEM] * count + [pl.BlockSpec(memory_space=pl.ANY)],
        aliases={count + 1: 0},
        **placing,
    )(ids, *[weights[i] for i in last], grad_weight)
    return (activations, grad_nodes, grad_weight, grad_bias.reshape(hidden))


def solution(mesh):
    in_specs = (
        P(("dom", "grp"), None),
        P(),
        P(),
        P(("dom", "grp"), None),
        P(),
        P("dom", None, None),
        P("dom", None, None),
        P("dom", None),
        P(),
        P("dom", None, None),
        P("dom", None, None),
    )
    out_specs = (P(("dom", "grp"), None), P(("dom", "grp"), None), P(), P())
    return jax.shard_map(
        per_device, mesh=mesh, in_specs=in_specs, out_specs=out_specs, check_vma=False
    )
```

```python
import functools

import jax
import jax.numpy as jnp
from jax import lax
from jax.experimental import pallas as pl
from jax.experimental.pallas import tpu as pltpu
from jax.sharding import PartitionSpec as P

VMEM = pl.BlockSpec(memory_space=pltpu.VMEM)
SMEM = pl.BlockSpec(memory_space=pltpu.SMEM)
EXTRA = 16
COPIES = 4
F32 = jnp.float32
BF16 = jnp.bfloat16


def call(
    body, out_shape, specs, scratch=(), flops=0, nbytes=0, name=None, out_specs=None, aliases=(), mib=16
):
    return pl.pallas_call(
        body,
        out_shape=out_shape,
        in_specs=specs,
        out_specs=jax.tree.map(lambda _: VMEM, out_shape) if out_specs is None else out_specs,
        scratch_shapes=list(scratch),
        input_output_aliases=dict(aliases),
        compiler_params=pltpu.CompilerParams(vmem_limit_bytes=mib * 1024 * 1024),
        cost_estimate=pl.CostEstimate(flops=flops, bytes_accessed=nbytes, transcendentals=0),
        name=name,
    )


def shape(dims, kind):
    return jax.ShapeDtypeStruct(tuple(dims), kind)


def dot(a, b):
    return jnp.dot(a, b, preferred_element_type=F32)


def bias_rows(total):
    high = total.astype(BF16).astype(F32)
    rest = jnp.zeros((EXTRA - 2, total.shape[1]), F32)
    return jnp.concatenate([high, total - high, rest], axis=0).astype(BF16)


def aligned(start, step):
    return pl.ds(pl.multiple_of(start * step, step), step)


def swap(value, axis, mask):
    return lax.ppermute(value, axis, [(i, i ^ mask) for i in range(lax.axis_size(axis))])


def exchange(parts, axis):
    return list(parts[:1]) + [swap(part, axis, m) for m, part in enumerate(parts[1:], 1)]


def spread(value, axis, ahead=None):
    size = lax.axis_size(axis)
    parts, masks = [value], [0]
    bit = size // 2
    while bit:
        if ahead is not None:
            parts[1:] = [lax.optimization_barrier((part, ahead))[0] for part in parts[1:]]
        parts = parts + [swap(part, axis, bit) for part in parts]
        masks = masks + [mask ^ bit for mask in masks]
        bit //= 2
    return parts, masks


def split_features(ids, feats, *refs):
    outs, sems = refs[:-1], refs[-1]
    group = ids[1]
    narrow = outs[0].shape[1]
    copies = [
        pltpu.make_async_copy(
            feats.at[:, aligned(jnp.bitwise_xor(group, m), narrow)], out, sems.at[m]
        )
        for m, out in enumerate(outs)
    ]
    for copy in copies:
        copy.start()
    for copy in copies:
        copy.wait()


def pick_blocks(groups, slots, at, tab, *refs):
    parts, (x, offered, *outs) = refs[:groups], refs[groups:]
    domain, group = tab[at["me"]], tab[at["me"] + 1]
    tile = x.shape[1]
    per = x.shape[0] // groups
    for m, part in enumerate(parts):
        owner = jnp.bitwise_xor(group, m)
        for j in range(per):
            x[owner * per + j] = part[j * tile : (j + 1) * tile]
    for j in range(offered.shape[0]):
        offered[j] = x[tab[at["pub"] + j]]
    for m, out in enumerate(outs, 1):
        reader = jnp.bitwise_xor(domain, m)
        for s in range(slots):
            entry = jnp.maximum(tab[at["out"] + reader * slots + s], 0)
            out[s * tile : (s + 1) * tile] = x[tab[at["pub"] + entry]]


def pick_relayed(slots, at, tab, offered, *outs):
    tile = offered.shape[1]
    for m, out in enumerate(outs, 1):
        reader = jnp.bitwise_xor(tab[at["me"]], m)
        for s in range(slots):
            entry = jnp.maximum(tab[at["out2"] + reader * slots + s], 0)
            out[s * tile : (s + 1) * tile] = offered[entry]


def local_sum(per_row, at, tab, bank, x, out):
    pair = 2 if per_row % 2 == 0 else 1

    @pl.loop(0, out.shape[0])
    def _(r):
        acc = jnp.zeros(out.shape[1:], F32)
        for k in range(0, per_row, pair):
            spots = [r * per_row + k + j for j in range(pair)]
            left = jnp.concatenate([bank[tab[at["banks"] + a]] for a in spots], axis=1)
            right = jnp.concatenate([x[tab[at["cols"] + a]] for a in spots], axis=0)
            acc += dot(left, right)
        out[r] = acc


def add_halo(half, groups, slots, at, tab, bank, local, mirrored, *refs):
    near, far = refs[: half - 1], refs[half - 1 : 2 * half - 2]
    outs, acc = refs[2 * half - 2 : -1], refs[-1]
    domain, group = tab[at["me"]], tab[at["me"] + 1]
    tile = local.shape[1]
    per = local.shape[0] // groups
    acc[...] = local[...]

    def add(source, get):
        for s in range(slots):
            i = source * slots + s
            entry = tab[at["in"] + i]

            @pl.when(entry >= 0)
            def _(i=i, s=s, entry=entry):
                acc[tab[at["hrows"] + i]] += dot(bank[tab[at["hbanks"] + i]], get(s, entry))

    for m, block in enumerate(near, 1):
        add(jnp.bitwise_xor(domain, m), lambda s, _, block=block: block[s * tile : (s + 1) * tile])
    add(jnp.bitwise_xor(domain, half), lambda _, entry: mirrored[jnp.maximum(entry, 0)])
    for m, block in enumerate(far, half + 1):
        add(jnp.bitwise_xor(domain, m), lambda s, _, block=block: block[s * tile : (s + 1) * tile])
    for m, out in enumerate(outs):
        owner = jnp.bitwise_xor(group, m)
        for j in range(per):
            out[j * tile : (j + 1) * tile] = acc[owner * per + j].astype(BF16)


def dense(groups, ids, weight, bias, cot, *refs):
    parts, (act, grad) = refs[:groups], refs[groups:]
    group = ids[1]
    narrow = parts[0].shape[1]
    wide = cot.shape[1] // groups
    total = None
    for m, part in enumerate(parts):
        term = dot(part[...], weight[aligned(jnp.bitwise_xor(group, m), narrow)])
        total = term if total is None else total + term
    pre = total + bias[...]
    act[...] = jnp.maximum(pre, 0.0).astype(BF16)
    masked = jnp.where(pre > 0, cot[...].astype(F32), 0.0).astype(BF16)
    for s in range(groups):
        grad[s] = masked[:, s * wide : (s + 1) * wide]


def back_halo(masks, slots, at, tab, bank_t, *refs):
    parts, (own, mine, kept, *terms) = refs[: len(masks)], refs[len(masks) :]
    domain, group = tab[at["me"]], tab[at["me"] + 1]
    tile = bank_t.shape[1]
    per = parts[0].shape[1] // tile
    half = len(terms) + 1
    total = jnp.zeros((1, own.shape[2]), F32)
    for mask, part in zip(masks, parts):
        owner = jnp.bitwise_xor(group, mask)
        piece = part[group]
        total += jnp.sum(piece.astype(F32), axis=0, keepdims=True)
        for j in range(per):
            own[owner * per + j] = piece[j * tile : (j + 1) * tile]
    mine[...] = total
    tail = bias_rows(total)

    def put(out, place, source):
        for s in range(slots):
            i = source * slots + s
            live = (tab[at["in"] + i] >= 0).astype(F32)
            value = dot(bank_t[tab[at["hbanks"] + i]], own[tab[at["hrows"] + i]]) * live
            spot = (place * slots + s) * tile
            out[spot : spot + tile] = value.astype(BF16)

    for m, term in enumerate(terms, 1):
        peer = jnp.bitwise_xor(domain, m)
        put(term, 0, peer)
        put(term, 1, jnp.bitwise_xor(peer, half))
        term[2 * slots * tile :] = tail
    put(kept, 0, jnp.bitwise_xor(domain, half))


def sum_mirror(slots, at, tab, mine, kept, *refs):
    recv, out, acc = refs[:-2], refs[-2], refs[-1]
    domain = tab[at["me"]]
    offered, tile = acc.shape[:2]
    acc[...] = jnp.zeros_like(acc)
    total = mine[...]
    for m, block in enumerate((kept,) + recv):
        reader = jnp.bitwise_xor(domain, m)
        for s in range(slots):
            entry = tab[at["out2"] + reader * slots + s]
            spot = (s + (slots if m else 0)) * tile

            @pl.when(entry >= 0)
            def _(entry=entry, spot=spot, block=block):
                acc[jnp.maximum(entry, 0)] += block[spot : spot + tile].astype(F32)

        if m:
            tail = block[2 * slots * tile :].astype(F32)
            total += tail[0:1] + tail[1:2]
    for j in range(offered):
        out[j * tile : (j + 1) * tile] = acc[j].astype(BF16)
    out[offered * tile :] = bias_rows(total)


def weight_slice(masks, *refs):
    groups = len(masks)
    aggs, parts, out = refs[:groups], refs[groups : 2 * groups], refs[2 * groups]
    total = None
    for agg, part in zip(aggs, parts):
        right = jnp.concatenate([part[s] for s in range(groups)], axis=1)
        term = lax.dot_general(
            agg[...], right, (((0,), (0,)), ((), ())), preferred_element_type=F32
        )
        total = term if total is None else total + term
    rows = out.shape[1]
    for d in range(out.shape[0]):
        out[d] = total[d * rows : (d + 1) * rows].astype(BF16)


def sum_shares(scale, shares, out):
    total = shares[0].astype(F32)
    for d in range(1, shares.shape[0]):
        total += shares[d].astype(F32)
    summed = (total * scale).astype(BF16)
    for d in range(out.shape[0]):
        out[d] = summed


def back_local(per_row, at, tab, bank_t, own, out):
    out[...] = jnp.zeros_like(out)

    @pl.loop(0, own.shape[0])
    def _(r):
        right = own[r]
        for k in range(per_row):
            spot = r * per_row + k
            out[tab[at["cols"] + spot]] += dot(bank_t[tab[at["banks"] + spot]], right)


def finish_nodes(half, slots, scale, at, tab, local, mine, mirrored, *refs):
    recv, outs, acc = refs[: half - 1], refs[half - 1 : -1], refs[-1]
    groups = len(outs)
    domain, group = tab[at["me"]], tab[at["me"] + 1]
    tile = local.shape[1]
    per = local.shape[0] // groups
    offered = (mirrored.shape[0] - EXTRA) // tile
    acc[...] = local[...]
    tail = mirrored[offered * tile :].astype(F32)
    for j in range(offered):
        acc[tab[at["pub"] + j]] += mirrored[j * tile : (j + 1) * tile].astype(F32)
    for m, block in enumerate(recv, 1):
        tail += block[2 * slots * tile :].astype(F32)
        reader = jnp.bitwise_xor(domain, m)
        for s in range(slots):
            entry = tab[at["out"] + reader * slots + s]

            @pl.when(entry >= 0)
            def _(s=s, entry=entry, block=block):
                spot = tab[at["pub"] + jnp.maximum(entry, 0)]
                acc[spot] += block[s * tile : (s + 1) * tile].astype(F32)

    rows = bias_rows((mine[...] + tail[0:1] + tail[1:2]) * scale)
    for m, out in enumerate(outs):
        owner = jnp.bitwise_xor(group, m)
        for j in range(per):
            out[j * tile : (j + 1) * tile] = acc[owner * per + j].astype(BF16)
        out[per * tile :] = rows


def node_grads(groups, ids, weight, *refs):
    parts, (out, bias_out, hid) = refs[:groups], refs[groups:]
    group = ids[1]
    rows = out.shape[0]
    for m, part in enumerate(parts):
        hid[jnp.bitwise_xor(group, m)] = part[...]
    left = jnp.concatenate([hid[s, :rows] for s in range(groups)], axis=1)
    out[...] = lax.dot_general(
        left, weight[...], (((1,), (1,)), ((), ())), preferred_element_type=F32
    ).astype(BF16)
    tail = jnp.concatenate([hid[s, rows:] for s in range(groups)], axis=1).astype(F32)
    bias_out[...] = tail[0:1] + tail[1:2]


def place_weight(masks, ids, *refs):
    parts, (out, wide, sems) = refs[: len(masks)], refs[-3:]
    group = ids[1]
    rows = parts[0].shape[0]
    copies = []
    step = rows // COPIES
    for i, (mask, part) in enumerate(zip(masks, parts)):
        for j in range(COPIES):
            wide[i, j * step : (j + 1) * step] = part[j * step : (j + 1) * step].astype(F32)
            spot = out.at[aligned(jnp.bitwise_xor(group, mask) * COPIES + j, step)]
            piece = wide.at[i, pl.ds(j * step, step)]
            copies.append(pltpu.make_async_copy(piece, spot, sems.at[i, j]))
            copies[-1].start()
    for copy in copies:
        copy.wait()


def per_device(
    node_feats,
    weight,
    bias,
    cotangent,
    tile_bank,
    local_cols,
    local_banks,
    published,
    send_table,
    halo_rows,
    halo_banks,
):
    domains = lax.axis_size("dom")
    groups = lax.axis_size("grp")
    domain_index = lax.axis_index("dom")
    rows_here, embed = node_feats.shape
    hidden = weight.shape[1]
    tile = tile_bank.shape[1]
    slots = send_table.shape[2]
    per_row = local_cols.shape[2]
    part_rows = rows_here * groups
    blocks = part_rows // tile
    narrow = embed // groups
    wide = hidden // groups
    share = narrow // domains
    half = domains // 2
    peers = half - 1
    offers = published.shape[1]

    ids = jnp.stack([domain_index, lax.axis_index("grp")]).astype(jnp.int32)
    tables = {
        "cols": local_cols[0],
        "banks": local_banks[0],
        "pub": published[0],
        "out": lax.dynamic_index_in_dim(send_table, domain_index, 0, keepdims=False),
        "out2": lax.dynamic_index_in_dim(send_table, domain_index ^ half, 0, keepdims=False),
        "in": lax.dynamic_index_in_dim(send_table, domain_index, 1, keepdims=False),
        "hrows": halo_rows[0],
        "hbanks": halo_banks[0],
        "me": ids,
    }
    at, place = {}, 0
    for name, table in tables.items():
        at[name] = place
        place += table.size
    tab = jnp.concatenate([table.reshape(-1) for table in tables.values()])
    bank_t = jnp.swapaxes(tile_bank, 1, 2)

    feats = call(
        split_features,
        [shape((rows_here, narrow), BF16)] * groups,
        [SMEM, pl.BlockSpec(memory_space=pltpu.HBM)],
        [pltpu.SemaphoreType.DMA((groups,))],
        nbytes=4 * rows_here * embed,
        name="split_features",
        mib=60,
    )(ids, node_feats)
    feats = exchange(feats, "grp")
    x, offered, *picked = call(
        functools.partial(pick_blocks, groups, slots, at),
        [shape((blocks, tile, narrow), BF16), shape((offers, tile, narrow), BF16)]
        + [shape((slots * tile, narrow), BF16)] * peers,
        [SMEM] + [VMEM] * groups,
        nbytes=4 * (peers * slots + blocks + offers) * tile * narrow,
        name="pick_blocks",
    )(tab, *feats)
    mirrored = swap(offered, "dom", half)
    near = exchange([None] + picked, "dom")[1:]
    local = call(
        functools.partial(local_sum, per_row, at),
        shape((blocks, tile, narrow), F32),
        [SMEM, VMEM, VMEM],
        flops=2 * blocks * per_row * tile * tile * narrow,
        nbytes=blocks * tile * narrow * 6,
        name="local_sum",
    )(tab, tile_bank, x)
    mirrored, local = lax.optimization_barrier((mirrored, local))
    relayed = call(
        functools.partial(pick_relayed, slots, at),
        [shape((slots * tile, narrow), BF16)] * peers,
        [SMEM, VMEM],
        nbytes=4 * peers * slots * tile * narrow,
        name="pick_relayed",
    )(tab, mirrored)
    far = exchange([None, *relayed], "dom")[1:]
    aggs = call(
        functools.partial(add_halo, half, groups, slots, at),
        [shape((rows_here, narrow), BF16)] * groups,
        [SMEM, VMEM, VMEM, VMEM] + [VMEM] * (2 * peers),
        [pltpu.VMEM((blocks, tile, narrow), F32)],
        flops=4 * half * slots * tile * tile * narrow,
        nbytes=blocks * tile * narrow * 8,
        name="add_halo",
    )(tab, tile_bank, local, mirrored, *near, *far)
    activations, grad = call(
        functools.partial(dense, groups),
        [shape((rows_here, hidden), BF16), shape((groups, rows_here, wide), BF16)],
        [SMEM] + [VMEM] * (3 + groups),
        flops=2 * rows_here * embed * hidden,
        nbytes=embed * hidden * 2 + rows_here * (embed + 3 * hidden) * 2,
        name="dense",
    )(ids, weight, bias.reshape(1, hidden), cotangent, *exchange(aggs, "grp"))

    grads, masks = spread(grad, "grp")
    norm_scale = float(rows_here * groups * domains) ** (-0.5)
    part = call(
        functools.partial(weight_slice, masks),
        shape((domains, share, hidden), BF16),
        [VMEM] * (2 * groups),
        flops=2 * part_rows * narrow * hidden,
        nbytes=part_rows * (narrow + hidden) * 2,
        name="weight_slice",
    )(*[aggs[m] for m in masks], *grads)
    shares = lax.all_to_all(part, "dom", split_axis=0, concat_axis=0, tiled=True)
    tab_after, _ = lax.optimization_barrier((tab, part))
    own, bias_here, kept, *terms = call(
        functools.partial(back_halo, masks, slots, at),
        [
            shape((blocks, tile, wide), BF16),
            shape((1, wide), F32),
            shape((slots * tile, wide), BF16),
        ]
        + [shape((2 * slots * tile + EXTRA, wide), BF16)] * peers,
        [SMEM, VMEM] + [VMEM] * len(masks),
        flops=2 * domains * slots * tile * tile * wide,
        nbytes=(domains * slots + blocks) * tile * wide * 2,
        name="back_halo",
    )(tab_after, bank_t, *grads)
    sent, terms = terms, exchange([None] + terms, "dom")[1:]
    crossing = call(
        functools.partial(sum_mirror, slots, at),
        shape((offers * tile + EXTRA, wide), BF16),
        [SMEM] + [VMEM] * (2 + peers),
        [pltpu.VMEM((offers, tile, wide), F32)],
        nbytes=4 * domains * slots * tile * wide,
        name="sum_mirror",
    )(tab, bias_here, kept, *terms)
    returned = swap(crossing, "dom", half)
    back = call(
        functools.partial(back_local, per_row, at),
        shape((blocks, tile, wide), F32),
        [SMEM, VMEM, VMEM],
        flops=2 * blocks * per_row * tile * tile * wide,
        nbytes=blocks * tile * wide * 6,
        name="back_local",
    )(tab, bank_t, own)
    shares, _ = lax.optimization_barrier((shares, sent))
    summed = call(
        functools.partial(sum_shares, norm_scale),
        shape((domains, share, hidden), BF16),
        [VMEM],
        nbytes=domains * share * hidden * 4,
        name="sum_shares",
    )(shares)
    joined = lax.all_to_all(summed, "dom", split_axis=0, concat_axis=0, tiled=True)
    joined = joined.reshape(narrow, hidden)
    joined, back, _ = lax.optimization_barrier((joined, back, crossing))
    hid = call(
        functools.partial(finish_nodes, half, slots, norm_scale, at),
        [shape((rows_here + EXTRA, wide), BF16)] * groups,
        [SMEM, VMEM, VMEM, VMEM] + [VMEM] * peers,
        [pltpu.VMEM((blocks, tile, wide), F32)],
        nbytes=domains * slots * tile * wide * 2 + blocks * tile * wide * 6,
        name="finish_nodes",
    )(tab, back, bias_here, returned, *terms)
    hid = exchange(hid, "grp")
    weights, masks = spread(joined, "grp", hid[-1])
    count = groups // 2
    first = [masks.index(m) for m in range(count)]
    last = [masks.index(m) for m in range(count, groups)]
    placing = dict(
        out_shape=shape((embed, hidden), F32),
        scratch=[pltpu.VMEM((count, narrow, hidden), F32), pltpu.SemaphoreType.DMA((count, COPIES))],
        nbytes=embed * hidden * 3,
        name="place_weight",
        out_specs=pl.BlockSpec(memory_space=pl.ANY),
    )
    grad_weight = call(
        functools.partial(place_weight, [masks[i] for i in first]),
        specs=[SMEM] + [VMEM] * count,
        **placing,
    )(ids, *[weights[i] for i in first])
    grad_weight, *hid = lax.optimization_barrier((grad_weight, *hid))
    grad_nodes, grad_bias = call(
        functools.partial(node_grads, groups),
        [shape((rows_here, embed), BF16), shape((1, hidden), F32)],
        [SMEM, VMEM] + [VMEM] * groups,
        [pltpu.VMEM((groups, rows_here + EXTRA, wide), BF16)],
        flops=2 * rows_here * embed * hidden,
        nbytes=embed * hidden * 2 + rows_here * (embed + hidden) * 2,
        name="node_grads",
    )(ids, weight, *hid)
    grad_weight = call(
        functools.partial(place_weight, [masks[i] for i in last]),
        specs=[SMEM] + [VMEM] * count + [pl.BlockSpec(memory_space=pl.ANY)],
        aliases={count + 1: 0},
        **placing,
    )(ids, *[weights[i] for i in last], grad_weight)
    return (activations, grad_nodes, grad_weight, grad_bias.reshape(hidden))


def solution(mesh):
    in_specs = (
        P(("dom", "grp"), None),
        P(),
        P(),
        P(("dom", "grp"), None),
        P(),
        P("dom", None, None),
        P("dom", None, None),
        P("dom", None),
        P(),
        P("dom", None, None),
        P("dom", None, None),
    )
    out_specs = (P(("dom", "grp"), None), P(("dom", "grp"), None), P(), P())
    return jax.shard_map(
        per_device, mesh=mesh, in_specs=in_specs, out_specs=out_specs, check_vma=False
    )
```

```python
import functools

import jax
import jax.numpy as jnp
from jax import lax
from jax.experimental import pallas as pl
from jax.experimental.pallas import tpu as pltpu
from jax.sharding import PartitionSpec as P

VMEM = pl.BlockSpec(memory_space=pltpu.VMEM)
SMEM = pl.BlockSpec(memory_space=pltpu.SMEM)
EXTRA = 16
COPIES = 4
F32 = jnp.float32
BF16 = jnp.bfloat16


def call(
    body, out_shape, specs, scratch=(), flops=0, nbytes=0, name=None, out_specs=None, aliases=(), mib=16
):
    return pl.pallas_call(
        body,
        out_shape=out_shape,
        in_specs=specs,
        out_specs=jax.tree.map(lambda _: VMEM, out_shape) if out_specs is None else out_specs,
        scratch_shapes=list(scratch),
        input_output_aliases=dict(aliases),
        compiler_params=pltpu.CompilerParams(vmem_limit_bytes=mib * 1024 * 1024),
        cost_estimate=pl.CostEstimate(flops=flops, bytes_accessed=nbytes, transcendentals=0),
        name=name,
    )


def shape(dims, kind):
    return jax.ShapeDtypeStruct(tuple(dims), kind)


def dot(a, b):
    return jnp.dot(a, b, preferred_element_type=F32)


def bias_rows(total):
    high = total.astype(BF16).astype(F32)
    rest = jnp.zeros((EXTRA - 2, total.shape[1]), F32)
    return jnp.concatenate([high, total - high, rest], axis=0).astype(BF16)


def aligned(start, step):
    return pl.ds(pl.multiple_of(start * step, step), step)


def swap(value, axis, mask):
    return lax.ppermute(value, axis, [(i, i ^ mask) for i in range(lax.axis_size(axis))])


def exchange(parts, axis):
    return list(parts[:1]) + [swap(part, axis, m) for m, part in enumerate(parts[1:], 1)]


def spread(value, axis, ahead=None):
    size = lax.axis_size(axis)
    parts, masks = [value], [0]
    bit = size // 2
    while bit:
        if ahead is not None:
            parts[1:] = [lax.optimization_barrier((part, ahead))[0] for part in parts[1:]]
        parts = parts + [swap(part, axis, bit) for part in parts]
        masks = masks + [mask ^ bit for mask in masks]
        bit //= 2
    return parts, masks


def split_features(ids, feats, *refs):
    outs, sems = refs[:-1], refs[-1]
    group = ids[1]
    narrow = outs[0].shape[1]
    copies = [
        pltpu.make_async_copy(
            feats.at[:, aligned(jnp.bitwise_xor(group, m), narrow)], out, sems.at[m]
        )
        for m, out in enumerate(outs)
    ]
    for copy in copies:
        copy.start()
    for copy in copies:
        copy.wait()


def pick_blocks(groups, slots, at, tab, *refs):
    parts, (x, offered, *outs) = refs[:groups], refs[groups:]
    domain, group = tab[at["me"]], tab[at["me"] + 1]
    tile = x.shape[1]
    per = x.shape[0] // groups
    for m, part in enumerate(parts):
        owner = jnp.bitwise_xor(group, m)
        for j in range(per):
            x[owner * per + j] = part[j * tile : (j + 1) * tile]
    for j in range(offered.shape[0]):
        offered[j] = x[tab[at["pub"] + j]]
    for m, out in enumerate(outs, 1):
        reader = jnp.bitwise_xor(domain, m)
        for s in range(slots):
            entry = jnp.maximum(tab[at["out"] + reader * slots + s], 0)
            out[s * tile : (s + 1) * tile] = x[tab[at["pub"] + entry]]


def pick_relayed(slots, at, tab, offered, *outs):
    tile = offered.shape[1]
    for m, out in enumerate(outs, 1):
        reader = jnp.bitwise_xor(tab[at["me"]], m)
        for s in range(slots):
            entry = jnp.maximum(tab[at["out2"] + reader * slots + s], 0)
            out[s * tile : (s + 1) * tile] = offered[entry]


def local_sum(per_row, at, tab, bank, x, out):
    pair = 2 if per_row % 2 == 0 else 1

    @pl.loop(0, out.shape[0])
    def _(r):
        acc = jnp.zeros(out.shape[1:], F32)
        for k in range(0, per_row, pair):
            spots = [r * per_row + k + j for j in range(pair)]
            left = jnp.concatenate([bank[tab[at["banks"] + a]] for a in spots], axis=1)
            right = jnp.concatenate([x[tab[at["cols"] + a]] for a in spots], axis=0)
            acc += dot(left, right)
        out[r] = acc


def add_halo(half, groups, slots, at, tab, bank, local, mirrored, *refs):
    near, far = refs[: half - 1], refs[half - 1 : 2 * half - 2]
    outs, acc = refs[2 * half - 2 : -1], refs[-1]
    domain, group = tab[at["me"]], tab[at["me"] + 1]
    tile = local.shape[1]
    per = local.shape[0] // groups
    acc[...] = local[...]

    def add(source, get):
        for s in range(slots):
            i = source * slots + s
            entry = tab[at["in"] + i]

            @pl.when(entry >= 0)
            def _(i=i, s=s, entry=entry):
                acc[tab[at["hrows"] + i]] += dot(bank[tab[at["hbanks"] + i]], get(s, entry))

    for m, block in enumerate(near, 1):
        add(jnp.bitwise_xor(domain, m), lambda s, _, block=block: block[s * tile : (s + 1) * tile])
    add(jnp.bitwise_xor(domain, half), lambda _, entry: mirrored[jnp.maximum(entry, 0)])
    for m, block in enumerate(far, half + 1):
        add(jnp.bitwise_xor(domain, m), lambda s, _, block=block: block[s * tile : (s + 1) * tile])
    for m, out in enumerate(outs):
        owner = jnp.bitwise_xor(group, m)
        for j in range(per):
            out[j * tile : (j + 1) * tile] = acc[owner * per + j].astype(BF16)


def dense(groups, ids, weight, bias, cot, *refs):
    parts, (act, grad) = refs[:groups], refs[groups:]
    group = ids[1]
    narrow = parts[0].shape[1]
    wide = cot.shape[1] // groups
    total = None
    for m, part in enumerate(parts):
        term = dot(part[...], weight[aligned(jnp.bitwise_xor(group, m), narrow)])
        total = term if total is None else total + term
    pre = total + bias[...]
    act[...] = jnp.maximum(pre, 0.0).astype(BF16)
    masked = jnp.where(pre > 0, cot[...].astype(F32), 0.0).astype(BF16)
    for s in range(groups):
        grad[s] = masked[:, s * wide : (s + 1) * wide]


def back_halo(masks, slots, at, tab, bank_t, *refs):
    parts, (own, mine, kept, *terms) = refs[: len(masks)], refs[len(masks) :]
    domain, group = tab[at["me"]], tab[at["me"] + 1]
    tile = bank_t.shape[1]
    per = parts[0].shape[1] // tile
    half = len(terms) + 1
    total = jnp.zeros((1, own.shape[2]), F32)
    for mask, part in zip(masks, parts):
        owner = jnp.bitwise_xor(group, mask)
        piece = part[group]
        total += jnp.sum(piece.astype(F32), axis=0, keepdims=True)
        for j in range(per):
            own[owner * per + j] = piece[j * tile : (j + 1) * tile]
    mine[...] = total
    tail = bias_rows(total)

    def put(out, place, source):
        for s in range(slots):
            i = source * slots + s
            live = (tab[at["in"] + i] >= 0).astype(F32)
            value = dot(bank_t[tab[at["hbanks"] + i]], own[tab[at["hrows"] + i]]) * live
            spot = (place * slots + s) * tile
            out[spot : spot + tile] = value.astype(BF16)

    for m, term in enumerate(terms, 1):
        peer = jnp.bitwise_xor(domain, m)
        put(term, 0, peer)
        put(term, 1, jnp.bitwise_xor(peer, half))
        term[2 * slots * tile :] = tail
    put(kept, 0, jnp.bitwise_xor(domain, half))


def sum_mirror(slots, at, tab, mine, kept, *refs):
    recv, out, acc = refs[:-2], refs[-2], refs[-1]
    domain = tab[at["me"]]
    offered, tile = acc.shape[:2]
    acc[...] = jnp.zeros_like(acc)
    total = mine[...]
    for m, block in enumerate((kept,) + recv):
        reader = jnp.bitwise_xor(domain, m)
        for s in range(slots):
            entry = tab[at["out2"] + reader * slots + s]
            spot = (s + (slots if m else 0)) * tile

            @pl.when(entry >= 0)
            def _(entry=entry, spot=spot, block=block):
                acc[jnp.maximum(entry, 0)] += block[spot : spot + tile].astype(F32)

        if m:
            tail = block[2 * slots * tile :].astype(F32)
            total += tail[0:1] + tail[1:2]
    for j in range(offered):
        out[j * tile : (j + 1) * tile] = acc[j].astype(BF16)
    out[offered * tile :] = bias_rows(total)


def weight_slice(masks, *refs):
    groups = len(masks)
    aggs, parts, out = refs[:groups], refs[groups : 2 * groups], refs[2 * groups]
    total = None
    for agg, part in zip(aggs, parts):
        right = jnp.concatenate([part[s] for s in range(groups)], axis=1)
        term = lax.dot_general(
            agg[...], right, (((0,), (0,)), ((), ())), preferred_element_type=F32
        )
        total = term if total is None else total + term
    rows = out.shape[1]
    for d in range(out.shape[0]):
        out[d] = total[d * rows : (d + 1) * rows].astype(BF16)


def sum_shares(scale, shares, out):
    total = shares[0].astype(F32)
    for d in range(1, shares.shape[0]):
        total += shares[d].astype(F32)
    summed = (total * scale).astype(BF16)
    for d in range(out.shape[0]):
        out[d] = summed


def back_local(per_row, at, tab, bank_t, own, out):
    out[...] = jnp.zeros_like(out)

    @pl.loop(0, own.shape[0])
    def _(r):
        right = own[r]
        for k in range(per_row):
            spot = r * per_row + k
            out[tab[at["cols"] + spot]] += dot(bank_t[tab[at["banks"] + spot]], right)


def finish_nodes(half, slots, scale, at, tab, local, mine, mirrored, *refs):
    recv, outs, acc = refs[: half - 1], refs[half - 1 : -1], refs[-1]
    groups = len(outs)
    domain, group = tab[at["me"]], tab[at["me"] + 1]
    tile = local.shape[1]
    per = local.shape[0] // groups
    offered = (mirrored.shape[0] - EXTRA) // tile
    acc[...] = local[...]
    tail = mirrored[offered * tile :].astype(F32)
    for j in range(offered):
        acc[tab[at["pub"] + j]] += mirrored[j * tile : (j + 1) * tile].astype(F32)
    for m, block in enumerate(recv, 1):
        tail += block[2 * slots * tile :].astype(F32)
        reader = jnp.bitwise_xor(domain, m)
        for s in range(slots):
            entry = tab[at["out"] + reader * slots + s]

            @pl.when(entry >= 0)
            def _(s=s, entry=entry, block=block):
                spot = tab[at["pub"] + jnp.maximum(entry, 0)]
                acc[spot] += block[s * tile : (s + 1) * tile].astype(F32)

    rows = bias_rows((mine[...] + tail[0:1] + tail[1:2]) * scale)
    for m, out in enumerate(outs):
        owner = jnp.bitwise_xor(group, m)
        for j in range(per):
            out[j * tile : (j + 1) * tile] = acc[owner * per + j].astype(BF16)
        out[per * tile :] = rows


def node_grads(groups, ids, weight, *refs):
    parts, (out, bias_out, hid) = refs[:groups], refs[groups:]
    group = ids[1]
    rows = out.shape[0]
    for m, part in enumerate(parts):
        hid[jnp.bitwise_xor(group, m)] = part[...]
    left = jnp.concatenate([hid[s, :rows] for s in range(groups)], axis=1)
    out[...] = lax.dot_general(
        left, weight[...], (((1,), (1,)), ((), ())), preferred_element_type=F32
    ).astype(BF16)
    tail = jnp.concatenate([hid[s, rows:] for s in range(groups)], axis=1).astype(F32)
    bias_out[...] = tail[0:1] + tail[1:2]


def place_weight(masks, ids, *refs):
    parts, (out, wide, sems) = refs[: len(masks)], refs[-3:]
    group = ids[1]
    rows = parts[0].shape[0]
    copies = []
    step = rows // COPIES
    for i, (mask, part) in enumerate(zip(masks, parts)):
        for j in range(COPIES):
            wide[i, j * step : (j + 1) * step] = part[j * step : (j + 1) * step].astype(F32)
            spot = out.at[aligned(jnp.bitwise_xor(group, mask) * COPIES + j, step)]
            piece = wide.at[i, pl.ds(j * step, step)]
            copies.append(pltpu.make_async_copy(piece, spot, sems.at[i, j]))
            copies[-1].start()
    for copy in copies:
        copy.wait()


def per_device(
    node_feats,
    weight,
    bias,
    cotangent,
    tile_bank,
    local_cols,
    local_banks,
    published,
    send_table,
    halo_rows,
    halo_banks,
):
    domains = lax.axis_size("dom")
    groups = lax.axis_size("grp")
    domain_index = lax.axis_index("dom")
    rows_here, embed = node_feats.shape
    hidden = weight.shape[1]
    tile = tile_bank.shape[1]
    slots = send_table.shape[2]
    per_row = local_cols.shape[2]
    part_rows = rows_here * groups
    blocks = part_rows // tile
    narrow = embed // groups
    wide = hidden // groups
    share = narrow // domains
    half = domains // 2
    peers = half - 1
    offers = published.shape[1]

    ids = jnp.stack([domain_index, lax.axis_index("grp")]).astype(jnp.int32)
    tables = {
        "cols": local_cols[0],
        "banks": local_banks[0],
        "pub": published[0],
        "out": lax.dynamic_index_in_dim(send_table, domain_index, 0, keepdims=False),
        "out2": lax.dynamic_index_in_dim(send_table, domain_index ^ half, 0, keepdims=False),
        "in": lax.dynamic_index_in_dim(send_table, domain_index, 1, keepdims=False),
        "hrows": halo_rows[0],
        "hbanks": halo_banks[0],
        "me": ids,
    }
    at, place = {}, 0
    for name, table in tables.items():
        at[name] = place
        place += table.size
    tab = jnp.concatenate([table.reshape(-1) for table in tables.values()])
    bank_t = jnp.swapaxes(tile_bank, 1, 2)

    feats = call(
        split_features,
        [shape((rows_here, narrow), BF16)] * groups,
        [SMEM, pl.BlockSpec(memory_space=pl.ANY)],
        [pltpu.SemaphoreType.DMA((groups,))],
        nbytes=4 * rows_here * embed,
        name="split_features",
    )(ids, node_feats)
    feats = exchange(feats, "grp")
    x, offered, *picked = call(
        functools.partial(pick_blocks, groups, slots, at),
        [shape((blocks, tile, narrow), BF16), shape((offers, tile, narrow), BF16)]
        + [shape((slots * tile, narrow), BF16)] * peers,
        [SMEM] + [VMEM] * groups,
        nbytes=4 * (peers * slots + blocks + offers) * tile * narrow,
        name="pick_blocks",
    )(tab, *feats)
    mirrored = swap(offered, "dom", half)
    near = exchange([None] + picked, "dom")[1:]
    local = call(
        functools.partial(local_sum, per_row, at),
        shape((blocks, tile, narrow), F32),
        [SMEM, VMEM, VMEM],
        flops=2 * blocks * per_row * tile * tile * narrow,
        nbytes=blocks * tile * narrow * 6,
        name="local_sum",
    )(tab, tile_bank, x)
    mirrored, local = lax.optimization_barrier((mirrored, local))
    relayed = call(
        functools.partial(pick_relayed, slots, at),
        [shape((slots * tile, narrow), BF16)] * peers,
        [SMEM, VMEM],
        nbytes=4 * peers * slots * tile * narrow,
        name="pick_relayed",
    )(tab, mirrored)
    far = exchange([None, *relayed], "dom")[1:]
    aggs = call(
        functools.partial(add_halo, half, groups, slots, at),
        [shape((rows_here, narrow), BF16)] * groups,
        [SMEM, VMEM, VMEM, VMEM] + [VMEM] * (2 * peers),
        [pltpu.VMEM((blocks, tile, narrow), F32)],
        flops=4 * half * slots * tile * tile * narrow,
        nbytes=blocks * tile * narrow * 8,
        name="add_halo",
    )(tab, tile_bank, local, mirrored, *near, *far)
    activations, grad = call(
        functools.partial(dense, groups),
        [shape((rows_here, hidden), BF16), shape((groups, rows_here, wide), BF16)],
        [SMEM] + [VMEM] * (3 + groups),
        flops=2 * rows_here * embed * hidden,
        nbytes=embed * hidden * 2 + rows_here * (embed + 3 * hidden) * 2,
        name="dense",
    )(ids, weight, bias.reshape(1, hidden), cotangent, *exchange(aggs, "grp"))

    grads, masks = spread(grad, "grp")
    norm_scale = float(rows_here * groups * domains) ** (-0.5)
    own, bias_here, kept, *terms = call(
        functools.partial(back_halo, masks, slots, at),
        [
            shape((blocks, tile, wide), BF16),
            shape((1, wide), F32),
            shape((slots * tile, wide), BF16),
        ]
        + [shape((2 * slots * tile + EXTRA, wide), BF16)] * peers,
        [SMEM, VMEM] + [VMEM] * len(masks),
        flops=2 * domains * slots * tile * tile * wide,
        nbytes=(domains * slots + blocks) * tile * wide * 2,
        name="back_halo",
    )(tab, bank_t, *grads)
    sent, terms = terms, exchange([None] + terms, "dom")[1:]
    crossing = call(
        functools.partial(sum_mirror, slots, at),
        shape((offers * tile + EXTRA, wide), BF16),
        [SMEM] + [VMEM] * (2 + peers),
        [pltpu.VMEM((offers, tile, wide), F32)],
        nbytes=4 * domains * slots * tile * wide,
        name="sum_mirror",
    )(tab, bias_here, kept, *terms)
    returned = swap(crossing, "dom", half)
    after, _ = lax.optimization_barrier(([aggs[m] for m in masks] + grads, sent))
    part = call(
        functools.partial(weight_slice, masks),
        shape((domains, share, hidden), BF16),
        [VMEM] * (2 * groups),
        flops=2 * part_rows * narrow * hidden,
        nbytes=part_rows * (narrow + hidden) * 2,
        name="weight_slice",
    )(*after)
    shares = lax.all_to_all(part, "dom", split_axis=0, concat_axis=0, tiled=True)
    back = call(
        functools.partial(back_local, per_row, at),
        shape((blocks, tile, wide), F32),
        [SMEM, VMEM, VMEM],
        flops=2 * blocks * per_row * tile * tile * wide,
        nbytes=blocks * tile * wide * 6,
        name="back_local",
    )(tab, bank_t, own)
    shares, _ = lax.optimization_barrier((shares, crossing))
    summed = call(
        functools.partial(sum_shares, norm_scale),
        shape((domains, share, hidden), BF16),
        [VMEM],
        nbytes=domains * share * hidden * 4,
        name="sum_shares",
    )(shares)
    joined = lax.all_to_all(summed, "dom", split_axis=0, concat_axis=0, tiled=True)
    joined = joined.reshape(narrow, hidden)
    hid = call(
        functools.partial(finish_nodes, half, slots, norm_scale, at),
        [shape((rows_here + EXTRA, wide), BF16)] * groups,
        [SMEM, VMEM, VMEM, VMEM] + [VMEM] * peers,
        [pltpu.VMEM((blocks, tile, wide), F32)],
        nbytes=domains * slots * tile * wide * 2 + blocks * tile * wide * 6,
        name="finish_nodes",
    )(tab, back, bias_here, returned, *terms)
    joined, _ = lax.optimization_barrier((joined, hid))
    hid = exchange(hid, "grp")
    weights, masks = spread(joined, "grp", hid[-1])
    count = groups // 2
    first = [masks.index(m) for m in range(count)]
    last = [masks.index(m) for m in range(count, groups)]
    placing = dict(
        out_shape=shape((embed, hidden), F32),
        scratch=[pltpu.VMEM((count, narrow, hidden), F32), pltpu.SemaphoreType.DMA((count, COPIES))],
        nbytes=embed * hidden * 3,
        name="place_weight",
        out_specs=pl.BlockSpec(memory_space=pl.ANY),
    )
    grad_weight = call(
        functools.partial(place_weight, [masks[i] for i in first]),
        specs=[SMEM] + [VMEM] * count,
        **placing,
    )(ids, *[weights[i] for i in first])
    grad_weight, *hid = lax.optimization_barrier((grad_weight, *hid))
    grad_nodes, grad_bias = call(
        functools.partial(node_grads, groups),
        [shape((rows_here, embed), BF16), shape((1, hidden), F32)],
        [SMEM, VMEM] + [VMEM] * groups,
        [pltpu.VMEM((groups, rows_here + EXTRA, wide), BF16)],
        flops=2 * rows_here * embed * hidden,
        nbytes=embed * hidden * 2 + rows_here * (embed + hidden) * 2,
        name="node_grads",
    )(ids, weight, *hid)
    grad_weight = call(
        functools.partial(place_weight, [masks[i] for i in last]),
        specs=[SMEM] + [VMEM] * count + [pl.BlockSpec(memory_space=pl.ANY)],
        aliases={count + 1: 0},
        **placing,
    )(ids, *[weights[i] for i in last], grad_weight)
    return (activations, grad_nodes, grad_weight, grad_bias.reshape(hidden))


def solution(mesh):
    in_specs = (
        P(("dom", "grp"), None),
        P(),
        P(),
        P(("dom", "grp"), None),
        P(),
        P("dom", None, None),
        P("dom", None, None),
        P("dom", None),
        P(),
        P("dom", None, None),
        P("dom", None, None),
    )
    out_specs = (P(("dom", "grp"), None), P(("dom", "grp"), None), P(), P())
    return jax.shard_map(
        per_device, mesh=mesh, in_specs=in_specs, out_specs=out_specs, check_vma=False
    )
```

```python
import functools

import jax
import jax.numpy as jnp
from jax import lax
from jax.experimental import pallas as pl
from jax.experimental.pallas import tpu as pltpu
from jax.sharding import PartitionSpec as P

VMEM = pl.BlockSpec(memory_space=pltpu.VMEM)
SMEM = pl.BlockSpec(memory_space=pltpu.SMEM)
EXTRA = 16
COPIES = 4
F32 = jnp.float32
BF16 = jnp.bfloat16


def call(
    body, out_shape, specs, scratch=(), flops=0, nbytes=0, name=None, out_specs=None, aliases=(), mib=16
):
    return pl.pallas_call(
        body,
        out_shape=out_shape,
        in_specs=specs,
        out_specs=jax.tree.map(lambda _: VMEM, out_shape) if out_specs is None else out_specs,
        scratch_shapes=list(scratch),
        input_output_aliases=dict(aliases),
        compiler_params=pltpu.CompilerParams(vmem_limit_bytes=mib * 1024 * 1024),
        cost_estimate=pl.CostEstimate(flops=flops, bytes_accessed=nbytes, transcendentals=0),
        name=name,
    )


def shape(dims, kind):
    return jax.ShapeDtypeStruct(tuple(dims), kind)


def dot(a, b):
    return jnp.dot(a, b, preferred_element_type=F32)


def bias_rows(total):
    high = total.astype(BF16).astype(F32)
    rest = jnp.zeros((EXTRA - 2, total.shape[1]), F32)
    return jnp.concatenate([high, total - high, rest], axis=0).astype(BF16)


def aligned(start, step):
    return pl.ds(pl.multiple_of(start * step, step), step)


def swap(value, axis, mask):
    return lax.ppermute(value, axis, [(i, i ^ mask) for i in range(lax.axis_size(axis))])


def exchange(parts, axis):
    return list(parts[:1]) + [swap(part, axis, m) for m, part in enumerate(parts[1:], 1)]


def spread(value, axis, ahead=None):
    size = lax.axis_size(axis)
    parts, masks = [value], [0]
    bit = size // 2
    while bit:
        if ahead is not None:
            parts[1:] = [lax.optimization_barrier((part, ahead))[0] for part in parts[1:]]
        parts = parts + [swap(part, axis, bit) for part in parts]
        masks = masks + [mask ^ bit for mask in masks]
        bit //= 2
    return parts, masks


def split_features(ids, feats, *refs):
    outs, sems = refs[:-1], refs[-1]
    group = ids[1]
    narrow = outs[0].shape[1]
    copies = [
        pltpu.make_async_copy(
            feats.at[:, aligned(jnp.bitwise_xor(group, m), narrow)], out, sems.at[m]
        )
        for m, out in enumerate(outs)
    ]
    for copy in copies:
        copy.start()
    for copy in copies:
        copy.wait()


def pick_blocks(groups, slots, at, tab, *refs):
    parts, (x, offered, *outs) = refs[:groups], refs[groups:]
    domain, group = tab[at["me"]], tab[at["me"] + 1]
    tile = x.shape[1]
    per = x.shape[0] // groups
    for m, part in enumerate(parts):
        owner = jnp.bitwise_xor(group, m)
        for j in range(per):
            x[owner * per + j] = part[j * tile : (j + 1) * tile]
    for j in range(offered.shape[0]):
        offered[j] = x[tab[at["pub"] + j]]
    for m, out in enumerate(outs, 1):
        reader = jnp.bitwise_xor(domain, m)
        for s in range(slots):
            entry = jnp.maximum(tab[at["out"] + reader * slots + s], 0)
            out[s * tile : (s + 1) * tile] = x[tab[at["pub"] + entry]]


def pick_relayed(slots, at, tab, offered, *outs):
    tile = offered.shape[1]
    for m, out in enumerate(outs, 1):
        reader = jnp.bitwise_xor(tab[at["me"]], m)
        for s in range(slots):
            entry = jnp.maximum(tab[at["out2"] + reader * slots + s], 0)
            out[s * tile : (s + 1) * tile] = offered[entry]


def local_sum(per_row, at, tab, bank, x, out):
    pair = 2 if per_row % 2 == 0 else 1

    @pl.loop(0, out.shape[0])
    def _(r):
        acc = jnp.zeros(out.shape[1:], F32)
        for k in range(0, per_row, pair):
            spots = [r * per_row + k + j for j in range(pair)]
            left = jnp.concatenate([bank[tab[at["banks"] + a]] for a in spots], axis=1)
            right = jnp.concatenate([x[tab[at["cols"] + a]] for a in spots], axis=0)
            acc += dot(left, right)
        out[r] = acc


def add_halo(half, groups, slots, at, tab, bank, local, mirrored, *refs):
    near, far = refs[: half - 1], refs[half - 1 : 2 * half - 2]
    outs, acc = refs[2 * half - 2 : -1], refs[-1]
    domain, group = tab[at["me"]], tab[at["me"] + 1]
    tile = local.shape[1]
    per = local.shape[0] // groups
    acc[...] = local[...]

    def add(source, get):
        for s in range(slots):
            i = source * slots + s
            entry = tab[at["in"] + i]

            @pl.when(entry >= 0)
            def _(i=i, s=s, entry=entry):
                acc[tab[at["hrows"] + i]] += dot(bank[tab[at["hbanks"] + i]], get(s, entry))

    for m, block in enumerate(near, 1):
        add(jnp.bitwise_xor(domain, m), lambda s, _, block=block: block[s * tile : (s + 1) * tile])
    add(jnp.bitwise_xor(domain, half), lambda _, entry: mirrored[jnp.maximum(entry, 0)])
    for m, block in enumerate(far, half + 1):
        add(jnp.bitwise_xor(domain, m), lambda s, _, block=block: block[s * tile : (s + 1) * tile])
    for m, out in enumerate(outs):
        owner = jnp.bitwise_xor(group, m)
        for j in range(per):
            out[j * tile : (j + 1) * tile] = acc[owner * per + j].astype(BF16)


def dense(groups, ids, weight, bias, cot, *refs):
    parts, (act, grad) = refs[:groups], refs[groups:]
    group = ids[1]
    narrow = parts[0].shape[1]
    wide = cot.shape[1] // groups
    total = None
    for m, part in enumerate(parts):
        term = dot(part[...], weight[aligned(jnp.bitwise_xor(group, m), narrow)])
        total = term if total is None else total + term
    pre = total + bias[...]
    act[...] = jnp.maximum(pre, 0.0).astype(BF16)
    masked = jnp.where(pre > 0, cot[...].astype(F32), 0.0).astype(BF16)
    for s in range(groups):
        grad[s] = masked[:, s * wide : (s + 1) * wide]


def back_halo(masks, slots, at, tab, bank_t, *refs):
    parts, (own, mine, kept, *terms) = refs[: len(masks)], refs[len(masks) :]
    domain, group = tab[at["me"]], tab[at["me"] + 1]
    tile = bank_t.shape[1]
    per = parts[0].shape[1] // tile
    half = len(terms) + 1
    total = jnp.zeros((1, own.shape[2]), F32)
    for mask, part in zip(masks, parts):
        owner = jnp.bitwise_xor(group, mask)
        piece = part[group]
        total += jnp.sum(piece.astype(F32), axis=0, keepdims=True)
        for j in range(per):
            own[owner * per + j] = piece[j * tile : (j + 1) * tile]
    mine[...] = total
    tail = bias_rows(total)

    def put(out, place, source):
        for s in range(slots):
            i = source * slots + s
            live = (tab[at["in"] + i] >= 0).astype(F32)
            value = dot(bank_t[tab[at["hbanks"] + i]], own[tab[at["hrows"] + i]]) * live
            spot = (place * slots + s) * tile
            out[spot : spot + tile] = value.astype(BF16)

    for m, term in enumerate(terms, 1):
        peer = jnp.bitwise_xor(domain, m)
        put(term, 0, peer)
        put(term, 1, jnp.bitwise_xor(peer, half))
        term[2 * slots * tile :] = tail
    put(kept, 0, jnp.bitwise_xor(domain, half))


def sum_mirror(slots, at, tab, mine, kept, *refs):
    recv, out, acc = refs[:-2], refs[-2], refs[-1]
    domain = tab[at["me"]]
    offered, tile = acc.shape[:2]
    acc[...] = jnp.zeros_like(acc)
    total = mine[...]
    for m, block in enumerate((kept,) + recv):
        reader = jnp.bitwise_xor(domain, m)
        for s in range(slots):
            entry = tab[at["out2"] + reader * slots + s]
            spot = (s + (slots if m else 0)) * tile

            @pl.when(entry >= 0)
            def _(entry=entry, spot=spot, block=block):
                acc[jnp.maximum(entry, 0)] += block[spot : spot + tile].astype(F32)

        if m:
            tail = block[2 * slots * tile :].astype(F32)
            total += tail[0:1] + tail[1:2]
    for j in range(offered):
        out[j * tile : (j + 1) * tile] = acc[j].astype(BF16)
    out[offered * tile :] = bias_rows(total)


def weight_slice(groups, masks, ids, *refs):
    aggs, parts = refs[:groups], refs[groups : 2 * groups]
    kept, *outs = refs[2 * groups : -1]
    total = refs[-1]
    domain = ids[0]
    half = len(outs) + 1
    whole = None
    for mask, part in zip(masks, parts):
        right = jnp.concatenate([part[s] for s in range(groups)], axis=1)
        term = lax.dot_general(
            aggs[mask][...], right, (((0,), (0,)), ((), ())), preferred_element_type=F32
        )
        whole = term if whole is None else whole + term
    rows = total.shape[1]
    for d in range(total.shape[0]):
        total[d] = whole[d * rows : (d + 1) * rows]
    for m, out in enumerate([kept] + outs):
        peer = jnp.bitwise_xor(domain, m)
        out[0] = total[peer].astype(out.dtype)
        out[1] = total[jnp.bitwise_xor(peer, half)].astype(out.dtype)


def sum_half(kept, *refs):
    recv, out = refs[:-1], refs[-1]
    for i in range(2):
        total = kept[i]
        for block in recv:
            total += block[i].astype(F32)
        out[i] = total.astype(BF16)


def sum_both(scale, here, there, out):
    for i in range(2):
        out[i] = ((here[i].astype(F32) + there[1 - i].astype(F32)) * scale).astype(BF16)


def join_shares(ids, *refs):
    parts, out = refs[:-1], refs[-1]
    for m, part in enumerate(parts):
        owner = jnp.bitwise_xor(ids[0], m)
        out[owner] = part[0]
        out[jnp.bitwise_xor(owner, len(parts))] = part[1]


def back_local(per_row, at, tab, bank_t, own, out):
    out[...] = jnp.zeros_like(out)

    @pl.loop(0, own.shape[0])
    def _(r):
        right = own[r]
        for k in range(per_row):
            spot = r * per_row + k
            out[tab[at["cols"] + spot]] += dot(bank_t[tab[at["banks"] + spot]], right)


def finish_nodes(half, slots, scale, at, tab, local, mine, mirrored, *refs):
    recv, outs, acc = refs[: half - 1], refs[half - 1 : -1], refs[-1]
    groups = len(outs)
    domain, group = tab[at["me"]], tab[at["me"] + 1]
    tile = local.shape[1]
    per = local.shape[0] // groups
    offered = (mirrored.shape[0] - EXTRA) // tile
    acc[...] = local[...]
    tail = mirrored[offered * tile :].astype(F32)
    for j in range(offered):
        acc[tab[at["pub"] + j]] += mirrored[j * tile : (j + 1) * tile].astype(F32)
    for m, block in enumerate(recv, 1):
        tail += block[2 * slots * tile :].astype(F32)
        reader = jnp.bitwise_xor(domain, m)
        for s in range(slots):
            entry = tab[at["out"] + reader * slots + s]

            @pl.when(entry >= 0)
            def _(s=s, entry=entry, block=block):
                spot = tab[at["pub"] + jnp.maximum(entry, 0)]
                acc[spot] += block[s * tile : (s + 1) * tile].astype(F32)

    rows = bias_rows((mine[...] + tail[0:1] + tail[1:2]) * scale)
    for m, out in enumerate(outs):
        owner = jnp.bitwise_xor(group, m)
        for j in range(per):
            out[j * tile : (j + 1) * tile] = acc[owner * per + j].astype(BF16)
        out[per * tile :] = rows


def node_grads(groups, ids, weight, *refs):
    parts, (out, bias_out, hid) = refs[:groups], refs[groups:]
    group = ids[1]
    rows = out.shape[0]
    for m, part in enumerate(parts):
        hid[jnp.bitwise_xor(group, m)] = part[...]
    left = jnp.concatenate([hid[s, :rows] for s in range(groups)], axis=1)
    out[...] = lax.dot_general(
        left, weight[...], (((1,), (1,)), ((), ())), preferred_element_type=F32
    ).astype(BF16)
    tail = jnp.concatenate([hid[s, rows:] for s in range(groups)], axis=1).astype(F32)
    bias_out[...] = tail[0:1] + tail[1:2]


def place_weight(masks, ids, *refs):
    parts, (out, wide, sems) = refs[: len(masks)], refs[-3:]
    group = ids[1]
    rows = parts[0].shape[0]
    copies = []
    step = rows // COPIES
    for i, (mask, part) in enumerate(zip(masks, parts)):
        for j in range(COPIES):
            wide[i, j * step : (j + 1) * step] = part[j * step : (j + 1) * step].astype(F32)
            spot = out.at[aligned(jnp.bitwise_xor(group, mask) * COPIES + j, step)]
            piece = wide.at[i, pl.ds(j * step, step)]
            copies.append(pltpu.make_async_copy(piece, spot, sems.at[i, j]))
            copies[-1].start()
    for copy in copies:
        copy.wait()


def per_device(
    node_feats,
    weight,
    bias,
    cotangent,
    tile_bank,
    local_cols,
    local_banks,
    published,
    send_table,
    halo_rows,
    halo_banks,
):
    domains = lax.axis_size("dom")
    groups = lax.axis_size("grp")
    domain_index = lax.axis_index("dom")
    rows_here, embed = node_feats.shape
    hidden = weight.shape[1]
    tile = tile_bank.shape[1]
    slots = send_table.shape[2]
    per_row = local_cols.shape[2]
    part_rows = rows_here * groups
    blocks = part_rows // tile
    narrow = embed // groups
    wide = hidden // groups
    share = narrow // domains
    half = domains // 2
    peers = half - 1
    offers = published.shape[1]

    ids = jnp.stack([domain_index, lax.axis_index("grp")]).astype(jnp.int32)
    tables = {
        "cols": local_cols[0],
        "banks": local_banks[0],
        "pub": published[0],
        "out": lax.dynamic_index_in_dim(send_table, domain_index, 0, keepdims=False),
        "out2": lax.dynamic_index_in_dim(send_table, domain_index ^ half, 0, keepdims=False),
        "in": lax.dynamic_index_in_dim(send_table, domain_index, 1, keepdims=False),
        "hrows": halo_rows[0],
        "hbanks": halo_banks[0],
        "me": ids,
    }
    at, place = {}, 0
    for name, table in tables.items():
        at[name] = place
        place += table.size
    tab = jnp.concatenate([table.reshape(-1) for table in tables.values()])
    bank_t = jnp.swapaxes(tile_bank, 1, 2)

    feats = call(
        split_features,
        [shape((rows_here, narrow), BF16)] * groups,
        [SMEM, pl.BlockSpec(memory_space=pl.ANY)],
        [pltpu.SemaphoreType.DMA((groups,))],
        nbytes=4 * rows_here * embed,
        name="split_features",
    )(ids, node_feats)
    feats = exchange(feats, "grp")
    x, offered, *picked = call(
        functools.partial(pick_blocks, groups, slots, at),
        [shape((blocks, tile, narrow), BF16), shape((offers, tile, narrow), BF16)]
        + [shape((slots * tile, narrow), BF16)] * peers,
        [SMEM] + [VMEM] * groups,
        nbytes=4 * (peers * slots + blocks + offers) * tile * narrow,
        name="pick_blocks",
    )(tab, *feats)
    mirrored = swap(offered, "dom", half)
    near = exchange([None] + picked, "dom")[1:]
    local = call(
        functools.partial(local_sum, per_row, at),
        shape((blocks, tile, narrow), F32),
        [SMEM, VMEM, VMEM],
        flops=2 * blocks * per_row * tile * tile * narrow,
        nbytes=blocks * tile * narrow * 6,
        name="local_sum",
    )(tab, tile_bank, x)
    mirrored, local = lax.optimization_barrier((mirrored, local))
    relayed = call(
        functools.partial(pick_relayed, slots, at),
        [shape((slots * tile, narrow), BF16)] * peers,
        [SMEM, VMEM],
        nbytes=4 * peers * slots * tile * narrow,
        name="pick_relayed",
    )(tab, mirrored)
    far = exchange([None, *relayed], "dom")[1:]
    aggs = call(
        functools.partial(add_halo, half, groups, slots, at),
        [shape((rows_here, narrow), BF16)] * groups,
        [SMEM, VMEM, VMEM, VMEM] + [VMEM] * (2 * peers),
        [pltpu.VMEM((blocks, tile, narrow), F32)],
        flops=4 * half * slots * tile * tile * narrow,
        nbytes=blocks * tile * narrow * 8,
        name="add_halo",
    )(tab, tile_bank, local, mirrored, *near, *far)
    activations, grad = call(
        functools.partial(dense, groups),
        [shape((rows_here, hidden), BF16), shape((groups, rows_here, wide), BF16)],
        [SMEM] + [VMEM] * (3 + groups),
        flops=2 * rows_here * embed * hidden,
        nbytes=embed * hidden * 2 + rows_here * (embed + 3 * hidden) * 2,
        name="dense",
    )(ids, weight, bias.reshape(1, hidden), cotangent, *exchange(aggs, "grp"))

    grads, masks = spread(grad, "grp")
    norm_scale = float(rows_here * groups * domains) ** (-0.5)
    norm_scale = float(rows_here * groups * domains) ** (-0.5)
    kept_shares, *shares = call(
        functools.partial(weight_slice, groups, masks),
        [shape((2, share, hidden), F32)] + [shape((2, share, hidden), BF16)] * peers,
        [SMEM] + [VMEM] * (2 * groups),
        [pltpu.VMEM((domains, share, hidden), F32)],
        flops=2 * part_rows * narrow * hidden,
        nbytes=part_rows * (narrow + hidden) * 2,
        name="weight_slice",
    )(ids, *aggs, *grads)
    tab_after, _ = lax.optimization_barrier((tab, shares))
    shares = exchange([None] + shares, "dom")[1:]
    own, bias_here, kept, *terms = call(
        functools.partial(back_halo, masks, slots, at),
        [
            shape((blocks, tile, wide), BF16),
            shape((1, wide), F32),
            shape((slots * tile, wide), BF16),
        ]
        + [shape((2 * slots * tile + EXTRA, wide), BF16)] * peers,
        [SMEM, VMEM] + [VMEM] * len(masks),
        flops=2 * domains * slots * tile * tile * wide,
        nbytes=(domains * slots + blocks) * tile * wide * 2,
        name="back_halo",
    )(tab_after, bank_t, *grads)
    shares, _ = lax.optimization_barrier((shares, terms))
    terms = exchange([None] + terms, "dom")[1:]
    here = call(
        sum_half,
        shape((2, share, hidden), BF16),
        [VMEM] * half,
        nbytes=2 * half * share * hidden * 2,
        name="sum_half",
    )(kept_shares, *shares)
    there = swap(here, "dom", half)
    back = call(
        functools.partial(back_local, per_row, at),
        shape((blocks, tile, wide), F32),
        [SMEM, VMEM, VMEM],
        flops=2 * blocks * per_row * tile * tile * wide,
        nbytes=blocks * tile * wide * 6,
        name="back_local",
    )(tab, bank_t, own)
    there, back = lax.optimization_barrier((there, back))
    summed = call(
        functools.partial(sum_both, norm_scale),
        shape((2, share, hidden), BF16),
        [VMEM, VMEM],
        nbytes=6 * share * hidden * 2,
        name="sum_both",
    )(here, there)
    terms, _ = lax.optimization_barrier((terms, summed))
    crossing = call(
        functools.partial(sum_mirror, slots, at),
        shape((offers * tile + EXTRA, wide), BF16),
        [SMEM] + [VMEM] * (2 + peers),
        [pltpu.VMEM((offers, tile, wide), F32)],
        nbytes=4 * domains * slots * tile * wide,
        name="sum_mirror",
    )(tab, bias_here, kept, *terms)
    gathered = exchange([summed] * half, "dom")
    gathered, _ = lax.optimization_barrier((gathered, crossing))
    returned = swap(crossing, "dom", half)
    joined = call(
        join_shares,
        shape((domains, share, hidden), BF16),
        [SMEM] + [VMEM] * half,
        nbytes=4 * narrow * hidden,
        name="join_shares",
    )(ids, *gathered).reshape(narrow, hidden)

    hid = call(
        functools.partial(finish_nodes, half, slots, norm_scale, at),
        [shape((rows_here + EXTRA, wide), BF16)] * groups,
        [SMEM, VMEM, VMEM, VMEM] + [VMEM] * peers,
        [pltpu.VMEM((blocks, tile, wide), F32)],
        nbytes=domains * slots * tile * wide * 2 + blocks * tile * wide * 6,
        name="finish_nodes",
    )(tab, back, bias_here, returned, *terms)
    weights, masks = spread(joined, "grp", hid[0])
    hid = exchange(hid, "grp")
    count = groups // 2
    first = [masks.index(m) for m in range(count)]
    last = [masks.index(m) for m in range(count, groups)]
    placing = dict(
        out_shape=shape((embed, hidden), F32),
        scratch=[pltpu.VMEM((count, narrow, hidden), F32), pltpu.SemaphoreType.DMA((count, COPIES))],
        nbytes=embed * hidden * 3,
        name="place_weight",
        out_specs=pl.BlockSpec(memory_space=pl.ANY),
    )
    grad_weight = call(
        functools.partial(place_weight, [masks[i] for i in first]),
        specs=[SMEM] + [VMEM] * count,
        **placing,
    )(ids, *[weights[i] for i in first])
    grad_weight, *hid = lax.optimization_barrier((grad_weight, *hid))
    grad_nodes, grad_bias = call(
        functools.partial(node_grads, groups),
        [shape((rows_here, embed), BF16), shape((1, hidden), F32)],
        [SMEM, VMEM] + [VMEM] * groups,
        [pltpu.VMEM((groups, rows_here + EXTRA, wide), BF16)],
        flops=2 * rows_here * embed * hidden,
        nbytes=embed * hidden * 2 + rows_here * (embed + hidden) * 2,
        name="node_grads",
    )(ids, weight, *hid)
    grad_weight = call(
        functools.partial(place_weight, [masks[i] for i in last]),
        specs=[SMEM] + [VMEM] * count + [pl.BlockSpec(memory_space=pl.ANY)],
        aliases={count + 1: 0},
        **placing,
    )(ids, *[weights[i] for i in last], grad_weight)
    return (activations, grad_nodes, grad_weight, grad_bias.reshape(hidden))


def solution(mesh):
    in_specs = (
        P(("dom", "grp"), None),
        P(),
        P(),
        P(("dom", "grp"), None),
        P(),
        P("dom", None, None),
        P("dom", None, None),
        P("dom", None),
        P(),
        P("dom", None, None),
        P("dom", None, None),
    )
    out_specs = (P(("dom", "grp"), None), P(("dom", "grp"), None), P(), P())
    return jax.shard_map(
        per_device, mesh=mesh, in_specs=in_specs, out_specs=out_specs, check_vma=False
    )
```

```python
import functools

import jax
import jax.numpy as jnp
from jax import lax
from jax.experimental import pallas as pl
from jax.experimental.pallas import tpu as pltpu
from jax.sharding import PartitionSpec as P

VMEM = pl.BlockSpec(memory_space=pltpu.VMEM)
SMEM = pl.BlockSpec(memory_space=pltpu.SMEM)
EXTRA = 16
COPIES = 4
F32 = jnp.float32
BF16 = jnp.bfloat16


def call(
    body, out_shape, specs, scratch=(), flops=0, nbytes=0, name=None, out_specs=None, aliases=(), mib=16
):
    return pl.pallas_call(
        body,
        out_shape=out_shape,
        in_specs=specs,
        out_specs=jax.tree.map(lambda _: VMEM, out_shape) if out_specs is None else out_specs,
        scratch_shapes=list(scratch),
        input_output_aliases=dict(aliases),
        compiler_params=pltpu.CompilerParams(vmem_limit_bytes=mib * 1024 * 1024),
        cost_estimate=pl.CostEstimate(flops=flops, bytes_accessed=nbytes, transcendentals=0),
        name=name,
    )


def shape(dims, kind):
    return jax.ShapeDtypeStruct(tuple(dims), kind)


def dot(a, b):
    return jnp.dot(a, b, preferred_element_type=F32)


def bias_rows(total):
    high = total.astype(BF16).astype(F32)
    rest = jnp.zeros((EXTRA - 2, total.shape[1]), F32)
    return jnp.concatenate([high, total - high, rest], axis=0).astype(BF16)


def aligned(start, step):
    return pl.ds(pl.multiple_of(start * step, step), step)


def swap(value, axis, mask):
    return lax.ppermute(value, axis, [(i, i ^ mask) for i in range(lax.axis_size(axis))])


def exchange(parts, axis):
    return list(parts[:1]) + [swap(part, axis, m) for m, part in enumerate(parts[1:], 1)]


def spread(value, axis, ahead=None):
    size = lax.axis_size(axis)
    parts, masks = [value], [0]
    bit = size // 2
    while bit:
        if ahead is not None:
            parts[1:] = [lax.optimization_barrier((part, ahead))[0] for part in parts[1:]]
        parts = parts + [swap(part, axis, bit) for part in parts]
        masks = masks + [mask ^ bit for mask in masks]
        bit //= 2
    return parts, masks


def split_features(ids, feats, *refs):
    outs, sems = refs[:-1], refs[-1]
    group = ids[1]
    narrow = outs[0].shape[1]
    copies = [
        pltpu.make_async_copy(
            feats.at[:, aligned(jnp.bitwise_xor(group, m), narrow)], out, sems.at[m]
        )
        for m, out in enumerate(outs)
    ]
    for copy in copies:
        copy.start()
    for copy in copies:
        copy.wait()


def pick_blocks(groups, slots, at, tab, *refs):
    parts, (x, offered, *outs) = refs[:groups], refs[groups:]
    domain, group = tab[at["me"]], tab[at["me"] + 1]
    tile = x.shape[1]
    per = x.shape[0] // groups
    for m, part in enumerate(parts):
        owner = jnp.bitwise_xor(group, m)
        for j in range(per):
            x[owner * per + j] = part[j * tile : (j + 1) * tile]
    for j in range(offered.shape[0]):
        offered[j] = x[tab[at["pub"] + j]]
    for m, out in enumerate(outs, 1):
        reader = jnp.bitwise_xor(domain, m)
        for s in range(slots):
            entry = jnp.maximum(tab[at["out"] + reader * slots + s], 0)
            out[s * tile : (s + 1) * tile] = x[tab[at["pub"] + entry]]


def pick_relayed(slots, at, tab, offered, *outs):
    tile = offered.shape[1]
    for m, out in enumerate(outs, 1):
        reader = jnp.bitwise_xor(tab[at["me"]], m)
        for s in range(slots):
            entry = jnp.maximum(tab[at["out2"] + reader * slots + s], 0)
            out[s * tile : (s + 1) * tile] = offered[entry]


def local_sum(per_row, at, tab, bank, x, out):
    pair = 2 if per_row % 2 == 0 else 1

    @pl.loop(0, out.shape[0])
    def _(r):
        acc = jnp.zeros(out.shape[1:], F32)
        for k in range(0, per_row, pair):
            spots = [r * per_row + k + j for j in range(pair)]
            left = jnp.concatenate([bank[tab[at["banks"] + a]] for a in spots], axis=1)
            right = jnp.concatenate([x[tab[at["cols"] + a]] for a in spots], axis=0)
            acc += dot(left, right)
        out[r] = acc


def halo_adder(slots, at, tab, bank, acc):
    def add(source, get):
        for s in range(slots):
            i = source * slots + s
            entry = tab[at["in"] + i]

            @pl.when(entry >= 0)
            def _(i=i, s=s, entry=entry):
                acc[tab[at["hrows"] + i]] += dot(bank[tab[at["hbanks"] + i]], get(s, entry))

    return add


def add_near(slots, at, tab, bank, local, mirrored, *refs):
    near, acc = refs[:-1], refs[-1]
    domain = tab[at["me"]]
    tile = local.shape[1]
    acc[...] = local[...]
    add = halo_adder(slots, at, tab, bank, acc)
    for m, block in enumerate(near, 1):
        add(jnp.bitwise_xor(domain, m), lambda s, _, block=block: block[s * tile : (s + 1) * tile])
    mirror = jnp.bitwise_xor(domain, len(near) + 1)
    add(mirror, lambda _, entry: mirrored[jnp.maximum(entry, 0)])


def add_far(half, groups, slots, at, tab, bank, local, *refs):
    far, outs, acc = refs[: half - 1], refs[half - 1 : -1], refs[-1]
    domain, group = tab[at["me"]], tab[at["me"] + 1]
    tile = local.shape[1]
    per = local.shape[0] // groups
    acc[...] = local[...]
    add = halo_adder(slots, at, tab, bank, acc)
    for m, block in enumerate(far, half + 1):
        add(jnp.bitwise_xor(domain, m), lambda s, _, block=block: block[s * tile : (s + 1) * tile])
    for m, out in enumerate(outs):
        owner = jnp.bitwise_xor(group, m)
        for j in range(per):
            out[j * tile : (j + 1) * tile] = acc[owner * per + j].astype(BF16)


def dense(groups, ids, weight, bias, cot, *refs):
    parts, (act, grad) = refs[:groups], refs[groups:]
    group = ids[1]
    narrow = parts[0].shape[1]
    wide = cot.shape[1] // groups
    left = jnp.concatenate([part[...] for part in parts], axis=1)
    spots = [aligned(jnp.bitwise_xor(group, m), narrow) for m in range(groups)]
    pre = dot(left, jnp.concatenate([weight[spot] for spot in spots], axis=0)) + bias[...]
    act[...] = jnp.maximum(pre, 0.0).astype(BF16)
    masked = jnp.where(pre > 0, cot[...].astype(F32), 0.0).astype(BF16)
    for s in range(groups):
        grad[s] = masked[:, s * wide : (s + 1) * wide]


def back_halo(masks, slots, at, tab, bank_t, *refs):
    parts, (own, mine, kept, *terms) = refs[: len(masks)], refs[len(masks) :]
    domain, group = tab[at["me"]], tab[at["me"] + 1]
    tile = bank_t.shape[1]
    per = parts[0].shape[1] // tile
    half = len(terms) + 1
    total = jnp.zeros((1, own.shape[2]), F32)
    for mask, part in zip(masks, parts):
        owner = jnp.bitwise_xor(group, mask)
        piece = part[group]
        total += jnp.sum(piece.astype(F32), axis=0, keepdims=True)
        for j in range(per):
            own[owner * per + j] = piece[j * tile : (j + 1) * tile]
    mine[...] = total
    tail = bias_rows(total)

    def put(out, place, source):
        for s in range(slots):
            i = source * slots + s
            live = (tab[at["in"] + i] >= 0).astype(F32)
            value = dot(bank_t[tab[at["hbanks"] + i]], own[tab[at["hrows"] + i]]) * live
            spot = (place * slots + s) * tile
            out[spot : spot + tile] = value.astype(BF16)

    for m, term in enumerate(terms, 1):
        peer = jnp.bitwise_xor(domain, m)
        put(term, 0, peer)
        put(term, 1, jnp.bitwise_xor(peer, half))
        term[2 * slots * tile :] = tail
    put(kept, 0, jnp.bitwise_xor(domain, half))


def sum_mirror(slots, at, tab, mine, kept, *refs):
    recv, out, acc = refs[:-2], refs[-2], refs[-1]
    domain = tab[at["me"]]
    offered, tile = acc.shape[:2]
    acc[...] = jnp.zeros_like(acc)
    total = mine[...]
    for m, block in enumerate((kept,) + recv):
        reader = jnp.bitwise_xor(domain, m)
        for s in range(slots):
            entry = tab[at["out2"] + reader * slots + s]
            spot = (s + (slots if m else 0)) * tile

            @pl.when(entry >= 0)
            def _(entry=entry, spot=spot, block=block):
                acc[jnp.maximum(entry, 0)] += block[spot : spot + tile].astype(F32)

        if m:
            tail = block[2 * slots * tile :].astype(F32)
            total += tail[0:1] + tail[1:2]
    for j in range(offered):
        out[j * tile : (j + 1) * tile] = acc[j].astype(BF16)
    out[offered * tile :] = bias_rows(total)


def weight_slice(groups, masks, ids, *refs):
    aggs, parts = refs[:groups], refs[groups : 2 * groups]
    kept, *outs = refs[2 * groups : -1]
    total = refs[-1]
    domain = ids[0]
    half = len(outs) + 1
    left = jnp.concatenate([aggs[mask][...] for mask in masks], axis=0)
    pieces = [jnp.concatenate([part[s] for part in parts], axis=0) for s in range(groups)]
    right = jnp.concatenate(pieces, axis=1)
    whole = lax.dot_general(left, right, (((0,), (0,)), ((), ())), preferred_element_type=F32)
    rows = total.shape[1]
    for d in range(total.shape[0]):
        total[d] = whole[d * rows : (d + 1) * rows]
    for m, out in enumerate([kept] + outs):
        peer = jnp.bitwise_xor(domain, m)
        out[0] = total[peer].astype(out.dtype)
        out[1] = total[jnp.bitwise_xor(peer, half)].astype(out.dtype)


def sum_half(kept, *refs):
    recv, out = refs[:-1], refs[-1]
    for i in range(2):
        total = kept[i]
        for block in recv:
            total += block[i].astype(F32)
        out[i] = total.astype(BF16)


def sum_both(scale, here, there, out):
    for i in range(2):
        out[i] = ((here[i].astype(F32) + there[1 - i].astype(F32)) * scale).astype(BF16)


def join_shares(ids, *refs):
    parts, out = refs[:-1], refs[-1]
    for m, part in enumerate(parts):
        owner = jnp.bitwise_xor(ids[0], m)
        out[owner] = part[0]
        out[jnp.bitwise_xor(owner, len(parts))] = part[1]


def back_local(per_row, at, tab, bank_t, own, out):
    out[...] = jnp.zeros_like(out)

    @pl.loop(0, own.shape[0])
    def _(r):
        right = own[r]
        for k in range(per_row):
            spot = r * per_row + k
            out[tab[at["cols"] + spot]] += dot(bank_t[tab[at["banks"] + spot]], right)


def finish_nodes(half, slots, scale, at, tab, local, mine, mirrored, *refs):
    recv, outs, acc = refs[: half - 1], refs[half - 1 : -1], refs[-1]
    groups = len(outs)
    domain, group = tab[at["me"]], tab[at["me"] + 1]
    tile = local.shape[1]
    per = local.shape[0] // groups
    offered = (mirrored.shape[0] - EXTRA) // tile
    acc[...] = local[...]
    tail = mirrored[offered * tile :].astype(F32)
    for j in range(offered):
        acc[tab[at["pub"] + j]] += mirrored[j * tile : (j + 1) * tile].astype(F32)
    for m, block in enumerate(recv, 1):
        tail += block[2 * slots * tile :].astype(F32)
        reader = jnp.bitwise_xor(domain, m)
        for s in range(slots):
            entry = tab[at["out"] + reader * slots + s]

            @pl.when(entry >= 0)
            def _(s=s, entry=entry, block=block):
                spot = tab[at["pub"] + jnp.maximum(entry, 0)]
                acc[spot] += block[s * tile : (s + 1) * tile].astype(F32)

    rows = bias_rows((mine[...] + tail[0:1] + tail[1:2]) * scale)
    for m, out in enumerate(outs):
        owner = jnp.bitwise_xor(group, m)
        for j in range(per):
            out[j * tile : (j + 1) * tile] = acc[owner * per + j].astype(BF16)
        out[per * tile :] = rows


def node_grads(groups, ids, weight, *refs):
    parts, (out, bias_out, hid) = refs[:groups], refs[groups:]
    group = ids[1]
    rows = out.shape[0]
    for m, part in enumerate(parts):
        hid[jnp.bitwise_xor(group, m)] = part[...]
    left = jnp.concatenate([hid[s, :rows] for s in range(groups)], axis=1)
    out[...] = lax.dot_general(
        left, weight[...], (((1,), (1,)), ((), ())), preferred_element_type=F32
    ).astype(BF16)
    tail = jnp.concatenate([hid[s, rows:] for s in range(groups)], axis=1).astype(F32)
    bias_out[...] = tail[0:1] + tail[1:2]


def place_weight(masks, ids, *refs):
    parts, (out, wide, sems) = refs[: len(masks)], refs[-3:]
    group = ids[1]
    rows = parts[0].shape[0]
    copies = []
    step = rows // COPIES
    for i, (mask, part) in enumerate(zip(masks, parts)):
        for j in range(COPIES):
            wide[i, j * step : (j + 1) * step] = part[j * step : (j + 1) * step].astype(F32)
            spot = out.at[aligned(jnp.bitwise_xor(group, mask) * COPIES + j, step)]
            piece = wide.at[i, pl.ds(j * step, step)]
            copies.append(pltpu.make_async_copy(piece, spot, sems.at[i, j]))
            copies[-1].start()
    for copy in copies:
        copy.wait()


def per_device(
    node_feats,
    weight,
    bias,
    cotangent,
    tile_bank,
    local_cols,
    local_banks,
    published,
    send_table,
    halo_rows,
    halo_banks,
):
    domains = lax.axis_size("dom")
    groups = lax.axis_size("grp")
    domain_index = lax.axis_index("dom")
    rows_here, embed = node_feats.shape
    hidden = weight.shape[1]
    tile = tile_bank.shape[1]
    slots = send_table.shape[2]
    per_row = local_cols.shape[2]
    part_rows = rows_here * groups
    blocks = part_rows // tile
    narrow = embed // groups
    wide = hidden // groups
    share = narrow // domains
    half = domains // 2
    peers = half - 1
    offers = published.shape[1]

    ids = jnp.stack([domain_index, lax.axis_index("grp")]).astype(jnp.int32)
    tables = {
        "cols": local_cols[0],
        "banks": local_banks[0],
        "pub": published[0],
        "out": lax.dynamic_index_in_dim(send_table, domain_index, 0, keepdims=False),
        "out2": lax.dynamic_index_in_dim(send_table, domain_index ^ half, 0, keepdims=False),
        "in": lax.dynamic_index_in_dim(send_table, domain_index, 1, keepdims=False),
        "hrows": halo_rows[0],
        "hbanks": halo_banks[0],
        "me": ids,
    }
    at, place = {}, 0
    for name, table in tables.items():
        at[name] = place
        place += table.size
    tab = jnp.concatenate([table.reshape(-1) for table in tables.values()])
    bank_t = jnp.swapaxes(tile_bank, 1, 2)

    feats = call(
        split_features,
        [shape((rows_here, narrow), BF16)] * groups,
        [SMEM, pl.BlockSpec(memory_space=pl.ANY)],
        [pltpu.SemaphoreType.DMA((groups,))],
        nbytes=4 * rows_here * embed,
        name="split_features",
    )(ids, node_feats)
    feats = exchange(feats, "grp")
    x, offered, *picked = call(
        functools.partial(pick_blocks, groups, slots, at),
        [shape((blocks, tile, narrow), BF16), shape((offers, tile, narrow), BF16)]
        + [shape((slots * tile, narrow), BF16)] * peers,
        [SMEM] + [VMEM] * groups,
        nbytes=4 * (peers * slots + blocks + offers) * tile * narrow,
        name="pick_blocks",
    )(tab, *feats)
    mirrored = swap(offered, "dom", half)
    near = exchange([None] + picked, "dom")[1:]
    local = call(
        functools.partial(local_sum, per_row, at),
        shape((blocks, tile, narrow), F32),
        [SMEM, VMEM, VMEM],
        flops=2 * blocks * per_row * tile * tile * narrow,
        nbytes=blocks * tile * narrow * 6,
        name="local_sum",
    )(tab, tile_bank, x)
    mirrored, local = lax.optimization_barrier((mirrored, local))
    relayed = call(
        functools.partial(pick_relayed, slots, at),
        [shape((slots * tile, narrow), BF16)] * peers,
        [SMEM, VMEM],
        nbytes=4 * peers * slots * tile * narrow,
        name="pick_relayed",
    )(tab, mirrored)
    far = exchange([None, *relayed], "dom")[1:]
    local = call(
        functools.partial(add_near, slots, at),
        shape((blocks, tile, narrow), F32),
        [SMEM, VMEM, VMEM, VMEM] + [VMEM] * peers,
        flops=2 * half * slots * tile * tile * narrow,
        nbytes=blocks * tile * narrow * 8,
        name="add_near",
    )(tab, tile_bank, local, mirrored, *near)
    far, local = lax.optimization_barrier((far, local))
    aggs = call(
        functools.partial(add_far, half, groups, slots, at),
        [shape((rows_here, narrow), BF16)] * groups,
        [SMEM, VMEM, VMEM] + [VMEM] * peers,
        [pltpu.VMEM((blocks, tile, narrow), F32)],
        flops=2 * half * slots * tile * tile * narrow,
        nbytes=blocks * tile * narrow * 8,
        name="add_far",
    )(tab, tile_bank, local, *far)
    activations, grad = call(
        functools.partial(dense, groups),
        [shape((rows_here, hidden), BF16), shape((groups, rows_here, wide), BF16)],
        [SMEM] + [VMEM] * (3 + groups),
        flops=2 * rows_here * embed * hidden,
        nbytes=embed * hidden * 2 + rows_here * (embed + 3 * hidden) * 2,
        name="dense",
    )(ids, weight, bias.reshape(1, hidden), cotangent, *exchange(aggs, "grp"))

    grads, masks = spread(grad, "grp")
    norm_scale = float(rows_here * groups * domains) ** (-0.5)
    norm_scale = float(rows_here * groups * domains) ** (-0.5)
    kept_shares, *shares = call(
        functools.partial(weight_slice, groups, masks),
        [shape((2, share, hidden), F32)] + [shape((2, share, hidden), BF16)] * peers,
        [SMEM] + [VMEM] * (2 * groups),
        [pltpu.VMEM((domains, share, hidden), F32)],
        flops=2 * part_rows * narrow * hidden,
        nbytes=part_rows * (narrow + hidden) * 2,
        name="weight_slice",
    )(ids, *aggs, *grads)
    tab_after, _ = lax.optimization_barrier((tab, shares))
    shares = exchange([None] + shares, "dom")[1:]
    own, bias_here, kept, *terms = call(
        functools.partial(back_halo, masks, slots, at),
        [
            shape((blocks, tile, wide), BF16),
            shape((1, wide), F32),
            shape((slots * tile, wide), BF16),
        ]
        + [shape((2 * slots * tile + EXTRA, wide), BF16)] * peers,
        [SMEM, VMEM] + [VMEM] * len(masks),
        flops=2 * domains * slots * tile * tile * wide,
        nbytes=(domains * slots + blocks) * tile * wide * 2,
        name="back_halo",
    )(tab_after, bank_t, *grads)
    shares, _ = lax.optimization_barrier((shares, terms))
    terms = exchange([None] + terms, "dom")[1:]
    here = call(
        sum_half,
        shape((2, share, hidden), BF16),
        [VMEM] * half,
        nbytes=2 * half * share * hidden * 2,
        name="sum_half",
    )(kept_shares, *shares)
    there = swap(here, "dom", half)
    terms, _ = lax.optimization_barrier((terms, here))
    crossing = call(
        functools.partial(sum_mirror, slots, at),
        shape((offers * tile + EXTRA, wide), BF16),
        [SMEM] + [VMEM] * (2 + peers),
        [pltpu.VMEM((offers, tile, wide), F32)],
        nbytes=4 * domains * slots * tile * wide,
        name="sum_mirror",
    )(tab, bias_here, kept, *terms)
    returned = swap(crossing, "dom", half)
    there, _ = lax.optimization_barrier((there, crossing))
    summed = call(
        functools.partial(sum_both, norm_scale),
        shape((2, share, hidden), BF16),
        [VMEM, VMEM],
        nbytes=6 * share * hidden * 2,
        name="sum_both",
    )(here, there)
    own, _ = lax.optimization_barrier((own, summed))
    back = call(
        functools.partial(back_local, per_row, at),
        shape((blocks, tile, wide), F32),
        [SMEM, VMEM, VMEM],
        flops=2 * blocks * per_row * tile * tile * wide,
        nbytes=blocks * tile * wide * 6,
        name="back_local",
    )(tab, bank_t, own)
    gathered = exchange([summed] * half, "dom")
    gathered, back, returned = lax.optimization_barrier((gathered, back, returned))
    joined = call(
        join_shares,
        shape((domains, share, hidden), BF16),
        [SMEM] + [VMEM] * half,
        nbytes=4 * narrow * hidden,
        name="join_shares",
    )(ids, *gathered).reshape(narrow, hidden)

    hid = call(
        functools.partial(finish_nodes, half, slots, norm_scale, at),
        [shape((rows_here + EXTRA, wide), BF16)] * groups,
        [SMEM, VMEM, VMEM, VMEM] + [VMEM] * peers,
        [pltpu.VMEM((blocks, tile, wide), F32)],
        nbytes=domains * slots * tile * wide * 2 + blocks * tile * wide * 6,
        name="finish_nodes",
    )(tab, back, bias_here, returned, *terms)
    hid = exchange(hid, "grp")
    weights, masks = spread(joined, "grp", hid)
    count = groups // 2
    first = [masks.index(m) for m in range(count)]
    last = [masks.index(m) for m in range(count, groups)]
    placing = dict(
        out_shape=shape((embed, hidden), F32),
        scratch=[pltpu.VMEM((count, narrow, hidden), F32), pltpu.SemaphoreType.DMA((count, COPIES))],
        nbytes=embed * hidden * 3,
        name="place_weight",
        out_specs=pl.BlockSpec(memory_space=pl.ANY),
    )
    grad_weight = call(
        functools.partial(place_weight, [masks[i] for i in first]),
        specs=[SMEM] + [VMEM] * count,
        **placing,
    )(ids, *[weights[i] for i in first])
    grad_weight, *hid = lax.optimization_barrier((grad_weight, *hid))
    grad_nodes, grad_bias = call(
        functools.partial(node_grads, groups),
        [shape((rows_here, embed), BF16), shape((1, hidden), F32)],
        [SMEM, VMEM] + [VMEM] * groups,
        [pltpu.VMEM((groups, rows_here + EXTRA, wide), BF16)],
        flops=2 * rows_here * embed * hidden,
        nbytes=embed * hidden * 2 + rows_here * (embed + hidden) * 2,
        name="node_grads",
    )(ids, weight, *hid)
    grad_weight = call(
        functools.partial(place_weight, [masks[i] for i in last]),
        specs=[SMEM] + [VMEM] * count + [pl.BlockSpec(memory_space=pl.ANY)],
        aliases={count + 1: 0},
        **placing,
    )(ids, *[weights[i] for i in last], grad_weight)
    return (activations, grad_nodes, grad_weight, grad_bias.reshape(hidden))


def solution(mesh):
    in_specs = (
        P(("dom", "grp"), None),
        P(),
        P(),
        P(("dom", "grp"), None),
        P(),
        P("dom", None, None),
        P("dom", None, None),
        P("dom", None),
        P(),
        P("dom", None, None),
        P("dom", None, None),
    )
    out_specs = (P(("dom", "grp"), None), P(("dom", "grp"), None), P(), P())
    return jax.shard_map(
        per_device, mesh=mesh, in_specs=in_specs, out_specs=out_specs, check_vma=False
    )
```

```python
import functools

import jax
import jax.numpy as jnp
from jax import lax
from jax.experimental import pallas as pl
from jax.experimental.pallas import tpu as pltpu
from jax.sharding import PartitionSpec as P

VMEM = pl.BlockSpec(memory_space=pltpu.VMEM)
SMEM = pl.BlockSpec(memory_space=pltpu.SMEM)
EXTRA = 16
COPIES = 4
F32 = jnp.float32
BF16 = jnp.bfloat16


def call(
    body, out_shape, specs, scratch=(), flops=0, nbytes=0, name=None, out_specs=None, aliases=(), mib=16
):
    return pl.pallas_call(
        body,
        out_shape=out_shape,
        in_specs=specs,
        out_specs=jax.tree.map(lambda _: VMEM, out_shape) if out_specs is None else out_specs,
        scratch_shapes=list(scratch),
        input_output_aliases=dict(aliases),
        compiler_params=pltpu.CompilerParams(vmem_limit_bytes=mib * 1024 * 1024),
        cost_estimate=pl.CostEstimate(flops=flops, bytes_accessed=nbytes, transcendentals=0),
        name=name,
    )


def shape(dims, kind):
    return jax.ShapeDtypeStruct(tuple(dims), kind)


def dot(a, b):
    return jnp.dot(a, b, preferred_element_type=F32)


def bias_rows(total):
    high = total.astype(BF16).astype(F32)
    rest = jnp.zeros((EXTRA - 2, total.shape[1]), F32)
    return jnp.concatenate([high, total - high, rest], axis=0).astype(BF16)


def aligned(start, step):
    return pl.ds(pl.multiple_of(start * step, step), step)


def swap(value, axis, mask):
    return lax.ppermute(value, axis, [(i, i ^ mask) for i in range(lax.axis_size(axis))])


def exchange(parts, axis):
    return list(parts[:1]) + [swap(part, axis, m) for m, part in enumerate(parts[1:], 1)]


def spread(value, axis, bit):
    parts, masks = [value], [0]
    while bit:
        parts = parts + [swap(part, axis, bit) for part in parts]
        masks = masks + [mask ^ bit for mask in masks]
        bit //= 2
    return parts, masks


def split_features(ids, feats, *refs):
    outs, sems = refs[:-1], refs[-1]
    group = ids[1]
    narrow = outs[0].shape[1]
    copies = [
        pltpu.make_async_copy(
            feats.at[:, aligned(jnp.bitwise_xor(group, m), narrow)], out, sems.at[m]
        )
        for m, out in enumerate(outs)
    ]
    for copy in copies:
        copy.start()
    for copy in copies:
        copy.wait()


def pick_blocks(groups, slots, at, tab, *refs):
    parts, (x, offered, *outs) = refs[:groups], refs[groups:]
    domain, group = tab[at["me"]], tab[at["me"] + 1]
    tile = x.shape[1]
    per = x.shape[0] // groups
    for m, part in enumerate(parts):
        owner = jnp.bitwise_xor(group, m)
        for j in range(per):
            x[owner * per + j] = part[j * tile : (j + 1) * tile]
    for j in range(offered.shape[0]):
        offered[j] = x[tab[at["pub"] + j]]
    for m, out in enumerate(outs, 1):
        reader = jnp.bitwise_xor(domain, m)
        for s in range(slots):
            entry = jnp.maximum(tab[at["out"] + reader * slots + s], 0)
            out[s * tile : (s + 1) * tile] = x[tab[at["pub"] + entry]]


def pick_relayed(slots, at, tab, offered, *outs):
    tile = offered.shape[1]
    for m, out in enumerate(outs, 1):
        reader = jnp.bitwise_xor(tab[at["me"]], m)
        for s in range(slots):
            entry = jnp.maximum(tab[at["out2"] + reader * slots + s], 0)
            out[s * tile : (s + 1) * tile] = offered[entry]


def local_sum(per_row, at, tab, bank, x, out):
    pair = 2 if per_row % 2 == 0 else 1

    @pl.loop(0, out.shape[0])
    def _(r):
        acc = jnp.zeros(out.shape[1:], F32)
        for k in range(0, per_row, pair):
            spots = [r * per_row + k + j for j in range(pair)]
            left = jnp.concatenate([bank[tab[at["banks"] + a]] for a in spots], axis=1)
            right = jnp.concatenate([x[tab[at["cols"] + a]] for a in spots], axis=0)
            acc += dot(left, right)
        out[r] = acc


def halo_adder(slots, at, tab, bank, acc):
    def add(source, get):
        for s in range(slots):
            i = source * slots + s
            entry = tab[at["in"] + i]

            @pl.when(entry >= 0)
            def _(i=i, s=s, entry=entry):
                acc[tab[at["hrows"] + i]] += dot(bank[tab[at["hbanks"] + i]], get(s, entry))

    return add


def add_near(slots, at, tab, bank, local, mirrored, *refs):
    near, acc = refs[:-1], refs[-1]
    domain = tab[at["me"]]
    tile = local.shape[1]
    acc[...] = local[...]
    add = halo_adder(slots, at, tab, bank, acc)
    for m, block in enumerate(near, 1):
        add(jnp.bitwise_xor(domain, m), lambda s, _, block=block: block[s * tile : (s + 1) * tile])
    mirror = jnp.bitwise_xor(domain, len(near) + 1)
    add(mirror, lambda _, entry: mirrored[jnp.maximum(entry, 0)])


def add_far(half, groups, slots, at, tab, bank, local, *refs):
    far, outs, acc = refs[: half - 1], refs[half - 1 : -1], refs[-1]
    domain, group = tab[at["me"]], tab[at["me"] + 1]
    tile = local.shape[1]
    per = local.shape[0] // groups
    acc[...] = local[...]
    add = halo_adder(slots, at, tab, bank, acc)
    for m, block in enumerate(far, half + 1):
        add(jnp.bitwise_xor(domain, m), lambda s, _, block=block: block[s * tile : (s + 1) * tile])
    for m, out in enumerate(outs):
        owner = jnp.bitwise_xor(group, m)
        for j in range(per):
            out[j * tile : (j + 1) * tile] = acc[owner * per + j].astype(BF16)


def dense(groups, ids, weight, bias, cot, *refs):
    parts, (act, grad) = refs[:groups], refs[groups:]
    group = ids[1]
    narrow = parts[0].shape[1]
    wide = cot.shape[1] // groups
    left = jnp.concatenate([part[...] for part in parts], axis=1)
    spots = [aligned(jnp.bitwise_xor(group, m), narrow) for m in range(groups)]
    pre = dot(left, jnp.concatenate([weight[spot] for spot in spots], axis=0)) + bias[...]
    act[...] = jnp.maximum(pre, 0.0).astype(BF16)
    masked = jnp.where(pre > 0, cot[...].astype(F32), 0.0).astype(BF16)
    for s in range(groups):
        grad[s] = masked[:, s * wide : (s + 1) * wide]


def back_halo(masks, slots, at, tab, bank_t, *refs):
    parts, (own, mine, kept, *terms) = refs[: len(masks)], refs[len(masks) :]
    domain, group = tab[at["me"]], tab[at["me"] + 1]
    tile = bank_t.shape[1]
    per = parts[0].shape[1] // tile
    half = len(terms) + 1
    total = jnp.zeros((1, own.shape[2]), F32)
    for mask, part in zip(masks, parts):
        owner = jnp.bitwise_xor(group, mask)
        piece = part[group]
        total += jnp.sum(piece.astype(F32), axis=0, keepdims=True)
        for j in range(per):
            own[owner * per + j] = piece[j * tile : (j + 1) * tile]
    mine[...] = total
    tail = bias_rows(total)

    def put(out, place, source):
        for s in range(slots):
            i = source * slots + s
            live = (tab[at["in"] + i] >= 0).astype(F32)
            value = dot(bank_t[tab[at["hbanks"] + i]], own[tab[at["hrows"] + i]]) * live
            spot = (place * slots + s) * tile
            out[spot : spot + tile] = value.astype(BF16)

    for m, term in enumerate(terms, 1):
        peer = jnp.bitwise_xor(domain, m)
        put(term, 0, peer)
        put(term, 1, jnp.bitwise_xor(peer, half))
        term[2 * slots * tile :] = tail
    put(kept, 0, jnp.bitwise_xor(domain, half))


def sum_mirror(slots, at, tab, mine, kept, *refs):
    recv, out, acc = refs[:-2], refs[-2], refs[-1]
    domain = tab[at["me"]]
    offered, tile = acc.shape[:2]
    acc[...] = jnp.zeros_like(acc)
    total = mine[...]
    for m, block in enumerate((kept,) + recv):
        reader = jnp.bitwise_xor(domain, m)
        for s in range(slots):
            entry = tab[at["out2"] + reader * slots + s]
            spot = (s + (slots if m else 0)) * tile

            @pl.when(entry >= 0)
            def _(entry=entry, spot=spot, block=block):
                acc[jnp.maximum(entry, 0)] += block[spot : spot + tile].astype(F32)

        if m:
            tail = block[2 * slots * tile :].astype(F32)
            total += tail[0:1] + tail[1:2]
    for j in range(offered):
        out[j * tile : (j + 1) * tile] = acc[j].astype(BF16)
    out[offered * tile :] = bias_rows(total)


def weight_slice(groups, masks, ids, *refs):
    aggs, parts = refs[:groups], refs[groups : 2 * groups]
    kept, *outs = refs[2 * groups : -1]
    total = refs[-1]
    domain = ids[0]
    half = len(outs) + 1
    left = jnp.concatenate([aggs[mask][...] for mask in masks], axis=0)
    pieces = [jnp.concatenate([part[s] for part in parts], axis=0) for s in range(groups)]
    right = jnp.concatenate(pieces, axis=1)
    whole = lax.dot_general(left, right, (((0,), (0,)), ((), ())), preferred_element_type=F32)
    rows = total.shape[1]
    for d in range(total.shape[0]):
        total[d] = whole[d * rows : (d + 1) * rows]
    for m, out in enumerate([kept] + outs):
        peer = jnp.bitwise_xor(domain, m)
        out[0] = total[peer].astype(out.dtype)
        out[1] = total[jnp.bitwise_xor(peer, half)].astype(out.dtype)


def sum_half(kept, *refs):
    recv, out = refs[:-1], refs[-1]
    for i in range(2):
        total = kept[i]
        for block in recv:
            total += block[i].astype(F32)
        out[i] = total.astype(BF16)


def sum_both(scale, here, there, out):
    for i in range(2):
        out[i] = ((here[i].astype(F32) + there[1 - i].astype(F32)) * scale).astype(BF16)


def join_shares(ids, *refs):
    parts, out = refs[:-1], refs[-1]
    for m, part in enumerate(parts):
        owner = jnp.bitwise_xor(ids[0], m)
        out[owner] = part[0]
        out[jnp.bitwise_xor(owner, len(parts))] = part[1]


def back_local(per_row, at, tab, bank_t, own, out):
    out[...] = jnp.zeros_like(out)

    @pl.loop(0, own.shape[0])
    def _(r):
        right = own[r]
        for k in range(per_row):
            spot = r * per_row + k
            out[tab[at["cols"] + spot]] += dot(bank_t[tab[at["banks"] + spot]], right)


def finish_nodes(half, slots, scale, at, tab, local, mine, mirrored, *refs):
    recv, outs, acc = refs[: half - 1], refs[half - 1 : -1], refs[-1]
    groups = len(outs)
    domain, group = tab[at["me"]], tab[at["me"] + 1]
    tile = local.shape[1]
    per = local.shape[0] // groups
    offered = (mirrored.shape[0] - EXTRA) // tile
    acc[...] = local[...]
    tail = mirrored[offered * tile :].astype(F32)
    for j in range(offered):
        acc[tab[at["pub"] + j]] += mirrored[j * tile : (j + 1) * tile].astype(F32)
    for m, block in enumerate(recv, 1):
        tail += block[2 * slots * tile :].astype(F32)
        reader = jnp.bitwise_xor(domain, m)
        for s in range(slots):
            entry = tab[at["out"] + reader * slots + s]

            @pl.when(entry >= 0)
            def _(s=s, entry=entry, block=block):
                spot = tab[at["pub"] + jnp.maximum(entry, 0)]
                acc[spot] += block[s * tile : (s + 1) * tile].astype(F32)

    rows = bias_rows((mine[...] + tail[0:1] + tail[1:2]) * scale)
    for m, out in enumerate(outs):
        owner = jnp.bitwise_xor(group, m)
        for j in range(per):
            out[j * tile : (j + 1) * tile] = acc[owner * per + j].astype(BF16)
        out[per * tile :] = rows


def node_grads(groups, ids, weight, *refs):
    parts, (out, bias_out, hid) = refs[:groups], refs[groups:]
    group = ids[1]
    rows = out.shape[0]
    for m, part in enumerate(parts):
        hid[jnp.bitwise_xor(group, m)] = part[...]
    left = jnp.concatenate([hid[s, :rows] for s in range(groups)], axis=1)
    out[...] = lax.dot_general(
        left, weight[...], (((1,), (1,)), ((), ())), preferred_element_type=F32
    ).astype(BF16)
    tail = jnp.concatenate([hid[s, rows:] for s in range(groups)], axis=1).astype(F32)
    bias_out[...] = tail[0:1] + tail[1:2]


def place_weight(masks, ids, *refs):
    parts, (out, wide, sems) = refs[: len(masks)], refs[-3:]
    group = ids[1]
    rows = parts[0].shape[0]
    copies = []
    step = rows // COPIES
    for i, (mask, part) in enumerate(zip(masks, parts)):
        for j in range(COPIES):
            wide[i, j * step : (j + 1) * step] = part[j * step : (j + 1) * step].astype(F32)
            spot = out.at[aligned(jnp.bitwise_xor(group, mask) * COPIES + j, step)]
            piece = wide.at[i, pl.ds(j * step, step)]
            copies.append(pltpu.make_async_copy(piece, spot, sems.at[i, j]))
            copies[-1].start()
    for copy in copies:
        copy.wait()


def per_device(
    node_feats,
    weight,
    bias,
    cotangent,
    tile_bank,
    local_cols,
    local_banks,
    published,
    send_table,
    halo_rows,
    halo_banks,
):
    domains = lax.axis_size("dom")
    groups = lax.axis_size("grp")
    domain_index = lax.axis_index("dom")
    rows_here, embed = node_feats.shape
    hidden = weight.shape[1]
    tile = tile_bank.shape[1]
    slots = send_table.shape[2]
    per_row = local_cols.shape[2]
    part_rows = rows_here * groups
    blocks = part_rows // tile
    narrow = embed // groups
    wide = hidden // groups
    share = narrow // domains
    half = domains // 2
    peers = half - 1
    offers = published.shape[1]

    ids = jnp.stack([domain_index, lax.axis_index("grp")]).astype(jnp.int32)
    tables = {
        "cols": local_cols[0],
        "banks": local_banks[0],
        "pub": published[0],
        "out": lax.dynamic_index_in_dim(send_table, domain_index, 0, keepdims=False),
        "out2": lax.dynamic_index_in_dim(send_table, domain_index ^ half, 0, keepdims=False),
        "in": lax.dynamic_index_in_dim(send_table, domain_index, 1, keepdims=False),
        "hrows": halo_rows[0],
        "hbanks": halo_banks[0],
        "me": ids,
    }
    at, place = {}, 0
    for name, table in tables.items():
        at[name] = place
        place += table.size
    tab = jnp.concatenate([table.reshape(-1) for table in tables.values()])
    bank_t = jnp.swapaxes(tile_bank, 1, 2)

    feats = call(
        split_features,
        [shape((rows_here, narrow), BF16)] * groups,
        [SMEM, pl.BlockSpec(memory_space=pl.ANY)],
        [pltpu.SemaphoreType.DMA((groups,))],
        nbytes=4 * rows_here * embed,
        name="split_features",
    )(ids, node_feats)
    feats = exchange(feats, "grp")
    x, offered, *picked = call(
        functools.partial(pick_blocks, groups, slots, at),
        [shape((blocks, tile, narrow), BF16), shape((offers, tile, narrow), BF16)]
        + [shape((slots * tile, narrow), BF16)] * peers,
        [SMEM] + [VMEM] * groups,
        nbytes=4 * (peers * slots + blocks + offers) * tile * narrow,
        name="pick_blocks",
    )(tab, *feats)
    mirrored = swap(offered, "dom", half)
    near = exchange([None] + picked, "dom")[1:]
    local = call(
        functools.partial(local_sum, per_row, at),
        shape((blocks, tile, narrow), F32),
        [SMEM, VMEM, VMEM],
        flops=2 * blocks * per_row * tile * tile * narrow,
        nbytes=blocks * tile * narrow * 6,
        name="local_sum",
    )(tab, tile_bank, x)
    mirrored, local = lax.optimization_barrier((mirrored, local))
    relayed = call(
        functools.partial(pick_relayed, slots, at),
        [shape((slots * tile, narrow), BF16)] * peers,
        [SMEM, VMEM],
        nbytes=4 * peers * slots * tile * narrow,
        name="pick_relayed",
    )(tab, mirrored)
    far = exchange([None, *relayed], "dom")[1:]
    local = call(
        functools.partial(add_near, slots, at),
        shape((blocks, tile, narrow), F32),
        [SMEM, VMEM, VMEM, VMEM] + [VMEM] * peers,
        flops=2 * half * slots * tile * tile * narrow,
        nbytes=blocks * tile * narrow * 8,
        name="add_near",
    )(tab, tile_bank, local, mirrored, *near)
    far, local = lax.optimization_barrier((far, local))
    aggs = call(
        functools.partial(add_far, half, groups, slots, at),
        [shape((rows_here, narrow), BF16)] * groups,
        [SMEM, VMEM, VMEM] + [VMEM] * peers,
        [pltpu.VMEM((blocks, tile, narrow), F32)],
        flops=2 * half * slots * tile * tile * narrow,
        nbytes=blocks * tile * narrow * 8,
        name="add_far",
    )(tab, tile_bank, local, *far)
    activations, grad = call(
        functools.partial(dense, groups),
        [shape((rows_here, hidden), BF16), shape((groups, rows_here, wide), BF16)],
        [SMEM] + [VMEM] * (3 + groups),
        flops=2 * rows_here * embed * hidden,
        nbytes=embed * hidden * 2 + rows_here * (embed + 3 * hidden) * 2,
        name="dense",
    )(ids, weight, bias.reshape(1, hidden), cotangent, *exchange(aggs, "grp"))

    grads, masks = spread(grad, "grp", groups // 2)
    norm_scale = float(rows_here * groups * domains) ** (-0.5)
    norm_scale = float(rows_here * groups * domains) ** (-0.5)
    kept_shares, *shares = call(
        functools.partial(weight_slice, groups, masks),
        [shape((2, share, hidden), F32)] + [shape((2, share, hidden), BF16)] * peers,
        [SMEM] + [VMEM] * (2 * groups),
        [pltpu.VMEM((domains, share, hidden), F32)],
        flops=2 * part_rows * narrow * hidden,
        nbytes=part_rows * (narrow + hidden) * 2,
        name="weight_slice",
    )(ids, *aggs, *grads)
    tab_after, _ = lax.optimization_barrier((tab, shares))
    shares = exchange([None] + shares, "dom")[1:]
    own, bias_here, kept, *terms = call(
        functools.partial(back_halo, masks, slots, at),
        [
            shape((blocks, tile, wide), BF16),
            shape((1, wide), F32),
            shape((slots * tile, wide), BF16),
        ]
        + [shape((2 * slots * tile + EXTRA, wide), BF16)] * peers,
        [SMEM, VMEM] + [VMEM] * len(masks),
        flops=2 * domains * slots * tile * tile * wide,
        nbytes=(domains * slots + blocks) * tile * wide * 2,
        name="back_halo",
    )(tab_after, bank_t, *grads)
    shares, _ = lax.optimization_barrier((shares, terms))
    terms = exchange([None] + terms, "dom")[1:]
    here = call(
        sum_half,
        shape((2, share, hidden), BF16),
        [VMEM] * half,
        nbytes=2 * half * share * hidden * 2,
        name="sum_half",
    )(kept_shares, *shares)
    there = swap(here, "dom", half)
    terms, there = lax.optimization_barrier((terms, there))
    crossing = call(
        functools.partial(sum_mirror, slots, at),
        shape((offers * tile + EXTRA, wide), BF16),
        [SMEM] + [VMEM] * (2 + peers),
        [pltpu.VMEM((offers, tile, wide), F32)],
        nbytes=4 * domains * slots * tile * wide,
        name="sum_mirror",
    )(tab, bias_here, kept, *terms)
    returned = swap(crossing, "dom", half)
    there, _ = lax.optimization_barrier((there, crossing))
    summed = call(
        functools.partial(sum_both, norm_scale),
        shape((2, share, hidden), BF16),
        [VMEM, VMEM],
        nbytes=6 * share * hidden * 2,
        name="sum_both",
    )(here, there)
    own, _ = lax.optimization_barrier((own, summed))
    back = call(
        functools.partial(back_local, per_row, at),
        shape((blocks, tile, wide), F32),
        [SMEM, VMEM, VMEM],
        flops=2 * blocks * per_row * tile * tile * wide,
        nbytes=blocks * tile * wide * 6,
        name="back_local",
    )(tab, bank_t, own)
    gathered = exchange([summed] * half, "dom")
    gathered, back, returned = lax.optimization_barrier((gathered, back, returned))
    joined = call(
        join_shares,
        shape((domains, share, hidden), BF16),
        [SMEM] + [VMEM] * half,
        nbytes=4 * narrow * hidden,
        name="join_shares",
    )(ids, *gathered).reshape(narrow, hidden)

    hid = call(
        functools.partial(finish_nodes, half, slots, norm_scale, at),
        [shape((rows_here + EXTRA, wide), BF16)] * groups,
        [SMEM, VMEM, VMEM, VMEM] + [VMEM] * peers,
        [pltpu.VMEM((blocks, tile, wide), F32)],
        nbytes=domains * slots * tile * wide * 2 + blocks * tile * wide * 6,
        name="finish_nodes",
    )(tab, back, bias_here, returned, *terms)
    hid = exchange(hid, "grp")
    count = groups // 2
    placing = dict(
        out_shape=shape((embed, hidden), F32),
        scratch=[pltpu.VMEM((count, narrow, hidden), F32), pltpu.SemaphoreType.DMA((count, COPIES))],
        nbytes=embed * hidden * 3,
        name="place_weight",
        out_specs=pl.BlockSpec(memory_space=pl.ANY),
    )
    across = swap(joined, "grp", count)
    parts, masks = spread(joined, "grp", count // 2)
    grad_weight = call(
        functools.partial(place_weight, masks),
        specs=[SMEM] + [VMEM] * count,
        **placing,
    )(ids, *parts)
    across, hid, grad_weight = lax.optimization_barrier((across, hid, grad_weight))
    parts, masks = spread(across, "grp", count // 2)
    grad_nodes, grad_bias = call(
        functools.partial(node_grads, groups),
        [shape((rows_here, embed), BF16), shape((1, hidden), F32)],
        [SMEM, VMEM] + [VMEM] * groups,
        [pltpu.VMEM((groups, rows_here + EXTRA, wide), BF16)],
        flops=2 * rows_here * embed * hidden,
        nbytes=embed * hidden * 2 + rows_here * (embed + hidden) * 2,
        name="node_grads",
    )(ids, weight, *hid)
    grad_weight = call(
        functools.partial(place_weight, [mask + count for mask in masks]),
        specs=[SMEM] + [VMEM] * count + [pl.BlockSpec(memory_space=pl.ANY)],
        aliases={count + 1: 0},
        **placing,
    )(ids, *parts, grad_weight)
    return (activations, grad_nodes, grad_weight, grad_bias.reshape(hidden))


def solution(mesh):
    in_specs = (
        P(("dom", "grp"), None),
        P(),
        P(),
        P(("dom", "grp"), None),
        P(),
        P("dom", None, None),
        P("dom", None, None),
        P("dom", None),
        P(),
        P("dom", None, None),
        P("dom", None, None),
    )
    out_specs = (P(("dom", "grp"), None), P(("dom", "grp"), None), P(), P())
    return jax.shard_map(
        per_device, mesh=mesh, in_specs=in_specs, out_specs=out_specs, check_vma=False
    )
```

```python
import functools

import jax
import jax.numpy as jnp
from jax import lax
from jax.experimental import pallas as pl
from jax.experimental.pallas import tpu as pltpu
from jax.sharding import PartitionSpec as P

VMEM = pl.BlockSpec(memory_space=pltpu.VMEM)
SMEM = pl.BlockSpec(memory_space=pltpu.SMEM)
EXTRA = 16
COPIES = 4
F32 = jnp.float32
BF16 = jnp.bfloat16


def call(
    body, out_shape, specs, scratch=(), flops=0, nbytes=0, name=None, out_specs=None, aliases=(), mib=16
):
    return pl.pallas_call(
        body,
        out_shape=out_shape,
        in_specs=specs,
        out_specs=jax.tree.map(lambda _: VMEM, out_shape) if out_specs is None else out_specs,
        scratch_shapes=list(scratch),
        input_output_aliases=dict(aliases),
        compiler_params=pltpu.CompilerParams(vmem_limit_bytes=mib * 1024 * 1024),
        cost_estimate=pl.CostEstimate(flops=flops, bytes_accessed=nbytes, transcendentals=0),
        name=name,
    )


def shape(dims, kind):
    return jax.ShapeDtypeStruct(tuple(dims), kind)


def dot(a, b):
    return jnp.dot(a, b, preferred_element_type=F32)


def bias_rows(total):
    high = total.astype(BF16).astype(F32)
    rest = jnp.zeros((EXTRA - 2, total.shape[1]), F32)
    return jnp.concatenate([high, total - high, rest], axis=0).astype(BF16)


def aligned(start, step):
    return pl.ds(pl.multiple_of(start * step, step), step)


def swap(value, axis, mask):
    return lax.ppermute(value, axis, [(i, i ^ mask) for i in range(lax.axis_size(axis))])


def exchange(parts, axis):
    return list(parts[:1]) + [swap(part, axis, m) for m, part in enumerate(parts[1:], 1)]


def spread(value, axis, bit):
    parts, masks = [value], [0]
    while bit:
        parts = parts + [swap(part, axis, bit) for part in parts]
        masks = masks + [mask ^ bit for mask in masks]
        bit //= 2
    return parts, masks


def split_features(ids, feats, *refs):
    outs, sems = refs[:-1], refs[-1]
    group = ids[1]
    narrow = outs[0].shape[1]
    copies = [
        pltpu.make_async_copy(
            feats.at[:, aligned(jnp.bitwise_xor(group, m), narrow)], out, sems.at[m]
        )
        for m, out in enumerate(outs)
    ]
    for copy in copies:
        copy.start()
    for copy in copies:
        copy.wait()


def pick_blocks(groups, slots, at, tab, *refs):
    parts, (x, offered, *outs) = refs[:groups], refs[groups:]
    domain, group = tab[at["me"]], tab[at["me"] + 1]
    tile = x.shape[1]
    per = x.shape[0] // groups
    for m, part in enumerate(parts):
        owner = jnp.bitwise_xor(group, m)
        for j in range(per):
            x[owner * per + j] = part[j * tile : (j + 1) * tile]
    for j in range(offered.shape[0]):
        offered[j] = x[tab[at["pub"] + j]]
    for m, out in enumerate(outs, 1):
        reader = jnp.bitwise_xor(domain, m)
        for s in range(slots):
            entry = jnp.maximum(tab[at["out"] + reader * slots + s], 0)
            out[s * tile : (s + 1) * tile] = x[tab[at["pub"] + entry]]


def pick_relayed(slots, at, tab, offered, *outs):
    tile = offered.shape[1]
    for m, out in enumerate(outs, 1):
        reader = jnp.bitwise_xor(tab[at["me"]], m)
        for s in range(slots):
            entry = jnp.maximum(tab[at["out2"] + reader * slots + s], 0)
            out[s * tile : (s + 1) * tile] = offered[entry]


def local_sum(per_row, at, tab, bank, x, out):
    pair = 2 if per_row % 2 == 0 else 1

    @pl.loop(0, out.shape[0])
    def _(r):
        acc = jnp.zeros(out.shape[1:], F32)
        for k in range(0, per_row, pair):
            spots = [r * per_row + k + j for j in range(pair)]
            left = jnp.concatenate([bank[tab[at["banks"] + a]] for a in spots], axis=1)
            right = jnp.concatenate([x[tab[at["cols"] + a]] for a in spots], axis=0)
            acc += dot(left, right)
        out[r] = acc


def halo_adder(slots, at, tab, bank, acc):
    def add(source, get):
        for s in range(slots):
            i = source * slots + s
            entry = tab[at["in"] + i]

            @pl.when(entry >= 0)
            def _(i=i, s=s, entry=entry):
                acc[tab[at["hrows"] + i]] += dot(bank[tab[at["hbanks"] + i]], get(s, entry))

    return add


def add_near(slots, at, tab, bank, local, mirrored, *refs):
    near, acc = refs[:-1], refs[-1]
    domain = tab[at["me"]]
    tile = local.shape[1]
    acc[...] = local[...]
    add = halo_adder(slots, at, tab, bank, acc)
    for m, block in enumerate(near, 1):
        add(jnp.bitwise_xor(domain, m), lambda s, _, block=block: block[s * tile : (s + 1) * tile])
    mirror = jnp.bitwise_xor(domain, len(near) + 1)
    add(mirror, lambda _, entry: mirrored[jnp.maximum(entry, 0)])


def add_far(half, groups, slots, at, tab, bank, local, *refs):
    far, outs, acc = refs[: half - 1], refs[half - 1 : -1], refs[-1]
    domain, group = tab[at["me"]], tab[at["me"] + 1]
    tile = local.shape[1]
    per = local.shape[0] // groups
    acc[...] = local[...]
    add = halo_adder(slots, at, tab, bank, acc)
    for m, block in enumerate(far, half + 1):
        add(jnp.bitwise_xor(domain, m), lambda s, _, block=block: block[s * tile : (s + 1) * tile])
    for m, out in enumerate(outs):
        owner = jnp.bitwise_xor(group, m)
        for j in range(per):
            out[j * tile : (j + 1) * tile] = acc[owner * per + j].astype(BF16)


def dense(groups, ids, weight, bias, cot, *refs):
    parts, (act, grad) = refs[:groups], refs[groups:]
    group = ids[1]
    narrow = parts[0].shape[1]
    wide = cot.shape[1] // groups
    left = jnp.concatenate([part[...] for part in parts], axis=1)
    spots = [aligned(jnp.bitwise_xor(group, m), narrow) for m in range(groups)]
    pre = dot(left, jnp.concatenate([weight[spot] for spot in spots], axis=0)) + bias[...]
    act[...] = jnp.maximum(pre, 0.0).astype(BF16)
    masked = jnp.where(pre > 0, cot[...].astype(F32), 0.0).astype(BF16)
    for s in range(groups):
        grad[s] = masked[:, s * wide : (s + 1) * wide]


def back_halo(masks, slots, at, tab, bank_t, *refs):
    parts, (own, mine, kept, *terms) = refs[: len(masks)], refs[len(masks) :]
    domain, group = tab[at["me"]], tab[at["me"] + 1]
    tile = bank_t.shape[1]
    per = parts[0].shape[1] // tile
    half = len(terms) + 1
    total = jnp.zeros((1, own.shape[2]), F32)
    for mask, part in zip(masks, parts):
        owner = jnp.bitwise_xor(group, mask)
        piece = part[group]
        total += jnp.sum(piece.astype(F32), axis=0, keepdims=True)
        for j in range(per):
            own[owner * per + j] = piece[j * tile : (j + 1) * tile]
    mine[...] = total
    tail = bias_rows(total)

    def put(out, place, source):
        for s in range(slots):
            i = source * slots + s
            live = (tab[at["in"] + i] >= 0).astype(F32)
            value = dot(bank_t[tab[at["hbanks"] + i]], own[tab[at["hrows"] + i]]) * live
            spot = (place * slots + s) * tile
            out[spot : spot + tile] = value.astype(BF16)

    for m, term in enumerate(terms, 1):
        peer = jnp.bitwise_xor(domain, m)
        put(term, 0, peer)
        put(term, 1, jnp.bitwise_xor(peer, half))
        term[2 * slots * tile :] = tail
    put(kept, 0, jnp.bitwise_xor(domain, half))


def sum_mirror(slots, at, tab, mine, kept, *refs):
    recv, out, acc = refs[:-2], refs[-2], refs[-1]
    domain = tab[at["me"]]
    offered, tile = acc.shape[:2]
    acc[...] = jnp.zeros_like(acc)
    total = mine[...]
    for m, block in enumerate((kept,) + recv):
        reader = jnp.bitwise_xor(domain, m)
        for s in range(slots):
            entry = tab[at["out2"] + reader * slots + s]
            spot = (s + (slots if m else 0)) * tile

            @pl.when(entry >= 0)
            def _(entry=entry, spot=spot, block=block):
                acc[jnp.maximum(entry, 0)] += block[spot : spot + tile].astype(F32)

        if m:
            tail = block[2 * slots * tile :].astype(F32)
            total += tail[0:1] + tail[1:2]
    for j in range(offered):
        out[j * tile : (j + 1) * tile] = acc[j].astype(BF16)
    out[offered * tile :] = bias_rows(total)


def weight_slice(groups, masks, ids, *refs):
    aggs, parts = refs[:groups], refs[groups : 2 * groups]
    kept, *outs = refs[2 * groups : -1]
    total = refs[-1]
    domain = ids[0]
    half = len(outs) + 1
    left = jnp.concatenate([aggs[mask][...] for mask in masks], axis=0)
    pieces = [jnp.concatenate([part[s] for part in parts], axis=0) for s in range(groups)]
    right = jnp.concatenate(pieces, axis=1)
    whole = lax.dot_general(left, right, (((0,), (0,)), ((), ())), preferred_element_type=F32)
    rows = total.shape[1]
    for d in range(total.shape[0]):
        total[d] = whole[d * rows : (d + 1) * rows]
    for m, out in enumerate([kept] + outs):
        peer = jnp.bitwise_xor(domain, m)
        out[0] = total[peer].astype(out.dtype)
        out[1] = total[jnp.bitwise_xor(peer, half)].astype(out.dtype)


def sum_half(kept, *refs):
    recv, out = refs[:-1], refs[-1]
    for i in range(2):
        total = kept[i]
        for block in recv:
            total += block[i].astype(F32)
        out[i] = total.astype(BF16)


def sum_both(scale, here, there, out):
    for i in range(2):
        out[i] = ((here[i].astype(F32) + there[1 - i].astype(F32)) * scale).astype(BF16)


def join_shares(ids, *refs):
    parts, out = refs[:-1], refs[-1]
    for m, part in enumerate(parts):
        owner = jnp.bitwise_xor(ids[0], m)
        out[owner] = part[0]
        out[jnp.bitwise_xor(owner, len(parts))] = part[1]


def back_local(per_row, at, tab, bank_t, own, out):
    out[...] = jnp.zeros_like(out)

    @pl.loop(0, own.shape[0])
    def _(r):
        right = own[r]
        for k in range(per_row):
            spot = r * per_row + k
            out[tab[at["cols"] + spot]] += dot(bank_t[tab[at["banks"] + spot]], right)


def finish_nodes(half, slots, scale, at, tab, local, mine, mirrored, *refs):
    recv, outs, acc = refs[: half - 1], refs[half - 1 : -1], refs[-1]
    groups = len(outs)
    domain, group = tab[at["me"]], tab[at["me"] + 1]
    tile = local.shape[1]
    per = local.shape[0] // groups
    offered = (mirrored.shape[0] - EXTRA) // tile
    acc[...] = local[...]
    tail = mirrored[offered * tile :].astype(F32)
    for j in range(offered):
        acc[tab[at["pub"] + j]] += mirrored[j * tile : (j + 1) * tile].astype(F32)
    for m, block in enumerate(recv, 1):
        tail += block[2 * slots * tile :].astype(F32)
        reader = jnp.bitwise_xor(domain, m)
        for s in range(slots):
            entry = tab[at["out"] + reader * slots + s]

            @pl.when(entry >= 0)
            def _(s=s, entry=entry, block=block):
                spot = tab[at["pub"] + jnp.maximum(entry, 0)]
                acc[spot] += block[s * tile : (s + 1) * tile].astype(F32)

    rows = bias_rows((mine[...] + tail[0:1] + tail[1:2]) * scale)
    for m, out in enumerate(outs):
        owner = jnp.bitwise_xor(group, m)
        for j in range(per):
            out[j * tile : (j + 1) * tile] = acc[owner * per + j].astype(BF16)
        out[per * tile :] = rows


def node_grads(groups, ids, weight, *refs):
    parts, (out, bias_out, hid) = refs[:groups], refs[groups:]
    group = ids[1]
    rows = out.shape[0]
    for m, part in enumerate(parts):
        hid[jnp.bitwise_xor(group, m)] = part[...]
    left = jnp.concatenate([hid[s, :rows] for s in range(groups)], axis=1)
    out[...] = lax.dot_general(
        left, weight[...], (((1,), (1,)), ((), ())), preferred_element_type=F32
    ).astype(BF16)
    tail = jnp.concatenate([hid[s, rows:] for s in range(groups)], axis=1).astype(F32)
    bias_out[...] = tail[0:1] + tail[1:2]


def place_weight(masks, ids, *refs):
    parts, (out, wide, sems) = refs[: len(masks)], refs[-3:]
    group = ids[1]
    rows = parts[0].shape[0]
    copies = []
    step = rows // COPIES
    for i, (mask, part) in enumerate(zip(masks, parts)):
        for j in range(COPIES):
            wide[i, j * step : (j + 1) * step] = part[j * step : (j + 1) * step].astype(F32)
            spot = out.at[aligned(jnp.bitwise_xor(group, mask) * COPIES + j, step)]
            piece = wide.at[i, pl.ds(j * step, step)]
            copies.append(pltpu.make_async_copy(piece, spot, sems.at[i, j]))
            copies[-1].start()
    for copy in copies:
        copy.wait()


def per_device(
    node_feats,
    weight,
    bias,
    cotangent,
    tile_bank,
    local_cols,
    local_banks,
    published,
    send_table,
    halo_rows,
    halo_banks,
):
    domains = lax.axis_size("dom")
    groups = lax.axis_size("grp")
    domain_index = lax.axis_index("dom")
    rows_here, embed = node_feats.shape
    hidden = weight.shape[1]
    tile = tile_bank.shape[1]
    slots = send_table.shape[2]
    per_row = local_cols.shape[2]
    part_rows = rows_here * groups
    blocks = part_rows // tile
    narrow = embed // groups
    wide = hidden // groups
    share = narrow // domains
    half = domains // 2
    peers = half - 1
    offers = published.shape[1]

    ids = jnp.stack([domain_index, lax.axis_index("grp")]).astype(jnp.int32)
    tables = {
        "cols": local_cols[0],
        "banks": local_banks[0],
        "pub": published[0],
        "out": lax.dynamic_index_in_dim(send_table, domain_index, 0, keepdims=False),
        "out2": lax.dynamic_index_in_dim(send_table, domain_index ^ half, 0, keepdims=False),
        "in": lax.dynamic_index_in_dim(send_table, domain_index, 1, keepdims=False),
        "hrows": halo_rows[0],
        "hbanks": halo_banks[0],
        "me": ids,
    }
    at, place = {}, 0
    for name, table in tables.items():
        at[name] = place
        place += table.size
    tab = jnp.concatenate([table.reshape(-1) for table in tables.values()])
    bank_t = jnp.swapaxes(tile_bank, 1, 2)

    feats = call(
        split_features,
        [shape((rows_here, narrow), BF16)] * groups,
        [SMEM, pl.BlockSpec(memory_space=pl.ANY)],
        [pltpu.SemaphoreType.DMA((groups,))],
        nbytes=4 * rows_here * embed,
        name="split_features",
    )(ids, node_feats)
    feats = exchange(feats, "grp")
    x, offered, *picked = call(
        functools.partial(pick_blocks, groups, slots, at),
        [shape((blocks, tile, narrow), BF16), shape((offers, tile, narrow), BF16)]
        + [shape((slots * tile, narrow), BF16)] * peers,
        [SMEM] + [VMEM] * groups,
        nbytes=4 * (peers * slots + blocks + offers) * tile * narrow,
        name="pick_blocks",
    )(tab, *feats)
    mirrored = swap(offered, "dom", half)
    near = exchange([None] + picked, "dom")[1:]
    local = call(
        functools.partial(local_sum, per_row, at),
        shape((blocks, tile, narrow), F32),
        [SMEM, VMEM, VMEM],
        flops=2 * blocks * per_row * tile * tile * narrow,
        nbytes=blocks * tile * narrow * 6,
        name="local_sum",
    )(tab, tile_bank, x)
    mirrored, local = lax.optimization_barrier((mirrored, local))
    relayed = call(
        functools.partial(pick_relayed, slots, at),
        [shape((slots * tile, narrow), BF16)] * peers,
        [SMEM, VMEM],
        nbytes=4 * peers * slots * tile * narrow,
        name="pick_relayed",
    )(tab, mirrored)
    far = exchange([None, *relayed], "dom")[1:]
    local = call(
        functools.partial(add_near, slots, at),
        shape((blocks, tile, narrow), F32),
        [SMEM, VMEM, VMEM, VMEM] + [VMEM] * peers,
        flops=2 * half * slots * tile * tile * narrow,
        nbytes=blocks * tile * narrow * 8,
        name="add_near",
    )(tab, tile_bank, local, mirrored, *near)
    far, local = lax.optimization_barrier((far, local))
    aggs = call(
        functools.partial(add_far, half, groups, slots, at),
        [shape((rows_here, narrow), BF16)] * groups,
        [SMEM, VMEM, VMEM] + [VMEM] * peers,
        [pltpu.VMEM((blocks, tile, narrow), F32)],
        flops=2 * half * slots * tile * tile * narrow,
        nbytes=blocks * tile * narrow * 8,
        name="add_far",
    )(tab, tile_bank, local, *far)
    activations, grad = call(
        functools.partial(dense, groups),
        [shape((rows_here, hidden), BF16), shape((groups, rows_here, wide), BF16)],
        [SMEM] + [VMEM] * (3 + groups),
        flops=2 * rows_here * embed * hidden,
        nbytes=embed * hidden * 2 + rows_here * (embed + 3 * hidden) * 2,
        name="dense",
    )(ids, weight, bias.reshape(1, hidden), cotangent, *exchange(aggs, "grp"))

    grads, masks = spread(grad, "grp", groups // 2)
    norm_scale = float(rows_here * groups * domains) ** (-0.5)
    norm_scale = float(rows_here * groups * domains) ** (-0.5)
    kept_shares, *shares = call(
        functools.partial(weight_slice, groups, masks),
        [shape((2, share, hidden), F32)] + [shape((2, share, hidden), BF16)] * peers,
        [SMEM] + [VMEM] * (2 * groups),
        [pltpu.VMEM((domains, share, hidden), F32)],
        flops=2 * part_rows * narrow * hidden,
        nbytes=part_rows * (narrow + hidden) * 2,
        name="weight_slice",
    )(ids, *aggs, *grads)
    tab_after, _ = lax.optimization_barrier((tab, shares))
    shares = exchange([None] + shares, "dom")[1:]
    own, bias_here, kept, *terms = call(
        functools.partial(back_halo, masks, slots, at),
        [
            shape((blocks, tile, wide), BF16),
            shape((1, wide), F32),
            shape((slots * tile, wide), BF16),
        ]
        + [shape((2 * slots * tile + EXTRA, wide), BF16)] * peers,
        [SMEM, VMEM] + [VMEM] * len(masks),
        flops=2 * domains * slots * tile * tile * wide,
        nbytes=(domains * slots + blocks) * tile * wide * 2,
        name="back_halo",
    )(tab_after, bank_t, *grads)
    shares, _ = lax.optimization_barrier((shares, terms))
    here = call(
        sum_half,
        shape((2, share, hidden), BF16),
        [VMEM] * half,
        nbytes=2 * half * share * hidden * 2,
        name="sum_half",
    )(kept_shares, *shares)
    there = swap(here, "dom", half)
    terms, _ = lax.optimization_barrier((terms, here))
    terms = exchange([None] + terms, "dom")[1:]
    there, terms[0] = lax.optimization_barrier((there, terms[0]))
    summed = call(
        functools.partial(sum_both, norm_scale),
        shape((2, share, hidden), BF16),
        [VMEM, VMEM],
        nbytes=6 * share * hidden * 2,
        name="sum_both",
    )(here, there)
    terms, _ = lax.optimization_barrier((terms, summed))
    crossing = call(
        functools.partial(sum_mirror, slots, at),
        shape((offers * tile + EXTRA, wide), BF16),
        [SMEM] + [VMEM] * (2 + peers),
        [pltpu.VMEM((offers, tile, wide), F32)],
        nbytes=4 * domains * slots * tile * wide,
        name="sum_mirror",
    )(tab, bias_here, kept, *terms)
    returned = swap(crossing, "dom", half)
    gathered = exchange([summed] * half, "dom")
    gathered, _ = lax.optimization_barrier((gathered, crossing))
    joined = call(
        join_shares,
        shape((domains, share, hidden), BF16),
        [SMEM] + [VMEM] * half,
        nbytes=4 * narrow * hidden,
        name="join_shares",
    )(ids, *gathered).reshape(narrow, hidden)

    own, _ = lax.optimization_barrier((own, joined))
    back = call(
        functools.partial(back_local, per_row, at),
        shape((blocks, tile, wide), F32),
        [SMEM, VMEM, VMEM],
        flops=2 * blocks * per_row * tile * tile * wide,
        nbytes=blocks * tile * wide * 6,
        name="back_local",
    )(tab, bank_t, own)
    hid = call(
        functools.partial(finish_nodes, half, slots, norm_scale, at),
        [shape((rows_here + EXTRA, wide), BF16)] * groups,
        [SMEM, VMEM, VMEM, VMEM] + [VMEM] * peers,
        [pltpu.VMEM((blocks, tile, wide), F32)],
        nbytes=domains * slots * tile * wide * 2 + blocks * tile * wide * 6,
        name="finish_nodes",
    )(tab, back, bias_here, returned, *terms)
    hid = exchange(hid, "grp")
    count = groups // 2
    placing = dict(
        out_shape=shape((embed, hidden), F32),
        scratch=[pltpu.VMEM((count, narrow, hidden), F32), pltpu.SemaphoreType.DMA((count, COPIES))],
        nbytes=embed * hidden * 3,
        name="place_weight",
        out_specs=pl.BlockSpec(memory_space=pl.ANY),
    )
    across = swap(joined, "grp", count)
    parts, masks = spread(joined, "grp", count // 2)
    grad_weight = call(
        functools.partial(place_weight, masks),
        specs=[SMEM] + [VMEM] * count,
        **placing,
    )(ids, *parts)
    across, hid, grad_weight = lax.optimization_barrier((across, hid, grad_weight))
    parts, masks = spread(across, "grp", count // 2)
    grad_nodes, grad_bias = call(
        functools.partial(node_grads, groups),
        [shape((rows_here, embed), BF16), shape((1, hidden), F32)],
        [SMEM, VMEM] + [VMEM] * groups,
        [pltpu.VMEM((groups, rows_here + EXTRA, wide), BF16)],
        flops=2 * rows_here * embed * hidden,
        nbytes=embed * hidden * 2 + rows_here * (embed + hidden) * 2,
        name="node_grads",
    )(ids, weight, *hid)
    grad_weight = call(
        functools.partial(place_weight, [mask + count for mask in masks]),
        specs=[SMEM] + [VMEM] * count + [pl.BlockSpec(memory_space=pl.ANY)],
        aliases={count + 1: 0},
        **placing,
    )(ids, *parts, grad_weight)
    return (activations, grad_nodes, grad_weight, grad_bias.reshape(hidden))


def solution(mesh):
    in_specs = (
        P(("dom", "grp"), None),
        P(),
        P(),
        P(("dom", "grp"), None),
        P(),
        P("dom", None, None),
        P("dom", None, None),
        P("dom", None),
        P(),
        P("dom", None, None),
        P("dom", None, None),
    )
    out_specs = (P(("dom", "grp"), None), P(("dom", "grp"), None), P(), P())
    return jax.shard_map(
        per_device, mesh=mesh, in_specs=in_specs, out_specs=out_specs, check_vma=False
    )
```

```python
import functools

import jax
import jax.numpy as jnp
from jax import lax
from jax.experimental import pallas as pl
from jax.experimental.pallas import tpu as pltpu
from jax.sharding import PartitionSpec as P

VMEM = pl.BlockSpec(memory_space=pltpu.VMEM)
SMEM = pl.BlockSpec(memory_space=pltpu.SMEM)
EXTRA = 16
COPIES = 4
F32 = jnp.float32
BF16 = jnp.bfloat16


def call(
    body, out_shape, specs, scratch=(), flops=0, nbytes=0, name=None, out_specs=None, aliases=(), mib=16
):
    return pl.pallas_call(
        body,
        out_shape=out_shape,
        in_specs=specs,
        out_specs=jax.tree.map(lambda _: VMEM, out_shape) if out_specs is None else out_specs,
        scratch_shapes=list(scratch),
        input_output_aliases=dict(aliases),
        compiler_params=pltpu.CompilerParams(vmem_limit_bytes=mib * 1024 * 1024),
        cost_estimate=pl.CostEstimate(flops=flops, bytes_accessed=nbytes, transcendentals=0),
        name=name,
    )


def shape(dims, kind):
    return jax.ShapeDtypeStruct(tuple(dims), kind)


def dot(a, b):
    return jnp.dot(a, b, preferred_element_type=F32)


def bias_rows(total):
    high = total.astype(BF16).astype(F32)
    rest = jnp.zeros((EXTRA - 2, total.shape[1]), F32)
    return jnp.concatenate([high, total - high, rest], axis=0).astype(BF16)


def aligned(start, step):
    return pl.ds(pl.multiple_of(start * step, step), step)


def swap(value, axis, mask):
    return lax.ppermute(value, axis, [(i, i ^ mask) for i in range(lax.axis_size(axis))])


def exchange(parts, axis):
    return list(parts[:1]) + [swap(part, axis, m) for m, part in enumerate(parts[1:], 1)]


def spread(value, axis, bit):
    parts, masks = [value], [0]
    while bit:
        parts = parts + [swap(part, axis, bit) for part in parts]
        masks = masks + [mask ^ bit for mask in masks]
        bit //= 2
    return parts, masks


def split_features(ids, feats, *refs):
    outs, sems = refs[:-1], refs[-1]
    group = ids[1]
    narrow = outs[0].shape[1]
    copies = [
        pltpu.make_async_copy(
            feats.at[:, aligned(jnp.bitwise_xor(group, m), narrow)], out, sems.at[m]
        )
        for m, out in enumerate(outs)
    ]
    for copy in copies:
        copy.start()
    for copy in copies:
        copy.wait()


def pick_blocks(groups, slots, at, tab, *refs):
    parts, (x, offered, *outs) = refs[:groups], refs[groups:]
    domain, group = tab[at["me"]], tab[at["me"] + 1]
    tile = x.shape[1]
    per = x.shape[0] // groups
    for m, part in enumerate(parts):
        owner = jnp.bitwise_xor(group, m)
        for j in range(per):
            x[owner * per + j] = part[j * tile : (j + 1) * tile]
    for j in range(offered.shape[0]):
        offered[j] = x[tab[at["pub"] + j]]
    for m, out in enumerate(outs, 1):
        reader = jnp.bitwise_xor(domain, m)
        for s in range(slots):
            entry = jnp.maximum(tab[at["out"] + reader * slots + s], 0)
            out[s * tile : (s + 1) * tile] = x[tab[at["pub"] + entry]]


def pick_relayed(slots, at, tab, offered, *outs):
    tile = offered.shape[1]
    for m, out in enumerate(outs, 1):
        reader = jnp.bitwise_xor(tab[at["me"]], m)
        for s in range(slots):
            entry = jnp.maximum(tab[at["out2"] + reader * slots + s], 0)
            out[s * tile : (s + 1) * tile] = offered[entry]


def local_sum(per_row, at, tab, bank, x, out):
    pair = 2 if per_row % 2 == 0 else 1

    @pl.loop(0, out.shape[0])
    def _(r):
        acc = jnp.zeros(out.shape[1:], F32)
        for k in range(0, per_row, pair):
            spots = [r * per_row + k + j for j in range(pair)]
            left = jnp.concatenate([bank[tab[at["banks"] + a]] for a in spots], axis=1)
            right = jnp.concatenate([x[tab[at["cols"] + a]] for a in spots], axis=0)
            acc += dot(left, right)
        out[r] = acc


def halo_adder(slots, at, tab, bank, acc):
    def add(source, get):
        for s in range(slots):
            i = source * slots + s
            entry = tab[at["in"] + i]

            @pl.when(entry >= 0)
            def _(i=i, s=s, entry=entry):
                acc[tab[at["hrows"] + i]] += dot(bank[tab[at["hbanks"] + i]], get(s, entry))

    return add


def add_near(slots, at, tab, bank, local, mirrored, *refs):
    near, acc = refs[:-1], refs[-1]
    domain = tab[at["me"]]
    tile = local.shape[1]
    acc[...] = local[...]
    add = halo_adder(slots, at, tab, bank, acc)
    for m, block in enumerate(near, 1):
        add(jnp.bitwise_xor(domain, m), lambda s, _, block=block: block[s * tile : (s + 1) * tile])
    mirror = jnp.bitwise_xor(domain, len(near) + 1)
    add(mirror, lambda _, entry: mirrored[jnp.maximum(entry, 0)])


def add_far(half, groups, slots, at, tab, bank, local, *refs):
    far, outs, acc = refs[: half - 1], refs[half - 1 : -1], refs[-1]
    domain, group = tab[at["me"]], tab[at["me"] + 1]
    tile = local.shape[1]
    per = local.shape[0] // groups
    acc[...] = local[...]
    add = halo_adder(slots, at, tab, bank, acc)
    for m, block in enumerate(far, half + 1):
        add(jnp.bitwise_xor(domain, m), lambda s, _, block=block: block[s * tile : (s + 1) * tile])
    for m, out in enumerate(outs):
        owner = jnp.bitwise_xor(group, m)
        for j in range(per):
            out[j * tile : (j + 1) * tile] = acc[owner * per + j].astype(BF16)


def dense(groups, ids, weight, bias, cot, *refs):
    parts, (act, grad) = refs[:groups], refs[groups:]
    group = ids[1]
    narrow = parts[0].shape[1]
    wide = cot.shape[1] // groups
    left = jnp.concatenate([part[...] for part in parts], axis=1)
    spots = [aligned(jnp.bitwise_xor(group, m), narrow) for m in range(groups)]
    pre = dot(left, jnp.concatenate([weight[spot] for spot in spots], axis=0)) + bias[...]
    act[...] = jnp.maximum(pre, 0.0).astype(BF16)
    masked = jnp.where(pre > 0, cot[...].astype(F32), 0.0).astype(BF16)
    for s in range(groups):
        grad[s] = masked[:, s * wide : (s + 1) * wide]


def back_terms(masks, slots, at, tab, bank_t, *refs):
    groups = len(masks)
    aggs, parts = refs[:groups], refs[groups : 2 * groups]
    own, mine, kept, kept_shares, *terms = refs[2 * groups : -1]
    total = refs[-1]
    domain, group = tab[at["me"]], tab[at["me"] + 1]
    tile = bank_t.shape[1]
    per = parts[0].shape[1] // tile
    half = len(terms) + 1
    share, wide = total.shape[2:]
    step = kept_shares.shape[2]
    base = 2 * slots * tile + EXTRA
    bias = jnp.zeros((1, wide), F32)
    for mask, part in zip(masks, parts):
        owner = jnp.bitwise_xor(group, mask)
        piece = part[group]
        bias += jnp.sum(piece.astype(F32), axis=0, keepdims=True)
        for j in range(per):
            own[owner * per + j] = piece[j * tile : (j + 1) * tile]
    mine[...] = bias
    tail = bias_rows(bias)
    left = jnp.concatenate([aggs[mask][...] for mask in masks], axis=0)
    for s in range(groups):
        right = jnp.concatenate([part[s] for part in parts], axis=0)
        whole = lax.dot_general(left, right, (((0,), (0,)), ((), ())), preferred_element_type=F32)
        for d in range(total.shape[0]):
            total[d, s] = whole[d * share : (d + 1) * share]

    def put(out, place, source):
        for s in range(slots):
            i = source * slots + s
            live = (tab[at["in"] + i] >= 0).astype(F32)
            value = dot(bank_t[tab[at["hbanks"] + i]], own[tab[at["hrows"] + i]]) * live
            spot = (place * slots + s) * tile
            out[spot : spot + tile] = value.astype(BF16)

    put(kept, 0, jnp.bitwise_xor(domain, half))
    for s in range(groups):
        kept_shares[0, s, :share] = total[domain, s]
        kept_shares[1, s, :share] = total[jnp.bitwise_xor(domain, half), s]
    for m, term in enumerate(terms, 1):
        peer = jnp.bitwise_xor(domain, m)
        mirror = jnp.bitwise_xor(peer, half)
        put(term, 0, peer)
        put(term, 1, mirror)
        term[base - EXTRA : base] = tail
        for i, owner in enumerate((peer, mirror)):
            for s in range(groups):
                spot = base + (i * groups + s) * step
                term[spot : spot + share] = total[owner, s].astype(BF16)


def sum_mirror(slots, at, tab, mine, kept, *refs):
    recv, out, acc = refs[:-2], refs[-2], refs[-1]
    domain = tab[at["me"]]
    offered, tile = acc.shape[:2]
    acc[...] = jnp.zeros_like(acc)
    total = mine[...]
    for m, block in enumerate((kept,) + recv):
        reader = jnp.bitwise_xor(domain, m)
        for s in range(slots):
            entry = tab[at["out2"] + reader * slots + s]
            spot = (s + (slots if m else 0)) * tile

            @pl.when(entry >= 0)
            def _(entry=entry, spot=spot, block=block):
                acc[jnp.maximum(entry, 0)] += block[spot : spot + tile].astype(F32)

        if m:
            tail = block[2 * slots * tile : 2 * slots * tile + EXTRA].astype(F32)
            total += tail[0:1] + tail[1:2]
    for j in range(offered):
        out[j * tile : (j + 1) * tile] = acc[j].astype(BF16)
    out[offered * tile :] = bias_rows(total)


def sum_half(base, kept, *refs):
    recv, out = refs[:-1], refs[-1]
    groups, step = out.shape[1:3]
    for i in range(2):
        for s in range(groups):
            spot = base + (i * groups + s) * step
            total = kept[i, s]
            for block in recv:
                total += block[spot : spot + step].astype(F32)
            out[i, s] = total.astype(BF16)


def sum_both(scale, here, there, out):
    for i in range(2):
        out[i] = ((here[i].astype(F32) + there[1 - i].astype(F32)) * scale).astype(BF16)


def join_shares(ids, *refs):
    parts, out = refs[:-1], refs[-1]
    share = out.shape[1]
    for m, part in enumerate(parts):
        for i in range(2):
            owner = jnp.bitwise_xor(ids[0], m + i * len(parts))
            pieces = [part[i, s, :share] for s in range(part.shape[1])]
            out[owner] = jnp.concatenate(pieces, axis=1)


def back_local(per_row, at, tab, bank_t, own, out):
    out[...] = jnp.zeros_like(out)

    @pl.loop(0, own.shape[0])
    def _(r):
        right = own[r]
        for k in range(per_row):
            spot = r * per_row + k
            out[tab[at["cols"] + spot]] += dot(bank_t[tab[at["banks"] + spot]], right)


def finish_nodes(half, slots, scale, at, tab, local, mine, mirrored, *refs):
    recv, outs, acc = refs[: half - 1], refs[half - 1 : -1], refs[-1]
    groups = len(outs)
    domain, group = tab[at["me"]], tab[at["me"] + 1]
    tile = local.shape[1]
    per = local.shape[0] // groups
    offered = (mirrored.shape[0] - EXTRA) // tile
    acc[...] = local[...]
    tail = mirrored[offered * tile :].astype(F32)
    for j in range(offered):
        acc[tab[at["pub"] + j]] += mirrored[j * tile : (j + 1) * tile].astype(F32)
    for m, block in enumerate(recv, 1):
        tail += block[2 * slots * tile : 2 * slots * tile + EXTRA].astype(F32)
        reader = jnp.bitwise_xor(domain, m)
        for s in range(slots):
            entry = tab[at["out"] + reader * slots + s]

            @pl.when(entry >= 0)
            def _(s=s, entry=entry, block=block):
                spot = tab[at["pub"] + jnp.maximum(entry, 0)]
                acc[spot] += block[s * tile : (s + 1) * tile].astype(F32)

    rows = bias_rows((mine[...] + tail[0:1] + tail[1:2]) * scale)
    for m, out in enumerate(outs):
        owner = jnp.bitwise_xor(group, m)
        for j in range(per):
            out[j * tile : (j + 1) * tile] = acc[owner * per + j].astype(BF16)
        out[per * tile :] = rows


def node_grads(groups, ids, weight, *refs):
    parts, (out, bias_out, hid) = refs[:groups], refs[groups:]
    group = ids[1]
    rows = out.shape[0]
    for m, part in enumerate(parts):
        hid[jnp.bitwise_xor(group, m)] = part[...]
    left = jnp.concatenate([hid[s, :rows] for s in range(groups)], axis=1)
    out[...] = lax.dot_general(
        left, weight[...], (((1,), (1,)), ((), ())), preferred_element_type=F32
    ).astype(BF16)
    tail = jnp.concatenate([hid[s, rows:] for s in range(groups)], axis=1).astype(F32)
    bias_out[...] = tail[0:1] + tail[1:2]


def place_weight(masks, ids, *refs):
    parts, (out, wide, sems) = refs[: len(masks)], refs[-3:]
    group = ids[1]
    rows = parts[0].shape[0]
    copies = []
    step = rows // COPIES
    for i, (mask, part) in enumerate(zip(masks, parts)):
        for j in range(COPIES):
            wide[i, j * step : (j + 1) * step] = part[j * step : (j + 1) * step].astype(F32)
            spot = out.at[aligned(jnp.bitwise_xor(group, mask) * COPIES + j, step)]
            piece = wide.at[i, pl.ds(j * step, step)]
            copies.append(pltpu.make_async_copy(piece, spot, sems.at[i, j]))
            copies[-1].start()
    for copy in copies:
        copy.wait()


def per_device(
    node_feats,
    weight,
    bias,
    cotangent,
    tile_bank,
    local_cols,
    local_banks,
    published,
    send_table,
    halo_rows,
    halo_banks,
):
    domains = lax.axis_size("dom")
    groups = lax.axis_size("grp")
    domain_index = lax.axis_index("dom")
    rows_here, embed = node_feats.shape
    hidden = weight.shape[1]
    tile = tile_bank.shape[1]
    slots = send_table.shape[2]
    per_row = local_cols.shape[2]
    part_rows = rows_here * groups
    blocks = part_rows // tile
    narrow = embed // groups
    wide = hidden // groups
    share = narrow // domains
    half = domains // 2
    peers = half - 1
    offers = published.shape[1]

    ids = jnp.stack([domain_index, lax.axis_index("grp")]).astype(jnp.int32)
    tables = {
        "cols": local_cols[0],
        "banks": local_banks[0],
        "pub": published[0],
        "out": lax.dynamic_index_in_dim(send_table, domain_index, 0, keepdims=False),
        "out2": lax.dynamic_index_in_dim(send_table, domain_index ^ half, 0, keepdims=False),
        "in": lax.dynamic_index_in_dim(send_table, domain_index, 1, keepdims=False),
        "hrows": halo_rows[0],
        "hbanks": halo_banks[0],
        "me": ids,
    }
    at, place = {}, 0
    for name, table in tables.items():
        at[name] = place
        place += table.size
    tab = jnp.concatenate([table.reshape(-1) for table in tables.values()])
    bank_t = jnp.swapaxes(tile_bank, 1, 2)

    feats = call(
        split_features,
        [shape((rows_here, narrow), BF16)] * groups,
        [SMEM, pl.BlockSpec(memory_space=pl.ANY)],
        [pltpu.SemaphoreType.DMA((groups,))],
        nbytes=4 * rows_here * embed,
        name="split_features",
    )(ids, node_feats)
    feats = exchange(feats, "grp")
    x, offered, *picked = call(
        functools.partial(pick_blocks, groups, slots, at),
        [shape((blocks, tile, narrow), BF16), shape((offers, tile, narrow), BF16)]
        + [shape((slots * tile, narrow), BF16)] * peers,
        [SMEM] + [VMEM] * groups,
        nbytes=4 * (peers * slots + blocks + offers) * tile * narrow,
        name="pick_blocks",
    )(tab, *feats)
    mirrored = swap(offered, "dom", half)
    near = exchange([None] + picked, "dom")[1:]
    local = call(
        functools.partial(local_sum, per_row, at),
        shape((blocks, tile, narrow), F32),
        [SMEM, VMEM, VMEM],
        flops=2 * blocks * per_row * tile * tile * narrow,
        nbytes=blocks * tile * narrow * 6,
        name="local_sum",
    )(tab, tile_bank, x)
    mirrored, local = lax.optimization_barrier((mirrored, local))
    relayed = call(
        functools.partial(pick_relayed, slots, at),
        [shape((slots * tile, narrow), BF16)] * peers,
        [SMEM, VMEM],
        nbytes=4 * peers * slots * tile * narrow,
        name="pick_relayed",
    )(tab, mirrored)
    far = exchange([None, *relayed], "dom")[1:]
    local = call(
        functools.partial(add_near, slots, at),
        shape((blocks, tile, narrow), F32),
        [SMEM, VMEM, VMEM, VMEM] + [VMEM] * peers,
        flops=2 * half * slots * tile * tile * narrow,
        nbytes=blocks * tile * narrow * 8,
        name="add_near",
    )(tab, tile_bank, local, mirrored, *near)
    far, local = lax.optimization_barrier((far, local))
    aggs = call(
        functools.partial(add_far, half, groups, slots, at),
        [shape((rows_here, narrow), BF16)] * groups,
        [SMEM, VMEM, VMEM] + [VMEM] * peers,
        [pltpu.VMEM((blocks, tile, narrow), F32)],
        flops=2 * half * slots * tile * tile * narrow,
        nbytes=blocks * tile * narrow * 8,
        name="add_far",
    )(tab, tile_bank, local, *far)
    activations, grad = call(
        functools.partial(dense, groups),
        [shape((rows_here, hidden), BF16), shape((groups, rows_here, wide), BF16)],
        [SMEM] + [VMEM] * (3 + groups),
        flops=2 * rows_here * embed * hidden,
        nbytes=embed * hidden * 2 + rows_here * (embed + 3 * hidden) * 2,
        name="dense",
    )(ids, weight, bias.reshape(1, hidden), cotangent, *exchange(aggs, "grp"))

    grads, masks = spread(grad, "grp", groups // 2)
    norm_scale = float(rows_here * groups * domains) ** (-0.5)
    norm_scale = float(rows_here * groups * domains) ** (-0.5)
    base = 2 * slots * tile + EXTRA
    step = -(-share // 16) * 16
    own, bias_here, kept, kept_shares, *terms = call(
        functools.partial(back_terms, masks, slots, at),
        [
            shape((blocks, tile, wide), BF16),
            shape((1, wide), F32),
            shape((slots * tile, wide), BF16),
            shape((2, groups, step, wide), F32),
        ]
        + [shape((base + 2 * groups * step, wide), BF16)] * peers,
        [SMEM, VMEM] + [VMEM] * (2 * groups),
        [pltpu.VMEM((domains, groups, share, wide), F32)],
        flops=2 * domains * slots * tile * tile * wide + 2 * part_rows * narrow * hidden,
        nbytes=(domains * slots + blocks) * tile * wide * 2 + part_rows * (narrow + hidden) * 2,
        name="back_terms",
    )(tab, bank_t, *aggs, *grads)
    terms = exchange([None] + terms, "dom")[1:]
    here = call(
        functools.partial(sum_half, base),
        shape((2, groups, step, wide), BF16),
        [VMEM] * half,
        nbytes=2 * half * share * hidden * 2,
        name="sum_half",
    )(kept_shares, *terms)
    there = swap(here, "dom", half)
    own, _ = lax.optimization_barrier((own, here))
    back = call(
        functools.partial(back_local, per_row, at),
        shape((blocks, tile, wide), F32),
        [SMEM, VMEM, VMEM],
        flops=2 * blocks * per_row * tile * tile * wide,
        nbytes=blocks * tile * wide * 6,
        name="back_local",
    )(tab, bank_t, own)
    there, back = lax.optimization_barrier((there, back))
    summed = call(
        functools.partial(sum_both, norm_scale),
        shape((2, groups, step, wide), BF16),
        [VMEM, VMEM],
        nbytes=6 * share * hidden * 2,
        name="sum_both",
    )(here, there)
    terms, _ = lax.optimization_barrier((terms, summed))
    crossing = call(
        functools.partial(sum_mirror, slots, at),
        shape((offers * tile + EXTRA, wide), BF16),
        [SMEM] + [VMEM] * (2 + peers),
        [pltpu.VMEM((offers, tile, wide), F32)],
        nbytes=4 * domains * slots * tile * wide,
        name="sum_mirror",
    )(tab, bias_here, kept, *terms)
    returned = swap(crossing, "dom", half)
    gathered = exchange([summed] * half, "dom")
    gathered, _ = lax.optimization_barrier((gathered, crossing))
    joined = call(
        join_shares,
        shape((domains, share, hidden), BF16),
        [SMEM] + [VMEM] * half,
        nbytes=4 * narrow * hidden,
        name="join_shares",
    )(ids, *gathered).reshape(narrow, hidden)
    hid = call(
        functools.partial(finish_nodes, half, slots, norm_scale, at),
        [shape((rows_here + EXTRA, wide), BF16)] * groups,
        [SMEM, VMEM, VMEM, VMEM] + [VMEM] * peers,
        [pltpu.VMEM((blocks, tile, wide), F32)],
        nbytes=domains * slots * tile * wide * 2 + blocks * tile * wide * 6,
        name="finish_nodes",
    )(tab, back, bias_here, returned, *terms)
    hid = exchange(hid, "grp")
    count = groups // 2
    placing = dict(
        out_shape=shape((embed, hidden), F32),
        scratch=[pltpu.VMEM((count, narrow, hidden), F32), pltpu.SemaphoreType.DMA((count, COPIES))],
        nbytes=embed * hidden * 3,
        name="place_weight",
        out_specs=pl.BlockSpec(memory_space=pl.ANY),
    )
    across = swap(joined, "grp", count)
    parts, masks = spread(joined, "grp", count // 2)
    grad_weight = call(
        functools.partial(place_weight, masks),
        specs=[SMEM] + [VMEM] * count,
        **placing,
    )(ids, *parts)
    across, hid, grad_weight = lax.optimization_barrier((across, hid, grad_weight))
    parts, masks = spread(across, "grp", count // 2)
    grad_nodes, grad_bias = call(
        functools.partial(node_grads, groups),
        [shape((rows_here, embed), BF16), shape((1, hidden), F32)],
        [SMEM, VMEM] + [VMEM] * groups,
        [pltpu.VMEM((groups, rows_here + EXTRA, wide), BF16)],
        flops=2 * rows_here * embed * hidden,
        nbytes=embed * hidden * 2 + rows_here * (embed + hidden) * 2,
        name="node_grads",
    )(ids, weight, *hid)
    grad_weight = call(
        functools.partial(place_weight, [mask + count for mask in masks]),
        specs=[SMEM] + [VMEM] * count + [pl.BlockSpec(memory_space=pl.ANY)],
        aliases={count + 1: 0},
        **placing,
    )(ids, *parts, grad_weight)
    return (activations, grad_nodes, grad_weight, grad_bias.reshape(hidden))


def solution(mesh):
    in_specs = (
        P(("dom", "grp"), None),
        P(),
        P(),
        P(("dom", "grp"), None),
        P(),
        P("dom", None, None),
        P("dom", None, None),
        P("dom", None),
        P(),
        P("dom", None, None),
        P("dom", None, None),
    )
    out_specs = (P(("dom", "grp"), None), P(("dom", "grp"), None), P(), P())
    return jax.shard_map(
        per_device, mesh=mesh, in_specs=in_specs, out_specs=out_specs, check_vma=False
    )
```

```python
import functools

import jax
import jax.numpy as jnp
from jax import lax
from jax.experimental import pallas as pl
from jax.experimental.pallas import tpu as pltpu
from jax.sharding import PartitionSpec as P

VMEM = pl.BlockSpec(memory_space=pltpu.VMEM)
SMEM = pl.BlockSpec(memory_space=pltpu.SMEM)
EXTRA = 16
COPIES = 4
F32 = jnp.float32
BF16 = jnp.bfloat16


def call(
    body, out_shape, specs, scratch=(), flops=0, nbytes=0, name=None, out_specs=None, aliases=(), mib=16
):
    return pl.pallas_call(
        body,
        out_shape=out_shape,
        in_specs=specs,
        out_specs=jax.tree.map(lambda _: VMEM, out_shape) if out_specs is None else out_specs,
        scratch_shapes=list(scratch),
        input_output_aliases=dict(aliases),
        compiler_params=pltpu.CompilerParams(vmem_limit_bytes=mib * 1024 * 1024),
        cost_estimate=pl.CostEstimate(flops=flops, bytes_accessed=nbytes, transcendentals=0),
        name=name,
    )


def shape(dims, kind):
    return jax.ShapeDtypeStruct(tuple(dims), kind)


def dot(a, b):
    return jnp.dot(a, b, preferred_element_type=F32)


def bias_rows(total):
    high = total.astype(BF16).astype(F32)
    rest = jnp.zeros((EXTRA - 2, total.shape[1]), F32)
    return jnp.concatenate([high, total - high, rest], axis=0).astype(BF16)


def aligned(start, step):
    return pl.ds(pl.multiple_of(start * step, step), step)


def swap(value, axis, mask):
    return lax.ppermute(value, axis, [(i, i ^ mask) for i in range(lax.axis_size(axis))])


def exchange(parts, axis):
    return list(parts[:1]) + [swap(part, axis, m) for m, part in enumerate(parts[1:], 1)]


def spread(value, axis, bit):
    parts, masks = [value], [0]
    while bit:
        parts = parts + [swap(part, axis, bit) for part in parts]
        masks = masks + [mask ^ bit for mask in masks]
        bit //= 2
    return parts, masks


def split_features(ids, feats, *refs):
    outs, sems = refs[:-1], refs[-1]
    group = ids[1]
    narrow = outs[0].shape[1]
    copies = [
        pltpu.make_async_copy(
            feats.at[:, aligned(jnp.bitwise_xor(group, m), narrow)], out, sems.at[m]
        )
        for m, out in enumerate(outs)
    ]
    for copy in copies:
        copy.start()
    for copy in copies:
        copy.wait()


def pick_blocks(groups, slots, at, tab, *refs):
    parts, (x, offered, *outs) = refs[:groups], refs[groups:]
    domain, group = tab[at["me"]], tab[at["me"] + 1]
    tile = x.shape[1]
    per = x.shape[0] // groups
    for m, part in enumerate(parts):
        owner = jnp.bitwise_xor(group, m)
        for j in range(per):
            x[owner * per + j] = part[j * tile : (j + 1) * tile]
    for j in range(offered.shape[0]):
        offered[j] = x[tab[at["pub"] + j]]
    for m, out in enumerate(outs, 1):
        reader = jnp.bitwise_xor(domain, m)
        for s in range(slots):
            entry = jnp.maximum(tab[at["out"] + reader * slots + s], 0)
            out[s * tile : (s + 1) * tile] = x[tab[at["pub"] + entry]]


def pick_relayed(slots, at, tab, offered, *outs):
    tile = offered.shape[1]
    for m, out in enumerate(outs, 1):
        reader = jnp.bitwise_xor(tab[at["me"]], m)
        for s in range(slots):
            entry = jnp.maximum(tab[at["out2"] + reader * slots + s], 0)
            out[s * tile : (s + 1) * tile] = offered[entry]


def local_sum(per_row, at, tab, bank, x, out):
    pair = 2 if per_row % 2 == 0 else 1

    @pl.loop(0, out.shape[0])
    def _(r):
        acc = jnp.zeros(out.shape[1:], F32)
        for k in range(0, per_row, pair):
            spots = [r * per_row + k + j for j in range(pair)]
            left = jnp.concatenate([bank[tab[at["banks"] + a]] for a in spots], axis=1)
            right = jnp.concatenate([x[tab[at["cols"] + a]] for a in spots], axis=0)
            acc += dot(left, right)
        out[r] = acc


def halo_adder(slots, at, tab, bank, acc):
    def add(source, get):
        for s in range(slots):
            i = source * slots + s
            entry = tab[at["in"] + i]

            @pl.when(entry >= 0)
            def _(i=i, s=s, entry=entry):
                acc[tab[at["hrows"] + i]] += dot(bank[tab[at["hbanks"] + i]], get(s, entry))

    return add


def add_near(slots, at, tab, bank, local, mirrored, *refs):
    near, acc = refs[:-1], refs[-1]
    domain = tab[at["me"]]
    tile = local.shape[1]
    acc[...] = local[...]
    add = halo_adder(slots, at, tab, bank, acc)
    for m, block in enumerate(near, 1):
        add(jnp.bitwise_xor(domain, m), lambda s, _, block=block: block[s * tile : (s + 1) * tile])
    mirror = jnp.bitwise_xor(domain, len(near) + 1)
    add(mirror, lambda _, entry: mirrored[jnp.maximum(entry, 0)])


def add_far(half, groups, slots, at, tab, bank, local, *refs):
    far, outs, acc = refs[: half - 1], refs[half - 1 : -1], refs[-1]
    domain, group = tab[at["me"]], tab[at["me"] + 1]
    tile = local.shape[1]
    per = local.shape[0] // groups
    acc[...] = local[...]
    add = halo_adder(slots, at, tab, bank, acc)
    for m, block in enumerate(far, half + 1):
        add(jnp.bitwise_xor(domain, m), lambda s, _, block=block: block[s * tile : (s + 1) * tile])
    for m, out in enumerate(outs):
        owner = jnp.bitwise_xor(group, m)
        for j in range(per):
            out[j * tile : (j + 1) * tile] = acc[owner * per + j].astype(BF16)


def dense(groups, ids, weight, bias, cot, *refs):
    parts, (act, grad, *slices) = refs[:groups], refs[groups:]
    group = ids[1]
    narrow = parts[0].shape[1]
    wide = cot.shape[1] // groups
    left = jnp.concatenate([part[...] for part in parts], axis=1)
    spots = [aligned(jnp.bitwise_xor(group, m), narrow) for m in range(groups)]
    pre = dot(left, jnp.concatenate([weight[spot] for spot in spots], axis=0)) + bias[...]
    act[...] = jnp.maximum(pre, 0.0).astype(BF16)
    masked = jnp.where(pre > 0, cot[...].astype(F32), 0.0).astype(BF16)
    for s in range(groups):
        grad[s] = masked[:, s * wide : (s + 1) * wide]
    for m, out in enumerate(slices):
        out[...] = grad[jnp.bitwise_xor(group, m)]


def back_halo(groups, slots, at, tab, bank_t, *refs):
    parts, (own, mine, kept, *terms) = refs[:groups], refs[groups:]
    domain, group = tab[at["me"]], tab[at["me"] + 1]
    tile = bank_t.shape[1]
    per = parts[0].shape[0] // tile
    half = len(terms) + 1
    total = jnp.zeros((1, own.shape[2]), F32)
    for m, part in enumerate(parts):
        owner = jnp.bitwise_xor(group, m)
        piece = part[...]
        total += jnp.sum(piece.astype(F32), axis=0, keepdims=True)
        for j in range(per):
            own[owner * per + j] = piece[j * tile : (j + 1) * tile]
    mine[...] = total
    tail = bias_rows(total)

    def put(out, place, source):
        for s in range(slots):
            i = source * slots + s
            live = (tab[at["in"] + i] >= 0).astype(F32)
            value = dot(bank_t[tab[at["hbanks"] + i]], own[tab[at["hrows"] + i]]) * live
            spot = (place * slots + s) * tile
            out[spot : spot + tile] = value.astype(BF16)

    for m, term in enumerate(terms, 1):
        peer = jnp.bitwise_xor(domain, m)
        put(term, 0, peer)
        put(term, 1, jnp.bitwise_xor(peer, half))
        term[2 * slots * tile :] = tail
    put(kept, 0, jnp.bitwise_xor(domain, half))


def sum_mirror(slots, at, tab, mine, kept, *refs):
    recv, out, acc = refs[:-2], refs[-2], refs[-1]
    domain = tab[at["me"]]
    offered, tile = acc.shape[:2]
    acc[...] = jnp.zeros_like(acc)
    total = mine[...]
    for m, block in enumerate((kept,) + recv):
        reader = jnp.bitwise_xor(domain, m)
        for s in range(slots):
            entry = tab[at["out2"] + reader * slots + s]
            spot = (s + (slots if m else 0)) * tile

            @pl.when(entry >= 0)
            def _(entry=entry, spot=spot, block=block):
                acc[jnp.maximum(entry, 0)] += block[spot : spot + tile].astype(F32)

        if m:
            tail = block[2 * slots * tile :].astype(F32)
            total += tail[0:1] + tail[1:2]
    for j in range(offered):
        out[j * tile : (j + 1) * tile] = acc[j].astype(BF16)
    out[offered * tile :] = bias_rows(total)


def weight_part(groups, *refs):
    aggs, (grad, send, keep) = refs[:groups], refs[groups:]
    right = jnp.concatenate([grad[s] for s in range(groups)], axis=1)
    for m, agg in enumerate(aggs):
        value = lax.dot_general(
            agg[...], right, (((0,), (0,)), ((), ())), preferred_element_type=F32
        )
        out = send if m % 2 else keep
        out[m // 2] = value.astype(out.dtype)


def fold(kept, recv, send, keep):
    for j in range(kept.shape[0]):
        out = send if j % 2 else keep
        out[j // 2] = (kept[j] + recv[j].astype(F32)).astype(out.dtype)


def weight_shares(ids, whole, recv, *refs):
    kept, *outs = refs[:-1]
    total = refs[-1]
    domain = ids[0]
    half = len(outs) + 1
    rows = total.shape[1]
    value = whole[0] + recv[0].astype(F32)
    for d in range(total.shape[0]):
        total[d] = value[d * rows : (d + 1) * rows]
    for m, out in enumerate([kept] + outs):
        peer = jnp.bitwise_xor(domain, m)
        out[0] = total[peer].astype(out.dtype)
        out[1] = total[jnp.bitwise_xor(peer, half)].astype(out.dtype)


def sum_half(kept, *refs):
    recv, out = refs[:-1], refs[-1]
    for i in range(2):
        total = kept[i]
        for block in recv:
            total += block[i].astype(F32)
        out[i] = total.astype(BF16)


def sum_both(scale, here, there, out):
    for i in range(2):
        out[i] = ((here[i].astype(F32) + there[1 - i].astype(F32)) * scale).astype(BF16)


def join_shares(ids, *refs):
    parts, out = refs[:-1], refs[-1]
    for m, part in enumerate(parts):
        owner = jnp.bitwise_xor(ids[0], m)
        out[owner] = part[0]
        out[jnp.bitwise_xor(owner, len(parts))] = part[1]


def back_local(per_row, at, tab, bank_t, own, out):
    out[...] = jnp.zeros_like(out)

    @pl.loop(0, own.shape[0])
    def _(r):
        right = own[r]
        for k in range(per_row):
            spot = r * per_row + k
            out[tab[at["cols"] + spot]] += dot(bank_t[tab[at["banks"] + spot]], right)


def finish_nodes(half, slots, scale, at, tab, local, mine, mirrored, *refs):
    recv, outs, acc = refs[: half - 1], refs[half - 1 : -1], refs[-1]
    groups = len(outs)
    domain, group = tab[at["me"]], tab[at["me"] + 1]
    tile = local.shape[1]
    per = local.shape[0] // groups
    offered = (mirrored.shape[0] - EXTRA) // tile
    acc[...] = local[...]
    tail = mirrored[offered * tile :].astype(F32)
    for j in range(offered):
        acc[tab[at["pub"] + j]] += mirrored[j * tile : (j + 1) * tile].astype(F32)
    for m, block in enumerate(recv, 1):
        tail += block[2 * slots * tile :].astype(F32)
        reader = jnp.bitwise_xor(domain, m)
        for s in range(slots):
            entry = tab[at["out"] + reader * slots + s]

            @pl.when(entry >= 0)
            def _(s=s, entry=entry, block=block):
                spot = tab[at["pub"] + jnp.maximum(entry, 0)]
                acc[spot] += block[s * tile : (s + 1) * tile].astype(F32)

    rows = bias_rows((mine[...] + tail[0:1] + tail[1:2]) * scale)
    for m, out in enumerate(outs):
        owner = jnp.bitwise_xor(group, m)
        for j in range(per):
            out[j * tile : (j + 1) * tile] = acc[owner * per + j].astype(BF16)
        out[per * tile :] = rows


def node_grads(groups, ids, weight, *refs):
    parts, (out, bias_out, hid) = refs[:groups], refs[groups:]
    group = ids[1]
    rows = out.shape[0]
    for m, part in enumerate(parts):
        hid[jnp.bitwise_xor(group, m)] = part[...]
    left = jnp.concatenate([hid[s, :rows] for s in range(groups)], axis=1)
    out[...] = lax.dot_general(
        left, weight[...], (((1,), (1,)), ((), ())), preferred_element_type=F32
    ).astype(BF16)
    tail = jnp.concatenate([hid[s, rows:] for s in range(groups)], axis=1).astype(F32)
    bias_out[...] = tail[0:1] + tail[1:2]


def place_weight(masks, ids, *refs):
    parts, (out, wide, sems) = refs[: len(masks)], refs[-3:]
    group = ids[1]
    rows = parts[0].shape[0]
    copies = []
    step = rows // COPIES
    for i, (mask, part) in enumerate(zip(masks, parts)):
        for j in range(COPIES):
            wide[i, j * step : (j + 1) * step] = part[j * step : (j + 1) * step].astype(F32)
            spot = out.at[aligned(jnp.bitwise_xor(group, mask) * COPIES + j, step)]
            piece = wide.at[i, pl.ds(j * step, step)]
            copies.append(pltpu.make_async_copy(piece, spot, sems.at[i, j]))
            copies[-1].start()
    for copy in copies:
        copy.wait()


def per_device(
    node_feats,
    weight,
    bias,
    cotangent,
    tile_bank,
    local_cols,
    local_banks,
    published,
    send_table,
    halo_rows,
    halo_banks,
):
    domains = lax.axis_size("dom")
    groups = lax.axis_size("grp")
    domain_index = lax.axis_index("dom")
    rows_here, embed = node_feats.shape
    hidden = weight.shape[1]
    tile = tile_bank.shape[1]
    slots = send_table.shape[2]
    per_row = local_cols.shape[2]
    part_rows = rows_here * groups
    blocks = part_rows // tile
    narrow = embed // groups
    wide = hidden // groups
    share = narrow // domains
    half = domains // 2
    peers = half - 1
    offers = published.shape[1]

    ids = jnp.stack([domain_index, lax.axis_index("grp")]).astype(jnp.int32)
    tables = {
        "cols": local_cols[0],
        "banks": local_banks[0],
        "pub": published[0],
        "out": lax.dynamic_index_in_dim(send_table, domain_index, 0, keepdims=False),
        "out2": lax.dynamic_index_in_dim(send_table, domain_index ^ half, 0, keepdims=False),
        "in": lax.dynamic_index_in_dim(send_table, domain_index, 1, keepdims=False),
        "hrows": halo_rows[0],
        "hbanks": halo_banks[0],
        "me": ids,
    }
    at, place = {}, 0
    for name, table in tables.items():
        at[name] = place
        place += table.size
    tab = jnp.concatenate([table.reshape(-1) for table in tables.values()])
    bank_t = jnp.swapaxes(tile_bank, 1, 2)

    feats = call(
        split_features,
        [shape((rows_here, narrow), BF16)] * groups,
        [SMEM, pl.BlockSpec(memory_space=pl.ANY)],
        [pltpu.SemaphoreType.DMA((groups,))],
        nbytes=4 * rows_here * embed,
        name="split_features",
    )(ids, node_feats)
    feats = exchange(feats, "grp")
    x, offered, *picked = call(
        functools.partial(pick_blocks, groups, slots, at),
        [shape((blocks, tile, narrow), BF16), shape((offers, tile, narrow), BF16)]
        + [shape((slots * tile, narrow), BF16)] * peers,
        [SMEM] + [VMEM] * groups,
        nbytes=4 * (peers * slots + blocks + offers) * tile * narrow,
        name="pick_blocks",
    )(tab, *feats)
    mirrored = swap(offered, "dom", half)
    near = exchange([None] + picked, "dom")[1:]
    local = call(
        functools.partial(local_sum, per_row, at),
        shape((blocks, tile, narrow), F32),
        [SMEM, VMEM, VMEM],
        flops=2 * blocks * per_row * tile * tile * narrow,
        nbytes=blocks * tile * narrow * 6,
        name="local_sum",
    )(tab, tile_bank, x)
    mirrored, local = lax.optimization_barrier((mirrored, local))
    relayed = call(
        functools.partial(pick_relayed, slots, at),
        [shape((slots * tile, narrow), BF16)] * peers,
        [SMEM, VMEM],
        nbytes=4 * peers * slots * tile * narrow,
        name="pick_relayed",
    )(tab, mirrored)
    far = exchange([None, *relayed], "dom")[1:]
    local = call(
        functools.partial(add_near, slots, at),
        shape((blocks, tile, narrow), F32),
        [SMEM, VMEM, VMEM, VMEM] + [VMEM] * peers,
        flops=2 * half * slots * tile * tile * narrow,
        nbytes=blocks * tile * narrow * 8,
        name="add_near",
    )(tab, tile_bank, local, mirrored, *near)
    far, local = lax.optimization_barrier((far, local))
    aggs = call(
        functools.partial(add_far, half, groups, slots, at),
        [shape((rows_here, narrow), BF16)] * groups,
        [SMEM, VMEM, VMEM] + [VMEM] * peers,
        [pltpu.VMEM((blocks, tile, narrow), F32)],
        flops=2 * half * slots * tile * tile * narrow,
        nbytes=blocks * tile * narrow * 8,
        name="add_far",
    )(tab, tile_bank, local, *far)
    mine = exchange(aggs, "grp")
    activations, grad, *grads = call(
        functools.partial(dense, groups),
        [shape((rows_here, hidden), BF16), shape((groups, rows_here, wide), BF16)]
        + [shape((rows_here, wide), BF16)] * groups,
        [SMEM] + [VMEM] * (3 + groups),
        flops=2 * rows_here * embed * hidden,
        nbytes=embed * hidden * 2 + rows_here * (embed + 4 * hidden) * 2,
        name="dense",
    )(ids, weight, bias.reshape(1, hidden), cotangent, *mine)
    grads = exchange(grads, "grp")
    norm_scale = float(rows_here * groups * domains) ** (-0.5)
    norm_scale = float(rows_here * groups * domains) ** (-0.5)
    send, keep = call(
        functools.partial(weight_part, groups),
        [
            shape((groups // 2, narrow, hidden), BF16),
            shape((groups // 2, narrow, hidden), F32),
        ],
        [VMEM] * (groups + 1),
        flops=2 * rows_here * embed * hidden,
        nbytes=rows_here * (embed + hidden) * 2 + embed * hidden * 3,
        name="weight_part",
    )(*mine, grad)
    tab_after, _ = lax.optimization_barrier((tab, send))
    own, bias_here, kept, *terms = call(
        functools.partial(back_halo, groups, slots, at),
        [
            shape((blocks, tile, wide), BF16),
            shape((1, wide), F32),
            shape((slots * tile, wide), BF16),
        ]
        + [shape((2 * slots * tile + EXTRA, wide), BF16)] * peers,
        [SMEM, VMEM] + [VMEM] * groups,
        flops=2 * domains * slots * tile * tile * wide,
        nbytes=(domains * slots + blocks) * tile * wide * 2,
        name="back_halo",
    )(tab_after, bank_t, *grads)
    sent, terms = terms, exchange([None] + terms, "dom")[1:]
    recv = swap(send, "grp", 1)
    recv, _ = lax.optimization_barrier((recv, sent))
    bit = 2
    while bit < groups:
        count = groups // (2 * bit)
        send, keep = call(
            fold,
            [shape((count, narrow, hidden), BF16), shape((count, narrow, hidden), F32)],
            [VMEM, VMEM],
            nbytes=count * narrow * hidden * 18,
            name="fold",
        )(keep, recv)
        recv = swap(send, "grp", bit)
        bit *= 2
    terms, _ = lax.optimization_barrier((terms, send))
    crossing = call(
        functools.partial(sum_mirror, slots, at),
        shape((offers * tile + EXTRA, wide), BF16),
        [SMEM] + [VMEM] * (2 + peers),
        [pltpu.VMEM((offers, tile, wide), F32)],
        nbytes=4 * domains * slots * tile * wide,
        name="sum_mirror",
    )(tab, bias_here, kept, *terms)
    returned = swap(crossing, "dom", half)
    own, _ = lax.optimization_barrier((own, crossing))
    back = call(
        functools.partial(back_local, per_row, at),
        shape((blocks, tile, wide), F32),
        [SMEM, VMEM, VMEM],
        flops=2 * blocks * per_row * tile * tile * wide,
        nbytes=blocks * tile * wide * 6,
        name="back_local",
    )(tab, bank_t, own)
    recv, back = lax.optimization_barrier((recv, back))
    kept_shares, *shares = call(
        weight_shares,
        [shape((2, share, hidden), F32)] + [shape((2, share, hidden), BF16)] * peers,
        [SMEM, VMEM, VMEM],
        [pltpu.VMEM((domains, share, hidden), F32)],
        nbytes=narrow * hidden * 8,
        name="weight_shares",
    )(ids, keep, recv)
    shares = exchange([None] + shares, "dom")[1:]
    hid = call(
        functools.partial(finish_nodes, half, slots, norm_scale, at),
        [shape((rows_here + EXTRA, wide), BF16)] * groups,
        [SMEM, VMEM, VMEM, VMEM] + [VMEM] * peers,
        [pltpu.VMEM((blocks, tile, wide), F32)],
        nbytes=domains * slots * tile * wide * 2 + blocks * tile * wide * 6,
        name="finish_nodes",
    )(tab, back, bias_here, returned, *terms)
    shares, hid = lax.optimization_barrier((shares, hid))
    here = call(
        sum_half,
        shape((2, share, hidden), BF16),
        [VMEM] * half,
        nbytes=2 * half * share * hidden * 2,
        name="sum_half",
    )(kept_shares, *shares)
    there = swap(here, "dom", half)
    summed = call(
        functools.partial(sum_both, norm_scale),
        shape((2, share, hidden), BF16),
        [VMEM, VMEM],
        nbytes=6 * share * hidden * 2,
        name="sum_both",
    )(here, there)
    gathered = exchange([summed] * half, "dom")
    hid = exchange(hid, "grp")
    grad_nodes, grad_bias = call(
        functools.partial(node_grads, groups),
        [shape((rows_here, embed), BF16), shape((1, hidden), F32)],
        [SMEM, VMEM] + [VMEM] * groups,
        [pltpu.VMEM((groups, rows_here + EXTRA, wide), BF16)],
        flops=2 * rows_here * embed * hidden,
        nbytes=embed * hidden * 2 + rows_here * (embed + hidden) * 2,
        name="node_grads",
    )(ids, weight, *hid)
    gathered, grad_nodes = lax.optimization_barrier((gathered, grad_nodes))
    joined = call(
        join_shares,
        shape((domains, share, hidden), BF16),
        [SMEM] + [VMEM] * half,
        nbytes=4 * narrow * hidden,
        name="join_shares",
    )(ids, *gathered).reshape(narrow, hidden)
    count = groups // 2
    placing = dict(
        out_shape=shape((embed, hidden), F32),
        scratch=[pltpu.VMEM((count, narrow, hidden), F32), pltpu.SemaphoreType.DMA((count, COPIES))],
        nbytes=embed * hidden * 3,
        name="place_weight",
        out_specs=pl.BlockSpec(memory_space=pl.ANY),
    )
    across = swap(joined, "grp", count)
    parts, masks = spread(joined, "grp", count // 2)
    grad_weight = call(
        functools.partial(place_weight, masks),
        specs=[SMEM] + [VMEM] * count,
        **placing,
    )(ids, *parts)
    across, grad_weight = lax.optimization_barrier((across, grad_weight))
    parts, masks = spread(across, "grp", count // 2)
    grad_weight = call(
        functools.partial(place_weight, [mask + count for mask in masks]),
        specs=[SMEM] + [VMEM] * count + [pl.BlockSpec(memory_space=pl.ANY)],
        aliases={count + 1: 0},
        **placing,
    )(ids, *parts, grad_weight)
    return (activations, grad_nodes, grad_weight, grad_bias.reshape(hidden))


def solution(mesh):
    in_specs = (
        P(("dom", "grp"), None),
        P(),
        P(),
        P(("dom", "grp"), None),
        P(),
        P("dom", None, None),
        P("dom", None, None),
        P("dom", None),
        P(),
        P("dom", None, None),
        P("dom", None, None),
    )
    out_specs = (P(("dom", "grp"), None), P(("dom", "grp"), None), P(), P())
    return jax.shard_map(
        per_device, mesh=mesh, in_specs=in_specs, out_specs=out_specs, check_vma=False
    )
```

```python
import functools

import jax
import jax.numpy as jnp
from jax import lax
from jax.experimental import pallas as pl
from jax.experimental.pallas import tpu as pltpu
from jax.sharding import PartitionSpec as P

VMEM = pl.BlockSpec(memory_space=pltpu.VMEM)
SMEM = pl.BlockSpec(memory_space=pltpu.SMEM)
EXTRA = 16
COPIES = 4
F32 = jnp.float32
BF16 = jnp.bfloat16


def call(
    body, out_shape, specs, scratch=(), flops=0, nbytes=0, name=None, out_specs=None, aliases=(), mib=16
):
    return pl.pallas_call(
        body,
        out_shape=out_shape,
        in_specs=specs,
        out_specs=jax.tree.map(lambda _: VMEM, out_shape) if out_specs is None else out_specs,
        scratch_shapes=list(scratch),
        input_output_aliases=dict(aliases),
        compiler_params=pltpu.CompilerParams(vmem_limit_bytes=mib * 1024 * 1024),
        cost_estimate=pl.CostEstimate(flops=flops, bytes_accessed=nbytes, transcendentals=0),
        name=name,
    )


def shape(dims, kind):
    return jax.ShapeDtypeStruct(tuple(dims), kind)


def dot(a, b):
    return jnp.dot(a, b, preferred_element_type=F32)


def bias_rows(total):
    high = total.astype(BF16).astype(F32)
    rest = jnp.zeros((EXTRA - 2, total.shape[1]), F32)
    return jnp.concatenate([high, total - high, rest], axis=0).astype(BF16)


def aligned(start, step):
    return pl.ds(pl.multiple_of(start * step, step), step)


def swap(value, axis, mask):
    return lax.ppermute(value, axis, [(i, i ^ mask) for i in range(lax.axis_size(axis))])


def exchange(parts, axis):
    return list(parts[:1]) + [swap(part, axis, m) for m, part in enumerate(parts[1:], 1)]


def spread(value, axis, bit):
    parts, masks = [value], [0]
    while bit:
        parts = parts + [swap(part, axis, bit) for part in parts]
        masks = masks + [mask ^ bit for mask in masks]
        bit //= 2
    return parts, masks


def split_features(ids, feats, *refs):
    outs, sems = refs[:-1], refs[-1]
    group = ids[1]
    narrow = outs[0].shape[1]
    copies = [
        pltpu.make_async_copy(
            feats.at[:, aligned(jnp.bitwise_xor(group, m), narrow)], out, sems.at[m]
        )
        for m, out in enumerate(outs)
    ]
    for copy in copies:
        copy.start()
    for copy in copies:
        copy.wait()


def pick_blocks(groups, slots, at, tab, *refs):
    parts, (x, offered, *outs) = refs[:groups], refs[groups:]
    domain, group = tab[at["me"]], tab[at["me"] + 1]
    tile = x.shape[1]
    per = x.shape[0] // groups
    for m, part in enumerate(parts):
        owner = jnp.bitwise_xor(group, m)
        for j in range(per):
            x[owner * per + j] = part[j * tile : (j + 1) * tile]
    for j in range(offered.shape[0]):
        offered[j] = x[tab[at["pub"] + j]]
    for m, out in enumerate(outs, 1):
        reader = jnp.bitwise_xor(domain, m)
        for s in range(slots):
            entry = jnp.maximum(tab[at["out"] + reader * slots + s], 0)
            out[s * tile : (s + 1) * tile] = x[tab[at["pub"] + entry]]


def pick_relayed(slots, at, tab, offered, *outs):
    tile = offered.shape[1]
    for m, out in enumerate(outs, 1):
        reader = jnp.bitwise_xor(tab[at["me"]], m)
        for s in range(slots):
            entry = jnp.maximum(tab[at["out2"] + reader * slots + s], 0)
            out[s * tile : (s + 1) * tile] = offered[entry]


def local_sum(per_row, at, tab, bank, x, out):
    pair = 2 if per_row % 2 == 0 else 1

    @pl.loop(0, out.shape[0])
    def _(r):
        acc = jnp.zeros(out.shape[1:], F32)
        for k in range(0, per_row, pair):
            spots = [r * per_row + k + j for j in range(pair)]
            left = jnp.concatenate([bank[tab[at["banks"] + a]] for a in spots], axis=1)
            right = jnp.concatenate([x[tab[at["cols"] + a]] for a in spots], axis=0)
            acc += dot(left, right)
        out[r] = acc


def halo_adder(slots, at, tab, bank, acc):
    def add(source, get):
        for s in range(slots):
            i = source * slots + s
            entry = tab[at["in"] + i]

            @pl.when(entry >= 0)
            def _(i=i, s=s, entry=entry):
                acc[tab[at["hrows"] + i]] += dot(bank[tab[at["hbanks"] + i]], get(s, entry))

    return add


def add_near(slots, at, tab, bank, local, mirrored, *refs):
    near, acc = refs[:-1], refs[-1]
    domain = tab[at["me"]]
    tile = local.shape[1]
    acc[...] = local[...]
    add = halo_adder(slots, at, tab, bank, acc)
    for m, block in enumerate(near, 1):
        add(jnp.bitwise_xor(domain, m), lambda s, _, block=block: block[s * tile : (s + 1) * tile])
    mirror = jnp.bitwise_xor(domain, len(near) + 1)
    add(mirror, lambda _, entry: mirrored[jnp.maximum(entry, 0)])


def add_far(half, groups, slots, at, tab, bank, local, *refs):
    far, outs, acc = refs[: half - 1], refs[half - 1 : -1], refs[-1]
    domain, group = tab[at["me"]], tab[at["me"] + 1]
    tile = local.shape[1]
    per = local.shape[0] // groups
    acc[...] = local[...]
    add = halo_adder(slots, at, tab, bank, acc)
    for m, block in enumerate(far, half + 1):
        add(jnp.bitwise_xor(domain, m), lambda s, _, block=block: block[s * tile : (s + 1) * tile])
    for m, out in enumerate(outs):
        owner = jnp.bitwise_xor(group, m)
        for j in range(per):
            out[j * tile : (j + 1) * tile] = acc[owner * per + j].astype(BF16)


def dense(groups, ids, weight, bias, cot, *refs):
    parts, (act, grad, *slices) = refs[:groups], refs[groups:]
    group = ids[1]
    narrow = parts[0].shape[1]
    wide = cot.shape[1] // groups
    left = jnp.concatenate([part[...] for part in parts], axis=1)
    spots = [aligned(jnp.bitwise_xor(group, m), narrow) for m in range(groups)]
    pre = dot(left, jnp.concatenate([weight[spot] for spot in spots], axis=0)) + bias[...]
    act[...] = jnp.maximum(pre, 0.0).astype(BF16)
    masked = jnp.where(pre > 0, cot[...].astype(F32), 0.0).astype(BF16)
    for s in range(groups):
        grad[s] = masked[:, s * wide : (s + 1) * wide]
    for m, out in enumerate(slices):
        out[...] = grad[jnp.bitwise_xor(group, m)]


def back_halo(groups, slots, at, tab, bank_t, *refs):
    parts, (own, mine, kept, *terms) = refs[:groups], refs[groups:]
    domain, group = tab[at["me"]], tab[at["me"] + 1]
    tile = bank_t.shape[1]
    per = parts[0].shape[0] // tile
    half = len(terms) + 1
    total = jnp.zeros((1, own.shape[2]), F32)
    for m, part in enumerate(parts):
        owner = jnp.bitwise_xor(group, m)
        piece = part[...]
        total += jnp.sum(piece.astype(F32), axis=0, keepdims=True)
        for j in range(per):
            own[owner * per + j] = piece[j * tile : (j + 1) * tile]
    mine[...] = total
    tail = bias_rows(total)

    def put(out, place, source):
        for s in range(slots):
            i = source * slots + s
            live = (tab[at["in"] + i] >= 0).astype(F32)
            value = dot(bank_t[tab[at["hbanks"] + i]], own[tab[at["hrows"] + i]]) * live
            spot = (place * slots + s) * tile
            out[spot : spot + tile] = value.astype(BF16)

    for m, term in enumerate(terms, 1):
        peer = jnp.bitwise_xor(domain, m)
        put(term, 0, peer)
        put(term, 1, jnp.bitwise_xor(peer, half))
        term[2 * slots * tile :] = tail
    put(kept, 0, jnp.bitwise_xor(domain, half))


def sum_mirror(slots, at, tab, mine, kept, *refs):
    recv, out, acc = refs[:-2], refs[-2], refs[-1]
    domain = tab[at["me"]]
    offered, tile = acc.shape[:2]
    acc[...] = jnp.zeros_like(acc)
    total = mine[...]
    for m, block in enumerate((kept,) + recv):
        reader = jnp.bitwise_xor(domain, m)
        for s in range(slots):
            entry = tab[at["out2"] + reader * slots + s]
            spot = (s + (slots if m else 0)) * tile

            @pl.when(entry >= 0)
            def _(entry=entry, spot=spot, block=block):
                acc[jnp.maximum(entry, 0)] += block[spot : spot + tile].astype(F32)

        if m:
            tail = block[2 * slots * tile :].astype(F32)
            total += tail[0:1] + tail[1:2]
    for j in range(offered):
        out[j * tile : (j + 1) * tile] = acc[j].astype(BF16)
    out[offered * tile :] = bias_rows(total)


def weight_part(groups, *refs):
    aggs, (grad, send, keep) = refs[:groups], refs[groups:]
    right = jnp.concatenate([grad[s] for s in range(groups)], axis=1)
    for m, agg in enumerate(aggs):
        value = lax.dot_general(
            agg[...], right, (((0,), (0,)), ((), ())), preferred_element_type=F32
        )
        out = send if m % 2 else keep
        out[m // 2] = value.astype(out.dtype)


def fold(kept, recv, send, keep):
    for j in range(kept.shape[0]):
        out = send if j % 2 else keep
        out[j // 2] = (kept[j] + recv[j].astype(F32)).astype(out.dtype)


def weight_shares(ids, whole, recv, *refs):
    kept, *outs = refs[:-1]
    total = refs[-1]
    domain = ids[0]
    half = len(outs) + 1
    rows = total.shape[1]
    value = whole[0] + recv[0].astype(F32)
    for d in range(total.shape[0]):
        total[d] = value[d * rows : (d + 1) * rows]
    for m, out in enumerate([kept] + outs):
        peer = jnp.bitwise_xor(domain, m)
        out[0] = total[peer].astype(out.dtype)
        out[1] = total[jnp.bitwise_xor(peer, half)].astype(out.dtype)


def sum_half(kept, *refs):
    recv, out = refs[:-1], refs[-1]
    for i in range(2):
        total = kept[i]
        for block in recv:
            total += block[i].astype(F32)
        out[i] = total.astype(BF16)


def sum_both(scale, here, there, out):
    for i in range(2):
        out[i] = ((here[i].astype(F32) + there[1 - i].astype(F32)) * scale).astype(BF16)


def join_shares(ids, *refs):
    parts, out = refs[:-1], refs[-1]
    for m, part in enumerate(parts):
        owner = jnp.bitwise_xor(ids[0], m)
        out[owner] = part[0]
        out[jnp.bitwise_xor(owner, len(parts))] = part[1]


def back_local(per_row, at, tab, bank_t, own, out):
    out[...] = jnp.zeros_like(out)

    @pl.loop(0, own.shape[0])
    def _(r):
        right = own[r]
        for k in range(per_row):
            spot = r * per_row + k
            out[tab[at["cols"] + spot]] += dot(bank_t[tab[at["banks"] + spot]], right)


def finish_nodes(half, slots, scale, at, tab, local, mine, mirrored, *refs):
    recv, outs, acc = refs[: half - 1], refs[half - 1 : -1], refs[-1]
    groups = len(outs)
    domain, group = tab[at["me"]], tab[at["me"] + 1]
    tile = local.shape[1]
    per = local.shape[0] // groups
    offered = (mirrored.shape[0] - EXTRA) // tile
    acc[...] = local[...]
    tail = mirrored[offered * tile :].astype(F32)
    for j in range(offered):
        acc[tab[at["pub"] + j]] += mirrored[j * tile : (j + 1) * tile].astype(F32)
    for m, block in enumerate(recv, 1):
        tail += block[2 * slots * tile :].astype(F32)
        reader = jnp.bitwise_xor(domain, m)
        for s in range(slots):
            entry = tab[at["out"] + reader * slots + s]

            @pl.when(entry >= 0)
            def _(s=s, entry=entry, block=block):
                spot = tab[at["pub"] + jnp.maximum(entry, 0)]
                acc[spot] += block[s * tile : (s + 1) * tile].astype(F32)

    rows = bias_rows((mine[...] + tail[0:1] + tail[1:2]) * scale)
    for m, out in enumerate(outs):
        owner = jnp.bitwise_xor(group, m)
        for j in range(per):
            out[j * tile : (j + 1) * tile] = acc[owner * per + j].astype(BF16)
        out[per * tile :] = rows


def node_grads(groups, ids, weight, *refs):
    parts, (out, bias_out, hid) = refs[:groups], refs[groups:]
    group = ids[1]
    rows = out.shape[0]
    for m, part in enumerate(parts):
        hid[jnp.bitwise_xor(group, m)] = part[...]
    left = jnp.concatenate([hid[s, :rows] for s in range(groups)], axis=1)
    out[...] = lax.dot_general(
        left, weight[...], (((1,), (1,)), ((), ())), preferred_element_type=F32
    ).astype(BF16)
    tail = jnp.concatenate([hid[s, rows:] for s in range(groups)], axis=1).astype(F32)
    bias_out[...] = tail[0:1] + tail[1:2]


def place_weight(masks, ids, *refs):
    parts, (out, wide, sems) = refs[: len(masks)], refs[-3:]
    group = ids[1]
    rows = parts[0].shape[0]
    copies = []
    step = rows // COPIES
    for i, (mask, part) in enumerate(zip(masks, parts)):
        for j in range(COPIES):
            wide[i, j * step : (j + 1) * step] = part[j * step : (j + 1) * step].astype(F32)
            spot = out.at[aligned(jnp.bitwise_xor(group, mask) * COPIES + j, step)]
            piece = wide.at[i, pl.ds(j * step, step)]
            copies.append(pltpu.make_async_copy(piece, spot, sems.at[i, j]))
            copies[-1].start()
    for copy in copies:
        copy.wait()


def per_device(
    node_feats,
    weight,
    bias,
    cotangent,
    tile_bank,
    local_cols,
    local_banks,
    published,
    send_table,
    halo_rows,
    halo_banks,
):
    domains = lax.axis_size("dom")
    groups = lax.axis_size("grp")
    domain_index = lax.axis_index("dom")
    rows_here, embed = node_feats.shape
    hidden = weight.shape[1]
    tile = tile_bank.shape[1]
    slots = send_table.shape[2]
    per_row = local_cols.shape[2]
    part_rows = rows_here * groups
    blocks = part_rows // tile
    narrow = embed // groups
    wide = hidden // groups
    share = narrow // domains
    half = domains // 2
    peers = half - 1
    offers = published.shape[1]

    ids = jnp.stack([domain_index, lax.axis_index("grp")]).astype(jnp.int32)
    tables = {
        "cols": local_cols[0],
        "banks": local_banks[0],
        "pub": published[0],
        "out": lax.dynamic_index_in_dim(send_table, domain_index, 0, keepdims=False),
        "out2": lax.dynamic_index_in_dim(send_table, domain_index ^ half, 0, keepdims=False),
        "in": lax.dynamic_index_in_dim(send_table, domain_index, 1, keepdims=False),
        "hrows": halo_rows[0],
        "hbanks": halo_banks[0],
        "me": ids,
    }
    at, place = {}, 0
    for name, table in tables.items():
        at[name] = place
        place += table.size
    tab = jnp.concatenate([table.reshape(-1) for table in tables.values()])
    bank_t = jnp.swapaxes(tile_bank, 1, 2)

    feats = call(
        split_features,
        [shape((rows_here, narrow), BF16)] * groups,
        [SMEM, pl.BlockSpec(memory_space=pl.ANY)],
        [pltpu.SemaphoreType.DMA((groups,))],
        nbytes=4 * rows_here * embed,
        name="split_features",
    )(ids, node_feats)
    feats = exchange(feats, "grp")
    x, offered, *picked = call(
        functools.partial(pick_blocks, groups, slots, at),
        [shape((blocks, tile, narrow), BF16), shape((offers, tile, narrow), BF16)]
        + [shape((slots * tile, narrow), BF16)] * peers,
        [SMEM] + [VMEM] * groups,
        nbytes=4 * (peers * slots + blocks + offers) * tile * narrow,
        name="pick_blocks",
    )(tab, *feats)
    mirrored = swap(offered, "dom", half)
    near = exchange([None] + picked, "dom")[1:]
    local = call(
        functools.partial(local_sum, per_row, at),
        shape((blocks, tile, narrow), F32),
        [SMEM, VMEM, VMEM],
        flops=2 * blocks * per_row * tile * tile * narrow,
        nbytes=blocks * tile * narrow * 6,
        name="local_sum",
    )(tab, tile_bank, x)
    mirrored, local = lax.optimization_barrier((mirrored, local))
    relayed = call(
        functools.partial(pick_relayed, slots, at),
        [shape((slots * tile, narrow), BF16)] * peers,
        [SMEM, VMEM],
        nbytes=4 * peers * slots * tile * narrow,
        name="pick_relayed",
    )(tab, mirrored)
    far = exchange([None, *relayed], "dom")[1:]
    local = call(
        functools.partial(add_near, slots, at),
        shape((blocks, tile, narrow), F32),
        [SMEM, VMEM, VMEM, VMEM] + [VMEM] * peers,
        flops=2 * half * slots * tile * tile * narrow,
        nbytes=blocks * tile * narrow * 8,
        name="add_near",
    )(tab, tile_bank, local, mirrored, *near)
    far, local = lax.optimization_barrier((far, local))
    aggs = call(
        functools.partial(add_far, half, groups, slots, at),
        [shape((rows_here, narrow), BF16)] * groups,
        [SMEM, VMEM, VMEM] + [VMEM] * peers,
        [pltpu.VMEM((blocks, tile, narrow), F32)],
        flops=2 * half * slots * tile * tile * narrow,
        nbytes=blocks * tile * narrow * 8,
        name="add_far",
    )(tab, tile_bank, local, *far)
    mine = exchange(aggs, "grp")
    activations, grad, *grads = call(
        functools.partial(dense, groups),
        [shape((rows_here, hidden), BF16), shape((groups, rows_here, wide), BF16)]
        + [shape((rows_here, wide), BF16)] * groups,
        [SMEM] + [VMEM] * (3 + groups),
        flops=2 * rows_here * embed * hidden,
        nbytes=embed * hidden * 2 + rows_here * (embed + 4 * hidden) * 2,
        name="dense",
    )(ids, weight, bias.reshape(1, hidden), cotangent, *mine)
    grads = exchange(grads, "grp")
    norm_scale = float(rows_here * groups * domains) ** (-0.5)
    norm_scale = float(rows_here * groups * domains) ** (-0.5)
    send, keep = call(
        functools.partial(weight_part, groups),
        [
            shape((groups // 2, narrow, hidden), BF16),
            shape((groups // 2, narrow, hidden), F32),
        ],
        [VMEM] * (groups + 1),
        flops=2 * rows_here * embed * hidden,
        nbytes=rows_here * (embed + hidden) * 2 + embed * hidden * 3,
        name="weight_part",
    )(*mine, grad)
    tab_after, _ = lax.optimization_barrier((tab, send))
    own, bias_here, kept, *terms = call(
        functools.partial(back_halo, groups, slots, at),
        [
            shape((blocks, tile, wide), BF16),
            shape((1, wide), F32),
            shape((slots * tile, wide), BF16),
        ]
        + [shape((2 * slots * tile + EXTRA, wide), BF16)] * peers,
        [SMEM, VMEM] + [VMEM] * groups,
        flops=2 * domains * slots * tile * tile * wide,
        nbytes=(domains * slots + blocks) * tile * wide * 2,
        name="back_halo",
    )(tab_after, bank_t, *grads)
    sent, terms = terms, exchange([None] + terms, "dom")[1:]
    recv = swap(send, "grp", 1)
    recv, _ = lax.optimization_barrier((recv, sent))
    bit = 2
    while bit < groups:
        count = groups // (2 * bit)
        send, keep = call(
            fold,
            [shape((count, narrow, hidden), BF16), shape((count, narrow, hidden), F32)],
            [VMEM, VMEM],
            nbytes=count * narrow * hidden * 18,
            name="fold",
        )(keep, recv)
        recv = swap(send, "grp", bit)
        bit *= 2
    recv, terms[0] = lax.optimization_barrier((recv, terms[0]))
    kept_shares, *shares = call(
        weight_shares,
        [shape((2, share, hidden), F32)] + [shape((2, share, hidden), BF16)] * peers,
        [SMEM, VMEM, VMEM],
        [pltpu.VMEM((domains, share, hidden), F32)],
        nbytes=narrow * hidden * 8,
        name="weight_shares",
    )(ids, keep, recv)
    terms, _ = lax.optimization_barrier((terms, shares))
    shares = exchange([None] + shares, "dom")[1:]
    crossing = call(
        functools.partial(sum_mirror, slots, at),
        shape((offers * tile + EXTRA, wide), BF16),
        [SMEM] + [VMEM] * (2 + peers),
        [pltpu.VMEM((offers, tile, wide), F32)],
        nbytes=4 * domains * slots * tile * wide,
        name="sum_mirror",
    )(tab, bias_here, kept, *terms)
    returned = swap(crossing, "dom", half)
    shares, _ = lax.optimization_barrier((shares, crossing))
    here = call(
        sum_half,
        shape((2, share, hidden), BF16),
        [VMEM] * half,
        nbytes=2 * half * share * hidden * 2,
        name="sum_half",
    )(kept_shares, *shares)
    there = swap(here, "dom", half)
    own, _ = lax.optimization_barrier((own, here))
    back = call(
        functools.partial(back_local, per_row, at),
        shape((blocks, tile, wide), F32),
        [SMEM, VMEM, VMEM],
        flops=2 * blocks * per_row * tile * tile * wide,
        nbytes=blocks * tile * wide * 6,
        name="back_local",
    )(tab, bank_t, own)
    there, back = lax.optimization_barrier((there, back))
    summed = call(
        functools.partial(sum_both, norm_scale),
        shape((2, share, hidden), BF16),
        [VMEM, VMEM],
        nbytes=6 * share * hidden * 2,
        name="sum_both",
    )(here, there)
    gathered = exchange([summed] * half, "dom")
    hid = call(
        functools.partial(finish_nodes, half, slots, norm_scale, at),
        [shape((rows_here + EXTRA, wide), BF16)] * groups,
        [SMEM, VMEM, VMEM, VMEM] + [VMEM] * peers,
        [pltpu.VMEM((blocks, tile, wide), F32)],
        nbytes=domains * slots * tile * wide * 2 + blocks * tile * wide * 6,
        name="finish_nodes",
    )(tab, back, bias_here, returned, *terms)
    gathered, _ = lax.optimization_barrier((gathered, hid))
    hid = exchange(hid, "grp")
    grad_nodes, grad_bias = call(
        functools.partial(node_grads, groups),
        [shape((rows_here, embed), BF16), shape((1, hidden), F32)],
        [SMEM, VMEM] + [VMEM] * groups,
        [pltpu.VMEM((groups, rows_here + EXTRA, wide), BF16)],
        flops=2 * rows_here * embed * hidden,
        nbytes=embed * hidden * 2 + rows_here * (embed + hidden) * 2,
        name="node_grads",
    )(ids, weight, *hid)
    joined = call(
        join_shares,
        shape((domains, share, hidden), BF16),
        [SMEM] + [VMEM] * half,
        nbytes=4 * narrow * hidden,
        name="join_shares",
    )(ids, *gathered).reshape(narrow, hidden)
    count = groups // 2
    placing = dict(
        out_shape=shape((embed, hidden), F32),
        scratch=[pltpu.VMEM((count, narrow, hidden), F32), pltpu.SemaphoreType.DMA((count, COPIES))],
        nbytes=embed * hidden * 3,
        name="place_weight",
        out_specs=pl.BlockSpec(memory_space=pl.ANY),
    )
    across = swap(joined, "grp", count)
    parts, masks = spread(joined, "grp", count // 2)
    grad_weight = call(
        functools.partial(place_weight, masks),
        specs=[SMEM] + [VMEM] * count,
        **placing,
    )(ids, *parts)
    across, grad_weight, grad_nodes = lax.optimization_barrier((across, grad_weight, grad_nodes))
    parts, masks = spread(across, "grp", count // 2)
    grad_weight = call(
        functools.partial(place_weight, [mask + count for mask in masks]),
        specs=[SMEM] + [VMEM] * count + [pl.BlockSpec(memory_space=pl.ANY)],
        aliases={count + 1: 0},
        **placing,
    )(ids, *parts, grad_weight)
    return (activations, grad_nodes, grad_weight, grad_bias.reshape(hidden))


def solution(mesh):
    in_specs = (
        P(("dom", "grp"), None),
        P(),
        P(),
        P(("dom", "grp"), None),
        P(),
        P("dom", None, None),
        P("dom", None, None),
        P("dom", None),
        P(),
        P("dom", None, None),
        P("dom", None, None),
    )
    out_specs = (P(("dom", "grp"), None), P(("dom", "grp"), None), P(), P())
    return jax.shard_map(
        per_device, mesh=mesh, in_specs=in_specs, out_specs=out_specs, check_vma=False
    )
```

```python
import functools

import jax
import jax.numpy as jnp
from jax import lax
from jax.experimental import pallas as pl
from jax.experimental.pallas import tpu as pltpu
from jax.sharding import PartitionSpec as P

VMEM = pl.BlockSpec(memory_space=pltpu.VMEM)
SMEM = pl.BlockSpec(memory_space=pltpu.SMEM)
EXTRA = 16
COPIES = 4
F32 = jnp.float32
BF16 = jnp.bfloat16


def call(
    body, out_shape, specs, scratch=(), flops=0, nbytes=0, name=None, out_specs=None, aliases=(), mib=16
):
    return pl.pallas_call(
        body,
        out_shape=out_shape,
        in_specs=specs,
        out_specs=jax.tree.map(lambda _: VMEM, out_shape) if out_specs is None else out_specs,
        scratch_shapes=list(scratch),
        input_output_aliases=dict(aliases),
        compiler_params=pltpu.CompilerParams(vmem_limit_bytes=mib * 1024 * 1024),
        cost_estimate=pl.CostEstimate(flops=flops, bytes_accessed=nbytes, transcendentals=0),
        name=name,
    )


def shape(dims, kind):
    return jax.ShapeDtypeStruct(tuple(dims), kind)


def dot(a, b):
    return jnp.dot(a, b, preferred_element_type=F32)


def bias_rows(total):
    high = total.astype(BF16).astype(F32)
    rest = jnp.zeros((EXTRA - 2, total.shape[1]), F32)
    return jnp.concatenate([high, total - high, rest], axis=0).astype(BF16)


def aligned(start, step):
    return pl.ds(pl.multiple_of(start * step, step), step)


def swap(value, axis, mask):
    return lax.ppermute(value, axis, [(i, i ^ mask) for i in range(lax.axis_size(axis))])


def exchange(parts, axis):
    return list(parts[:1]) + [swap(part, axis, m) for m, part in enumerate(parts[1:], 1)]


def spread(value, axis, bit):
    parts, masks = [value], [0]
    while bit:
        parts = parts + [swap(part, axis, bit) for part in parts]
        masks = masks + [mask ^ bit for mask in masks]
        bit //= 2
    return parts, masks


def split_features(ids, feats, *refs):
    outs, sems = refs[:-1], refs[-1]
    group = ids[1]
    narrow = outs[0].shape[1]
    copies = [
        pltpu.make_async_copy(
            feats.at[:, aligned(jnp.bitwise_xor(group, m), narrow)], out, sems.at[m]
        )
        for m, out in enumerate(outs)
    ]
    for copy in copies:
        copy.start()
    for copy in copies:
        copy.wait()


def pick_blocks(groups, slots, at, tab, *refs):
    parts, (x, offered, *outs) = refs[:groups], refs[groups:]
    domain, group = tab[at["me"]], tab[at["me"] + 1]
    tile = x.shape[1]
    per = x.shape[0] // groups
    for m, part in enumerate(parts):
        owner = jnp.bitwise_xor(group, m)
        for j in range(per):
            x[owner * per + j] = part[j * tile : (j + 1) * tile]
    for j in range(offered.shape[0]):
        offered[j] = x[tab[at["pub"] + j]]
    for m, out in enumerate(outs, 1):
        reader = jnp.bitwise_xor(domain, m)
        for s in range(slots):
            entry = jnp.maximum(tab[at["out"] + reader * slots + s], 0)
            out[s * tile : (s + 1) * tile] = x[tab[at["pub"] + entry]]


def pick_relayed(slots, at, tab, offered, *outs):
    tile = offered.shape[1]
    for m, out in enumerate(outs, 1):
        reader = jnp.bitwise_xor(tab[at["me"]], m)
        for s in range(slots):
            entry = jnp.maximum(tab[at["out2"] + reader * slots + s], 0)
            out[s * tile : (s + 1) * tile] = offered[entry]


def local_sum(per_row, at, tab, bank, x, out):
    pair = 2 if per_row % 2 == 0 else 1

    @pl.loop(0, out.shape[0])
    def _(r):
        acc = jnp.zeros(out.shape[1:], F32)
        for k in range(0, per_row, pair):
            spots = [r * per_row + k + j for j in range(pair)]
            left = jnp.concatenate([bank[tab[at["banks"] + a]] for a in spots], axis=1)
            right = jnp.concatenate([x[tab[at["cols"] + a]] for a in spots], axis=0)
            acc += dot(left, right)
        out[r] = acc


def halo_adder(slots, at, tab, bank, acc):
    def add(source, get):
        for s in range(slots):
            i = source * slots + s
            entry = tab[at["in"] + i]

            @pl.when(entry >= 0)
            def _(i=i, s=s, entry=entry):
                acc[tab[at["hrows"] + i]] += dot(bank[tab[at["hbanks"] + i]], get(s, entry))

    return add


def add_near(slots, at, tab, bank, local, mirrored, *refs):
    near, acc = refs[:-1], refs[-1]
    domain = tab[at["me"]]
    tile = local.shape[1]
    acc[...] = local[...]
    add = halo_adder(slots, at, tab, bank, acc)
    for m, block in enumerate(near, 1):
        add(jnp.bitwise_xor(domain, m), lambda s, _, block=block: block[s * tile : (s + 1) * tile])
    mirror = jnp.bitwise_xor(domain, len(near) + 1)
    add(mirror, lambda _, entry: mirrored[jnp.maximum(entry, 0)])


def add_far(half, groups, slots, at, tab, bank, local, *refs):
    far, outs, acc = refs[: half - 1], refs[half - 1 : -1], refs[-1]
    domain, group = tab[at["me"]], tab[at["me"] + 1]
    tile = local.shape[1]
    per = local.shape[0] // groups
    acc[...] = local[...]
    add = halo_adder(slots, at, tab, bank, acc)
    for m, block in enumerate(far, half + 1):
        add(jnp.bitwise_xor(domain, m), lambda s, _, block=block: block[s * tile : (s + 1) * tile])
    for m, out in enumerate(outs):
        owner = jnp.bitwise_xor(group, m)
        for j in range(per):
            out[j * tile : (j + 1) * tile] = acc[owner * per + j].astype(BF16)


def dense(groups, ids, weight, bias, cot, *refs):
    parts, (act, grad, *slices) = refs[:groups], refs[groups:]
    group = ids[1]
    narrow = parts[0].shape[1]
    wide = cot.shape[1] // groups
    left = jnp.concatenate([part[...] for part in parts], axis=1)
    spots = [aligned(jnp.bitwise_xor(group, m), narrow) for m in range(groups)]
    pre = dot(left, jnp.concatenate([weight[spot] for spot in spots], axis=0)) + bias[...]
    act[...] = jnp.maximum(pre, 0.0).astype(BF16)
    masked = jnp.where(pre > 0, cot[...].astype(F32), 0.0).astype(BF16)
    for s in range(groups):
        grad[s] = masked[:, s * wide : (s + 1) * wide]
    for m, out in enumerate(slices):
        out[...] = grad[jnp.bitwise_xor(group, m)]


def back_halo(groups, slots, at, tab, bank_t, *refs):
    parts, (own, mine, kept, *terms) = refs[:groups], refs[groups:]
    domain, group = tab[at["me"]], tab[at["me"] + 1]
    tile = bank_t.shape[1]
    per = parts[0].shape[0] // tile
    half = len(terms) + 1
    total = jnp.zeros((1, own.shape[2]), F32)
    for m, part in enumerate(parts):
        owner = jnp.bitwise_xor(group, m)
        piece = part[...]
        total += jnp.sum(piece.astype(F32), axis=0, keepdims=True)
        for j in range(per):
            own[owner * per + j] = piece[j * tile : (j + 1) * tile]
    mine[...] = total
    tail = bias_rows(total)

    def put(out, place, source):
        for s in range(slots):
            i = source * slots + s
            live = (tab[at["in"] + i] >= 0).astype(F32)
            value = dot(bank_t[tab[at["hbanks"] + i]], own[tab[at["hrows"] + i]]) * live
            spot = (place * slots + s) * tile
            out[spot : spot + tile] = value.astype(BF16)

    for m, term in enumerate(terms, 1):
        peer = jnp.bitwise_xor(domain, m)
        put(term, 0, peer)
        put(term, 1, jnp.bitwise_xor(peer, half))
        term[2 * slots * tile :] = tail
    put(kept, 0, jnp.bitwise_xor(domain, half))


def sum_mirror(slots, at, tab, mine, kept, *refs):
    recv, out, acc = refs[:-2], refs[-2], refs[-1]
    domain = tab[at["me"]]
    offered, tile = acc.shape[:2]
    acc[...] = jnp.zeros_like(acc)
    total = mine[...]
    for m, block in enumerate((kept,) + recv):
        reader = jnp.bitwise_xor(domain, m)
        for s in range(slots):
            entry = tab[at["out2"] + reader * slots + s]
            spot = (s + (slots if m else 0)) * tile

            @pl.when(entry >= 0)
            def _(entry=entry, spot=spot, block=block):
                acc[jnp.maximum(entry, 0)] += block[spot : spot + tile].astype(F32)

        if m:
            tail = block[2 * slots * tile :].astype(F32)
            total += tail[0:1] + tail[1:2]
    for j in range(offered):
        out[j * tile : (j + 1) * tile] = acc[j].astype(BF16)
    out[offered * tile :] = bias_rows(total)


def weight_part(groups, *refs):
    aggs, (grad, send, keep) = refs[:groups], refs[groups:]
    right = jnp.concatenate([grad[s] for s in range(groups)], axis=1)
    for m, agg in enumerate(aggs):
        value = lax.dot_general(
            agg[...], right, (((0,), (0,)), ((), ())), preferred_element_type=F32
        )
        out = send if m % 2 else keep
        out[m // 2] = value.astype(out.dtype)


def fold(kept, recv, send, keep):
    for j in range(kept.shape[0]):
        out = send if j % 2 else keep
        out[j // 2] = (kept[j] + recv[j].astype(F32)).astype(out.dtype)


def weight_shares(ids, whole, recv, *refs):
    kept, *outs = refs[:-1]
    total = refs[-1]
    domain = ids[0]
    half = len(outs) + 1
    rows = total.shape[1]
    value = whole[0] + recv[0].astype(F32)
    for d in range(total.shape[0]):
        total[d] = value[d * rows : (d + 1) * rows]
    for m, out in enumerate([kept] + outs):
        peer = jnp.bitwise_xor(domain, m)
        out[0] = total[peer].astype(out.dtype)
        out[1] = total[jnp.bitwise_xor(peer, half)].astype(out.dtype)


def sum_half(kept, *refs):
    recv, out = refs[:-1], refs[-1]
    for i in range(2):
        total = kept[i]
        for block in recv:
            total += block[i].astype(F32)
        out[i] = total.astype(BF16)


def sum_both(scale, here, there, out):
    for i in range(2):
        out[i] = ((here[i].astype(F32) + there[1 - i].astype(F32)) * scale).astype(BF16)


def join_shares(ids, *refs):
    parts, out = refs[:-1], refs[-1]
    for m, part in enumerate(parts):
        owner = jnp.bitwise_xor(ids[0], m)
        out[owner] = part[0]
        out[jnp.bitwise_xor(owner, len(parts))] = part[1]


def back_local(per_row, at, tab, bank_t, own, out):
    out[...] = jnp.zeros_like(out)

    @pl.loop(0, own.shape[0])
    def _(r):
        right = own[r]
        for k in range(per_row):
            spot = r * per_row + k
            out[tab[at["cols"] + spot]] += dot(bank_t[tab[at["banks"] + spot]], right)


def finish_nodes(half, slots, scale, at, tab, local, mine, mirrored, *refs):
    recv, outs, acc = refs[: half - 1], refs[half - 1 : -1], refs[-1]
    groups = len(outs)
    domain, group = tab[at["me"]], tab[at["me"] + 1]
    tile = local.shape[1]
    per = local.shape[0] // groups
    offered = (mirrored.shape[0] - EXTRA) // tile
    acc[...] = local[...]
    tail = mirrored[offered * tile :].astype(F32)
    for j in range(offered):
        acc[tab[at["pub"] + j]] += mirrored[j * tile : (j + 1) * tile].astype(F32)
    for m, block in enumerate(recv, 1):
        tail += block[2 * slots * tile :].astype(F32)
        reader = jnp.bitwise_xor(domain, m)
        for s in range(slots):
            entry = tab[at["out"] + reader * slots + s]

            @pl.when(entry >= 0)
            def _(s=s, entry=entry, block=block):
                spot = tab[at["pub"] + jnp.maximum(entry, 0)]
                acc[spot] += block[s * tile : (s + 1) * tile].astype(F32)

    rows = bias_rows((mine[...] + tail[0:1] + tail[1:2]) * scale)
    for m, out in enumerate(outs):
        owner = jnp.bitwise_xor(group, m)
        for j in range(per):
            out[j * tile : (j + 1) * tile] = acc[owner * per + j].astype(BF16)
        out[per * tile :] = rows


def node_grads(groups, ids, weight, *refs):
    parts, (out, bias_out, hid) = refs[:groups], refs[groups:]
    group = ids[1]
    rows = out.shape[0]
    for m, part in enumerate(parts):
        hid[jnp.bitwise_xor(group, m)] = part[...]
    left = jnp.concatenate([hid[s, :rows] for s in range(groups)], axis=1)
    out[...] = lax.dot_general(
        left, weight[...], (((1,), (1,)), ((), ())), preferred_element_type=F32
    ).astype(BF16)
    tail = jnp.concatenate([hid[s, rows:] for s in range(groups)], axis=1).astype(F32)
    bias_out[...] = tail[0:1] + tail[1:2]


def place_weight(masks, ids, *refs):
    parts, (out, wide, sems) = refs[: len(masks)], refs[-3:]
    group = ids[1]
    rows = parts[0].shape[0]
    copies = []
    step = rows // COPIES
    for i, (mask, part) in enumerate(zip(masks, parts)):
        for j in range(COPIES):
            wide[i, j * step : (j + 1) * step] = part[j * step : (j + 1) * step].astype(F32)
            spot = out.at[aligned(jnp.bitwise_xor(group, mask) * COPIES + j, step)]
            piece = wide.at[i, pl.ds(j * step, step)]
            copies.append(pltpu.make_async_copy(piece, spot, sems.at[i, j]))
            copies[-1].start()
    for copy in copies:
        copy.wait()


def per_device(
    node_feats,
    weight,
    bias,
    cotangent,
    tile_bank,
    local_cols,
    local_banks,
    published,
    send_table,
    halo_rows,
    halo_banks,
):
    domains = lax.axis_size("dom")
    groups = lax.axis_size("grp")
    domain_index = lax.axis_index("dom")
    rows_here, embed = node_feats.shape
    hidden = weight.shape[1]
    tile = tile_bank.shape[1]
    slots = send_table.shape[2]
    per_row = local_cols.shape[2]
    part_rows = rows_here * groups
    blocks = part_rows // tile
    narrow = embed // groups
    wide = hidden // groups
    share = narrow // domains
    half = domains // 2
    peers = half - 1
    offers = published.shape[1]

    ids = jnp.stack([domain_index, lax.axis_index("grp")]).astype(jnp.int32)
    tables = {
        "cols": local_cols[0],
        "banks": local_banks[0],
        "pub": published[0],
        "out": lax.dynamic_index_in_dim(send_table, domain_index, 0, keepdims=False),
        "out2": lax.dynamic_index_in_dim(send_table, domain_index ^ half, 0, keepdims=False),
        "in": lax.dynamic_index_in_dim(send_table, domain_index, 1, keepdims=False),
        "hrows": halo_rows[0],
        "hbanks": halo_banks[0],
        "me": ids,
    }
    at, place = {}, 0
    for name, table in tables.items():
        at[name] = place
        place += table.size
    tab = jnp.concatenate([table.reshape(-1) for table in tables.values()])
    bank_t = jnp.swapaxes(tile_bank, 1, 2)

    feats = call(
        split_features,
        [shape((rows_here, narrow), BF16)] * groups,
        [SMEM, pl.BlockSpec(memory_space=pl.ANY)],
        [pltpu.SemaphoreType.DMA((groups,))],
        nbytes=4 * rows_here * embed,
        name="split_features",
    )(ids, node_feats)
    feats = exchange(feats, "grp")
    x, offered, *picked = call(
        functools.partial(pick_blocks, groups, slots, at),
        [shape((blocks, tile, narrow), BF16), shape((offers, tile, narrow), BF16)]
        + [shape((slots * tile, narrow), BF16)] * peers,
        [SMEM] + [VMEM] * groups,
        nbytes=4 * (peers * slots + blocks + offers) * tile * narrow,
        name="pick_blocks",
    )(tab, *feats)
    mirrored = swap(offered, "dom", half)
    near = exchange([None] + picked, "dom")[1:]
    local = call(
        functools.partial(local_sum, per_row, at),
        shape((blocks, tile, narrow), F32),
        [SMEM, VMEM, VMEM],
        flops=2 * blocks * per_row * tile * tile * narrow,
        nbytes=blocks * tile * narrow * 6,
        name="local_sum",
    )(tab, tile_bank, x)
    mirrored, local = lax.optimization_barrier((mirrored, local))
    relayed = call(
        functools.partial(pick_relayed, slots, at),
        [shape((slots * tile, narrow), BF16)] * peers,
        [SMEM, VMEM],
        nbytes=4 * peers * slots * tile * narrow,
        name="pick_relayed",
    )(tab, mirrored)
    far = exchange([None, *relayed], "dom")[1:]
    local = call(
        functools.partial(add_near, slots, at),
        shape((blocks, tile, narrow), F32),
        [SMEM, VMEM, VMEM, VMEM] + [VMEM] * peers,
        flops=2 * half * slots * tile * tile * narrow,
        nbytes=blocks * tile * narrow * 8,
        name="add_near",
    )(tab, tile_bank, local, mirrored, *near)
    far, local = lax.optimization_barrier((far, local))
    aggs = call(
        functools.partial(add_far, half, groups, slots, at),
        [shape((rows_here, narrow), BF16)] * groups,
        [SMEM, VMEM, VMEM] + [VMEM] * peers,
        [pltpu.VMEM((blocks, tile, narrow), F32)],
        flops=2 * half * slots * tile * tile * narrow,
        nbytes=blocks * tile * narrow * 8,
        name="add_far",
    )(tab, tile_bank, local, *far)
    mine = exchange(aggs, "grp")
    activations, grad, *grads = call(
        functools.partial(dense, groups),
        [shape((rows_here, hidden), BF16), shape((groups, rows_here, wide), BF16)]
        + [shape((rows_here, wide), BF16)] * groups,
        [SMEM] + [VMEM] * (3 + groups),
        flops=2 * rows_here * embed * hidden,
        nbytes=embed * hidden * 2 + rows_here * (embed + 4 * hidden) * 2,
        name="dense",
    )(ids, weight, bias.reshape(1, hidden), cotangent, *mine)
    grads = exchange(grads, "grp")
    norm_scale = float(rows_here * groups * domains) ** (-0.5)
    norm_scale = float(rows_here * groups * domains) ** (-0.5)
    send, keep = call(
        functools.partial(weight_part, groups),
        [
            shape((groups // 2, narrow, hidden), BF16),
            shape((groups // 2, narrow, hidden), F32),
        ],
        [VMEM] * (groups + 1),
        flops=2 * rows_here * embed * hidden,
        nbytes=rows_here * (embed + hidden) * 2 + embed * hidden * 3,
        name="weight_part",
    )(*mine, grad)
    tab_after, _ = lax.optimization_barrier((tab, send))
    own, bias_here, kept, *terms = call(
        functools.partial(back_halo, groups, slots, at),
        [
            shape((blocks, tile, wide), BF16),
            shape((1, wide), F32),
            shape((slots * tile, wide), BF16),
        ]
        + [shape((2 * slots * tile + EXTRA, wide), BF16)] * peers,
        [SMEM, VMEM] + [VMEM] * groups,
        flops=2 * domains * slots * tile * tile * wide,
        nbytes=(domains * slots + blocks) * tile * wide * 2,
        name="back_halo",
    )(tab_after, bank_t, *grads)
    sent, terms = terms, exchange([None] + terms, "dom")[1:]
    recv = swap(send, "grp", 1)
    recv, _ = lax.optimization_barrier((recv, sent))
    bit = 2
    while bit < groups:
        count = groups // (2 * bit)
        send, keep = call(
            fold,
            [shape((count, narrow, hidden), BF16), shape((count, narrow, hidden), F32)],
            [VMEM, VMEM],
            nbytes=count * narrow * hidden * 18,
            name="fold",
        )(keep, recv)
        recv = swap(send, "grp", bit)
        bit *= 2
    recv, terms[0] = lax.optimization_barrier((recv, terms[0]))
    kept_shares, *shares = call(
        weight_shares,
        [shape((2, share, hidden), F32)] + [shape((2, share, hidden), BF16)] * peers,
        [SMEM, VMEM, VMEM],
        [pltpu.VMEM((domains, share, hidden), F32)],
        nbytes=narrow * hidden * 8,
        name="weight_shares",
    )(ids, keep, recv)
    terms, _ = lax.optimization_barrier((terms, shares))
    shares = exchange([None] + shares, "dom")[1:]
    crossing = call(
        functools.partial(sum_mirror, slots, at),
        shape((offers * tile + EXTRA, wide), BF16),
        [SMEM] + [VMEM] * (2 + peers),
        [pltpu.VMEM((offers, tile, wide), F32)],
        nbytes=4 * domains * slots * tile * wide,
        name="sum_mirror",
    )(tab, bias_here, kept, *terms)
    returned = swap(crossing, "dom", half)
    shares, _ = lax.optimization_barrier((shares, crossing))
    here = call(
        sum_half,
        shape((2, share, hidden), BF16),
        [VMEM] * half,
        nbytes=2 * half * share * hidden * 2,
        name="sum_half",
    )(kept_shares, *shares)
    there = swap(here, "dom", half)
    own, _ = lax.optimization_barrier((own, here))
    back = call(
        functools.partial(back_local, per_row, at),
        shape((blocks, tile, wide), F32),
        [SMEM, VMEM, VMEM],
        flops=2 * blocks * per_row * tile * tile * wide,
        nbytes=blocks * tile * wide * 6,
        name="back_local",
    )(tab, bank_t, own)
    there, back = lax.optimization_barrier((there, back))
    summed = call(
        functools.partial(sum_both, norm_scale),
        shape((2, share, hidden), BF16),
        [VMEM, VMEM],
        nbytes=6 * share * hidden * 2,
        name="sum_both",
    )(here, there)
    gathered = exchange([summed] * half, "dom")
    hid = call(
        functools.partial(finish_nodes, half, slots, norm_scale, at),
        [shape((rows_here + EXTRA, wide), BF16)] * groups,
        [SMEM, VMEM, VMEM, VMEM] + [VMEM] * peers,
        [pltpu.VMEM((blocks, tile, wide), F32)],
        nbytes=domains * slots * tile * wide * 2 + blocks * tile * wide * 6,
        name="finish_nodes",
    )(tab, back, bias_here, returned, *terms)
    hid = exchange(hid, "grp")
    gathered, hid = lax.optimization_barrier((gathered, hid))
    grad_nodes, grad_bias = call(
        functools.partial(node_grads, groups),
        [shape((rows_here, embed), BF16), shape((1, hidden), F32)],
        [SMEM, VMEM] + [VMEM] * groups,
        [pltpu.VMEM((groups, rows_here + EXTRA, wide), BF16)],
        flops=2 * rows_here * embed * hidden,
        nbytes=embed * hidden * 2 + rows_here * (embed + hidden) * 2,
        name="node_grads",
    )(ids, weight, *hid)
    joined = call(
        join_shares,
        shape((domains, share, hidden), BF16),
        [SMEM] + [VMEM] * half,
        nbytes=4 * narrow * hidden,
        name="join_shares",
    )(ids, *gathered).reshape(narrow, hidden)
    count = groups // 2
    placing = dict(
        out_shape=shape((embed, hidden), F32),
        scratch=[pltpu.VMEM((count, narrow, hidden), F32), pltpu.SemaphoreType.DMA((count, COPIES))],
        nbytes=embed * hidden * 3,
        name="place_weight",
        out_specs=pl.BlockSpec(memory_space=pl.ANY),
    )
    across = swap(joined, "grp", count)
    parts, masks = spread(joined, "grp", count // 2)
    grad_weight = call(
        functools.partial(place_weight, masks),
        specs=[SMEM] + [VMEM] * count,
        **placing,
    )(ids, *parts)
    across, grad_weight, grad_nodes = lax.optimization_barrier((across, grad_weight, grad_nodes))
    parts, masks = spread(across, "grp", count // 2)
    grad_weight = call(
        functools.partial(place_weight, [mask + count for mask in masks]),
        specs=[SMEM] + [VMEM] * count + [pl.BlockSpec(memory_space=pl.ANY)],
        aliases={count + 1: 0},
        **placing,
    )(ids, *parts, grad_weight)
    return (activations, grad_nodes, grad_weight, grad_bias.reshape(hidden))


def solution(mesh):
    in_specs = (
        P(("dom", "grp"), None),
        P(),
        P(),
        P(("dom", "grp"), None),
        P(),
        P("dom", None, None),
        P("dom", None, None),
        P("dom", None),
        P(),
        P("dom", None, None),
        P("dom", None, None),
    )
    out_specs = (P(("dom", "grp"), None), P(("dom", "grp"), None), P(), P())
    return jax.shard_map(
        per_device, mesh=mesh, in_specs=in_specs, out_specs=out_specs, check_vma=False
    )
```

```python
import functools

import jax
import jax.numpy as jnp
from jax import lax
from jax.experimental import pallas as pl
from jax.experimental.pallas import tpu as pltpu
from jax.sharding import PartitionSpec as P

VMEM = pl.BlockSpec(memory_space=pltpu.VMEM)
SMEM = pl.BlockSpec(memory_space=pltpu.SMEM)
EXTRA = 16
COPIES = 4
F32 = jnp.float32
BF16 = jnp.bfloat16


def call(
    body, out_shape, specs, scratch=(), flops=0, nbytes=0, name=None, out_specs=None, aliases=(), mib=16
):
    return pl.pallas_call(
        body,
        out_shape=out_shape,
        in_specs=specs,
        out_specs=jax.tree.map(lambda _: VMEM, out_shape) if out_specs is None else out_specs,
        scratch_shapes=list(scratch),
        input_output_aliases=dict(aliases),
        compiler_params=pltpu.CompilerParams(vmem_limit_bytes=mib * 1024 * 1024),
        cost_estimate=pl.CostEstimate(flops=flops, bytes_accessed=nbytes, transcendentals=0),
        name=name,
    )


def shape(dims, kind):
    return jax.ShapeDtypeStruct(tuple(dims), kind)


def dot(a, b):
    return jnp.dot(a, b, preferred_element_type=F32)


def bias_rows(total):
    high = total.astype(BF16).astype(F32)
    rest = jnp.zeros((EXTRA - 2, total.shape[1]), F32)
    return jnp.concatenate([high, total - high, rest], axis=0).astype(BF16)


def aligned(start, step):
    return pl.ds(pl.multiple_of(start * step, step), step)


def swap(value, axis, mask):
    return lax.ppermute(value, axis, [(i, i ^ mask) for i in range(lax.axis_size(axis))])


def exchange(parts, axis):
    return list(parts[:1]) + [swap(part, axis, m) for m, part in enumerate(parts[1:], 1)]


def spread(value, axis, bit):
    parts, masks = [value], [0]
    while bit:
        parts = parts + [swap(part, axis, bit) for part in parts]
        masks = masks + [mask ^ bit for mask in masks]
        bit //= 2
    return parts, masks


def split_features(ids, feats, *refs):
    outs, sems = refs[:-1], refs[-1]
    group = ids[1]
    narrow = outs[0].shape[1]
    copies = [
        pltpu.make_async_copy(
            feats.at[:, aligned(jnp.bitwise_xor(group, m), narrow)], out, sems.at[m]
        )
        for m, out in enumerate(outs)
    ]
    for copy in copies:
        copy.start()
    for copy in copies:
        copy.wait()


def pick_blocks(groups, slots, at, tab, *refs):
    parts, (x, offered, *outs) = refs[:groups], refs[groups:]
    domain, group = tab[at["me"]], tab[at["me"] + 1]
    tile = x.shape[1]
    per = x.shape[0] // groups
    for m, part in enumerate(parts):
        owner = jnp.bitwise_xor(group, m)
        for j in range(per):
            x[owner * per + j] = part[j * tile : (j + 1) * tile]
    for j in range(offered.shape[0]):
        offered[j] = x[tab[at["pub"] + j]]
    for m, out in enumerate(outs, 1):
        reader = jnp.bitwise_xor(domain, m)
        for s in range(slots):
            entry = jnp.maximum(tab[at["out"] + reader * slots + s], 0)
            out[s * tile : (s + 1) * tile] = x[tab[at["pub"] + entry]]


def pick_relayed(slots, at, tab, offered, *outs):
    tile = offered.shape[1]
    for m, out in enumerate(outs, 1):
        reader = jnp.bitwise_xor(tab[at["me"]], m)
        for s in range(slots):
            entry = jnp.maximum(tab[at["out2"] + reader * slots + s], 0)
            out[s * tile : (s + 1) * tile] = offered[entry]


def local_sum(per_row, at, tab, bank, x, out):
    pair = 2 if per_row % 2 == 0 else 1

    @pl.loop(0, out.shape[0])
    def _(r):
        acc = jnp.zeros(out.shape[1:], F32)
        for k in range(0, per_row, pair):
            spots = [r * per_row + k + j for j in range(pair)]
            left = jnp.concatenate([bank[tab[at["banks"] + a]] for a in spots], axis=1)
            right = jnp.concatenate([x[tab[at["cols"] + a]] for a in spots], axis=0)
            acc += dot(left, right)
        out[r] = acc


def halo_adder(slots, at, tab, bank, acc):
    def add(source, get):
        for s in range(slots):
            i = source * slots + s
            entry = tab[at["in"] + i]

            @pl.when(entry >= 0)
            def _(i=i, s=s, entry=entry):
                acc[tab[at["hrows"] + i]] += dot(bank[tab[at["hbanks"] + i]], get(s, entry))

    return add


def add_near(slots, at, tab, bank, local, mirrored, *refs):
    near, acc = refs[:-1], refs[-1]
    domain = tab[at["me"]]
    tile = local.shape[1]
    acc[...] = local[...]
    add = halo_adder(slots, at, tab, bank, acc)
    for m, block in enumerate(near, 1):
        add(jnp.bitwise_xor(domain, m), lambda s, _, block=block: block[s * tile : (s + 1) * tile])
    mirror = jnp.bitwise_xor(domain, len(near) + 1)
    add(mirror, lambda _, entry: mirrored[jnp.maximum(entry, 0)])


def add_far(half, groups, slots, at, tab, bank, local, *refs):
    far, outs, acc = refs[: half - 1], refs[half - 1 : -1], refs[-1]
    domain, group = tab[at["me"]], tab[at["me"] + 1]
    tile = local.shape[1]
    per = local.shape[0] // groups
    acc[...] = local[...]
    add = halo_adder(slots, at, tab, bank, acc)
    for m, block in enumerate(far, half + 1):
        add(jnp.bitwise_xor(domain, m), lambda s, _, block=block: block[s * tile : (s + 1) * tile])
    for m, out in enumerate(outs):
        owner = jnp.bitwise_xor(group, m)
        for j in range(per):
            out[j * tile : (j + 1) * tile] = acc[owner * per + j].astype(BF16)


def dense(groups, ids, weight, bias, cot, *refs):
    parts, (act, grad, *slices) = refs[:groups], refs[groups:]
    group = ids[1]
    narrow = parts[0].shape[1]
    wide = cot.shape[1] // groups
    left = jnp.concatenate([part[...] for part in parts], axis=1)
    spots = [aligned(jnp.bitwise_xor(group, m), narrow) for m in range(groups)]
    pre = dot(left, jnp.concatenate([weight[spot] for spot in spots], axis=0)) + bias[...]
    act[...] = jnp.maximum(pre, 0.0).astype(BF16)
    masked = jnp.where(pre > 0, cot[...].astype(F32), 0.0).astype(BF16)
    for s in range(groups):
        grad[s] = masked[:, s * wide : (s + 1) * wide]
    for m, out in enumerate(slices):
        out[...] = grad[jnp.bitwise_xor(group, m)]


def back_halo(groups, slots, at, tab, bank_t, *refs):
    parts, (own, mine, kept, *terms) = refs[:groups], refs[groups:]
    domain, group = tab[at["me"]], tab[at["me"] + 1]
    tile = bank_t.shape[1]
    per = parts[0].shape[0] // tile
    half = len(terms) + 1
    total = jnp.zeros((1, own.shape[2]), F32)
    for m, part in enumerate(parts):
        owner = jnp.bitwise_xor(group, m)
        piece = part[...]
        total += jnp.sum(piece.astype(F32), axis=0, keepdims=True)
        for j in range(per):
            own[owner * per + j] = piece[j * tile : (j + 1) * tile]
    mine[...] = total
    tail = bias_rows(total)

    def put(out, place, source):
        for s in range(slots):
            i = source * slots + s
            live = (tab[at["in"] + i] >= 0).astype(F32)
            value = dot(bank_t[tab[at["hbanks"] + i]], own[tab[at["hrows"] + i]]) * live
            spot = (place * slots + s) * tile
            out[spot : spot + tile] = value.astype(BF16)

    for m, term in enumerate(terms, 1):
        peer = jnp.bitwise_xor(domain, m)
        put(term, 0, peer)
        put(term, 1, jnp.bitwise_xor(peer, half))
        term[2 * slots * tile :] = tail
    put(kept, 0, jnp.bitwise_xor(domain, half))


def sum_mirror(slots, at, tab, mine, kept, *refs):
    recv, out, acc = refs[:-2], refs[-2], refs[-1]
    domain = tab[at["me"]]
    offered, tile = acc.shape[:2]
    acc[...] = jnp.zeros_like(acc)
    total = mine[...]
    for m, block in enumerate((kept,) + recv):
        reader = jnp.bitwise_xor(domain, m)
        for s in range(slots):
            entry = tab[at["out2"] + reader * slots + s]
            spot = (s + (slots if m else 0)) * tile

            @pl.when(entry >= 0)
            def _(entry=entry, spot=spot, block=block):
                acc[jnp.maximum(entry, 0)] += block[spot : spot + tile].astype(F32)

        if m:
            tail = block[2 * slots * tile :].astype(F32)
            total += tail[0:1] + tail[1:2]
    for j in range(offered):
        out[j * tile : (j + 1) * tile] = acc[j].astype(BF16)
    out[offered * tile :] = bias_rows(total)


def weight_part(groups, *refs):
    aggs, (grad, send, keep) = refs[:groups], refs[groups:]
    right = jnp.concatenate([grad[s] for s in range(groups)], axis=1)
    for m, agg in enumerate(aggs):
        value = lax.dot_general(
            agg[...], right, (((0,), (0,)), ((), ())), preferred_element_type=F32
        )
        out = send if m % 2 else keep
        out[m // 2] = value.astype(out.dtype)


def fold(kept, recv, send, keep):
    for j in range(kept.shape[0]):
        out = send if j % 2 else keep
        out[j // 2] = (kept[j] + recv[j].astype(F32)).astype(out.dtype)


def weight_shares(ids, whole, recv, *refs):
    kept, *outs = refs[:-1]
    total = refs[-1]
    domain = ids[0]
    half = len(outs) + 1
    rows = total.shape[1]
    value = whole[0] + recv[0].astype(F32)
    for d in range(total.shape[0]):
        total[d] = value[d * rows : (d + 1) * rows]
    for m, out in enumerate([kept] + outs):
        peer = jnp.bitwise_xor(domain, m)
        out[0] = total[peer].astype(out.dtype)
        out[1] = total[jnp.bitwise_xor(peer, half)].astype(out.dtype)


def sum_half(kept, *refs):
    recv, out = refs[:-1], refs[-1]
    for i in range(2):
        total = kept[i]
        for block in recv:
            total += block[i].astype(F32)
        out[i] = total.astype(BF16)


def sum_both(scale, here, there, out):
    for i in range(2):
        out[i] = ((here[i].astype(F32) + there[1 - i].astype(F32)) * scale).astype(BF16)


def join_shares(ids, *refs):
    parts, out = refs[:-1], refs[-1]
    for m, part in enumerate(parts):
        owner = jnp.bitwise_xor(ids[0], m)
        out[owner] = part[0]
        out[jnp.bitwise_xor(owner, len(parts))] = part[1]


def back_local(per_row, at, tab, bank_t, own, out):
    out[...] = jnp.zeros_like(out)

    @pl.loop(0, own.shape[0])
    def _(r):
        right = own[r]
        for k in range(per_row):
            spot = r * per_row + k
            out[tab[at["cols"] + spot]] += dot(bank_t[tab[at["banks"] + spot]], right)


def finish_nodes(half, slots, scale, at, tab, local, mine, mirrored, *refs):
    recv, outs, acc = refs[: half - 1], refs[half - 1 : -1], refs[-1]
    groups = len(outs)
    domain, group = tab[at["me"]], tab[at["me"] + 1]
    tile = local.shape[1]
    per = local.shape[0] // groups
    offered = (mirrored.shape[0] - EXTRA) // tile
    acc[...] = local[...]
    tail = mirrored[offered * tile :].astype(F32)
    for j in range(offered):
        acc[tab[at["pub"] + j]] += mirrored[j * tile : (j + 1) * tile].astype(F32)
    for m, block in enumerate(recv, 1):
        tail += block[2 * slots * tile :].astype(F32)
        reader = jnp.bitwise_xor(domain, m)
        for s in range(slots):
            entry = tab[at["out"] + reader * slots + s]

            @pl.when(entry >= 0)
            def _(s=s, entry=entry, block=block):
                spot = tab[at["pub"] + jnp.maximum(entry, 0)]
                acc[spot] += block[s * tile : (s + 1) * tile].astype(F32)

    rows = bias_rows((mine[...] + tail[0:1] + tail[1:2]) * scale)
    for m, out in enumerate(outs):
        owner = jnp.bitwise_xor(group, m)
        for j in range(per):
            out[j * tile : (j + 1) * tile] = acc[owner * per + j].astype(BF16)
        out[per * tile :] = rows


def node_grads(groups, ids, weight, *refs):
    parts, (out, bias_out, hid) = refs[:groups], refs[groups:]
    group = ids[1]
    rows = out.shape[0]
    for m, part in enumerate(parts):
        hid[jnp.bitwise_xor(group, m)] = part[...]
    left = jnp.concatenate([hid[s, :rows] for s in range(groups)], axis=1)
    out[...] = lax.dot_general(
        left, weight[...], (((1,), (1,)), ((), ())), preferred_element_type=F32
    ).astype(BF16)
    tail = jnp.concatenate([hid[s, rows:] for s in range(groups)], axis=1).astype(F32)
    bias_out[...] = tail[0:1] + tail[1:2]


def place_weight(masks, ids, *refs):
    parts, (out, wide, sems) = refs[: len(masks)], refs[-3:]
    group = ids[1]
    rows = parts[0].shape[0]
    copies = []
    step = rows // COPIES
    for i, (mask, part) in enumerate(zip(masks, parts)):
        for j in range(COPIES):
            wide[i, j * step : (j + 1) * step] = part[j * step : (j + 1) * step].astype(F32)
            spot = out.at[aligned(jnp.bitwise_xor(group, mask) * COPIES + j, step)]
            piece = wide.at[i, pl.ds(j * step, step)]
            copies.append(pltpu.make_async_copy(piece, spot, sems.at[i, j]))
            copies[-1].start()
    for copy in copies:
        copy.wait()


def per_device(
    node_feats,
    weight,
    bias,
    cotangent,
    tile_bank,
    local_cols,
    local_banks,
    published,
    send_table,
    halo_rows,
    halo_banks,
):
    domains = lax.axis_size("dom")
    groups = lax.axis_size("grp")
    domain_index = lax.axis_index("dom")
    rows_here, embed = node_feats.shape
    hidden = weight.shape[1]
    tile = tile_bank.shape[1]
    slots = send_table.shape[2]
    per_row = local_cols.shape[2]
    part_rows = rows_here * groups
    blocks = part_rows // tile
    narrow = embed // groups
    wide = hidden // groups
    share = narrow // domains
    half = domains // 2
    peers = half - 1
    offers = published.shape[1]

    ids = jnp.stack([domain_index, lax.axis_index("grp")]).astype(jnp.int32)
    tables = {
        "cols": local_cols[0],
        "banks": local_banks[0],
        "pub": published[0],
        "out": lax.dynamic_index_in_dim(send_table, domain_index, 0, keepdims=False),
        "out2": lax.dynamic_index_in_dim(send_table, domain_index ^ half, 0, keepdims=False),
        "in": lax.dynamic_index_in_dim(send_table, domain_index, 1, keepdims=False),
        "hrows": halo_rows[0],
        "hbanks": halo_banks[0],
        "me": ids,
    }
    at, place = {}, 0
    for name, table in tables.items():
        at[name] = place
        place += table.size
    tab = jnp.concatenate([table.reshape(-1) for table in tables.values()])
    bank_t = jnp.swapaxes(tile_bank, 1, 2)

    feats = call(
        split_features,
        [shape((rows_here, narrow), BF16)] * groups,
        [SMEM, pl.BlockSpec(memory_space=pl.ANY)],
        [pltpu.SemaphoreType.DMA((groups,))],
        nbytes=4 * rows_here * embed,
        name="split_features",
    )(ids, node_feats)
    feats = exchange(feats, "grp")
    x, offered, *picked = call(
        functools.partial(pick_blocks, groups, slots, at),
        [shape((blocks, tile, narrow), BF16), shape((offers, tile, narrow), BF16)]
        + [shape((slots * tile, narrow), BF16)] * peers,
        [SMEM] + [VMEM] * groups,
        nbytes=4 * (peers * slots + blocks + offers) * tile * narrow,
        name="pick_blocks",
    )(tab, *feats)
    mirrored = swap(offered, "dom", half)
    near = exchange([None] + picked, "dom")[1:]
    local = call(
        functools.partial(local_sum, per_row, at),
        shape((blocks, tile, narrow), F32),
        [SMEM, VMEM, VMEM],
        flops=2 * blocks * per_row * tile * tile * narrow,
        nbytes=blocks * tile * narrow * 6,
        name="local_sum",
    )(tab, tile_bank, x)
    mirrored, local = lax.optimization_barrier((mirrored, local))
    relayed = call(
        functools.partial(pick_relayed, slots, at),
        [shape((slots * tile, narrow), BF16)] * peers,
        [SMEM, VMEM],
        nbytes=4 * peers * slots * tile * narrow,
        name="pick_relayed",
    )(tab, mirrored)
    far = exchange([None, *relayed], "dom")[1:]
    local = call(
        functools.partial(add_near, slots, at),
        shape((blocks, tile, narrow), F32),
        [SMEM, VMEM, VMEM, VMEM] + [VMEM] * peers,
        flops=2 * half * slots * tile * tile * narrow,
        nbytes=blocks * tile * narrow * 8,
        name="add_near",
    )(tab, tile_bank, local, mirrored, *near)
    far, local = lax.optimization_barrier((far, local))
    aggs = call(
        functools.partial(add_far, half, groups, slots, at),
        [shape((rows_here, narrow), BF16)] * groups,
        [SMEM, VMEM, VMEM] + [VMEM] * peers,
        [pltpu.VMEM((blocks, tile, narrow), F32)],
        flops=2 * half * slots * tile * tile * narrow,
        nbytes=blocks * tile * narrow * 8,
        name="add_far",
    )(tab, tile_bank, local, *far)
    mine = exchange(aggs, "grp")
    activations, grad, *grads = call(
        functools.partial(dense, groups),
        [shape((rows_here, hidden), BF16), shape((groups, rows_here, wide), BF16)]
        + [shape((rows_here, wide), BF16)] * groups,
        [SMEM] + [VMEM] * (3 + groups),
        flops=2 * rows_here * embed * hidden,
        nbytes=embed * hidden * 2 + rows_here * (embed + 4 * hidden) * 2,
        name="dense",
    )(ids, weight, bias.reshape(1, hidden), cotangent, *mine)
    grads = exchange(grads, "grp")
    norm_scale = float(rows_here * groups * domains) ** (-0.5)
    norm_scale = float(rows_here * groups * domains) ** (-0.5)
    send, keep = call(
        functools.partial(weight_part, groups),
        [
            shape((groups // 2, narrow, hidden), BF16),
            shape((groups // 2, narrow, hidden), F32),
        ],
        [VMEM] * (groups + 1),
        flops=2 * rows_here * embed * hidden,
        nbytes=rows_here * (embed + hidden) * 2 + embed * hidden * 3,
        name="weight_part",
    )(*mine, grad)
    recv = swap(send, "grp", 1)
    recv, grads = lax.optimization_barrier((recv, grads))
    bit = 2
    while bit < groups:
        count = groups // (2 * bit)
        send, keep = call(
            fold,
            [shape((count, narrow, hidden), BF16), shape((count, narrow, hidden), F32)],
            [VMEM, VMEM],
            nbytes=count * narrow * hidden * 18,
            name="fold",
        )(keep, recv)
        recv = swap(send, "grp", bit)
        bit *= 2
    tab_after, _ = lax.optimization_barrier((tab, send))
    own, bias_here, kept, *terms = call(
        functools.partial(back_halo, groups, slots, at),
        [
            shape((blocks, tile, wide), BF16),
            shape((1, wide), F32),
            shape((slots * tile, wide), BF16),
        ]
        + [shape((2 * slots * tile + EXTRA, wide), BF16)] * peers,
        [SMEM, VMEM] + [VMEM] * groups,
        flops=2 * domains * slots * tile * tile * wide,
        nbytes=(domains * slots + blocks) * tile * wide * 2,
        name="back_halo",
    )(tab_after, bank_t, *grads)
    terms = exchange([None] + terms, "dom")[1:]
    recv, terms[0] = lax.optimization_barrier((recv, terms[0]))
    kept_shares, *shares = call(
        weight_shares,
        [shape((2, share, hidden), F32)] + [shape((2, share, hidden), BF16)] * peers,
        [SMEM, VMEM, VMEM],
        [pltpu.VMEM((domains, share, hidden), F32)],
        nbytes=narrow * hidden * 8,
        name="weight_shares",
    )(ids, keep, recv)
    terms, _ = lax.optimization_barrier((terms, shares))
    shares = exchange([None] + shares, "dom")[1:]
    crossing = call(
        functools.partial(sum_mirror, slots, at),
        shape((offers * tile + EXTRA, wide), BF16),
        [SMEM] + [VMEM] * (2 + peers),
        [pltpu.VMEM((offers, tile, wide), F32)],
        nbytes=4 * domains * slots * tile * wide,
        name="sum_mirror",
    )(tab, bias_here, kept, *terms)
    returned = swap(crossing, "dom", half)
    shares, _ = lax.optimization_barrier((shares, crossing))
    here = call(
        sum_half,
        shape((2, share, hidden), BF16),
        [VMEM] * half,
        nbytes=2 * half * share * hidden * 2,
        name="sum_half",
    )(kept_shares, *shares)
    there = swap(here, "dom", half)
    own, _ = lax.optimization_barrier((own, here))
    back = call(
        functools.partial(back_local, per_row, at),
        shape((blocks, tile, wide), F32),
        [SMEM, VMEM, VMEM],
        flops=2 * blocks * per_row * tile * tile * wide,
        nbytes=blocks * tile * wide * 6,
        name="back_local",
    )(tab, bank_t, own)
    there, back = lax.optimization_barrier((there, back))
    summed = call(
        functools.partial(sum_both, norm_scale),
        shape((2, share, hidden), BF16),
        [VMEM, VMEM],
        nbytes=6 * share * hidden * 2,
        name="sum_both",
    )(here, there)
    gathered = exchange([summed] * half, "dom")
    hid = call(
        functools.partial(finish_nodes, half, slots, norm_scale, at),
        [shape((rows_here + EXTRA, wide), BF16)] * groups,
        [SMEM, VMEM, VMEM, VMEM] + [VMEM] * peers,
        [pltpu.VMEM((blocks, tile, wide), F32)],
        nbytes=domains * slots * tile * wide * 2 + blocks * tile * wide * 6,
        name="finish_nodes",
    )(tab, back, bias_here, returned, *terms)
    hid = exchange(hid, "grp")
    gathered, hid = lax.optimization_barrier((gathered, hid))
    grad_nodes, grad_bias = call(
        functools.partial(node_grads, groups),
        [shape((rows_here, embed), BF16), shape((1, hidden), F32)],
        [SMEM, VMEM] + [VMEM] * groups,
        [pltpu.VMEM((groups, rows_here + EXTRA, wide), BF16)],
        flops=2 * rows_here * embed * hidden,
        nbytes=embed * hidden * 2 + rows_here * (embed + hidden) * 2,
        name="node_grads",
    )(ids, weight, *hid)
    joined = call(
        join_shares,
        shape((domains, share, hidden), BF16),
        [SMEM] + [VMEM] * half,
        nbytes=4 * narrow * hidden,
        name="join_shares",
    )(ids, *gathered).reshape(narrow, hidden)
    count = groups // 2

    def place(parts, masks, before=()):
        return call(
            functools.partial(place_weight, masks),
            out_shape=shape((embed, hidden), F32),
            specs=[SMEM] + [VMEM] * len(parts) + [pl.BlockSpec(memory_space=pl.ANY)] * len(before),
            scratch=[
                pltpu.VMEM((len(parts), narrow, hidden), F32),
                pltpu.SemaphoreType.DMA((len(parts), COPIES)),
            ],
            nbytes=embed * hidden * 3,
            name="place_weight",
            out_specs=pl.BlockSpec(memory_space=pl.ANY),
            aliases={len(parts) + 1: 0} if before else {},
        )(ids, *parts, *before)

    across = swap(joined, "grp", count)
    parts, masks = spread(joined, "grp", count // 2)
    grad_weight = place(parts, masks)
    across, grad_weight, grad_nodes = lax.optimization_barrier((across, grad_weight, grad_nodes))
    parts, masks = spread(across, "grp", count // 2)
    grad_weight = place([across], [count], [grad_weight])
    grad_weight = place(parts[1:], [mask + count for mask in masks[1:]], [grad_weight])
    return (activations, grad_nodes, grad_weight, grad_bias.reshape(hidden))


def solution(mesh):
    in_specs = (
        P(("dom", "grp"), None),
        P(),
        P(),
        P(("dom", "grp"), None),
        P(),
        P("dom", None, None),
        P("dom", None, None),
        P("dom", None),
        P(),
        P("dom", None, None),
        P("dom", None, None),
    )
    out_specs = (P(("dom", "grp"), None), P(("dom", "grp"), None), P(), P())
    return jax.shard_map(
        per_device, mesh=mesh, in_specs=in_specs, out_specs=out_specs, check_vma=False
    )
```

```python
import functools

import jax
import jax.numpy as jnp
from jax import lax
from jax.experimental import pallas as pl
from jax.experimental.pallas import tpu as pltpu
from jax.sharding import PartitionSpec as P

VMEM = pl.BlockSpec(memory_space=pltpu.VMEM)
SMEM = pl.BlockSpec(memory_space=pltpu.SMEM)
EXTRA = 16
COPIES = 4
F32 = jnp.float32
BF16 = jnp.bfloat16


def call(
    body, out_shape, specs, scratch=(), flops=0, nbytes=0, name=None, out_specs=None, aliases=(), mib=16
):
    return pl.pallas_call(
        body,
        out_shape=out_shape,
        in_specs=specs,
        out_specs=jax.tree.map(lambda _: VMEM, out_shape) if out_specs is None else out_specs,
        scratch_shapes=list(scratch),
        input_output_aliases=dict(aliases),
        compiler_params=pltpu.CompilerParams(vmem_limit_bytes=mib * 1024 * 1024),
        cost_estimate=pl.CostEstimate(flops=flops, bytes_accessed=nbytes, transcendentals=0),
        name=name,
    )


def shape(dims, kind):
    return jax.ShapeDtypeStruct(tuple(dims), kind)


def dot(a, b):
    return jnp.dot(a, b, preferred_element_type=F32)


def bias_rows(total):
    high = total.astype(BF16).astype(F32)
    rest = jnp.zeros((EXTRA - 2, total.shape[1]), F32)
    return jnp.concatenate([high, total - high, rest], axis=0).astype(BF16)


def aligned(start, step):
    return pl.ds(pl.multiple_of(start * step, step), step)


def swap(value, axis, mask):
    return lax.ppermute(value, axis, [(i, i ^ mask) for i in range(lax.axis_size(axis))])


def exchange(parts, axis):
    return list(parts[:1]) + [swap(part, axis, m) for m, part in enumerate(parts[1:], 1)]


def spread(value, axis, bit):
    parts, masks = [value], [0]
    while bit:
        parts = parts + [swap(part, axis, bit) for part in parts]
        masks = masks + [mask ^ bit for mask in masks]
        bit //= 2
    return parts, masks


def split_features(ids, feats, *refs):
    outs, sems = refs[:-1], refs[-1]
    group = ids[1]
    narrow = outs[0].shape[1]
    copies = [
        pltpu.make_async_copy(
            feats.at[:, aligned(jnp.bitwise_xor(group, m), narrow)], out, sems.at[m]
        )
        for m, out in enumerate(outs)
    ]
    for copy in copies:
        copy.start()
    for copy in copies:
        copy.wait()


def pick_blocks(groups, slots, at, tab, *refs):
    parts, (x, offered, *outs) = refs[:groups], refs[groups:]
    domain, group = tab[at["me"]], tab[at["me"] + 1]
    tile = x.shape[1]
    per = x.shape[0] // groups
    for m, part in enumerate(parts):
        owner = jnp.bitwise_xor(group, m)
        for j in range(per):
            x[owner * per + j] = part[j * tile : (j + 1) * tile]
    for j in range(offered.shape[0]):
        offered[j] = x[tab[at["pub"] + j]]
    for m, out in enumerate(outs, 1):
        reader = jnp.bitwise_xor(domain, m)
        for s in range(slots):
            entry = jnp.maximum(tab[at["out"] + reader * slots + s], 0)
            out[s * tile : (s + 1) * tile] = x[tab[at["pub"] + entry]]


def pick_relayed(slots, at, tab, offered, *outs):
    tile = offered.shape[1]
    for m, out in enumerate(outs, 1):
        reader = jnp.bitwise_xor(tab[at["me"]], m)
        for s in range(slots):
            entry = jnp.maximum(tab[at["out2"] + reader * slots + s], 0)
            out[s * tile : (s + 1) * tile] = offered[entry]


def local_sum(per_row, at, tab, bank, x, out):
    pair = 2 if per_row % 2 == 0 else 1

    @pl.loop(0, out.shape[0])
    def _(r):
        acc = jnp.zeros(out.shape[1:], F32)
        for k in range(0, per_row, pair):
            spots = [r * per_row + k + j for j in range(pair)]
            left = jnp.concatenate([bank[tab[at["banks"] + a]] for a in spots], axis=1)
            right = jnp.concatenate([x[tab[at["cols"] + a]] for a in spots], axis=0)
            acc += dot(left, right)
        out[r] = acc


def halo_adder(slots, at, tab, bank, acc):
    def add(source, get):
        for s in range(slots):
            i = source * slots + s
            entry = tab[at["in"] + i]

            @pl.when(entry >= 0)
            def _(i=i, s=s, entry=entry):
                acc[tab[at["hrows"] + i]] += dot(bank[tab[at["hbanks"] + i]], get(s, entry))

    return add


def add_near(slots, at, tab, bank, local, mirrored, *refs):
    near, acc = refs[:-1], refs[-1]
    domain = tab[at["me"]]
    tile = local.shape[1]
    acc[...] = local[...]
    add = halo_adder(slots, at, tab, bank, acc)
    for m, block in enumerate(near, 1):
        add(jnp.bitwise_xor(domain, m), lambda s, _, block=block: block[s * tile : (s + 1) * tile])
    mirror = jnp.bitwise_xor(domain, len(near) + 1)
    add(mirror, lambda _, entry: mirrored[jnp.maximum(entry, 0)])


def add_far(half, groups, slots, at, tab, bank, local, *refs):
    far, outs, acc = refs[: half - 1], refs[half - 1 : -1], refs[-1]
    domain, group = tab[at["me"]], tab[at["me"] + 1]
    tile = local.shape[1]
    per = local.shape[0] // groups
    acc[...] = local[...]
    add = halo_adder(slots, at, tab, bank, acc)
    for m, block in enumerate(far, half + 1):
        add(jnp.bitwise_xor(domain, m), lambda s, _, block=block: block[s * tile : (s + 1) * tile])
    for m, out in enumerate(outs):
        owner = jnp.bitwise_xor(group, m)
        for j in range(per):
            out[j * tile : (j + 1) * tile] = acc[owner * per + j].astype(BF16)


def dense(groups, ids, weight, bias, cot, *refs):
    parts, (act, grad, *slices) = refs[:groups], refs[groups:]
    group = ids[1]
    narrow = parts[0].shape[1]
    wide = cot.shape[1] // groups
    left = jnp.concatenate([part[...] for part in parts], axis=1)
    spots = [aligned(jnp.bitwise_xor(group, m), narrow) for m in range(groups)]
    pre = dot(left, jnp.concatenate([weight[spot] for spot in spots], axis=0)) + bias[...]
    act[...] = jnp.maximum(pre, 0.0).astype(BF16)
    masked = jnp.where(pre > 0, cot[...].astype(F32), 0.0).astype(BF16)
    for s in range(groups):
        grad[s] = masked[:, s * wide : (s + 1) * wide]
    for m, out in enumerate(slices):
        out[...] = grad[jnp.bitwise_xor(group, m)]


def write_out(value, out):
    out[...] = value[...]


def back_halo(groups, slots, at, tab, bank_t, *refs):
    parts, (own, mine, kept, *terms) = refs[:groups], refs[groups:]
    domain, group = tab[at["me"]], tab[at["me"] + 1]
    tile = bank_t.shape[1]
    per = parts[0].shape[0] // tile
    half = len(terms) + 1
    total = jnp.zeros((1, own.shape[2]), F32)
    for m, part in enumerate(parts):
        owner = jnp.bitwise_xor(group, m)
        piece = part[...]
        total += jnp.sum(piece.astype(F32), axis=0, keepdims=True)
        for j in range(per):
            own[owner * per + j] = piece[j * tile : (j + 1) * tile]
    mine[...] = total
    tail = bias_rows(total)

    def put(out, place, source):
        for s in range(slots):
            i = source * slots + s
            live = (tab[at["in"] + i] >= 0).astype(F32)
            value = dot(bank_t[tab[at["hbanks"] + i]], own[tab[at["hrows"] + i]]) * live
            spot = (place * slots + s) * tile
            out[spot : spot + tile] = value.astype(BF16)

    for m, term in enumerate(terms, 1):
        peer = jnp.bitwise_xor(domain, m)
        put(term, 0, peer)
        put(term, 1, jnp.bitwise_xor(peer, half))
        term[2 * slots * tile :] = tail
    put(kept, 0, jnp.bitwise_xor(domain, half))


def sum_mirror(slots, at, tab, mine, kept, *refs):
    recv, out, acc = refs[:-2], refs[-2], refs[-1]
    domain = tab[at["me"]]
    offered, tile = acc.shape[:2]
    acc[...] = jnp.zeros_like(acc)
    total = mine[...]
    for m, block in enumerate((kept,) + recv):
        reader = jnp.bitwise_xor(domain, m)
        for s in range(slots):
            entry = tab[at["out2"] + reader * slots + s]
            spot = (s + (slots if m else 0)) * tile

            @pl.when(entry >= 0)
            def _(entry=entry, spot=spot, block=block):
                acc[jnp.maximum(entry, 0)] += block[spot : spot + tile].astype(F32)

        if m:
            tail = block[2 * slots * tile :].astype(F32)
            total += tail[0:1] + tail[1:2]
    for j in range(offered):
        out[j * tile : (j + 1) * tile] = acc[j].astype(BF16)
    out[offered * tile :] = bias_rows(total)


def weight_part(groups, *refs):
    aggs, (grad, send, keep) = refs[:groups], refs[groups:]
    right = jnp.concatenate([grad[s] for s in range(groups)], axis=1)
    for m, agg in enumerate(aggs):
        value = lax.dot_general(
            agg[...], right, (((0,), (0,)), ((), ())), preferred_element_type=F32
        )
        out = send if m % 2 else keep
        out[m // 2] = value.astype(out.dtype)


def fold(kept, recv, send, keep):
    for j in range(kept.shape[0]):
        out = send if j % 2 else keep
        out[j // 2] = (kept[j] + recv[j].astype(F32)).astype(out.dtype)


def weight_shares(ids, whole, recv, *refs):
    kept, *outs = refs[:-1]
    total = refs[-1]
    domain = ids[0]
    half = len(outs) + 1
    rows = total.shape[1]
    value = whole[0] + recv[0].astype(F32)
    for d in range(total.shape[0]):
        total[d] = value[d * rows : (d + 1) * rows]
    for m, out in enumerate([kept] + outs):
        peer = jnp.bitwise_xor(domain, m)
        out[0] = total[peer].astype(out.dtype)
        out[1] = total[jnp.bitwise_xor(peer, half)].astype(out.dtype)


def sum_half(kept, *refs):
    recv, out = refs[:-1], refs[-1]
    for i in range(2):
        total = kept[i]
        for block in recv:
            total += block[i].astype(F32)
        out[i] = total.astype(BF16)


def sum_both(scale, here, there, out):
    for i in range(2):
        out[i] = ((here[i].astype(F32) + there[1 - i].astype(F32)) * scale).astype(BF16)


def join_shares(ids, *refs):
    parts, out = refs[:-1], refs[-1]
    for m, part in enumerate(parts):
        owner = jnp.bitwise_xor(ids[0], m)
        out[owner] = part[0]
        out[jnp.bitwise_xor(owner, len(parts))] = part[1]


def back_local(per_row, at, tab, bank_t, own, out):
    out[...] = jnp.zeros_like(out)

    @pl.loop(0, own.shape[0])
    def _(r):
        right = own[r]
        for k in range(per_row):
            spot = r * per_row + k
            out[tab[at["cols"] + spot]] += dot(bank_t[tab[at["banks"] + spot]], right)


def finish_nodes(half, slots, scale, at, tab, local, mine, mirrored, *refs):
    recv, outs, acc = refs[: half - 1], refs[half - 1 : -1], refs[-1]
    groups = len(outs)
    domain, group = tab[at["me"]], tab[at["me"] + 1]
    tile = local.shape[1]
    per = local.shape[0] // groups
    offered = (mirrored.shape[0] - EXTRA) // tile
    acc[...] = local[...]
    tail = mirrored[offered * tile :].astype(F32)
    for j in range(offered):
        acc[tab[at["pub"] + j]] += mirrored[j * tile : (j + 1) * tile].astype(F32)
    for m, block in enumerate(recv, 1):
        tail += block[2 * slots * tile :].astype(F32)
        reader = jnp.bitwise_xor(domain, m)
        for s in range(slots):
            entry = tab[at["out"] + reader * slots + s]

            @pl.when(entry >= 0)
            def _(s=s, entry=entry, block=block):
                spot = tab[at["pub"] + jnp.maximum(entry, 0)]
                acc[spot] += block[s * tile : (s + 1) * tile].astype(F32)

    rows = bias_rows((mine[...] + tail[0:1] + tail[1:2]) * scale)
    for m, out in enumerate(outs):
        owner = jnp.bitwise_xor(group, m)
        for j in range(per):
            out[j * tile : (j + 1) * tile] = acc[owner * per + j].astype(BF16)
        out[per * tile :] = rows


def node_grads(groups, ids, weight, *refs):
    parts, (out, bias_out, hid) = refs[:groups], refs[groups:]
    group = ids[1]
    rows = out.shape[0]
    for m, part in enumerate(parts):
        hid[jnp.bitwise_xor(group, m)] = part[...]
    left = jnp.concatenate([hid[s, :rows] for s in range(groups)], axis=1)
    out[...] = lax.dot_general(
        left, weight[...], (((1,), (1,)), ((), ())), preferred_element_type=F32
    ).astype(BF16)
    tail = jnp.concatenate([hid[s, rows:] for s in range(groups)], axis=1).astype(F32)
    bias_out[...] = tail[0:1] + tail[1:2]


def place_weight(masks, ids, *refs):
    parts, (out, wide, sems) = refs[: len(masks)], refs[-3:]
    group = ids[1]
    rows = parts[0].shape[0]
    copies = []
    step = rows // COPIES
    for i, (mask, part) in enumerate(zip(masks, parts)):
        for j in range(COPIES):
            wide[i, j * step : (j + 1) * step] = part[j * step : (j + 1) * step].astype(F32)
            spot = out.at[aligned(jnp.bitwise_xor(group, mask) * COPIES + j, step)]
            piece = wide.at[i, pl.ds(j * step, step)]
            copies.append(pltpu.make_async_copy(piece, spot, sems.at[i, j]))
            copies[-1].start()
    for copy in copies:
        copy.wait()


def per_device(
    node_feats,
    weight,
    bias,
    cotangent,
    tile_bank,
    local_cols,
    local_banks,
    published,
    send_table,
    halo_rows,
    halo_banks,
):
    domains = lax.axis_size("dom")
    groups = lax.axis_size("grp")
    domain_index = lax.axis_index("dom")
    rows_here, embed = node_feats.shape
    hidden = weight.shape[1]
    tile = tile_bank.shape[1]
    slots = send_table.shape[2]
    per_row = local_cols.shape[2]
    part_rows = rows_here * groups
    blocks = part_rows // tile
    narrow = embed // groups
    wide = hidden // groups
    share = narrow // domains
    half = domains // 2
    peers = half - 1
    offers = published.shape[1]

    ids = jnp.stack([domain_index, lax.axis_index("grp")]).astype(jnp.int32)
    tables = {
        "cols": local_cols[0],
        "banks": local_banks[0],
        "pub": published[0],
        "out": lax.dynamic_index_in_dim(send_table, domain_index, 0, keepdims=False),
        "out2": lax.dynamic_index_in_dim(send_table, domain_index ^ half, 0, keepdims=False),
        "in": lax.dynamic_index_in_dim(send_table, domain_index, 1, keepdims=False),
        "hrows": halo_rows[0],
        "hbanks": halo_banks[0],
        "me": ids,
    }
    at, place = {}, 0
    for name, table in tables.items():
        at[name] = place
        place += table.size
    tab = jnp.concatenate([table.reshape(-1) for table in tables.values()])
    bank_t = jnp.swapaxes(tile_bank, 1, 2)

    feats = call(
        split_features,
        [shape((rows_here, narrow), BF16)] * groups,
        [SMEM, pl.BlockSpec(memory_space=pl.ANY)],
        [pltpu.SemaphoreType.DMA((groups,))],
        nbytes=4 * rows_here * embed,
        name="split_features",
    )(ids, node_feats)
    feats = exchange(feats, "grp")
    x, offered, *picked = call(
        functools.partial(pick_blocks, groups, slots, at),
        [shape((blocks, tile, narrow), BF16), shape((offers, tile, narrow), BF16)]
        + [shape((slots * tile, narrow), BF16)] * peers,
        [SMEM] + [VMEM] * groups,
        nbytes=4 * (peers * slots + blocks + offers) * tile * narrow,
        name="pick_blocks",
    )(tab, *feats)
    mirrored = swap(offered, "dom", half)
    near = exchange([None] + picked, "dom")[1:]
    local = call(
        functools.partial(local_sum, per_row, at),
        shape((blocks, tile, narrow), F32),
        [SMEM, VMEM, VMEM],
        flops=2 * blocks * per_row * tile * tile * narrow,
        nbytes=blocks * tile * narrow * 6,
        name="local_sum",
    )(tab, tile_bank, x)
    mirrored, local = lax.optimization_barrier((mirrored, local))
    relayed = call(
        functools.partial(pick_relayed, slots, at),
        [shape((slots * tile, narrow), BF16)] * peers,
        [SMEM, VMEM],
        nbytes=4 * peers * slots * tile * narrow,
        name="pick_relayed",
    )(tab, mirrored)
    far = exchange([None, *relayed], "dom")[1:]
    local = call(
        functools.partial(add_near, slots, at),
        shape((blocks, tile, narrow), F32),
        [SMEM, VMEM, VMEM, VMEM] + [VMEM] * peers,
        flops=2 * half * slots * tile * tile * narrow,
        nbytes=blocks * tile * narrow * 8,
        name="add_near",
    )(tab, tile_bank, local, mirrored, *near)
    far, local = lax.optimization_barrier((far, local))
    aggs = call(
        functools.partial(add_far, half, groups, slots, at),
        [shape((rows_here, narrow), BF16)] * groups,
        [SMEM, VMEM, VMEM] + [VMEM] * peers,
        [pltpu.VMEM((blocks, tile, narrow), F32)],
        flops=2 * half * slots * tile * tile * narrow,
        nbytes=blocks * tile * narrow * 8,
        name="add_far",
    )(tab, tile_bank, local, *far)
    mine = exchange(aggs, "grp")
    activations, grad, *grads = call(
        functools.partial(dense, groups),
        [shape((rows_here, hidden), BF16), shape((groups, rows_here, wide), BF16)]
        + [shape((rows_here, wide), BF16)] * groups,
        [SMEM] + [VMEM] * (3 + groups),
        flops=2 * rows_here * embed * hidden,
        nbytes=embed * hidden * 2 + rows_here * (embed + 4 * hidden) * 2,
        name="dense",
    )(ids, weight, bias.reshape(1, hidden), cotangent, *mine)
    grads = exchange(grads, "grp")
    activations, _ = lax.optimization_barrier((activations, grads))
    activations = call(
        write_out,
        shape((rows_here, hidden), BF16),
        [VMEM],
        nbytes=4 * rows_here * hidden,
        name="write_out",
    )(activations)
    norm_scale = float(rows_here * groups * domains) ** (-0.5)
    norm_scale = float(rows_here * groups * domains) ** (-0.5)
    send, keep = call(
        functools.partial(weight_part, groups),
        [
            shape((groups // 2, narrow, hidden), BF16),
            shape((groups // 2, narrow, hidden), F32),
        ],
        [VMEM] * (groups + 1),
        flops=2 * rows_here * embed * hidden,
        nbytes=rows_here * (embed + hidden) * 2 + embed * hidden * 3,
        name="weight_part",
    )(*mine, grad)
    recv = swap(send, "grp", 1)
    recv, grads = lax.optimization_barrier((recv, grads))
    bit = 2
    while bit < groups:
        count = groups // (2 * bit)
        send, keep = call(
            fold,
            [shape((count, narrow, hidden), BF16), shape((count, narrow, hidden), F32)],
            [VMEM, VMEM],
            nbytes=count * narrow * hidden * 18,
            name="fold",
        )(keep, recv)
        recv = swap(send, "grp", bit)
        bit *= 2
    tab_after, _ = lax.optimization_barrier((tab, send))
    own, bias_here, kept, *terms = call(
        functools.partial(back_halo, groups, slots, at),
        [
            shape((blocks, tile, wide), BF16),
            shape((1, wide), F32),
            shape((slots * tile, wide), BF16),
        ]
        + [shape((2 * slots * tile + EXTRA, wide), BF16)] * peers,
        [SMEM, VMEM] + [VMEM] * groups,
        flops=2 * domains * slots * tile * tile * wide,
        nbytes=(domains * slots + blocks) * tile * wide * 2,
        name="back_halo",
    )(tab_after, bank_t, *grads)
    terms = exchange([None] + terms, "dom")[1:]
    recv, terms[0] = lax.optimization_barrier((recv, terms[0]))
    kept_shares, *shares = call(
        weight_shares,
        [shape((2, share, hidden), F32)] + [shape((2, share, hidden), BF16)] * peers,
        [SMEM, VMEM, VMEM],
        [pltpu.VMEM((domains, share, hidden), F32)],
        nbytes=narrow * hidden * 8,
        name="weight_shares",
    )(ids, keep, recv)
    terms, _ = lax.optimization_barrier((terms, shares))
    shares = exchange([None] + shares, "dom")[1:]
    crossing = call(
        functools.partial(sum_mirror, slots, at),
        shape((offers * tile + EXTRA, wide), BF16),
        [SMEM] + [VMEM] * (2 + peers),
        [pltpu.VMEM((offers, tile, wide), F32)],
        nbytes=4 * domains * slots * tile * wide,
        name="sum_mirror",
    )(tab, bias_here, kept, *terms)
    returned = swap(crossing, "dom", half)
    shares, _, activations = lax.optimization_barrier((shares, crossing, activations))
    here = call(
        sum_half,
        shape((2, share, hidden), BF16),
        [VMEM] * half,
        nbytes=2 * half * share * hidden * 2,
        name="sum_half",
    )(kept_shares, *shares)
    there = swap(here, "dom", half)
    own, _ = lax.optimization_barrier((own, here))
    back = call(
        functools.partial(back_local, per_row, at),
        shape((blocks, tile, wide), F32),
        [SMEM, VMEM, VMEM],
        flops=2 * blocks * per_row * tile * tile * wide,
        nbytes=blocks * tile * wide * 6,
        name="back_local",
    )(tab, bank_t, own)
    there, back = lax.optimization_barrier((there, back))
    summed = call(
        functools.partial(sum_both, norm_scale),
        shape((2, share, hidden), BF16),
        [VMEM, VMEM],
        nbytes=6 * share * hidden * 2,
        name="sum_both",
    )(here, there)
    gathered = exchange([summed] * half, "dom")
    hid = call(
        functools.partial(finish_nodes, half, slots, norm_scale, at),
        [shape((rows_here + EXTRA, wide), BF16)] * groups,
        [SMEM, VMEM, VMEM, VMEM] + [VMEM] * peers,
        [pltpu.VMEM((blocks, tile, wide), F32)],
        nbytes=domains * slots * tile * wide * 2 + blocks * tile * wide * 6,
        name="finish_nodes",
    )(tab, back, bias_here, returned, *terms)
    hid = exchange(hid, "grp")
    gathered, hid = lax.optimization_barrier((gathered, hid))
    grad_nodes, grad_bias = call(
        functools.partial(node_grads, groups),
        [shape((rows_here, embed), BF16), shape((1, hidden), F32)],
        [SMEM, VMEM] + [VMEM] * groups,
        [pltpu.VMEM((groups, rows_here + EXTRA, wide), BF16)],
        flops=2 * rows_here * embed * hidden,
        nbytes=embed * hidden * 2 + rows_here * (embed + hidden) * 2,
        name="node_grads",
    )(ids, weight, *hid)
    joined = call(
        join_shares,
        shape((domains, share, hidden), BF16),
        [SMEM] + [VMEM] * half,
        nbytes=4 * narrow * hidden,
        name="join_shares",
    )(ids, *gathered).reshape(narrow, hidden)
    count = groups // 2

    def place(parts, masks, before=()):
        return call(
            functools.partial(place_weight, masks),
            out_shape=shape((embed, hidden), F32),
            specs=[SMEM] + [VMEM] * len(parts) + [pl.BlockSpec(memory_space=pl.ANY)] * len(before),
            scratch=[
                pltpu.VMEM((len(parts), narrow, hidden), F32),
                pltpu.SemaphoreType.DMA((len(parts), COPIES)),
            ],
            nbytes=embed * hidden * 3,
            name="place_weight",
            out_specs=pl.BlockSpec(memory_space=pl.ANY),
            aliases={len(parts) + 1: 0} if before else {},
        )(ids, *parts, *before)

    across = swap(joined, "grp", count)
    parts, masks = spread(joined, "grp", count // 2)
    grad_weight = place(parts, masks)
    across, grad_weight, grad_nodes = lax.optimization_barrier((across, grad_weight, grad_nodes))
    parts, masks = spread(across, "grp", count // 2)
    grad_weight = place([across], [count], [grad_weight])
    grad_weight = place(parts[1:], [mask + count for mask in masks[1:]], [grad_weight])
    return (activations, grad_nodes, grad_weight, grad_bias.reshape(hidden))


def solution(mesh):
    in_specs = (
        P(("dom", "grp"), None),
        P(),
        P(),
        P(("dom", "grp"), None),
        P(),
        P("dom", None, None),
        P("dom", None, None),
        P("dom", None),
        P(),
        P("dom", None, None),
        P("dom", None, None),
    )
    out_specs = (P(("dom", "grp"), None), P(("dom", "grp"), None), P(), P())
    return jax.shard_map(
        per_device, mesh=mesh, in_specs=in_specs, out_specs=out_specs, check_vma=False
    )
```

```python
import functools

import jax
import jax.numpy as jnp
from jax import lax
from jax.experimental import pallas as pl
from jax.experimental.pallas import tpu as pltpu
from jax.sharding import PartitionSpec as P

VMEM = pl.BlockSpec(memory_space=pltpu.VMEM)
SMEM = pl.BlockSpec(memory_space=pltpu.SMEM)
EXTRA = 16
COPIES = 4
F32 = jnp.float32
BF16 = jnp.bfloat16


def call(
    body, out_shape, specs, scratch=(), flops=0, nbytes=0, name=None, out_specs=None, aliases=(), mib=16
):
    return pl.pallas_call(
        body,
        out_shape=out_shape,
        in_specs=specs,
        out_specs=jax.tree.map(lambda _: VMEM, out_shape) if out_specs is None else out_specs,
        scratch_shapes=list(scratch),
        input_output_aliases=dict(aliases),
        compiler_params=pltpu.CompilerParams(vmem_limit_bytes=mib * 1024 * 1024),
        cost_estimate=pl.CostEstimate(flops=flops, bytes_accessed=nbytes, transcendentals=0),
        name=name,
    )


def shape(dims, kind):
    return jax.ShapeDtypeStruct(tuple(dims), kind)


def dot(a, b):
    return jnp.dot(a, b, preferred_element_type=F32)


def bias_rows(total):
    high = total.astype(BF16).astype(F32)
    rest = jnp.zeros((EXTRA - 2, total.shape[1]), F32)
    return jnp.concatenate([high, total - high, rest], axis=0).astype(BF16)


def aligned(start, step):
    return pl.ds(pl.multiple_of(start * step, step), step)


def swap(value, axis, mask):
    return lax.ppermute(value, axis, [(i, i ^ mask) for i in range(lax.axis_size(axis))])


def exchange(parts, axis):
    return list(parts[:1]) + [swap(part, axis, m) for m, part in enumerate(parts[1:], 1)]


def spread(value, axis, bit):
    parts, masks = [value], [0]
    while bit:
        parts = parts + [swap(part, axis, bit) for part in parts]
        masks = masks + [mask ^ bit for mask in masks]
        bit //= 2
    return parts, masks


def split_features(ids, feats, *refs):
    outs, sems = refs[:-1], refs[-1]
    group = ids[1]
    narrow = outs[0].shape[1]
    copies = [
        pltpu.make_async_copy(
            feats.at[:, aligned(jnp.bitwise_xor(group, m), narrow)], out, sems.at[m]
        )
        for m, out in enumerate(outs)
    ]
    for copy in copies:
        copy.start()
    for copy in copies:
        copy.wait()


def pick_blocks(groups, slots, at, tab, *refs):
    parts, (x, offered, *outs) = refs[:groups], refs[groups:]
    domain, group = tab[at["me"]], tab[at["me"] + 1]
    tile = x.shape[1]
    per = x.shape[0] // groups
    for m, part in zip(reversed(range(groups)), parts):
        owner = jnp.bitwise_xor(group, m)
        for j in range(per):
            x[owner * per + j] = part[j * tile : (j + 1) * tile]
    for j in range(offered.shape[0]):
        offered[j] = x[tab[at["pub"] + j]]
    for m, out in enumerate(outs, 1):
        reader = jnp.bitwise_xor(domain, m)
        for s in range(slots):
            entry = jnp.maximum(tab[at["out"] + reader * slots + s], 0)
            out[s * tile : (s + 1) * tile] = x[tab[at["pub"] + entry]]


def pick_relayed(slots, at, tab, offered, *outs):
    tile = offered.shape[1]
    for m, out in enumerate(outs, 1):
        reader = jnp.bitwise_xor(tab[at["me"]], m)
        for s in range(slots):
            entry = jnp.maximum(tab[at["out2"] + reader * slots + s], 0)
            out[s * tile : (s + 1) * tile] = offered[entry]


def local_sum(per_row, at, tab, bank, x, out):
    pair = 2 if per_row % 2 == 0 else 1

    @pl.loop(0, out.shape[0])
    def _(r):
        acc = jnp.zeros(out.shape[1:], F32)
        for k in range(0, per_row, pair):
            spots = [r * per_row + k + j for j in range(pair)]
            left = jnp.concatenate([bank[tab[at["banks"] + a]] for a in spots], axis=1)
            right = jnp.concatenate([x[tab[at["cols"] + a]] for a in spots], axis=0)
            acc += dot(left, right)
        out[r] = acc


def halo_adder(slots, at, tab, bank, acc):
    def add(source, get):
        for s in range(slots):
            i = source * slots + s
            entry = tab[at["in"] + i]

            @pl.when(entry >= 0)
            def _(i=i, s=s, entry=entry):
                acc[tab[at["hrows"] + i]] += dot(bank[tab[at["hbanks"] + i]], get(s, entry))

    return add


def add_near(slots, at, tab, bank, local, mirrored, *refs):
    near, acc = refs[:-1], refs[-1]
    domain = tab[at["me"]]
    tile = local.shape[1]
    acc[...] = local[...]
    add = halo_adder(slots, at, tab, bank, acc)
    for m, block in enumerate(near, 1):
        add(jnp.bitwise_xor(domain, m), lambda s, _, block=block: block[s * tile : (s + 1) * tile])
    mirror = jnp.bitwise_xor(domain, len(near) + 1)
    add(mirror, lambda _, entry: mirrored[jnp.maximum(entry, 0)])


def add_far(half, groups, slots, at, tab, bank, local, *refs):
    far, outs, acc = refs[: half - 1], refs[half - 1 : -1], refs[-1]
    domain, group = tab[at["me"]], tab[at["me"] + 1]
    tile = local.shape[1]
    per = local.shape[0] // groups
    acc[...] = local[...]
    add = halo_adder(slots, at, tab, bank, acc)
    for m, block in enumerate(far, half + 1):
        add(jnp.bitwise_xor(domain, m), lambda s, _, block=block: block[s * tile : (s + 1) * tile])
    for m, out in enumerate(outs):
        owner = jnp.bitwise_xor(group, m)
        for j in range(per):
            out[j * tile : (j + 1) * tile] = acc[owner * per + j].astype(BF16)


def dense(groups, ids, weight, bias, cot, *refs):
    parts, (act, grad, *slices) = refs[:groups], refs[groups:]
    group = ids[1]
    narrow = parts[0].shape[1]
    wide = cot.shape[1] // groups
    left = jnp.concatenate([part[...] for part in parts], axis=1)
    spots = [aligned(jnp.bitwise_xor(group, m), narrow) for m in range(groups)]
    pre = dot(left, jnp.concatenate([weight[spot] for spot in spots], axis=0)) + bias[...]
    act[...] = jnp.maximum(pre, 0.0).astype(BF16)
    masked = jnp.where(pre > 0, cot[...].astype(F32), 0.0).astype(BF16)
    for s in range(groups):
        grad[s] = masked[:, s * wide : (s + 1) * wide]
    for m, out in enumerate(slices):
        out[...] = grad[jnp.bitwise_xor(group, m)]


def write_out(value, out):
    out[...] = value[...]


def back_halo(groups, slots, at, tab, bank_t, *refs):
    parts, (own, mine, kept, *terms) = refs[:groups], refs[groups:]
    domain, group = tab[at["me"]], tab[at["me"] + 1]
    tile = bank_t.shape[1]
    per = parts[0].shape[0] // tile
    half = len(terms) + 1
    total = jnp.zeros((1, own.shape[2]), F32)
    for m, part in enumerate(parts):
        owner = jnp.bitwise_xor(group, m)
        piece = part[...]
        total += jnp.sum(piece.astype(F32), axis=0, keepdims=True)
        for j in range(per):
            own[owner * per + j] = piece[j * tile : (j + 1) * tile]
    mine[...] = total
    tail = bias_rows(total)

    def put(out, place, source):
        for s in range(slots):
            i = source * slots + s
            live = (tab[at["in"] + i] >= 0).astype(F32)
            value = dot(bank_t[tab[at["hbanks"] + i]], own[tab[at["hrows"] + i]]) * live
            spot = (place * slots + s) * tile
            out[spot : spot + tile] = value.astype(BF16)

    for m, term in enumerate(terms, 1):
        peer = jnp.bitwise_xor(domain, m)
        put(term, 0, peer)
        put(term, 1, jnp.bitwise_xor(peer, half))
        term[2 * slots * tile :] = tail
    put(kept, 0, jnp.bitwise_xor(domain, half))


def sum_mirror(slots, at, tab, mine, kept, *refs):
    recv, out, acc = refs[:-2], refs[-2], refs[-1]
    domain = tab[at["me"]]
    offered, tile = acc.shape[:2]
    acc[...] = jnp.zeros_like(acc)
    total = mine[...]
    for m, block in enumerate((kept,) + recv):
        reader = jnp.bitwise_xor(domain, m)
        for s in range(slots):
            entry = tab[at["out2"] + reader * slots + s]
            spot = (s + (slots if m else 0)) * tile

            @pl.when(entry >= 0)
            def _(entry=entry, spot=spot, block=block):
                acc[jnp.maximum(entry, 0)] += block[spot : spot + tile].astype(F32)

        if m:
            tail = block[2 * slots * tile :].astype(F32)
            total += tail[0:1] + tail[1:2]
    for j in range(offered):
        out[j * tile : (j + 1) * tile] = acc[j].astype(BF16)
    out[offered * tile :] = bias_rows(total)


def weight_part(groups, *refs):
    aggs, (grad, send, keep) = refs[:groups], refs[groups:]
    right = jnp.concatenate([grad[s] for s in range(groups)], axis=1)
    for m, agg in enumerate(aggs):
        value = lax.dot_general(
            agg[...], right, (((0,), (0,)), ((), ())), preferred_element_type=F32
        )
        out = send if m % 2 else keep
        out[m // 2] = value.astype(out.dtype)


def fold(kept, recv, send, keep):
    for j in range(kept.shape[0]):
        out = send if j % 2 else keep
        out[j // 2] = (kept[j] + recv[j].astype(F32)).astype(out.dtype)


def weight_shares(ids, whole, recv, *refs):
    kept, *outs = refs[:-1]
    total = refs[-1]
    domain = ids[0]
    half = len(outs) + 1
    rows = total.shape[1]
    value = whole[0] + recv[0].astype(F32)
    for d in range(total.shape[0]):
        total[d] = value[d * rows : (d + 1) * rows]
    for m, out in enumerate([kept] + outs):
        peer = jnp.bitwise_xor(domain, m)
        out[0] = total[peer].astype(out.dtype)
        out[1] = total[jnp.bitwise_xor(peer, half)].astype(out.dtype)


def sum_half(kept, *refs):
    recv, out = refs[:-1], refs[-1]
    for i in range(2):
        total = kept[i]
        for block in recv:
            total += block[i].astype(F32)
        out[i] = total.astype(BF16)


def sum_both(scale, here, there, out):
    for i in range(2):
        out[i] = ((here[i].astype(F32) + there[1 - i].astype(F32)) * scale).astype(BF16)


def join_shares(ids, *refs):
    parts, out = refs[:-1], refs[-1]
    for m, part in enumerate(parts):
        owner = jnp.bitwise_xor(ids[0], m)
        out[owner] = part[0]
        out[jnp.bitwise_xor(owner, len(parts))] = part[1]


def back_local(per_row, at, tab, bank_t, own, out):
    out[...] = jnp.zeros_like(out)

    @pl.loop(0, own.shape[0])
    def _(r):
        right = own[r]
        for k in range(per_row):
            spot = r * per_row + k
            out[tab[at["cols"] + spot]] += dot(bank_t[tab[at["banks"] + spot]], right)


def finish_nodes(half, slots, scale, at, tab, local, mine, mirrored, *refs):
    recv, outs, acc = refs[: half - 1], refs[half - 1 : -1], refs[-1]
    groups = len(outs)
    domain, group = tab[at["me"]], tab[at["me"] + 1]
    tile = local.shape[1]
    per = local.shape[0] // groups
    offered = (mirrored.shape[0] - EXTRA) // tile
    acc[...] = local[...]
    tail = mirrored[offered * tile :].astype(F32)
    for j in range(offered):
        acc[tab[at["pub"] + j]] += mirrored[j * tile : (j + 1) * tile].astype(F32)
    for m, block in enumerate(recv, 1):
        tail += block[2 * slots * tile :].astype(F32)
        reader = jnp.bitwise_xor(domain, m)
        for s in range(slots):
            entry = tab[at["out"] + reader * slots + s]

            @pl.when(entry >= 0)
            def _(s=s, entry=entry, block=block):
                spot = tab[at["pub"] + jnp.maximum(entry, 0)]
                acc[spot] += block[s * tile : (s + 1) * tile].astype(F32)

    rows = bias_rows((mine[...] + tail[0:1] + tail[1:2]) * scale)
    for m, out in enumerate(outs):
        owner = jnp.bitwise_xor(group, m)
        for j in range(per):
            out[j * tile : (j + 1) * tile] = acc[owner * per + j].astype(BF16)
        out[per * tile :] = rows


def node_grads(groups, ids, weight, *refs):
    parts, (out, bias_out, hid) = refs[:groups], refs[groups:]
    group = ids[1]
    rows = out.shape[0]
    for m, part in enumerate(parts):
        hid[jnp.bitwise_xor(group, m)] = part[...]
    left = jnp.concatenate([hid[s, :rows] for s in range(groups)], axis=1)
    out[...] = lax.dot_general(
        left, weight[...], (((1,), (1,)), ((), ())), preferred_element_type=F32
    ).astype(BF16)
    tail = jnp.concatenate([hid[s, rows:] for s in range(groups)], axis=1).astype(F32)
    bias_out[...] = tail[0:1] + tail[1:2]


def place_weight(masks, ids, *refs):
    parts, (out, wide, sems) = refs[: len(masks)], refs[-3:]
    group = ids[1]
    rows = parts[0].shape[0]
    copies = []
    step = rows // COPIES
    for i, (mask, part) in enumerate(zip(masks, parts)):
        for j in range(COPIES):
            wide[i, j * step : (j + 1) * step] = part[j * step : (j + 1) * step].astype(F32)
            spot = out.at[aligned(jnp.bitwise_xor(group, mask) * COPIES + j, step)]
            piece = wide.at[i, pl.ds(j * step, step)]
            copies.append(pltpu.make_async_copy(piece, spot, sems.at[i, j]))
            copies[-1].start()
    for copy in copies:
        copy.wait()


def per_device(
    node_feats,
    weight,
    bias,
    cotangent,
    tile_bank,
    local_cols,
    local_banks,
    published,
    send_table,
    halo_rows,
    halo_banks,
):
    domains = lax.axis_size("dom")
    groups = lax.axis_size("grp")
    domain_index = lax.axis_index("dom")
    rows_here, embed = node_feats.shape
    hidden = weight.shape[1]
    tile = tile_bank.shape[1]
    slots = send_table.shape[2]
    per_row = local_cols.shape[2]
    part_rows = rows_here * groups
    blocks = part_rows // tile
    narrow = embed // groups
    wide = hidden // groups
    share = narrow // domains
    half = domains // 2
    peers = half - 1
    offers = published.shape[1]

    ids = jnp.stack([domain_index, lax.axis_index("grp")]).astype(jnp.int32)
    tables = {
        "cols": local_cols[0],
        "banks": local_banks[0],
        "pub": published[0],
        "out": lax.dynamic_index_in_dim(send_table, domain_index, 0, keepdims=False),
        "out2": lax.dynamic_index_in_dim(send_table, domain_index ^ half, 0, keepdims=False),
        "in": lax.dynamic_index_in_dim(send_table, domain_index, 1, keepdims=False),
        "hrows": halo_rows[0],
        "hbanks": halo_banks[0],
        "me": ids,
    }
    at, place = {}, 0
    for name, table in tables.items():
        at[name] = place
        place += table.size
    tab = jnp.concatenate([table.reshape(-1) for table in tables.values()])
    bank_t = jnp.swapaxes(tile_bank, 1, 2)

    feats = call(
        split_features,
        [shape((rows_here, narrow), BF16)] * groups,
        [SMEM, pl.BlockSpec(memory_space=pl.ANY)],
        [pltpu.SemaphoreType.DMA((groups,))],
        nbytes=4 * rows_here * embed,
        name="split_features",
    )(ids, node_feats)
    feats = exchange(feats, "grp")
    x, offered, *picked = call(
        functools.partial(pick_blocks, groups, slots, at),
        [shape((blocks, tile, narrow), BF16), shape((offers, tile, narrow), BF16)]
        + [shape((slots * tile, narrow), BF16)] * peers,
        [SMEM] + [VMEM] * groups,
        nbytes=4 * (peers * slots + blocks + offers) * tile * narrow,
        name="pick_blocks",
    )(tab, *reversed(feats))
    mirrored = swap(offered, "dom", half)
    near = exchange([None] + picked, "dom")[1:]
    local = call(
        functools.partial(local_sum, per_row, at),
        shape((blocks, tile, narrow), F32),
        [SMEM, VMEM, VMEM],
        flops=2 * blocks * per_row * tile * tile * narrow,
        nbytes=blocks * tile * narrow * 6,
        name="local_sum",
    )(tab, tile_bank, x)
    mirrored, local = lax.optimization_barrier((mirrored, local))
    relayed = call(
        functools.partial(pick_relayed, slots, at),
        [shape((slots * tile, narrow), BF16)] * peers,
        [SMEM, VMEM],
        nbytes=4 * peers * slots * tile * narrow,
        name="pick_relayed",
    )(tab, mirrored)
    far = exchange([None, *relayed], "dom")[1:]
    local = call(
        functools.partial(add_near, slots, at),
        shape((blocks, tile, narrow), F32),
        [SMEM, VMEM, VMEM, VMEM] + [VMEM] * peers,
        flops=2 * half * slots * tile * tile * narrow,
        nbytes=blocks * tile * narrow * 8,
        name="add_near",
    )(tab, tile_bank, local, mirrored, *near)
    far, local = lax.optimization_barrier((far, local))
    aggs = call(
        functools.partial(add_far, half, groups, slots, at),
        [shape((rows_here, narrow), BF16)] * groups,
        [SMEM, VMEM, VMEM] + [VMEM] * peers,
        [pltpu.VMEM((blocks, tile, narrow), F32)],
        flops=2 * half * slots * tile * tile * narrow,
        nbytes=blocks * tile * narrow * 8,
        name="add_far",
    )(tab, tile_bank, local, *far)
    mine = exchange(aggs, "grp")
    activations, grad, *grads = call(
        functools.partial(dense, groups),
        [shape((rows_here, hidden), BF16), shape((groups, rows_here, wide), BF16)]
        + [shape((rows_here, wide), BF16)] * groups,
        [SMEM] + [VMEM] * (3 + groups),
        flops=2 * rows_here * embed * hidden,
        nbytes=embed * hidden * 2 + rows_here * (embed + 4 * hidden) * 2,
        name="dense",
    )(ids, weight, bias.reshape(1, hidden), cotangent, *mine)
    grads = exchange(grads, "grp")
    activations = call(
        write_out,
        shape((rows_here, hidden), BF16),
        [VMEM],
        nbytes=4 * rows_here * hidden,
        name="write_out",
    )(activations)
    norm_scale = float(rows_here * groups * domains) ** (-0.5)
    norm_scale = float(rows_here * groups * domains) ** (-0.5)
    send, keep = call(
        functools.partial(weight_part, groups),
        [
            shape((groups // 2, narrow, hidden), BF16),
            shape((groups // 2, narrow, hidden), F32),
        ],
        [VMEM] * (groups + 1),
        flops=2 * rows_here * embed * hidden,
        nbytes=rows_here * (embed + hidden) * 2 + embed * hidden * 3,
        name="weight_part",
    )(*mine, grad)
    recv = swap(send, "grp", 1)
    recv, grads, activations = lax.optimization_barrier((recv, grads, activations))
    bit = 2
    while bit < groups:
        count = groups // (2 * bit)
        send, keep = call(
            fold,
            [shape((count, narrow, hidden), BF16), shape((count, narrow, hidden), F32)],
            [VMEM, VMEM],
            nbytes=count * narrow * hidden * 18,
            name="fold",
        )(keep, recv)
        recv = swap(send, "grp", bit)
        bit *= 2
    tab_after, _ = lax.optimization_barrier((tab, send))
    own, bias_here, kept, *terms = call(
        functools.partial(back_halo, groups, slots, at),
        [
            shape((blocks, tile, wide), BF16),
            shape((1, wide), F32),
            shape((slots * tile, wide), BF16),
        ]
        + [shape((2 * slots * tile + EXTRA, wide), BF16)] * peers,
        [SMEM, VMEM] + [VMEM] * groups,
        flops=2 * domains * slots * tile * tile * wide,
        nbytes=(domains * slots + blocks) * tile * wide * 2,
        name="back_halo",
    )(tab_after, bank_t, *grads)
    terms = exchange([None] + terms, "dom")[1:]
    recv, terms[0] = lax.optimization_barrier((recv, terms[0]))
    kept_shares, *shares = call(
        weight_shares,
        [shape((2, share, hidden), F32)] + [shape((2, share, hidden), BF16)] * peers,
        [SMEM, VMEM, VMEM],
        [pltpu.VMEM((domains, share, hidden), F32)],
        nbytes=narrow * hidden * 8,
        name="weight_shares",
    )(ids, keep, recv)
    terms, _ = lax.optimization_barrier((terms, shares))
    shares = exchange([None] + shares, "dom")[1:]
    crossing = call(
        functools.partial(sum_mirror, slots, at),
        shape((offers * tile + EXTRA, wide), BF16),
        [SMEM] + [VMEM] * (2 + peers),
        [pltpu.VMEM((offers, tile, wide), F32)],
        nbytes=4 * domains * slots * tile * wide,
        name="sum_mirror",
    )(tab, bias_here, kept, *terms)
    returned = swap(crossing, "dom", half)
    shares, _ = lax.optimization_barrier((shares, crossing))
    here = call(
        sum_half,
        shape((2, share, hidden), BF16),
        [VMEM] * half,
        nbytes=2 * half * share * hidden * 2,
        name="sum_half",
    )(kept_shares, *shares)
    there = swap(here, "dom", half)
    own, _ = lax.optimization_barrier((own, here))
    back = call(
        functools.partial(back_local, per_row, at),
        shape((blocks, tile, wide), F32),
        [SMEM, VMEM, VMEM],
        flops=2 * blocks * per_row * tile * tile * wide,
        nbytes=blocks * tile * wide * 6,
        name="back_local",
    )(tab, bank_t, own)
    there, back = lax.optimization_barrier((there, back))
    summed = call(
        functools.partial(sum_both, norm_scale),
        shape((2, share, hidden), BF16),
        [VMEM, VMEM],
        nbytes=6 * share * hidden * 2,
        name="sum_both",
    )(here, there)
    gathered = exchange([summed] * half, "dom")
    hid = call(
        functools.partial(finish_nodes, half, slots, norm_scale, at),
        [shape((rows_here + EXTRA, wide), BF16)] * groups,
        [SMEM, VMEM, VMEM, VMEM] + [VMEM] * peers,
        [pltpu.VMEM((blocks, tile, wide), F32)],
        nbytes=domains * slots * tile * wide * 2 + blocks * tile * wide * 6,
        name="finish_nodes",
    )(tab, back, bias_here, returned, *terms)
    hid = exchange(hid, "grp")
    gathered, hid = lax.optimization_barrier((gathered, hid))
    grad_nodes, grad_bias = call(
        functools.partial(node_grads, groups),
        [shape((rows_here, embed), BF16), shape((1, hidden), F32)],
        [SMEM, VMEM] + [VMEM] * groups,
        [pltpu.VMEM((groups, rows_here + EXTRA, wide), BF16)],
        flops=2 * rows_here * embed * hidden,
        nbytes=embed * hidden * 2 + rows_here * (embed + hidden) * 2,
        name="node_grads",
    )(ids, weight, *hid)
    joined = call(
        join_shares,
        shape((domains, share, hidden), BF16),
        [SMEM] + [VMEM] * half,
        nbytes=4 * narrow * hidden,
        name="join_shares",
    )(ids, *gathered).reshape(narrow, hidden)
    count = groups // 2

    def place(parts, masks, before=()):
        return call(
            functools.partial(place_weight, masks),
            out_shape=shape((embed, hidden), F32),
            specs=[SMEM] + [VMEM] * len(parts) + [pl.BlockSpec(memory_space=pl.ANY)] * len(before),
            scratch=[
                pltpu.VMEM((len(parts), narrow, hidden), F32),
                pltpu.SemaphoreType.DMA((len(parts), COPIES)),
            ],
            nbytes=embed * hidden * 3,
            name="place_weight",
            out_specs=pl.BlockSpec(memory_space=pl.ANY),
            aliases={len(parts) + 1: 0} if before else {},
        )(ids, *parts, *before)

    across = swap(joined, "grp", count)
    parts, masks = spread(joined, "grp", count // 2)
    grad_weight = place(parts, masks)
    across, grad_weight, grad_nodes = lax.optimization_barrier((across, grad_weight, grad_nodes))
    parts, masks = spread(across, "grp", count // 2)
    grad_weight = place([across], [count], [grad_weight])
    grad_weight = place(parts[1:], [mask + count for mask in masks[1:]], [grad_weight])
    return (activations, grad_nodes, grad_weight, grad_bias.reshape(hidden))


def solution(mesh):
    in_specs = (
        P(("dom", "grp"), None),
        P(),
        P(),
        P(("dom", "grp"), None),
        P(),
        P("dom", None, None),
        P("dom", None, None),
        P("dom", None),
        P(),
        P("dom", None, None),
        P("dom", None, None),
    )
    out_specs = (P(("dom", "grp"), None), P(("dom", "grp"), None), P(), P())
    return jax.shard_map(
        per_device, mesh=mesh, in_specs=in_specs, out_specs=out_specs, check_vma=False
    )
```

```python
import functools

import jax
import jax.numpy as jnp
from jax import lax
from jax.experimental import pallas as pl
from jax.experimental.pallas import tpu as pltpu
from jax.sharding import PartitionSpec as P

VMEM = pl.BlockSpec(memory_space=pltpu.VMEM)
SMEM = pl.BlockSpec(memory_space=pltpu.SMEM)
EXTRA = 16
COPIES = 4
F32 = jnp.float32
BF16 = jnp.bfloat16


def call(
    body, out_shape, specs, scratch=(), flops=0, nbytes=0, name=None, out_specs=None, aliases=(), mib=16
):
    return pl.pallas_call(
        body,
        out_shape=out_shape,
        in_specs=specs,
        out_specs=jax.tree.map(lambda _: VMEM, out_shape) if out_specs is None else out_specs,
        scratch_shapes=list(scratch),
        input_output_aliases=dict(aliases),
        compiler_params=pltpu.CompilerParams(vmem_limit_bytes=mib * 1024 * 1024),
        cost_estimate=pl.CostEstimate(flops=flops, bytes_accessed=nbytes, transcendentals=0),
        name=name,
    )


def shape(dims, kind):
    return jax.ShapeDtypeStruct(tuple(dims), kind)


def dot(a, b):
    return jnp.dot(a, b, preferred_element_type=F32)


def bias_rows(total):
    high = total.astype(BF16).astype(F32)
    rest = jnp.zeros((EXTRA - 2, total.shape[1]), F32)
    return jnp.concatenate([high, total - high, rest], axis=0).astype(BF16)


def aligned(start, step):
    return pl.ds(pl.multiple_of(start * step, step), step)


def swap(value, axis, mask):
    return lax.ppermute(value, axis, [(i, i ^ mask) for i in range(lax.axis_size(axis))])


def exchange(parts, axis):
    return list(parts[:1]) + [swap(part, axis, m) for m, part in enumerate(parts[1:], 1)]


def spread(value, axis, bit):
    parts, masks = [value], [0]
    while bit:
        parts = parts + [swap(part, axis, bit) for part in parts]
        masks = masks + [mask ^ bit for mask in masks]
        bit //= 2
    return parts, masks


def split_features(ids, feats, *refs):
    outs, sems = refs[:-1], refs[-1]
    group = ids[1]
    narrow = outs[0].shape[1]
    copies = [
        pltpu.make_async_copy(
            feats.at[:, aligned(jnp.bitwise_xor(group, m), narrow)], out, sems.at[m]
        )
        for m, out in enumerate(outs)
    ]
    for copy in copies:
        copy.start()
    for copy in copies:
        copy.wait()


def pick_blocks(groups, slots, at, tab, *refs):
    parts, (x, offered, *outs) = refs[:groups], refs[groups:]
    domain, group = tab[at["me"]], tab[at["me"] + 1]
    tile = x.shape[1]
    per = x.shape[0] // groups
    for m, part in zip(reversed(range(groups)), parts):
        owner = jnp.bitwise_xor(group, m)
        for j in range(per):
            x[owner * per + j] = part[j * tile : (j + 1) * tile]
    for j in range(offered.shape[0]):
        offered[j] = x[tab[at["pub"] + j]]
    for m, out in enumerate(outs, 1):
        reader = jnp.bitwise_xor(domain, m)
        for s in range(slots):
            entry = jnp.maximum(tab[at["out"] + reader * slots + s], 0)
            out[s * tile : (s + 1) * tile] = x[tab[at["pub"] + entry]]


def pick_relayed(slots, at, tab, offered, *outs):
    tile = offered.shape[1]
    for m, out in enumerate(outs, 1):
        reader = jnp.bitwise_xor(tab[at["me"]], m)
        for s in range(slots):
            entry = jnp.maximum(tab[at["out2"] + reader * slots + s], 0)
            out[s * tile : (s + 1) * tile] = offered[entry]


def local_sum(per_row, at, tab, bank, x, out):
    pair = 2 if per_row % 2 == 0 else 1

    @pl.loop(0, out.shape[0])
    def _(r):
        acc = jnp.zeros(out.shape[1:], F32)
        for k in range(0, per_row, pair):
            spots = [r * per_row + k + j for j in range(pair)]
            left = jnp.concatenate([bank[tab[at["banks"] + a]] for a in spots], axis=1)
            right = jnp.concatenate([x[tab[at["cols"] + a]] for a in spots], axis=0)
            acc += dot(left, right)
        out[r] = acc


def halo_adder(slots, at, tab, bank, acc):
    def add(source, get):
        for s in range(slots):
            i = source * slots + s
            entry = tab[at["in"] + i]

            @pl.when(entry >= 0)
            def _(i=i, s=s, entry=entry):
                acc[tab[at["hrows"] + i]] += dot(bank[tab[at["hbanks"] + i]], get(s, entry))

    return add


def add_near(slots, at, tab, bank, local, mirrored, *refs):
    near, acc = refs[:-1], refs[-1]
    domain = tab[at["me"]]
    tile = local.shape[1]
    acc[...] = local[...]
    add = halo_adder(slots, at, tab, bank, acc)
    for m, block in enumerate(near, 1):
        add(jnp.bitwise_xor(domain, m), lambda s, _, block=block: block[s * tile : (s + 1) * tile])
    mirror = jnp.bitwise_xor(domain, len(near) + 1)
    add(mirror, lambda _, entry: mirrored[jnp.maximum(entry, 0)])


def add_far(half, groups, slots, at, tab, bank, local, *refs):
    far, outs, acc = refs[: half - 1], refs[half - 1 : -1], refs[-1]
    domain, group = tab[at["me"]], tab[at["me"] + 1]
    tile = local.shape[1]
    per = local.shape[0] // groups
    acc[...] = local[...]
    add = halo_adder(slots, at, tab, bank, acc)
    for m, block in zip(reversed(range(half + 1, 2 * half)), far):
        add(jnp.bitwise_xor(domain, m), lambda s, _, block=block: block[s * tile : (s + 1) * tile])
    for m, out in enumerate(outs):
        owner = jnp.bitwise_xor(group, m)
        for j in range(per):
            out[j * tile : (j + 1) * tile] = acc[owner * per + j].astype(BF16)


def dense(groups, ids, weight, bias, cot, *refs):
    parts, (act, grad, *slices) = refs[:groups], refs[groups:]
    group = ids[1]
    narrow = parts[0].shape[1]
    wide = cot.shape[1] // groups
    left = jnp.concatenate([part[...] for part in parts], axis=1)
    spots = [aligned(jnp.bitwise_xor(group, m), narrow) for m in range(groups)]
    pre = dot(left, jnp.concatenate([weight[spot] for spot in spots], axis=0)) + bias[...]
    act[...] = jnp.maximum(pre, 0.0).astype(BF16)
    masked = jnp.where(pre > 0, cot[...].astype(F32), 0.0).astype(BF16)
    for s in range(groups):
        grad[s] = masked[:, s * wide : (s + 1) * wide]
    for m, out in enumerate(slices):
        out[...] = grad[jnp.bitwise_xor(group, m)]


def write_out(value, out):
    out[...] = value[...]


def back_halo(groups, slots, at, tab, bank_t, *refs):
    parts, (own, mine, kept, *terms) = refs[:groups], refs[groups:]
    domain, group = tab[at["me"]], tab[at["me"] + 1]
    tile = bank_t.shape[1]
    per = parts[0].shape[0] // tile
    half = len(terms) + 1
    total = jnp.zeros((1, own.shape[2]), F32)
    for m, part in enumerate(parts):
        owner = jnp.bitwise_xor(group, m)
        piece = part[...]
        total += jnp.sum(piece.astype(F32), axis=0, keepdims=True)
        for j in range(per):
            own[owner * per + j] = piece[j * tile : (j + 1) * tile]
    mine[...] = total
    tail = bias_rows(total)

    def put(out, place, source):
        for s in range(slots):
            i = source * slots + s
            live = (tab[at["in"] + i] >= 0).astype(F32)
            value = dot(bank_t[tab[at["hbanks"] + i]], own[tab[at["hrows"] + i]]) * live
            spot = (place * slots + s) * tile
            out[spot : spot + tile] = value.astype(BF16)

    for m, term in enumerate(terms, 1):
        peer = jnp.bitwise_xor(domain, m)
        put(term, 0, peer)
        put(term, 1, jnp.bitwise_xor(peer, half))
        term[2 * slots * tile :] = tail
    put(kept, 0, jnp.bitwise_xor(domain, half))


def sum_mirror(slots, at, tab, mine, kept, *refs):
    recv, out, acc = refs[:-2], refs[-2], refs[-1]
    domain = tab[at["me"]]
    offered, tile = acc.shape[:2]
    acc[...] = jnp.zeros_like(acc)
    total = mine[...]
    for m, block in enumerate((kept,) + recv):
        reader = jnp.bitwise_xor(domain, m)
        for s in range(slots):
            entry = tab[at["out2"] + reader * slots + s]
            spot = (s + (slots if m else 0)) * tile

            @pl.when(entry >= 0)
            def _(entry=entry, spot=spot, block=block):
                acc[jnp.maximum(entry, 0)] += block[spot : spot + tile].astype(F32)

        if m:
            tail = block[2 * slots * tile :].astype(F32)
            total += tail[0:1] + tail[1:2]
    for j in range(offered):
        out[j * tile : (j + 1) * tile] = acc[j].astype(BF16)
    out[offered * tile :] = bias_rows(total)


def weight_part(groups, *refs):
    aggs, (grad, send, keep) = refs[:groups], refs[groups:]
    right = jnp.concatenate([grad[s] for s in range(groups)], axis=1)
    for m, agg in enumerate(aggs):
        value = lax.dot_general(
            agg[...], right, (((0,), (0,)), ((), ())), preferred_element_type=F32
        )
        out = send if m % 2 else keep
        out[m // 2] = value.astype(out.dtype)


def fold(kept, recv, send, keep):
    for j in range(kept.shape[0]):
        out = send if j % 2 else keep
        out[j // 2] = (kept[j] + recv[j].astype(F32)).astype(out.dtype)


def weight_shares(ids, whole, recv, *refs):
    kept, *outs = refs[:-1]
    total = refs[-1]
    domain = ids[0]
    half = len(outs) + 1
    rows = total.shape[1]
    value = whole[0] + recv[0].astype(F32)
    for d in range(total.shape[0]):
        total[d] = value[d * rows : (d + 1) * rows]
    for m, out in enumerate([kept] + outs):
        peer = jnp.bitwise_xor(domain, m)
        out[0] = total[peer].astype(out.dtype)
        out[1] = total[jnp.bitwise_xor(peer, half)].astype(out.dtype)


def sum_half(kept, *refs):
    recv, out = refs[:-1], refs[-1]
    for i in range(2):
        total = kept[i]
        for block in recv:
            total += block[i].astype(F32)
        out[i] = total.astype(BF16)


def sum_both(scale, here, there, out):
    for i in range(2):
        out[i] = ((here[i].astype(F32) + there[1 - i].astype(F32)) * scale).astype(BF16)


def join_shares(ids, *refs):
    parts, out = refs[:-1], refs[-1]
    for m, part in enumerate(parts):
        owner = jnp.bitwise_xor(ids[0], m)
        out[owner] = part[0]
        out[jnp.bitwise_xor(owner, len(parts))] = part[1]


def back_local(per_row, at, tab, bank_t, own, out):
    out[...] = jnp.zeros_like(out)

    @pl.loop(0, own.shape[0])
    def _(r):
        right = own[r]
        for k in range(per_row):
            spot = r * per_row + k
            out[tab[at["cols"] + spot]] += dot(bank_t[tab[at["banks"] + spot]], right)


def finish_nodes(half, slots, scale, at, tab, local, mine, mirrored, *refs):
    recv, outs, acc = refs[: half - 1], refs[half - 1 : -1], refs[-1]
    groups = len(outs)
    domain, group = tab[at["me"]], tab[at["me"] + 1]
    tile = local.shape[1]
    per = local.shape[0] // groups
    offered = (mirrored.shape[0] - EXTRA) // tile
    acc[...] = local[...]
    tail = mirrored[offered * tile :].astype(F32)
    for j in range(offered):
        acc[tab[at["pub"] + j]] += mirrored[j * tile : (j + 1) * tile].astype(F32)
    for m, block in enumerate(recv, 1):
        tail += block[2 * slots * tile :].astype(F32)
        reader = jnp.bitwise_xor(domain, m)
        for s in range(slots):
            entry = tab[at["out"] + reader * slots + s]

            @pl.when(entry >= 0)
            def _(s=s, entry=entry, block=block):
                spot = tab[at["pub"] + jnp.maximum(entry, 0)]
                acc[spot] += block[s * tile : (s + 1) * tile].astype(F32)

    rows = bias_rows((mine[...] + tail[0:1] + tail[1:2]) * scale)
    for m, out in enumerate(outs):
        owner = jnp.bitwise_xor(group, m)
        for j in range(per):
            out[j * tile : (j + 1) * tile] = acc[owner * per + j].astype(BF16)
        out[per * tile :] = rows


def node_grads(groups, ids, weight, *refs):
    parts, (out, bias_out, hid) = refs[:groups], refs[groups:]
    group = ids[1]
    rows = out.shape[0]
    for m, part in enumerate(parts):
        hid[jnp.bitwise_xor(group, m)] = part[...]
    left = jnp.concatenate([hid[s, :rows] for s in range(groups)], axis=1)
    out[...] = lax.dot_general(
        left, weight[...], (((1,), (1,)), ((), ())), preferred_element_type=F32
    ).astype(BF16)
    tail = jnp.concatenate([hid[s, rows:] for s in range(groups)], axis=1).astype(F32)
    bias_out[...] = tail[0:1] + tail[1:2]


def place_weight(masks, ids, *refs):
    parts, (out, wide, sems) = refs[: len(masks)], refs[-3:]
    group = ids[1]
    rows = parts[0].shape[0]
    copies = []
    step = rows // COPIES
    for i, (mask, part) in enumerate(zip(masks, parts)):
        for j in range(COPIES):
            wide[i, j * step : (j + 1) * step] = part[j * step : (j + 1) * step].astype(F32)
            spot = out.at[aligned(jnp.bitwise_xor(group, mask) * COPIES + j, step)]
            piece = wide.at[i, pl.ds(j * step, step)]
            copies.append(pltpu.make_async_copy(piece, spot, sems.at[i, j]))
            copies[-1].start()
    for copy in copies:
        copy.wait()


def per_device(
    node_feats,
    weight,
    bias,
    cotangent,
    tile_bank,
    local_cols,
    local_banks,
    published,
    send_table,
    halo_rows,
    halo_banks,
):
    domains = lax.axis_size("dom")
    groups = lax.axis_size("grp")
    domain_index = lax.axis_index("dom")
    rows_here, embed = node_feats.shape
    hidden = weight.shape[1]
    tile = tile_bank.shape[1]
    slots = send_table.shape[2]
    per_row = local_cols.shape[2]
    part_rows = rows_here * groups
    blocks = part_rows // tile
    narrow = embed // groups
    wide = hidden // groups
    share = narrow // domains
    half = domains // 2
    peers = half - 1
    offers = published.shape[1]

    ids = jnp.stack([domain_index, lax.axis_index("grp")]).astype(jnp.int32)
    tables = {
        "cols": local_cols[0],
        "banks": local_banks[0],
        "pub": published[0],
        "out": lax.dynamic_index_in_dim(send_table, domain_index, 0, keepdims=False),
        "out2": lax.dynamic_index_in_dim(send_table, domain_index ^ half, 0, keepdims=False),
        "in": lax.dynamic_index_in_dim(send_table, domain_index, 1, keepdims=False),
        "hrows": halo_rows[0],
        "hbanks": halo_banks[0],
        "me": ids,
    }
    at, place = {}, 0
    for name, table in tables.items():
        at[name] = place
        place += table.size
    tab = jnp.concatenate([table.reshape(-1) for table in tables.values()])
    bank_t = jnp.swapaxes(tile_bank, 1, 2)

    feats = call(
        split_features,
        [shape((rows_here, narrow), BF16)] * groups,
        [SMEM, pl.BlockSpec(memory_space=pl.ANY)],
        [pltpu.SemaphoreType.DMA((groups,))],
        nbytes=4 * rows_here * embed,
        name="split_features",
    )(ids, node_feats)
    feats = exchange(feats, "grp")
    x, offered, *picked = call(
        functools.partial(pick_blocks, groups, slots, at),
        [shape((blocks, tile, narrow), BF16), shape((offers, tile, narrow), BF16)]
        + [shape((slots * tile, narrow), BF16)] * peers,
        [SMEM] + [VMEM] * groups,
        nbytes=4 * (peers * slots + blocks + offers) * tile * narrow,
        name="pick_blocks",
    )(tab, *reversed(feats))
    mirrored = swap(offered, "dom", half)
    near = exchange([None] + picked, "dom")[1:]
    local = call(
        functools.partial(local_sum, per_row, at),
        shape((blocks, tile, narrow), F32),
        [SMEM, VMEM, VMEM],
        flops=2 * blocks * per_row * tile * tile * narrow,
        nbytes=blocks * tile * narrow * 6,
        name="local_sum",
    )(tab, tile_bank, x)
    mirrored, local = lax.optimization_barrier((mirrored, local))
    relayed = call(
        functools.partial(pick_relayed, slots, at),
        [shape((slots * tile, narrow), BF16)] * peers,
        [SMEM, VMEM],
        nbytes=4 * peers * slots * tile * narrow,
        name="pick_relayed",
    )(tab, mirrored)
    far = exchange([None, *relayed], "dom")[1:]
    local = call(
        functools.partial(add_near, slots, at),
        shape((blocks, tile, narrow), F32),
        [SMEM, VMEM, VMEM, VMEM] + [VMEM] * peers,
        flops=2 * half * slots * tile * tile * narrow,
        nbytes=blocks * tile * narrow * 8,
        name="add_near",
    )(tab, tile_bank, local, mirrored, *near)
    far, local = lax.optimization_barrier((far, local))
    aggs = call(
        functools.partial(add_far, half, groups, slots, at),
        [shape((rows_here, narrow), BF16)] * groups,
        [SMEM, VMEM, VMEM] + [VMEM] * peers,
        [pltpu.VMEM((blocks, tile, narrow), F32)],
        flops=2 * half * slots * tile * tile * narrow,
        nbytes=blocks * tile * narrow * 8,
        name="add_far",
    )(tab, tile_bank, local, *reversed(far))
    mine = exchange(aggs, "grp")
    activations, grad, *grads = call(
        functools.partial(dense, groups),
        [shape((rows_here, hidden), BF16), shape((groups, rows_here, wide), BF16)]
        + [shape((rows_here, wide), BF16)] * groups,
        [SMEM] + [VMEM] * (3 + groups),
        flops=2 * rows_here * embed * hidden,
        nbytes=embed * hidden * 2 + rows_here * (embed + 4 * hidden) * 2,
        name="dense",
    )(ids, weight, bias.reshape(1, hidden), cotangent, *mine)
    grads = exchange(grads, "grp")
    activations = call(
        write_out,
        shape((rows_here, hidden), BF16),
        [VMEM],
        nbytes=4 * rows_here * hidden,
        name="write_out",
    )(activations)
    norm_scale = float(rows_here * groups * domains) ** (-0.5)
    norm_scale = float(rows_here * groups * domains) ** (-0.5)
    send, keep = call(
        functools.partial(weight_part, groups),
        [
            shape((groups // 2, narrow, hidden), BF16),
            shape((groups // 2, narrow, hidden), F32),
        ],
        [VMEM] * (groups + 1),
        flops=2 * rows_here * embed * hidden,
        nbytes=rows_here * (embed + hidden) * 2 + embed * hidden * 3,
        name="weight_part",
    )(*mine, grad)
    recv = swap(send, "grp", 1)
    recv, grads, activations = lax.optimization_barrier((recv, grads, activations))
    bit = 2
    while bit < groups:
        count = groups // (2 * bit)
        send, keep = call(
            fold,
            [shape((count, narrow, hidden), BF16), shape((count, narrow, hidden), F32)],
            [VMEM, VMEM],
            nbytes=count * narrow * hidden * 18,
            name="fold",
        )(keep, recv)
        recv = swap(send, "grp", bit)
        bit *= 2
    tab_after, _ = lax.optimization_barrier((tab, send))
    own, bias_here, kept, *terms = call(
        functools.partial(back_halo, groups, slots, at),
        [
            shape((blocks, tile, wide), BF16),
            shape((1, wide), F32),
            shape((slots * tile, wide), BF16),
        ]
        + [shape((2 * slots * tile + EXTRA, wide), BF16)] * peers,
        [SMEM, VMEM] + [VMEM] * groups,
        flops=2 * domains * slots * tile * tile * wide,
        nbytes=(domains * slots + blocks) * tile * wide * 2,
        name="back_halo",
    )(tab_after, bank_t, *grads)
    terms = exchange([None] + terms, "dom")[1:]
    recv, terms[0] = lax.optimization_barrier((recv, terms[0]))
    kept_shares, *shares = call(
        weight_shares,
        [shape((2, share, hidden), F32)] + [shape((2, share, hidden), BF16)] * peers,
        [SMEM, VMEM, VMEM],
        [pltpu.VMEM((domains, share, hidden), F32)],
        nbytes=narrow * hidden * 8,
        name="weight_shares",
    )(ids, keep, recv)
    terms, _ = lax.optimization_barrier((terms, shares))
    shares = exchange([None] + shares, "dom")[1:]
    crossing = call(
        functools.partial(sum_mirror, slots, at),
        shape((offers * tile + EXTRA, wide), BF16),
        [SMEM] + [VMEM] * (2 + peers),
        [pltpu.VMEM((offers, tile, wide), F32)],
        nbytes=4 * domains * slots * tile * wide,
        name="sum_mirror",
    )(tab, bias_here, kept, *terms)
    returned = swap(crossing, "dom", half)
    shares, _ = lax.optimization_barrier((shares, crossing))
    here = call(
        sum_half,
        shape((2, share, hidden), BF16),
        [VMEM] * half,
        nbytes=2 * half * share * hidden * 2,
        name="sum_half",
    )(kept_shares, *reversed(shares))
    there = swap(here, "dom", half)
    own, _ = lax.optimization_barrier((own, here))
    back = call(
        functools.partial(back_local, per_row, at),
        shape((blocks, tile, wide), F32),
        [SMEM, VMEM, VMEM],
        flops=2 * blocks * per_row * tile * tile * wide,
        nbytes=blocks * tile * wide * 6,
        name="back_local",
    )(tab, bank_t, own)
    there, back = lax.optimization_barrier((there, back))
    summed = call(
        functools.partial(sum_both, norm_scale),
        shape((2, share, hidden), BF16),
        [VMEM, VMEM],
        nbytes=6 * share * hidden * 2,
        name="sum_both",
    )(here, there)
    gathered = exchange([summed] * half, "dom")
    hid = call(
        functools.partial(finish_nodes, half, slots, norm_scale, at),
        [shape((rows_here + EXTRA, wide), BF16)] * groups,
        [SMEM, VMEM, VMEM, VMEM] + [VMEM] * peers,
        [pltpu.VMEM((blocks, tile, wide), F32)],
        nbytes=domains * slots * tile * wide * 2 + blocks * tile * wide * 6,
        name="finish_nodes",
    )(tab, back, bias_here, returned, *terms)
    hid = exchange(hid, "grp")
    gathered, hid = lax.optimization_barrier((gathered, hid))
    grad_nodes, grad_bias = call(
        functools.partial(node_grads, groups),
        [shape((rows_here, embed), BF16), shape((1, hidden), F32)],
        [SMEM, VMEM] + [VMEM] * groups,
        [pltpu.VMEM((groups, rows_here + EXTRA, wide), BF16)],
        flops=2 * rows_here * embed * hidden,
        nbytes=embed * hidden * 2 + rows_here * (embed + hidden) * 2,
        name="node_grads",
    )(ids, weight, *hid)
    joined = call(
        join_shares,
        shape((domains, share, hidden), BF16),
        [SMEM] + [VMEM] * half,
        nbytes=4 * narrow * hidden,
        name="join_shares",
    )(ids, *gathered).reshape(narrow, hidden)
    count = groups // 2

    def place(parts, masks, before=()):
        return call(
            functools.partial(place_weight, masks),
            out_shape=shape((embed, hidden), F32),
            specs=[SMEM] + [VMEM] * len(parts) + [pl.BlockSpec(memory_space=pl.ANY)] * len(before),
            scratch=[
                pltpu.VMEM((len(parts), narrow, hidden), F32),
                pltpu.SemaphoreType.DMA((len(parts), COPIES)),
            ],
            nbytes=embed * hidden * 3,
            name="place_weight",
            out_specs=pl.BlockSpec(memory_space=pl.ANY),
            aliases={len(parts) + 1: 0} if before else {},
        )(ids, *parts, *before)

    across = swap(joined, "grp", count)
    parts, masks = spread(joined, "grp", count // 2)
    grad_weight = place(parts, masks)
    across, grad_weight, grad_nodes = lax.optimization_barrier((across, grad_weight, grad_nodes))
    parts, masks = spread(across, "grp", count // 2)
    grad_weight = place([across], [count], [grad_weight])
    grad_weight = place(parts[1:], [mask + count for mask in masks[1:]], [grad_weight])
    return (activations, grad_nodes, grad_weight, grad_bias.reshape(hidden))


def solution(mesh):
    in_specs = (
        P(("dom", "grp"), None),
        P(),
        P(),
        P(("dom", "grp"), None),
        P(),
        P("dom", None, None),
        P("dom", None, None),
        P("dom", None),
        P(),
        P("dom", None, None),
        P("dom", None, None),
    )
    out_specs = (P(("dom", "grp"), None), P(("dom", "grp"), None), P(), P())
    return jax.shard_map(
        per_device, mesh=mesh, in_specs=in_specs, out_specs=out_specs, check_vma=False
    )
```

```python
import functools

import jax
import jax.numpy as jnp
from jax import lax
from jax.experimental import pallas as pl
from jax.experimental.pallas import tpu as pltpu
from jax.sharding import PartitionSpec as P

VMEM = pl.BlockSpec(memory_space=pltpu.VMEM)
SMEM = pl.BlockSpec(memory_space=pltpu.SMEM)
EXTRA = 16
COPIES = 4
F32 = jnp.float32
BF16 = jnp.bfloat16


def call(
    body, out_shape, specs, scratch=(), flops=0, nbytes=0, name=None, out_specs=None, aliases=(), mib=16
):
    return pl.pallas_call(
        body,
        out_shape=out_shape,
        in_specs=specs,
        out_specs=jax.tree.map(lambda _: VMEM, out_shape) if out_specs is None else out_specs,
        scratch_shapes=list(scratch),
        input_output_aliases=dict(aliases),
        compiler_params=pltpu.CompilerParams(vmem_limit_bytes=mib * 1024 * 1024),
        cost_estimate=pl.CostEstimate(flops=flops, bytes_accessed=nbytes, transcendentals=0),
        name=name,
    )


def shape(dims, kind):
    return jax.ShapeDtypeStruct(tuple(dims), kind)


def dot(a, b):
    return jnp.dot(a, b, preferred_element_type=F32)


def bias_rows(total):
    high = total.astype(BF16).astype(F32)
    rest = jnp.zeros((EXTRA - 2, total.shape[1]), F32)
    return jnp.concatenate([high, total - high, rest], axis=0).astype(BF16)


def aligned(start, step):
    return pl.ds(pl.multiple_of(start * step, step), step)


def swap(value, axis, mask):
    return lax.ppermute(value, axis, [(i, i ^ mask) for i in range(lax.axis_size(axis))])


def exchange(parts, axis):
    return list(parts[:1]) + [swap(part, axis, m) for m, part in enumerate(parts[1:], 1)]


def spread(value, axis, bit):
    parts, masks = [value], [0]
    while bit:
        parts = parts + [swap(part, axis, bit) for part in parts]
        masks = masks + [mask ^ bit for mask in masks]
        bit //= 2
    return parts, masks


def split_features(ids, feats, *refs):
    outs, sems = refs[:-1], refs[-1]
    group = ids[1]
    narrow = outs[0].shape[1]
    copies = [
        pltpu.make_async_copy(
            feats.at[:, aligned(jnp.bitwise_xor(group, m), narrow)], out, sems.at[m]
        )
        for m, out in enumerate(outs)
    ]
    for copy in copies:
        copy.start()
    for copy in copies:
        copy.wait()


def pick_blocks(groups, slots, at, tab, *refs):
    parts, (x, offered, *outs) = refs[:groups], refs[groups:]
    domain, group = tab[at["me"]], tab[at["me"] + 1]
    tile = x.shape[1]
    per = x.shape[0] // groups
    for m, part in zip(reversed(range(groups)), parts):
        owner = jnp.bitwise_xor(group, m)
        for j in range(per):
            x[owner * per + j] = part[j * tile : (j + 1) * tile]
    for j in range(offered.shape[0]):
        offered[j] = x[tab[at["pub"] + j]]
    for m, out in enumerate(outs, 1):
        reader = jnp.bitwise_xor(domain, m)
        for s in range(slots):
            entry = jnp.maximum(tab[at["out"] + reader * slots + s], 0)
            out[s * tile : (s + 1) * tile] = x[tab[at["pub"] + entry]]


def pick_relayed(slots, at, tab, offered, *outs):
    tile = offered.shape[1]
    for m, out in enumerate(outs, 1):
        reader = jnp.bitwise_xor(tab[at["me"]], m)
        for s in range(slots):
            entry = jnp.maximum(tab[at["out2"] + reader * slots + s], 0)
            out[s * tile : (s + 1) * tile] = offered[entry]


def local_sum(per_row, at, tab, bank, x, out):
    pair = 2 if per_row % 2 == 0 else 1

    @pl.loop(0, out.shape[0])
    def _(r):
        acc = jnp.zeros(out.shape[1:], F32)
        for k in range(0, per_row, pair):
            spots = [r * per_row + k + j for j in range(pair)]
            left = jnp.concatenate([bank[tab[at["banks"] + a]] for a in spots], axis=1)
            right = jnp.concatenate([x[tab[at["cols"] + a]] for a in spots], axis=0)
            acc += dot(left, right)
        out[r] = acc


def halo_adder(slots, at, tab, bank, acc):
    def add(source, get):
        for s in range(slots):
            i = source * slots + s
            entry = tab[at["in"] + i]

            @pl.when(entry >= 0)
            def _(i=i, s=s, entry=entry):
                acc[tab[at["hrows"] + i]] += dot(bank[tab[at["hbanks"] + i]], get(s, entry))

    return add


def add_near(slots, at, tab, bank, local, mirrored, *refs):
    near, acc = refs[:-1], refs[-1]
    domain = tab[at["me"]]
    tile = local.shape[1]
    acc[...] = local[...]
    add = halo_adder(slots, at, tab, bank, acc)
    for m, block in enumerate(near, 1):
        add(jnp.bitwise_xor(domain, m), lambda s, _, block=block: block[s * tile : (s + 1) * tile])
    mirror = jnp.bitwise_xor(domain, len(near) + 1)
    add(mirror, lambda _, entry: mirrored[jnp.maximum(entry, 0)])


def add_far(half, groups, slots, at, tab, bank, local, *refs):
    far, outs, acc = refs[: half - 1], refs[half - 1 : -1], refs[-1]
    domain, group = tab[at["me"]], tab[at["me"] + 1]
    tile = local.shape[1]
    per = local.shape[0] // groups
    acc[...] = local[...]
    add = halo_adder(slots, at, tab, bank, acc)
    for m, block in enumerate(far, half + 1):
        add(jnp.bitwise_xor(domain, m), lambda s, _, block=block: block[s * tile : (s + 1) * tile])
    for m, out in enumerate(outs):
        owner = jnp.bitwise_xor(group, m)
        for j in range(per):
            out[j * tile : (j + 1) * tile] = acc[owner * per + j].astype(BF16)


def dense(groups, ids, weight, bias, cot, *refs):
    parts, (act, grad, *slices) = refs[:groups], refs[groups:]
    group = ids[1]
    narrow = parts[0].shape[1]
    wide = cot.shape[1] // groups
    left = jnp.concatenate([part[...] for part in parts], axis=1)
    spots = [aligned(jnp.bitwise_xor(group, m), narrow) for m in range(groups)]
    pre = dot(left, jnp.concatenate([weight[spot] for spot in spots], axis=0)) + bias[...]
    act[...] = jnp.maximum(pre, 0.0).astype(BF16)
    masked = jnp.where(pre > 0, cot[...].astype(F32), 0.0).astype(BF16)
    for s in range(groups):
        grad[s] = masked[:, s * wide : (s + 1) * wide]
    for m, out in enumerate(slices):
        out[...] = grad[jnp.bitwise_xor(group, m)]


def write_out(value, out):
    out[...] = value[...]


def back_halo(groups, slots, at, tab, bank_t, *refs):
    parts, (own, mine, kept, *terms) = refs[:groups], refs[groups:]
    domain, group = tab[at["me"]], tab[at["me"] + 1]
    tile = bank_t.shape[1]
    per = parts[0].shape[0] // tile
    half = len(terms) + 1
    total = jnp.zeros((1, own.shape[2]), F32)
    for m, part in enumerate(parts):
        owner = jnp.bitwise_xor(group, m)
        piece = part[...]
        total += jnp.sum(piece.astype(F32), axis=0, keepdims=True)
        for j in range(per):
            own[owner * per + j] = piece[j * tile : (j + 1) * tile]
    mine[...] = total
    tail = bias_rows(total)

    def put(out, place, source):
        for s in range(slots):
            i = source * slots + s
            live = (tab[at["in"] + i] >= 0).astype(F32)
            value = dot(bank_t[tab[at["hbanks"] + i]], own[tab[at["hrows"] + i]]) * live
            spot = (place * slots + s) * tile
            out[spot : spot + tile] = value.astype(BF16)

    for m, term in enumerate(terms, 1):
        peer = jnp.bitwise_xor(domain, m)
        put(term, 0, peer)
        put(term, 1, jnp.bitwise_xor(peer, half))
        term[2 * slots * tile :] = tail
    put(kept, 0, jnp.bitwise_xor(domain, half))


def sum_mirror(slots, at, tab, mine, kept, *refs):
    recv, out, acc = refs[:-2], refs[-2], refs[-1]
    domain = tab[at["me"]]
    offered, tile = acc.shape[:2]
    acc[...] = jnp.zeros_like(acc)
    total = mine[...]
    for m, block in enumerate((kept,) + recv):
        reader = jnp.bitwise_xor(domain, m)
        for s in range(slots):
            entry = tab[at["out2"] + reader * slots + s]
            spot = (s + (slots if m else 0)) * tile

            @pl.when(entry >= 0)
            def _(entry=entry, spot=spot, block=block):
                acc[jnp.maximum(entry, 0)] += block[spot : spot + tile].astype(F32)

        if m:
            tail = block[2 * slots * tile :].astype(F32)
            total += tail[0:1] + tail[1:2]
    for j in range(offered):
        out[j * tile : (j + 1) * tile] = acc[j].astype(BF16)
    out[offered * tile :] = bias_rows(total)


def weight_part(groups, *refs):
    aggs, (grad, send, keep) = refs[:groups], refs[groups:]
    right = jnp.concatenate([grad[s] for s in range(groups)], axis=1)
    for m, agg in enumerate(aggs):
        value = lax.dot_general(
            agg[...], right, (((0,), (0,)), ((), ())), preferred_element_type=F32
        )
        out = send if m % 2 else keep
        out[m // 2] = value.astype(out.dtype)


def fold(kept, recv, send, keep):
    for j in range(kept.shape[0]):
        out = send if j % 2 else keep
        out[j // 2] = (kept[j] + recv[j].astype(F32)).astype(out.dtype)


def weight_shares(ids, whole, recv, *refs):
    kept, *outs = refs[:-1]
    total = refs[-1]
    domain = ids[0]
    half = len(outs) + 1
    rows = total.shape[1]
    value = whole[0] + recv[0].astype(F32)
    for d in range(total.shape[0]):
        total[d] = value[d * rows : (d + 1) * rows]
    for m, out in enumerate([kept] + outs):
        peer = jnp.bitwise_xor(domain, m)
        out[0] = total[peer].astype(out.dtype)
        out[1] = total[jnp.bitwise_xor(peer, half)].astype(out.dtype)


def sum_half(kept, *refs):
    recv, out = refs[:-1], refs[-1]
    for i in range(2):
        total = kept[i]
        for block in recv:
            total += block[i].astype(F32)
        out[i] = total.astype(BF16)


def sum_both(scale, here, there, out):
    for i in range(2):
        out[i] = ((here[i].astype(F32) + there[1 - i].astype(F32)) * scale).astype(BF16)


def join_shares(ids, *refs):
    parts, out = refs[:-1], refs[-1]
    for m, part in zip(reversed(range(len(parts))), parts):
        owner = jnp.bitwise_xor(ids[0], m)
        out[owner] = part[0]
        out[jnp.bitwise_xor(owner, len(parts))] = part[1]


def back_local(per_row, at, tab, bank_t, own, out):
    out[...] = jnp.zeros_like(out)

    @pl.loop(0, own.shape[0])
    def _(r):
        right = own[r]
        for k in range(per_row):
            spot = r * per_row + k
            out[tab[at["cols"] + spot]] += dot(bank_t[tab[at["banks"] + spot]], right)


def finish_nodes(half, slots, scale, at, tab, local, mine, mirrored, *refs):
    recv, outs, acc = refs[: half - 1], refs[half - 1 : -1], refs[-1]
    groups = len(outs)
    domain, group = tab[at["me"]], tab[at["me"] + 1]
    tile = local.shape[1]
    per = local.shape[0] // groups
    offered = (mirrored.shape[0] - EXTRA) // tile
    acc[...] = local[...]
    tail = mirrored[offered * tile :].astype(F32)
    for j in range(offered):
        acc[tab[at["pub"] + j]] += mirrored[j * tile : (j + 1) * tile].astype(F32)
    for m, block in enumerate(recv, 1):
        tail += block[2 * slots * tile :].astype(F32)
        reader = jnp.bitwise_xor(domain, m)
        for s in range(slots):
            entry = tab[at["out"] + reader * slots + s]

            @pl.when(entry >= 0)
            def _(s=s, entry=entry, block=block):
                spot = tab[at["pub"] + jnp.maximum(entry, 0)]
                acc[spot] += block[s * tile : (s + 1) * tile].astype(F32)

    rows = bias_rows((mine[...] + tail[0:1] + tail[1:2]) * scale)
    for m, out in enumerate(outs):
        owner = jnp.bitwise_xor(group, m)
        for j in range(per):
            out[j * tile : (j + 1) * tile] = acc[owner * per + j].astype(BF16)
        out[per * tile :] = rows


def node_grads(groups, ids, weight, *refs):
    parts, (out, bias_out, hid) = refs[:groups], refs[groups:]
    group = ids[1]
    rows = out.shape[0]
    for m, part in enumerate(parts):
        hid[jnp.bitwise_xor(group, m)] = part[...]
    left = jnp.concatenate([hid[s, :rows] for s in range(groups)], axis=1)
    out[...] = lax.dot_general(
        left, weight[...], (((1,), (1,)), ((), ())), preferred_element_type=F32
    ).astype(BF16)
    tail = jnp.concatenate([hid[s, rows:] for s in range(groups)], axis=1).astype(F32)
    bias_out[...] = tail[0:1] + tail[1:2]


def place_weight(masks, ids, *refs):
    parts, (out, wide, sems) = refs[: len(masks)], refs[-3:]
    group = ids[1]
    rows = parts[0].shape[0]
    copies = []
    step = rows // COPIES
    for i, (mask, part) in enumerate(zip(masks, parts)):
        for j in range(COPIES):
            wide[i, j * step : (j + 1) * step] = part[j * step : (j + 1) * step].astype(F32)
            spot = out.at[aligned(jnp.bitwise_xor(group, mask) * COPIES + j, step)]
            piece = wide.at[i, pl.ds(j * step, step)]
            copies.append(pltpu.make_async_copy(piece, spot, sems.at[i, j]))
            copies[-1].start()
    for copy in copies:
        copy.wait()


def per_device(
    node_feats,
    weight,
    bias,
    cotangent,
    tile_bank,
    local_cols,
    local_banks,
    published,
    send_table,
    halo_rows,
    halo_banks,
):
    domains = lax.axis_size("dom")
    groups = lax.axis_size("grp")
    domain_index = lax.axis_index("dom")
    rows_here, embed = node_feats.shape
    hidden = weight.shape[1]
    tile = tile_bank.shape[1]
    slots = send_table.shape[2]
    per_row = local_cols.shape[2]
    part_rows = rows_here * groups
    blocks = part_rows // tile
    narrow = embed // groups
    wide = hidden // groups
    share = narrow // domains
    half = domains // 2
    peers = half - 1
    offers = published.shape[1]

    ids = jnp.stack([domain_index, lax.axis_index("grp")]).astype(jnp.int32)
    tables = {
        "cols": local_cols[0],
        "banks": local_banks[0],
        "pub": published[0],
        "out": lax.dynamic_index_in_dim(send_table, domain_index, 0, keepdims=False),
        "out2": lax.dynamic_index_in_dim(send_table, domain_index ^ half, 0, keepdims=False),
        "in": lax.dynamic_index_in_dim(send_table, domain_index, 1, keepdims=False),
        "hrows": halo_rows[0],
        "hbanks": halo_banks[0],
        "me": ids,
    }
    at, place = {}, 0
    for name, table in tables.items():
        at[name] = place
        place += table.size
    tab = jnp.concatenate([table.reshape(-1) for table in tables.values()])
    bank_t = jnp.swapaxes(tile_bank, 1, 2)

    feats = call(
        split_features,
        [shape((rows_here, narrow), BF16)] * groups,
        [SMEM, pl.BlockSpec(memory_space=pl.ANY)],
        [pltpu.SemaphoreType.DMA((groups,))],
        nbytes=4 * rows_here * embed,
        name="split_features",
    )(ids, node_feats)
    feats = exchange(feats, "grp")
    x, offered, *picked = call(
        functools.partial(pick_blocks, groups, slots, at),
        [shape((blocks, tile, narrow), BF16), shape((offers, tile, narrow), BF16)]
        + [shape((slots * tile, narrow), BF16)] * peers,
        [SMEM] + [VMEM] * groups,
        nbytes=4 * (peers * slots + blocks + offers) * tile * narrow,
        name="pick_blocks",
    )(tab, *reversed(feats))
    mirrored = swap(offered, "dom", half)
    near = exchange([None] + picked, "dom")[1:]
    local = call(
        functools.partial(local_sum, per_row, at),
        shape((blocks, tile, narrow), F32),
        [SMEM, VMEM, VMEM],
        flops=2 * blocks * per_row * tile * tile * narrow,
        nbytes=blocks * tile * narrow * 6,
        name="local_sum",
    )(tab, tile_bank, x)
    mirrored, local = lax.optimization_barrier((mirrored, local))
    relayed = call(
        functools.partial(pick_relayed, slots, at),
        [shape((slots * tile, narrow), BF16)] * peers,
        [SMEM, VMEM],
        nbytes=4 * peers * slots * tile * narrow,
        name="pick_relayed",
    )(tab, mirrored)
    far = exchange([None, *relayed], "dom")[1:]
    local = call(
        functools.partial(add_near, slots, at),
        shape((blocks, tile, narrow), F32),
        [SMEM, VMEM, VMEM, VMEM] + [VMEM] * peers,
        flops=2 * half * slots * tile * tile * narrow,
        nbytes=blocks * tile * narrow * 8,
        name="add_near",
    )(tab, tile_bank, local, mirrored, *near)
    far, local = lax.optimization_barrier((far, local))
    aggs = call(
        functools.partial(add_far, half, groups, slots, at),
        [shape((rows_here, narrow), BF16)] * groups,
        [SMEM, VMEM, VMEM] + [VMEM] * peers,
        [pltpu.VMEM((blocks, tile, narrow), F32)],
        flops=2 * half * slots * tile * tile * narrow,
        nbytes=blocks * tile * narrow * 8,
        name="add_far",
    )(tab, tile_bank, local, *far)
    mine = exchange(aggs, "grp")
    activations, grad, *grads = call(
        functools.partial(dense, groups),
        [shape((rows_here, hidden), BF16), shape((groups, rows_here, wide), BF16)]
        + [shape((rows_here, wide), BF16)] * groups,
        [SMEM] + [VMEM] * (3 + groups),
        flops=2 * rows_here * embed * hidden,
        nbytes=embed * hidden * 2 + rows_here * (embed + 4 * hidden) * 2,
        name="dense",
    )(ids, weight, bias.reshape(1, hidden), cotangent, *mine)
    grads = exchange(grads, "grp")
    activations = call(
        write_out,
        shape((rows_here, hidden), BF16),
        [VMEM],
        nbytes=4 * rows_here * hidden,
        name="write_out",
    )(activations)
    norm_scale = float(rows_here * groups * domains) ** (-0.5)
    norm_scale = float(rows_here * groups * domains) ** (-0.5)
    send, keep = call(
        functools.partial(weight_part, groups),
        [
            shape((groups // 2, narrow, hidden), BF16),
            shape((groups // 2, narrow, hidden), F32),
        ],
        [VMEM] * (groups + 1),
        flops=2 * rows_here * embed * hidden,
        nbytes=rows_here * (embed + hidden) * 2 + embed * hidden * 3,
        name="weight_part",
    )(*mine, grad)
    recv = swap(send, "grp", 1)
    recv, grads, activations = lax.optimization_barrier((recv, grads, activations))
    bit = 2
    while bit < groups:
        count = groups // (2 * bit)
        send, keep = call(
            fold,
            [shape((count, narrow, hidden), BF16), shape((count, narrow, hidden), F32)],
            [VMEM, VMEM],
            nbytes=count * narrow * hidden * 18,
            name="fold",
        )(keep, recv)
        recv = swap(send, "grp", bit)
        bit *= 2
    tab_after, _ = lax.optimization_barrier((tab, send))
    own, bias_here, kept, *terms = call(
        functools.partial(back_halo, groups, slots, at),
        [
            shape((blocks, tile, wide), BF16),
            shape((1, wide), F32),
            shape((slots * tile, wide), BF16),
        ]
        + [shape((2 * slots * tile + EXTRA, wide), BF16)] * peers,
        [SMEM, VMEM] + [VMEM] * groups,
        flops=2 * domains * slots * tile * tile * wide,
        nbytes=(domains * slots + blocks) * tile * wide * 2,
        name="back_halo",
    )(tab_after, bank_t, *grads)
    terms = exchange([None] + terms, "dom")[1:]
    recv, terms[0] = lax.optimization_barrier((recv, terms[0]))
    kept_shares, *shares = call(
        weight_shares,
        [shape((2, share, hidden), F32)] + [shape((2, share, hidden), BF16)] * peers,
        [SMEM, VMEM, VMEM],
        [pltpu.VMEM((domains, share, hidden), F32)],
        nbytes=narrow * hidden * 8,
        name="weight_shares",
    )(ids, keep, recv)
    terms, _ = lax.optimization_barrier((terms, shares))
    shares = exchange([None] + shares, "dom")[1:]
    crossing = call(
        functools.partial(sum_mirror, slots, at),
        shape((offers * tile + EXTRA, wide), BF16),
        [SMEM] + [VMEM] * (2 + peers),
        [pltpu.VMEM((offers, tile, wide), F32)],
        nbytes=4 * domains * slots * tile * wide,
        name="sum_mirror",
    )(tab, bias_here, kept, *terms)
    returned = swap(crossing, "dom", half)
    shares, _ = lax.optimization_barrier((shares, crossing))
    here = call(
        sum_half,
        shape((2, share, hidden), BF16),
        [VMEM] * half,
        nbytes=2 * half * share * hidden * 2,
        name="sum_half",
    )(kept_shares, *shares)
    there = swap(here, "dom", half)
    own, _ = lax.optimization_barrier((own, here))
    back = call(
        functools.partial(back_local, per_row, at),
        shape((blocks, tile, wide), F32),
        [SMEM, VMEM, VMEM],
        flops=2 * blocks * per_row * tile * tile * wide,
        nbytes=blocks * tile * wide * 6,
        name="back_local",
    )(tab, bank_t, own)
    there, back = lax.optimization_barrier((there, back))
    summed = call(
        functools.partial(sum_both, norm_scale),
        shape((2, share, hidden), BF16),
        [VMEM, VMEM],
        nbytes=6 * share * hidden * 2,
        name="sum_both",
    )(here, there)
    gathered = exchange([summed] * half, "dom")
    hid = call(
        functools.partial(finish_nodes, half, slots, norm_scale, at),
        [shape((rows_here + EXTRA, wide), BF16)] * groups,
        [SMEM, VMEM, VMEM, VMEM] + [VMEM] * peers,
        [pltpu.VMEM((blocks, tile, wide), F32)],
        nbytes=domains * slots * tile * wide * 2 + blocks * tile * wide * 6,
        name="finish_nodes",
    )(tab, back, bias_here, returned, *terms)
    hid = exchange(hid, "grp")
    gathered, hid = lax.optimization_barrier((gathered, hid))
    grad_nodes, grad_bias = call(
        functools.partial(node_grads, groups),
        [shape((rows_here, embed), BF16), shape((1, hidden), F32)],
        [SMEM, VMEM] + [VMEM] * groups,
        [pltpu.VMEM((groups, rows_here + EXTRA, wide), BF16)],
        flops=2 * rows_here * embed * hidden,
        nbytes=embed * hidden * 2 + rows_here * (embed + hidden) * 2,
        name="node_grads",
    )(ids, weight, *hid)
    joined = call(
        join_shares,
        shape((domains, share, hidden), BF16),
        [SMEM] + [VMEM] * half,
        nbytes=4 * narrow * hidden,
        name="join_shares",
    )(ids, *reversed(gathered)).reshape(narrow, hidden)
    count = groups // 2

    def place(parts, masks, before=()):
        return call(
            functools.partial(place_weight, masks),
            out_shape=shape((embed, hidden), F32),
            specs=[SMEM] + [VMEM] * len(parts) + [pl.BlockSpec(memory_space=pl.ANY)] * len(before),
            scratch=[
                pltpu.VMEM((len(parts), narrow, hidden), F32),
                pltpu.SemaphoreType.DMA((len(parts), COPIES)),
            ],
            nbytes=embed * hidden * 3,
            name="place_weight",
            out_specs=pl.BlockSpec(memory_space=pl.ANY),
            aliases={len(parts) + 1: 0} if before else {},
        )(ids, *parts, *before)

    across = swap(joined, "grp", count)
    parts, masks = spread(joined, "grp", count // 2)
    grad_weight = place(parts, masks)
    across, grad_weight, grad_nodes = lax.optimization_barrier((across, grad_weight, grad_nodes))
    parts, masks = spread(across, "grp", count // 2)
    grad_weight = place([across], [count], [grad_weight])
    grad_weight = place(parts[1:], [mask + count for mask in masks[1:]], [grad_weight])
    return (activations, grad_nodes, grad_weight, grad_bias.reshape(hidden))


def solution(mesh):
    in_specs = (
        P(("dom", "grp"), None),
        P(),
        P(),
        P(("dom", "grp"), None),
        P(),
        P("dom", None, None),
        P("dom", None, None),
        P("dom", None),
        P(),
        P("dom", None, None),
        P("dom", None, None),
    )
    out_specs = (P(("dom", "grp"), None), P(("dom", "grp"), None), P(), P())
    return jax.shard_map(
        per_device, mesh=mesh, in_specs=in_specs, out_specs=out_specs, check_vma=False
    )
```
